32 devices in a mesh: dp: 8 (over y, x, core), mp: 4 (over z).
Axes of the slice: x: 2, y: 2, z: 4, core: 2. Of those that a mesh axis runs over, the one named last changes fastest.
Arguments:
- block_input: bfloat16 [16384, 256], P(('dp', 'mp')), may hold values from -6 to 6
- memory: bfloat16 [45056, 256], P(('dp', 'mp')), may hold values from -6 to 6
- tok_lengths: int32 [8, 51], P('dp'), may hold values from 1 to 200, 2048 in all within a row
- frame_lengths: int32 [8, 51], P('dp'), may hold values from 1 to 600, 5632 in all within a row
- cotangent: bfloat16 [16384, 256], P(('dp', 'mp')), may hold values from -6 to 6
- norm_gain: float32 [3, 256], replicated, may hold values from 0.25 to 1.75
- norm_shift: float32 [3, 256], replicated, may hold values from -2 to 2
- self_weights: bfloat16 [3, 256, 256], P(None, None, 'mp'), may hold values from -0.375 to 0.375
- self_biases: float32 [2, 256], P(None, 'mp'), may hold values from -3 to 3
- self_output: bfloat16 [256, 256], P('mp'), may hold values from -1.5 to 1.5
- self_offset: float32 [256], replicated, may hold values from -2 to 2
- cross_weights: bfloat16 [3, 256, 256], P(None, None, 'mp'), may hold values from -0.375 to 0.375
- cross_biases: float32 [2, 256], P(None, 'mp'), may hold values from -3 to 3
- cross_output: bfloat16 [256, 256], P('mp'), may hold values from -2 to 2
- cross_offset: float32 [256], replicated, may hold values from -2 to 2
- inner_weight: bfloat16 [256, 2048], P(None, 'mp'), may hold values from -0.375 to 0.375
- inner_bias: float32 [2048], P('mp'), may hold values from -3 to 3
- outer_weight: bfloat16 [2048, 256], P('mp'), may hold values from -0.1875 to 0.1875
- outer_offset: float32 [256], replicated, may hold values from -2 to 2
Outputs:
- block_output: float32 [16384, 256], P(('dp', 'mp'))
- input_grad: float32 [16384, 256], P(('dp', 'mp'))
- memory_grad: float32 [45056, 256], P(('dp', 'mp'))
- norm_gain_grad: float32 [3, 256], replicated
- norm_shift_grad: float32 [3, 256], replicated
- self_weights_grad: float32 [3, 256, 256], P(None, None, 'mp')
- self_biases_grad: float32 [2, 256], P(None, 'mp')
- self_output_grad: float32 [256, 256], P('mp')
- self_offset_grad: float32 [256], replicated
- cross_weights_grad: float32 [3, 256, 256], P(None, None, 'mp')
- cross_biases_grad: float32 [2, 256], P(None, 'mp')
- cross_output_grad: float32 [256, 256], P('mp')
- cross_offset_grad: float32 [256], replicated
- inner_weight_grad: float32 [256, 2048], P(None, 'mp')
- inner_bias_grad: float32 [2048], P('mp')
- outer_weight_grad: float32 [2048, 256], P('mp')
- outer_offset_grad: float32 [256], replicated
The draws below stay inside these ranges and needn't reach their ends.
Inputs may be any that keep to these rules, and one draw needn't show every extreme that they name: `tok_lengths`: row g holds the lengths of the 51 transcripts packed in order into group g's 2048 token rows; they add up to 2048, and the longest is exactly 200. `frame_lengths`: row g holds the frame counts of the same 51 utterances, packed in order into group g's 5632 frames; they add up to 5632, and the largest is exactly 600.
All inputs are finite; a program needn't handle non-finite values.
Results may differ from the reference program's by a relative error of at most 0.022.
Values may be sent and summed in bfloat16 or wider, within the bound.
A program may use at most 128 MiB of HBM per device.

```python
import math
from functools import partial
import jax
import jax.numpy as jnp
import numpy as np
from jax import lax

D = 256
HEADS = 4
HEAD = 64
FF = 2048
LONGEST = 200
FRAME_MOST = 600
ROWS = 2048
UTT = 51
FRAMES_GRP = 5632
TOKENS = 16384
FRAMES = 45056
N_DP = 8


def shard_levels(stream_key, shape, pieces, smallest, high):
    loudness = 1.0
    for position, parts in pieces:
        steps = jax.random.uniform(jax.random.fold_in(jax.random.fold_in(stream_key, 6), position), (parts,), jnp.float32, smallest / len(pieces), high / len(pieces))
        loudness = loudness * jnp.repeat(jnp.exp(steps), shape[position] // parts).reshape((-1,) + (1,) * (len(shape) - 1 - position))
    return loudness


def profile(number_of, total, reach, lean):
    weights = [(1 << 20) // math.isqrt(grade ** lean) + 1 for grade in range(2, number_of + 1)]
    spare, counts = total - reach - (number_of - 1), [1] * (number_of - 1)
    while spare > 0:
        free = [i for i in range(number_of - 1) if counts[i] < reach]
        pool, remaining = sum([weights[i] for i in free]), spare
        for i in free:
            extra = min(reach - counts[i], max(1, remaining * weights[i] // pool), spare)
            counts[i] = counts[i] + extra
            spare = spare - extra
    return np.array([reach] + counts)


def uneven_parts(own_key, number_of, total, reach, skew):
    if number_of == 2:
        one = jax.random.randint(own_key, (), max(1, total - reach), min(reach, total - 1) + 1)
        return jnp.stack([one, total - one])
    tallies = jnp.asarray(profile(number_of, total, reach, skew), jnp.int32)
    twos = (number_of - 1) // 2
    giver, sink = tallies[1:1 + 2 * twos:2], tallies[2:2 + 2 * twos:2]
    margin = jnp.minimum(giver - 1, reach - sink)
    passed = jax.random.randint(jax.random.fold_in(own_key, 1), (twos,), 0, 1 << 20) % (margin + 1)
    tallies = tallies.at[1:1 + 2 * twos:2].set(giver - passed).at[2:2 + 2 * twos:2].set(sink + passed)
    return tallies[jax.random.permutation(jax.random.fold_in(own_key, 2), number_of)]


def normal_values(stream_key, dims, scale, limit, pieces=(), kind=jnp.bfloat16):
    values = jax.random.normal(stream_key, dims, jnp.float32) * scale
    if len(pieces) > 0:
        values = shard_levels(stream_key, dims, pieces, -0.22, 0.18) * values
    return jnp.clip(values, min=-limit, max=limit).astype(kind)


def setup_inputs(seed: int = 0) -> dict:
    seeds = jax.random.split(jax.random.key(seed), 20)
    return {
        "block_input": normal_values(seeds[0], (TOKENS, D), 1.0, 6.0, ((0, 32),)),
        "memory": normal_values(seeds[1], (FRAMES, D), 1.0, 6.0, ((0, 32),)),
        "tok_lengths": jax.vmap(lambda own: uneven_parts(own, UTT, ROWS, LONGEST, 2))(jax.random.split(seeds[2], N_DP)).reshape((N_DP, UTT)).astype(jnp.int32),
        "frame_lengths": jax.vmap(lambda own: uneven_parts(own, UTT, FRAMES_GRP, FRAME_MOST, 2))(jax.random.split(seeds[3], N_DP)).reshape((N_DP, UTT)).astype(jnp.int32),
        "cotangent": normal_values(seeds[4], (TOKENS, D), 1.0, 6.0, ((0, 32),)),
        "norm_gain": jnp.clip(1.0 + 0.15 * jax.random.normal(seeds[5], (3, D), jnp.float32), 0.25, 1.75),
        "norm_shift": normal_values(seeds[6], (3, D), 0.3, 2.0, (), jnp.float32),
        "self_weights": normal_values(seeds[7], (3, D, D), D ** -0.5, 0.375, ((2, 4),)),
        "self_biases": normal_values(seeds[8], (2, D), 0.5, 3.0, ((1, 4),), jnp.float32),
        "self_output": normal_values(seeds[9], (D, D), (D // 16) ** -0.5, 1.5, ((0, 4),)),
        "self_offset": normal_values(seeds[10], (D,), 0.3, 2.0, (), jnp.float32),
        "cross_weights": normal_values(seeds[11], (3, D, D), D ** -0.5, 0.375, ((2, 4),)),
        "cross_biases": normal_values(seeds[12], (2, D), 0.5, 3.0, ((1, 4),), jnp.float32),
        "cross_output": normal_values(seeds[13], (D, D), (D // 32) ** -0.5, 2.0, ((0, 4),)),
        "cross_offset": normal_values(seeds[14], (D,), 0.3, 2.0, (), jnp.float32),
        "inner_weight": normal_values(seeds[15], (D, FF), D ** -0.5, 0.375, ((1, 4),)),
        "inner_bias": normal_values(seeds[16], (FF,), 0.5, 3.0, ((0, 4),), jnp.float32),
        "outer_weight": normal_values(seeds[17], (FF, D), (FF // 2) ** -0.5, 0.1875, ((0, 4),)),
        "outer_offset": normal_values(seeds[18], (D,), 0.3, 2.0, (), jnp.float32),
    }


HIGHEST = lax.Precision.HIGHEST
NEGATIVE = -1e+30
EPSILON = 1e-05

@jax.custom_vjp
def low(v):
    return lax.optimization_barrier(v.astype(jnp.bfloat16)).astype(jnp.float32)

@jax.custom_vjp
def low_back(v):
    return v

def low_keep(v):
    return (low(v), None)

def low_pass(kept, grad):
    return (grad,)

def back_keep(v):
    return (v, None)

def back_low(kept, grad):
    return (low(grad),)
low.defvjp(low_keep, low_pass)
low_back.defvjp(back_keep, back_low)

def rounded(values):
    return low(low_back(values))

def product(left_side, right_side):
    return jnp.dot(left_side, right_side, precision=HIGHEST, preferred_element_type=jnp.float32)

def layer_norm(values, gain_row, shift_row):
    center = values - lax.optimization_barrier(jnp.mean(values, axis=-1, keepdims=True))
    spread = lax.optimization_barrier(jnp.mean(center * center, axis=-1, keepdims=True))
    return center * lax.rsqrt(spread + EPSILON) * gain_row + shift_row

def segments(lengths, row_count):
    boundary = jnp.cumsum(lengths)
    places = jnp.arange(row_count, dtype=jnp.int32)
    return lax.optimization_barrier(jnp.sum((places[:, None] >= boundary[None, :]).astype(jnp.int32), axis=1))

def attention(queries, key_rows, value_rows, query_segment, key_segment, causal):
    row_count = queries.shape[0]
    block_rows = min(512, row_count)
    blocks = row_count // block_rows
    factor = 1.0 / math.sqrt(HEAD)
    head_queries = queries.reshape(blocks, block_rows, HEADS, HEAD)
    head_keys = key_rows.reshape(-1, HEADS, HEAD)
    head_values = value_rows.reshape(-1, HEADS, HEAD)
    key_places = jnp.arange(key_rows.shape[0], dtype=jnp.int32)
    block_segments = query_segment.reshape(blocks, block_rows)
    block_places = jnp.arange(row_count, dtype=jnp.int32).reshape(blocks, block_rows)

    def one_block(inputs):
        block_query, segment_row, place_row = inputs
        scores = low_back(jnp.einsum('qhd,khd->hqk', block_query, head_keys, precision=HIGHEST) * factor)
        allowed = segment_row[:, None] == key_segment[None, :]
        if causal:
            allowed = allowed & (key_places[None, :] <= place_row[:, None])
        scores = jnp.where(allowed[None], scores, NEGATIVE)
        shares = jax.nn.softmax(scores, axis=-1)
        return jnp.einsum('hqk,khd->qhd', low(shares), head_values, precision=HIGHEST)
    attended = lax.map(jax.checkpoint(one_block), (head_queries, block_segments, block_places))
    return attended.reshape(row_count, HEADS * HEAD)

def apply_block(hidden_rows, memory_rows, weights, token_segment, frame_segment):
    norm_gain, norm_shift, self_weights, self_biases, self_output, self_offset, cross_weights, cross_biases, cross_output, cross_offset, inner_weight, inner_bias, outer_weight, outer_offset = weights
    normed = low(layer_norm(hidden_rows, norm_gain[0], norm_shift[0]))
    queries = rounded(product(normed, self_weights[0]) + self_biases[0])
    key_rows = rounded(product(normed, self_weights[1]))
    value_rows = rounded(product(normed, self_weights[2]) + self_biases[1])
    attended = rounded(attention(queries, key_rows, value_rows, token_segment, token_segment, True))
    after_self = hidden_rows + low_back(product(attended, self_output) + self_offset)
    normed = low(layer_norm(after_self, norm_gain[1], norm_shift[1]))
    queries = rounded(product(normed, cross_weights[0]) + cross_biases[0])
    key_rows = rounded(product(memory_rows, cross_weights[1]))
    value_rows = rounded(product(memory_rows, cross_weights[2]) + cross_biases[1])
    attended = rounded(attention(queries, key_rows, value_rows, token_segment, frame_segment, False))
    after_cross = after_self + low_back(product(attended, cross_output) + cross_offset)
    normed = low(layer_norm(after_cross, norm_gain[2], norm_shift[2]))
    before = low_back(product(normed, inner_weight) + inner_bias)
    active = low(jax.nn.gelu(before, approximate=True))
    return after_cross + low_back(product(active, outer_weight) + outer_offset)

def reference(block_input, memory, tok_lengths, frame_lengths, cotangent, norm_gain, norm_shift, self_weights, self_biases, self_output, self_offset, cross_weights, cross_biases, cross_output, cross_offset, inner_weight, inner_bias, outer_weight, outer_offset):
    weights = tuple((tensor.astype(jnp.float32) for tensor in (norm_gain, norm_shift, self_weights, self_biases, self_output, self_offset, cross_weights, cross_biases, cross_output, cross_offset, inner_weight, inner_bias, outer_weight, outer_offset)))
    groups = tok_lengths.shape[0]
    width = block_input.shape[1]
    states = block_input.astype(jnp.float32).reshape(groups, -1, width)
    memories = memory.astype(jnp.float32).reshape(groups, -1, width)
    cotangents = cotangent.astype(jnp.float32).reshape(groups, -1, width)

    def one_group(running, inputs):
        hidden_rows, memory_rows, cotangent_rows, token_row, frame_row = inputs
        token_segment = segments(token_row, hidden_rows.shape[0])
        frame_segment = segments(frame_row, memory_rows.shape[0])
        applied = partial(apply_block, token_segment=token_segment, frame_segment=frame_segment)
        output_rows, pullback = jax.vjp(applied, hidden_rows, memory_rows, weights)
        hidden_grad, memory_part, weight_grads = pullback(cotangent_rows)
        running = jax.tree.map(jnp.add, running, weight_grads)
        return (running, (output_rows, hidden_grad, memory_part))
    totals, (outputs, hidden_grads, memory_grads) = lax.scan(one_group, jax.tree.map(jnp.zeros_like, weights), (states, memories, cotangents, tok_lengths, frame_lengths))
    return (outputs.reshape(-1, width), hidden_grads.reshape(-1, width), memory_grads.reshape(-1, width), totals[0], totals[1], totals[2], totals[3], totals[4], totals[5], totals[6], totals[7], totals[8], totals[9], totals[10], totals[11], totals[12], totals[13])
```

```python
import functools
import math

import jax
import jax.numpy as jnp
from jax import lax
from jax.experimental import pallas as pl
from jax.experimental.pallas import tpu as pltpu
from jax.sharding import PartitionSpec as P

HEAD = 64
LONGEST = 200
NEGATIVE = -1e30
EPSILON = 1e-05
BLOCK = 128
CHUNK = 256
HALO = 256
F32 = jnp.float32
BF16 = jnp.bfloat16
GELU_A = math.sqrt(2.0 / math.pi)
GELU_B = 0.044715


def mm(a, b, ca=1, cb=0):
    return lax.dot_general(a, b, (((ca,), (cb,)), ((), ())), preferred_element_type=F32)


def normed(values):
    center = values - jnp.mean(values, axis=-1, keepdims=True)
    spread = jnp.mean(center * center, axis=-1, keepdims=True)
    scale = lax.rsqrt(spread + EPSILON)
    return center * scale, scale


def norm_back(grad, gain, xhat, scale):
    gn = grad * gain
    first = jnp.mean(gn, axis=-1, keepdims=True)
    second = jnp.mean(gn * xhat, axis=-1, keepdims=True)
    return (gn - first - xhat * second) * scale


def column_sums(values):
    return jnp.sum(values, axis=0, keepdims=True)


def head_stack(values):
    rows, width = values.shape
    lane = lax.broadcasted_iota(jnp.int32, (rows, width), 1) // HEAD
    zero = jnp.zeros_like(values)
    return jnp.concatenate([jnp.where(lane == h, values, zero) for h in range(width // HEAD)], axis=0)


def head_diagonal(values, heads):
    rows = values.shape[1] // heads
    return jnp.concatenate(
        [values[h * HEAD : (h + 1) * HEAD, h * rows : (h + 1) * rows] for h in range(heads)], axis=0
    )


def per_head(row, heads):
    return jnp.concatenate([row] * heads, axis=1)


def token_rows(tok_ref, frm_ref, base, count):
    place = lax.broadcasted_iota(jnp.int32, (1, count), 1) + base
    zero = jnp.zeros((1, count), jnp.int32)

    def step(u, carry):
        start, first_row, first_frame, end_frame = carry
        tokens, frames = tok_ref[0, u], frm_ref[0, u]
        end = start + tokens
        done = place >= end
        first_row = first_row + jnp.where(done, tokens, 0)
        first_frame = first_frame + jnp.where(done, frames, 0)
        end_frame = end_frame + jnp.where(place >= start, frames, 0)
        return end, first_row, first_frame, end_frame

    _, first_row, first_frame, end_frame = lax.fori_loop(
        0, tok_ref.shape[1], step, (jnp.int32(0), zero, zero, zero)
    )
    return place, first_row, first_frame, end_frame


def block_frames(tok_ref, frm_ref, base, count):
    blocks = count // BLOCK

    def step(u, carry):
        start, low, high = carry
        tokens, frames = tok_ref[0, u], frm_ref[0, u]
        end = start + tokens
        low = tuple(
            v + jnp.where(base + b * BLOCK >= end, frames, 0) for b, v in enumerate(low)
        )
        high = tuple(
            v + jnp.where(base + (b + 1) * BLOCK - 1 >= start, frames, 0) for b, v in enumerate(high)
        )
        return end, low, high

    zeros = (jnp.int32(0),) * blocks
    _, low, high = lax.fori_loop(0, tok_ref.shape[1], step, (jnp.int32(0), zeros, zeros))
    return low, high


def window_mask(place, first_row, base, block, count):
    keys = lax.broadcasted_iota(jnp.int32, (count, BLOCK), 0) + (base - HALO + block * BLOCK)
    here = slice(block * BLOCK, (block + 1) * BLOCK)
    return (keys >= first_row[:, here]) & (keys <= place[:, here])


def self_probs(queries, key_window, mask, heads):
    scores = mm(key_window, queries, 1, 1)
    parts = []
    for h in range(heads):
        part = jnp.where(mask, scores[:, h * BLOCK : (h + 1) * BLOCK], NEGATIVE)
        raised = jnp.exp(part - jnp.max(part, axis=0, keepdims=True))
        parts.append(raised * (1.0 / jnp.sum(raised, axis=0, keepdims=True)))
    return jnp.concatenate(parts, axis=1)


def prologue(
    tok, frm, x_ref, halo_ref, w_ref, bias_ref, vec_ref,
    n1_ref, q_ref, k_ref, v_ref, att_ref, after_ref, cq_ref,
):
    rows, width = x_ref.shape
    heads = width // HEAD
    base = lax.axis_index("mp") * rows
    place, first_row, _, _ = token_rows(tok, frm, base, rows)
    both = jnp.concatenate([halo_ref[...], x_ref[...]], axis=0).astype(F32)
    xhat, _ = normed(both)
    n1 = (xhat * vec_ref[0:1] + vec_ref[3:4]).astype(BF16)
    n1_ref[...] = n1
    q_ref[...] = ((mm(n1[HALO:], w_ref[0], 1, 1) + bias_ref[0:1]).astype(BF16) * 0.125).astype(BF16)
    k_ref[...] = mm(n1, w_ref[1], 1, 1).astype(BF16)
    v_ref[...] = (mm(n1, w_ref[2], 1, 1) + bias_ref[1:2]).astype(BF16)
    count = HALO + BLOCK
    for b in range(rows // BLOCK):
        queries = head_stack(q_ref[b * BLOCK : (b + 1) * BLOCK])
        window = slice(b * BLOCK, b * BLOCK + count)
        mask = window_mask(place, first_row, base, b, count)
        probs = self_probs(queries, k_ref[window], mask, heads).astype(BF16)
        out = head_diagonal(mm(v_ref[window], probs, 0, 0), heads)
        att_ref[b * BLOCK : (b + 1) * BLOCK] = out.T.astype(BF16)
    after = x_ref[...].astype(F32) + mm(att_ref[...], w_ref[3]) + vec_ref[6:7]
    after_ref[...] = after
    xhat, _ = normed(after)
    n2 = (xhat * vec_ref[1:2] + vec_ref[4:5]).astype(BF16)
    cq_ref[...] = ((mm(n2, w_ref[4], 1, 1) + bias_ref[2:3]).astype(BF16) * 0.125).astype(BF16)


def project_frames(mem, w_ref, bias_ref, ck_ref, cv_ref):
    ck_ref[...] = mm(mem, w_ref[5], 1, 1).astype(BF16)
    cv_ref[...] = (mm(mem, w_ref[6], 1, 1) + bias_ref[3:4]).astype(BF16)


def middle(
    tok, frm, cq_ref, after_ref, mem_ref, cot_ref, w_ref, wi_ref, wo_ref, bias_ref, ib_ref, vec_ref,
    out_ref, grad_ref, mgrad_ref, dw_ref, dwi_ref, dwo_ref, small_ref,
    ck_ref, cv_ref, qbig, gbig, lse_ref, dot_ref, acc, dq_ref, dk_ref, dv_ref,
):
    rows, width = cq_ref.shape
    heads = width // HEAD
    blocks = rows // BLOCK
    frames = mem_ref.shape[0]
    base = lax.axis_index("mp") * rows
    _, _, first_frame, end_frame = token_rows(tok, frm, base, rows)
    low, high = block_frames(tok, frm, base, rows)
    small_ref[...] = jnp.zeros_like(small_ref)

    def project(c, carry):
        here = pl.ds(pl.multiple_of(c * CHUNK, CHUNK), CHUNK)
        ck_ref[here] = mm(mem_ref[here], w_ref[5], 1, 1).astype(BF16)
        cv_ref[here] = (mm(mem_ref[here], w_ref[6], 1, 1) + bias_ref[3:4]).astype(BF16)
        return carry

    lax.fori_loop(0, frames // CHUNK, project, 0)

    def chunk_mask(c, b):
        frame = lax.broadcasted_iota(jnp.int32, (CHUNK, BLOCK), 0) + c * CHUNK
        here = slice(b * BLOCK, (b + 1) * BLOCK)
        return (frame >= first_frame[:, here]) & (frame < end_frame[:, here])

    attended = []
    for b in range(blocks):
        qbig[b] = head_stack(cq_ref[b * BLOCK : (b + 1) * BLOCK])
        acc[...] = jnp.zeros_like(acc)

        def step(c, carry):
            largest, total = carry
            here = pl.ds(pl.multiple_of(c * CHUNK, CHUNK), CHUNK)
            scores = mm(ck_ref[here], qbig[b], 1, 1)
            mask = chunk_mask(c, b)
            scores = jnp.where(jnp.concatenate([mask] * heads, axis=1), scores, NEGATIVE)
            now = jnp.maximum(largest, jnp.max(scores, axis=0, keepdims=True))
            fade = jnp.exp(largest - now)
            raised = jnp.exp(scores - now)
            total = total * fade + jnp.sum(raised, axis=0, keepdims=True)
            part = mm(cv_ref[here], raised.astype(BF16), 0, 0)
            for h in range(heads):
                r, l = slice(h * HEAD, (h + 1) * HEAD), slice(h * BLOCK, (h + 1) * BLOCK)
                acc[r] = acc[r] * fade[:, l] + part[r, l]
            return now, total

        start = (jnp.full((1, heads * BLOCK), NEGATIVE, F32), jnp.zeros((1, heads * BLOCK), F32))
        largest, total = lax.fori_loop(low[b] // CHUNK, (high[b] + CHUNK - 1) // CHUNK, step, start)
        lse_ref[b] = largest + jnp.log(total)
        share = 1.0 / total
        for h in range(heads):
            r, l = slice(h * HEAD, (h + 1) * HEAD), slice(h * BLOCK, (h + 1) * BLOCK)
            acc[r] = acc[r] * share[:, l]
        attended.append(acc[...])
    att_t = jnp.concatenate(attended, axis=1)
    att = att_t.T.astype(BF16)
    after_self = after_ref[...]
    after_cross = after_self + mm(att, w_ref[7]) + vec_ref[7:8]
    xhat3, scale3 = normed(after_cross)
    n3 = (xhat3 * vec_ref[2:3] + vec_ref[5:6]).astype(BF16)
    sent = cot_ref[...]
    small_ref[8:9] = column_sums(sent.astype(F32))
    hidden = wi_ref.shape[0]
    tile = 512
    out = after_cross + vec_ref[8:9]
    dn3 = jnp.zeros((rows, width), F32)
    for f in range(hidden // tile):
        here = slice(f * tile, (f + 1) * tile)
        before = mm(n3, wi_ref[here], 1, 1) + ib_ref[:, here]
        square = before * before
        inner = jnp.tanh(GELU_A * (before + GELU_B * (before * square)))
        half = 0.5 * (1.0 + inner)
        active = (before * half).astype(BF16)
        slope = half + 0.5 * before * (1.0 - inner * inner) * (
            GELU_A + (3.0 * GELU_A * GELU_B) * square
        )
        out = out + mm(active, wo_ref[here])
        back = (slope * mm(sent, wo_ref[here], 1, 1)).astype(BF16)
        dn3 = dn3 + mm(back, wi_ref[here])
        dwo_ref[here] = mm(active, sent, 0, 0)
        dwi_ref[here] = mm(back, n3, 0, 0)
        sums = column_sums(back.astype(F32))
        for i in range(tile // width):
            r = 16 + f * (tile // width) + i
            small_ref[r : r + 1] = sums[:, i * width : (i + 1) * width]
    out_ref[...] = out
    small_ref[2:3] = column_sums(dn3 * xhat3)
    small_ref[5:6] = column_sums(dn3)
    grad = sent.astype(F32) + norm_back(dn3, vec_ref[2:3], xhat3, scale3)
    sent2 = grad.astype(BF16)
    small_ref[7:8] = column_sums(sent2.astype(F32))
    dw_ref[3] = mm(att, sent2, 0, 0)
    go = mm(sent2, w_ref[7], 1, 1).astype(BF16)
    got = mm(w_ref[7], sent2, 1, 1).astype(BF16).astype(F32)
    prod = got * att_t
    for b in range(blocks):
        gbig[b] = head_stack(go[b * BLOCK : (b + 1) * BLOCK])
        for h in range(heads):
            piece = prod[h * HEAD : (h + 1) * HEAD, b * BLOCK : (b + 1) * BLOCK]
            dot_ref[b, :, h * BLOCK : (h + 1) * BLOCK] = column_sums(piece)
    dq_ref[...] = jnp.zeros_like(dq_ref)
    dw_ref[1] = jnp.zeros((width, width), F32)
    dw_ref[2] = jnp.zeros((width, width), F32)

    def frame_step(c, carry):
        here = pl.ds(pl.multiple_of(c * CHUNK, CHUNK), CHUNK)
        meets = [(low[b] < (c + 1) * CHUNK) & (high[b] > c * CHUNK) for b in range(blocks)]
        some = functools.reduce(jnp.logical_or, meets)

        @pl.when(some)
        def _():
            dk_ref[...] = jnp.zeros_like(dk_ref)
            dv_ref[...] = jnp.zeros_like(dv_ref)
            for b in range(blocks):

                @pl.when(meets[b])
                def _():
                    keys, values = ck_ref[here], cv_ref[here]
                    scores = mm(keys, qbig[b], 1, 1)
                    mask = chunk_mask(c, b)
                    mask = jnp.concatenate([mask] * heads, axis=1)
                    shares = jnp.where(mask, jnp.exp(scores - lse_ref[b]), 0.0)
                    dp = mm(values, gbig[b], 1, 1)
                    ds = (shares * (dp - dot_ref[b])).astype(BF16)
                    dv_ref[...] += mm(shares.astype(BF16), gbig[b])
                    dk_ref[...] += mm(ds, qbig[b])
                    l = slice(b * BLOCK, (b + 1) * BLOCK)
                    dq_ref[:, l] += head_diagonal(mm(keys, ds, 0, 0), heads)

            dk, dv = dk_ref[...].astype(BF16), dv_ref[...].astype(BF16)
            mgrad_ref[here] = (mm(dk, w_ref[5]) + mm(dv, w_ref[6])).astype(BF16)
            frame_rows = mem_ref[here]
            dw_ref[1] += mm(dk, frame_rows, 0, 0)
            dw_ref[2] += mm(dv, frame_rows, 0, 0)
            small_ref[12:13] += column_sums(dv.astype(F32))

        @pl.when(jnp.logical_not(some))
        def _():
            mgrad_ref[here] = jnp.zeros((CHUNK, width), BF16)

        return carry

    lax.fori_loop(0, frames // CHUNK, frame_step, 0)
    dq = (dq_ref[...] * 0.125).T.astype(BF16)
    small_ref[11:12] = column_sums(dq.astype(F32))
    xhat2, scale2 = normed(after_self)
    n2 = (xhat2 * vec_ref[1:2] + vec_ref[4:5]).astype(BF16)
    dw_ref[0] = mm(dq, n2, 0, 0)
    dn2 = mm(dq, w_ref[4])
    small_ref[1:2] = column_sums(dn2 * xhat2)
    small_ref[4:5] = column_sums(dn2)
    grad_ref[...] = grad + norm_back(dn2, vec_ref[1:2], xhat2, scale2)


def epilogue(
    tok, frm, n1_ref, q_ref, k_ref, v_ref, att_ref, grad_ref, w_ref, small_in,
    dn_ref, halo_ref, dw_ref, small_ref,
    dk_ref, dv_ref, dq_ref,
):
    rows, width = q_ref.shape
    heads = width // HEAD
    base = lax.axis_index("mp") * rows
    place, first_row, _, _ = token_rows(tok, frm, base, rows)
    small_ref[...] = small_in[...]
    sent = grad_ref[...].astype(BF16)
    small_ref[6:7] = column_sums(sent.astype(F32))
    dw_ref[3] = mm(att_ref[...], sent, 0, 0)
    go = mm(sent, w_ref[3], 1, 1).astype(BF16)
    dk_ref[...] = jnp.zeros_like(dk_ref)
    dv_ref[...] = jnp.zeros_like(dv_ref)
    count = HALO + BLOCK
    for b in range(rows // BLOCK):
        here = slice(b * BLOCK, (b + 1) * BLOCK)
        window = slice(b * BLOCK, b * BLOCK + count)
        queries, grads = head_stack(q_ref[here]), head_stack(go[here])
        mask = window_mask(place, first_row, base, b, count)
        shares = self_probs(queries, k_ref[window], mask, heads)
        dp = mm(v_ref[window], grads, 1, 1)
        ds = (shares * (dp - jnp.sum(shares * dp, axis=0, keepdims=True))).astype(BF16)
        dv_ref[window] += mm(shares.astype(BF16), grads)
        dk_ref[window] += mm(ds, queries)
        dq_ref[here] = (head_diagonal(mm(k_ref[window], ds, 0, 0), heads) * 0.125).T.astype(BF16)
    dq = dq_ref[...]
    dk, dv = dk_ref[...].astype(BF16), dv_ref[...].astype(BF16)
    n1 = n1_ref[...]
    dw_ref[0] = mm(dq, n1[HALO:], 0, 0)
    dw_ref[1] = mm(dk, n1, 0, 0)
    dw_ref[2] = mm(dv, n1, 0, 0)
    small_ref[9:10] = column_sums(dq.astype(F32))
    small_ref[10:11] = column_sums(dv.astype(F32))
    dn = mm(dk, w_ref[1]) + mm(dv, w_ref[2])
    halo_ref[...] = dn[:HALO].astype(BF16)
    dn_ref[...] = dn[HALO:] + mm(dq, w_ref[0])


def call(body, outs, smem, scratch=()):
    def run(*args):
        vmem = pl.BlockSpec(memory_space=pltpu.VMEM)
        scalar = pl.BlockSpec(memory_space=pltpu.SMEM)
        return pl.pallas_call(
            body,
            out_shape=[jax.ShapeDtypeStruct(s, t) for s, t in outs],
            in_specs=[scalar] * smem + [vmem] * (len(args) - smem),
            out_specs=[vmem] * len(outs),
            scratch_shapes=[pltpu.VMEM(s, t) for s, t in scratch],
            compiler_params=pltpu.CompilerParams(vmem_limit_bytes=56 << 20),
        )(*args)

    return run


def shards(
    block_input,
    memory,
    tok_lengths,
    frame_lengths,
    cotangent,
    norm_gain,
    norm_shift,
    self_weights,
    self_biases,
    self_output,
    self_offset,
    cross_weights,
    cross_biases,
    cross_output,
    cross_offset,
    inner_weight,
    inner_bias,
    outer_weight,
    outer_offset,
):
    rows, width = block_input.shape
    parts = lax.axis_size("mp")
    frames = memory.shape[0] * parts
    heads = width // HEAD
    blocks = rows // BLOCK
    own_hidden = inner_weight.shape[1]
    hidden = own_hidden * parts
    own = width // parts

    def turned(weights):
        return jnp.swapaxes(weights, 1, 2)

    attention = jnp.concatenate(
        [turned(self_weights), self_output[None], turned(cross_weights), cross_output[None]], axis=0
    )
    attention = jnp.swapaxes(lax.all_gather(attention, "mp"), 0, 1).reshape(8, width, width)
    inner = lax.all_gather(inner_weight.T, "mp", axis=0, tiled=True)
    outer = lax.all_gather(outer_weight, "mp", axis=0, tiled=True)
    small = jnp.concatenate([self_biases, cross_biases], axis=0)
    biases = jnp.swapaxes(lax.all_gather(small, "mp"), 0, 1).reshape(4, width)
    inner_row = lax.all_gather(inner_bias, "mp", axis=0, tiled=True).reshape(1, hidden)
    memory_rows = lax.all_gather(memory, "mp", axis=0, tiled=True)
    vectors = jnp.concatenate(
        [
            norm_gain,
            norm_shift,
            self_offset[None],
            cross_offset[None],
            outer_offset[None],
            jnp.zeros((7, width), F32),
        ],
        axis=0,
    )
    halo = lax.ppermute(
        block_input[rows - HALO :], "mp", [(i, i + 1) for i in range(parts - 1)]
    )

    n1, q, k, v, att, after, cq = call(
        prologue,
        [
            ((rows + HALO, width), BF16),
            ((rows, width), BF16),
            ((rows + HALO, width), BF16),
            ((rows + HALO, width), BF16),
            ((rows, width), BF16),
            ((rows, width), F32),
            ((rows, width), BF16),
        ],
        2,
    )(tok_lengths, frame_lengths, block_input, halo, attention, biases, vectors)

    small_rows = 16 + hidden // width
    block_output, grad, mgrad, dw_cross, dwi, dwo, small = call(
        middle,
        [
            ((rows, width), F32),
            ((rows, width), F32),
            ((frames, width), BF16),
            ((4, width, width), F32),
            ((hidden, width), F32),
            ((hidden, width), F32),
            ((small_rows, width), F32),
        ],
        2,
        [
            ((frames, width), BF16),
            ((frames, width), BF16),
            ((blocks, heads * BLOCK, width), BF16),
            ((blocks, heads * BLOCK, width), BF16),
            ((blocks, 1, heads * BLOCK), F32),
            ((blocks, 1, heads * BLOCK), F32),
            ((width, BLOCK), F32),
            ((width, rows), F32),
            ((CHUNK, width), F32),
            ((CHUNK, width), F32),
        ],
    )(
        tok_lengths, frame_lengths, cq, after, memory_rows, cotangent, attention, inner, outer, biases,
        inner_row, vectors,
    )

    memory_grad = lax.psum_scatter(mgrad, "mp", scatter_dimension=0, tiled=True).astype(F32)

    dn, halo_grad, dw_self, small = call(
        epilogue,
        [
            ((rows, width), F32),
            ((HALO, width), BF16),
            ((4, width, width), F32),
            ((small_rows, width), F32),
        ],
        2,
        [
            ((rows + HALO, width), F32),
            ((rows + HALO, width), F32),
            ((rows, width), BF16),
        ],
    )(tok_lengths, frame_lengths, n1, q, k, v, att, grad, attention, small)
    arrived = lax.ppermute(halo_grad, "mp", [(i + 1, i) for i in range(parts - 1)])
    dn = dn + jnp.pad(arrived.astype(F32), ((rows - HALO, 0), (0, 0)))
    xhat, scale = normed(block_input.astype(F32))
    input_grad = grad + norm_back(dn, norm_gain[0], xhat, scale)
    small = small.at[0].set(jnp.sum(dn * xhat, axis=0)).at[3].set(jnp.sum(dn, axis=0))

    small = lax.psum(small, ("dp", "mp"))

    def collected(values):
        mine = lax.psum_scatter(values, "mp", scatter_dimension=values.ndim - 2, tiled=True)
        return lax.psum(mine, "dp")

    dw = collected(jnp.concatenate([dw_self, dw_cross], axis=0))
    dffn = collected(jnp.stack([dwi, dwo]))
    me = lax.axis_index("mp")
    biases_grad = lax.dynamic_slice_in_dim(small, me * own, own, axis=1)
    inner_bias_grad = lax.dynamic_slice_in_dim(
        small[16:].reshape(hidden), me * own_hidden, own_hidden, axis=0
    )
    return (
        block_output,
        input_grad,
        memory_grad,
        small[0:3],
        small[3:6],
        turned(dw[0:3]),
        biases_grad[9:11],
        dw[3],
        small[6],
        turned(dw[4:7]),
        biases_grad[11:13],
        dw[7],
        small[7],
        dffn[0].T,
        inner_bias_grad,
        dffn[1],
        small[8],
    )


def solution(mesh):
    in_specs = (
        P(("dp", "mp"), None),
        P(("dp", "mp"), None),
        P("dp", None),
        P("dp", None),
        P(("dp", "mp"), None),
        P(),
        P(),
        P(None, None, "mp"),
        P(None, "mp"),
        P("mp", None),
        P(),
        P(None, None, "mp"),
        P(None, "mp"),
        P("mp", None),
        P(),
        P(None, "mp"),
        P("mp"),
        P("mp", None),
        P(),
    )
    out_specs = (
        P(("dp", "mp"), None),
        P(("dp", "mp"), None),
        P(("dp", "mp"), None),
        P(),
        P(),
        P(None, None, "mp"),
        P(None, "mp"),
        P("mp", None),
        P(),
        P(None, None, "mp"),
        P(None, "mp"),
        P("mp", None),
        P(),
        P(None, "mp"),
        P("mp"),
        P("mp", None),
        P(),
    )
    return jax.shard_map(shards, mesh=mesh, in_specs=in_specs, out_specs=out_specs, check_vma=False)
```

```python
import functools
import math

import jax
import jax.numpy as jnp
from jax import lax
from jax.experimental import pallas as pl
from jax.experimental.pallas import tpu as pltpu
from jax.sharding import PartitionSpec as P

HEAD = 64
NEGATIVE = -1e30
EPSILON = 1e-05
BLOCK = 128
CHUNK = 256
HALO = 256
F32 = jnp.float32
BF16 = jnp.bfloat16
MESH = pl.DeviceIdType.MESH
HALF = HEAD // 2
SLICES = 8
PIECES = 4
GELU_A = math.sqrt(2.0 / math.pi)
GELU_B = 0.044715


def mm(a, b, ca=1, cb=0):
    return lax.dot_general(a, b, (((ca,), (cb,)), ((), ())), preferred_element_type=F32)


def normed(values):
    center = values - jnp.mean(values, axis=-1, keepdims=True)
    spread = jnp.mean(center * center, axis=-1, keepdims=True)
    scale = lax.rsqrt(spread + EPSILON)
    return center * scale, scale


def norm_back(grad, gain, xhat, scale):
    gn = grad * gain
    first = jnp.mean(gn, axis=-1, keepdims=True)
    second = jnp.mean(gn * xhat, axis=-1, keepdims=True)
    return (gn - first - xhat * second) * scale


def column_sums(values):
    return jnp.sum(values, axis=0, keepdims=True)


def head_stack(values):
    rows, width = values.shape
    heads = width // HEAD
    lane = lax.broadcasted_iota(jnp.int32, (rows, width), 1) // HALF % heads
    zero = jnp.zeros_like(values)
    return jnp.concatenate([jnp.where(lane == h, values, zero) for h in range(heads)], axis=0)


def head_rows(heads):
    return [
        (slice((i * heads + h) * HALF, (i * heads + h + 1) * HALF), h)
        for i in range(2)
        for h in range(heads)
    ]


def head_diagonal(values, heads):
    rows = values.shape[1] // heads
    return jnp.concatenate(
        [values[r, h * rows : (h + 1) * rows] for r, h in head_rows(heads)], axis=0
    )


def token_rows(tok_ref, frm_ref, base, count):
    place = lax.broadcasted_iota(jnp.int32, (1, count), 1) + base
    zero = jnp.zeros((1, count), jnp.int32)

    def step(u, carry):
        start, first_row, first_frame, end_frame = carry
        tokens, frames = tok_ref[0, u], frm_ref[0, u]
        end = start + tokens
        done = place >= end
        first_row = first_row + jnp.where(done, tokens, 0)
        first_frame = first_frame + jnp.where(done, frames, 0)
        end_frame = end_frame + jnp.where(place >= start, frames, 0)
        return end, first_row, first_frame, end_frame

    _, first_row, first_frame, end_frame = lax.fori_loop(
        0, tok_ref.shape[1], step, (jnp.int32(0), zero, zero, zero)
    )
    return place, first_row, first_frame, end_frame


def block_frames(tok_ref, frm_ref, base, count):
    blocks = count // BLOCK

    def step(u, carry):
        start, low, high = carry
        tokens, frames = tok_ref[0, u], frm_ref[0, u]
        end = start + tokens
        low = tuple(
            v + jnp.where(base + b * BLOCK >= end, frames, 0) for b, v in enumerate(low)
        )
        high = tuple(
            v + jnp.where(base + (b + 1) * BLOCK - 1 >= start, frames, 0) for b, v in enumerate(high)
        )
        return end, low, high

    zeros = (jnp.int32(0),) * blocks
    _, low, high = lax.fori_loop(0, tok_ref.shape[1], step, (jnp.int32(0), zeros, zeros))
    return low, high


def window_mask(place, first_row, base, block, count):
    keys = lax.broadcasted_iota(jnp.int32, (count, BLOCK), 0) + (base - HALO + block * BLOCK)
    here = slice(block * BLOCK, (block + 1) * BLOCK)
    return (keys >= first_row[:, here]) & (keys <= place[:, here])


def self_probs(queries, key_window, mask, heads):
    scores = mm(key_window, queries, 1, 1)
    parts = []
    for h in range(heads):
        part = jnp.where(mask, scores[:, h * BLOCK : (h + 1) * BLOCK], NEGATIVE)
        raised = jnp.exp(part - jnp.max(part, axis=0, keepdims=True))
        parts.append(raised * (1.0 / jnp.sum(raised, axis=0, keepdims=True)))
    return jnp.concatenate(parts, axis=1)


def rcopy(src, dst, send, recv, **device):
    return pltpu.make_async_remote_copy(
        src_ref=src, dst_ref=dst, send_sem=send, recv_sem=recv, device_id=device, device_id_type=MESH
    )


def at_rows(start, count):
    return pl.ds(pl.multiple_of(start, 16), count)


def flipped(index, bit):
    return index + bit - 2 * bit * (index // bit % 2)


def greet(z, parts, d, bits):
    barrier = pltpu.get_barrier_semaphore()
    for step in range(1, parts):
        device = {"mp": (z + step) % parts}
        pl.semaphore_signal(barrier, inc=1, device_id=device, device_id_type=MESH)
    for bit in bits:
        device = {"dp": flipped(d, bit)}
        pl.semaphore_signal(barrier, inc=1, device_id=device, device_id_type=MESH)
    return barrier, parts - 1 + len(bits)


class Line:
    def __init__(self, z, parts, own, place, sems):
        self.z, self.parts, self.own, self.place, self.sems = z, parts, own, place, sems

    def copy(self, k, up):
        shard = self.z - k if up else self.z + k
        kind = 0 if up else 2
        return rcopy(
            self.own if k == 0 else self.place(shard),
            self.place(shard),
            self.sems.at[kind, k],
            self.sems.at[kind + 1, k],
            mp=self.z + 1 if up else self.z - 1,
        )

    def sends(self, k, up):
        if up:
            return (self.z >= k) & (self.z < self.parts - 1)
        return (self.z + k < self.parts) & (self.z > 0)

    def send(self, k):
        for up in (True, False):

            @pl.when(self.sends(k, up))
            def _():
                self.copy(k, up).start()

    def arrive(self, k, up):
        shard = self.z - 1 - k if up else self.z + 1 + k
        kind = 0 if up else 2
        rcopy(
            self.place(shard),
            self.place(shard),
            self.sems.at[kind, k],
            self.sems.at[kind + 1, k],
            mp=self.z - 1 if up else self.z + 1,
        ).wait_recv()

    def comes(self, k, up):
        return self.z >= k + 1 if up else self.z + 1 + k < self.parts

    def arrived(self, k):
        for up in (True, False):

            @pl.when(self.comes(k, up))
            def _():
                self.arrive(k, up)

    def close(self):
        for k in range(self.parts - 1):
            for up in (True, False):

                @pl.when(self.sends(k, up))
                def _():
                    self.copy(k, up).wait_send()


DP_BITS = (2, 4, 1)
SLICE_BITS = (1, 2, 4)


class Plane:
    def __init__(self, d, s, buffer, rows, sems):
        self.d, self.s, self.buffer, self.rows, self.sems = d, s, buffer, rows, sems

    def block(self, s, p):
        bit = SLICE_BITS[p]
        return self.buffer.at[at_rows((s - s % bit) * self.rows, bit * self.rows)]

    def copy(self, p, s):
        block = self.block(s, p)
        device = flipped(self.d, DP_BITS[p])
        return rcopy(block, block, self.sems.at[0, p], self.sems.at[1, p], dp=device)

    def send(self, p):
        self.copy(p, self.s).start()

    def arrived(self, p):
        self.copy(p, flipped(self.s, SLICE_BITS[p])).wait_recv()

    def close(self):
        for p in range(3):
            self.copy(p, self.s).wait_send()


def gather(
    tok, frm, x_ref, mem, sw, so, cw, co, inner, outer, sb, cb, ib, gain, shift, offset,
    wself_out, wcross_out, inner_out, outer_out, ib_out, mem_out, ck_out, cv_out,
    n1_ref, q_ref, k_ref, v_ref, att_ref, after_ref, cq_ref,
    gself, gcross, ginner, gouter, gmem, sck, scv, pself, pcross, pinner, halo, pbias, gbias,
    line_sems, mem_sems, plane_sems, bias_sems, halo_sems, own_sem, out_sems, weight_sems,
):
    rows, width = x_ref.shape
    heads = width // HEAD
    parts = width // sw.shape[2]
    own = sw.shape[2]
    shard_rows = mem.shape[0]
    piece = shard_rows // PIECES
    z, d = lax.axis_index("mp"), lax.axis_index("dp")
    s = d % 2 * 4 + d // 2 % 4
    barrier, greetings = greet(z, parts, d, DP_BITS)

    for source, last, packed in ((sw, so, pself), (cw, co, pcross)):
        for i in range(3):
            packed[i * own : (i + 1) * own] = source[i].T
        packed[3 * own :] = last[...]
    pbias[...] = jnp.zeros_like(pbias)
    pbias[0:1] = ib[...]
    for i in range(2):
        pbias[1:2, i * own : (i + 1) * own] = sb[i : i + 1]
        pbias[1:2, (2 + i) * own : (3 + i) * own] = cb[i : i + 1]
    pinner[...] = inner[...].T
    groups = []
    for i, (packed, buffer) in enumerate(
        ((pself, gself), (pcross, gcross), (pinner, ginner), (outer, gouter))
    ):
        n = packed.shape[0] // SLICES
        mine = packed.at[at_rows(s * n, n)]

        def place(shard, buffer=buffer, n=n):
            return buffer.at[at_rows((s * parts + shard) * n, n)]

        line = Line(z, parts, mine, place, line_sems.at[i])
        plane = Plane(d, s, buffer, parts * n, plane_sems.at[i])
        groups.append((line, plane))
        buffer[at_rows((s * parts + z) * n, n)] = packed[at_rows(s * n, n)]
    memory = []
    for c in range(PIECES):

        def place(shard, c=c):
            return gmem.at[at_rows(shard * shard_rows + c * piece, piece)]

        memory.append(Line(z, parts, mem.at[c * piece : (c + 1) * piece], place, mem_sems.at[c]))

    def bias_copy(step):
        return rcopy(
            pbias, gbias.at[z], bias_sems.at[0, step], bias_sems.at[1, step], mp=(z + step) % parts
        )

    def bias_arrival(step):
        other = (z - step + parts) % parts
        return rcopy(pbias, gbias.at[other], bias_sems.at[0, step], bias_sems.at[1, step], mp=other)

    def halo_copy(other):
        return rcopy(x_ref.at[rows - HALO :], halo, halo_sems.at[0], halo_sems.at[1], mp=other)

    pl.semaphore_wait(barrier, greetings)
    for line, _ in groups[:2]:
        line.send(0)
    for step in range(1, parts):
        bias_copy(step).start()

    @pl.when(z < parts - 1)
    def _():
        halo_copy(z + 1).start()

    for line, _ in groups[2:]:
        line.send(0)
    for line in memory:
        line.send(0)
    own_rows = gmem.at[at_rows(z * shard_rows, shard_rows)]
    own_copy = pltpu.make_async_copy(mem, own_rows, own_sem)
    own_copy.start()
    gbias[z] = pbias[...]
    for k in range(parts - 1):
        for line, _ in groups[:2]:
            line.arrived(k)
            if k < parts - 2:
                line.send(k + 1)
    for _, plane in groups[:2]:
        plane.send(0)
    for k in range(parts - 1):
        for line, _ in groups[2:]:
            line.arrived(k)
            if k < parts - 2:
                line.send(k + 1)
    for line in memory[:1]:
        line.arrived(0)
        line.send(1)
    for _, plane in groups[:2]:
        plane.arrived(0)
        plane.send(1)
    for _, plane in groups[2:]:
        plane.send(0)
    for line in memory[1:2]:
        line.arrived(0)
        line.send(1)
    for _, plane in groups[:2]:
        plane.arrived(1)
        plane.send(2)
    for _, plane in groups[2:]:
        plane.arrived(0)
        plane.send(1)
    for line in memory[2:3]:
        line.arrived(0)
        line.send(1)
    for _, plane in groups[:2]:
        plane.arrived(2)

    for step in range(1, parts):
        bias_arrival(step).wait_recv()

    def head_bias(i):
        return jnp.concatenate(
            [
                gbias[o, 1:2, i * own + half * HALF : i * own + (half + 1) * HALF]
                for half in range(2)
                for o in range(parts)
            ],
            axis=1,
        )

    n = ginner.shape[0] // SLICES // parts
    for i in range(SLICES):
        ib_out[i : i + 1] = jnp.concatenate(
            [gbias[o, 0:1, i * n : (i + 1) * n] for o in range(parts)], axis=1
        )

    @pl.when(z > 0)
    def _():
        halo_copy(z - 1).wait_recv()

    @pl.when(z == 0)
    def _():
        halo[...] = jnp.zeros_like(halo)

    def weight(buffer, i):
        return buffer[i * width : (i + 1) * width]

    base = z * rows
    place_row, first_row, _, _ = token_rows(tok, frm, base, rows)
    for src, dst in ((halo, slice(0, HALO)), (x_ref, slice(HALO, HALO + rows))):
        xhat, _ = normed(src[...].astype(F32))
        n1_ref[dst] = (xhat * gain[0:1] + shift[0:1]).astype(BF16)
    n1 = n1_ref[...]
    query = mm(n1[HALO:], weight(gself, 0), 1, 1) + head_bias(0)
    q_ref[...] = query.astype(BF16) * jnp.asarray(0.125, BF16)
    k_ref[...] = mm(n1, weight(gself, 1), 1, 1).astype(BF16)
    v_ref[...] = (mm(n1, weight(gself, 2), 1, 1) + head_bias(1)).astype(BF16)
    count = HALO + BLOCK
    for b in range(rows // BLOCK):
        queries = head_stack(q_ref[b * BLOCK : (b + 1) * BLOCK])
        window = slice(b * BLOCK, b * BLOCK + count)
        mask = window_mask(place_row, first_row, base, b, count)
        probs = self_probs(queries, k_ref[window], mask, heads).astype(BF16)
        out = head_diagonal(mm(v_ref[window], probs, 0, 0), heads)
        att_ref[b * BLOCK : (b + 1) * BLOCK] = out.T.astype(BF16)
        if b == 0:
            for line in memory[3:]:
                line.arrived(0)
                line.send(1)
            for _, plane in groups[2:]:
                plane.arrived(1)
                plane.send(2)
    after = x_ref[...].astype(F32) + mm(att_ref[...], weight(gself, 3)) + offset[...]
    after_ref[...] = after
    xhat, _ = normed(after)
    n2 = (xhat * gain[1:2] + shift[1:2]).astype(BF16)
    query = mm(n2, weight(gcross, 0), 1, 1) + head_bias(2)
    cq_ref[...] = query.astype(BF16) * jnp.asarray(0.125, BF16)
    value_bias = head_bias(3)

    def project(start, size):
        here = at_rows(start, size)
        block = gmem[here]
        sck[here] = mm(block, weight(gcross, 1), 1, 1).astype(BF16)
        scv[here] = (mm(block, weight(gcross, 2), 1, 1) + value_bias).astype(BF16)

    def copies_out(shard):
        here = at_rows(shard * shard_rows, shard_rows)
        return [
            pltpu.make_async_copy(a.at[here], b.at[here], out_sems.at[shard, i])
            for i, (a, b) in enumerate(((gmem, mem_out), (sck, ck_out), (scv, cv_out)))
        ]

    def project_shard(shard):
        lax.fori_loop(
            0, PIECES, lambda c, _: (project(shard * shard_rows + c * piece, piece), 0)[1], 0
        )
        for copy in copies_out(shard):
            copy.start()

    own_copy.wait()
    project_shard(z)
    for _, plane in groups[2:]:
        plane.arrived(2)
    outs = [
        pltpu.make_async_copy(a, b, weight_sems.at[i])
        for i, (a, b) in enumerate(
            ((gself, wself_out), (gcross, wcross_out), (ginner, inner_out), (gouter, outer_out))
        )
    ]
    for copy in outs:
        copy.start()

    for up in (True, False):

        @pl.when(memory[0].comes(0, up))
        def _():
            project_shard(z - 1 if up else z + 1)

    for k in range(1, parts - 1):
        for line in memory:
            line.arrived(k)
            if k < parts - 2:
                line.send(k + 1)
        for up in (True, False):

            @pl.when(memory[0].comes(k, up))
            def _():
                project_shard(z - 1 - k if up else z + 1 + k)

    for copy in outs:
        copy.wait()

    def finish(shard, carry):
        for copy in copies_out(shard):
            copy.wait()
        return carry

    lax.fori_loop(0, parts, finish, 0)
    for line, plane in groups:
        line.close()
        plane.close()
    for line in memory:
        line.close()
    for step in range(1, parts):
        bias_copy(step).wait_send()

    @pl.when(z < parts - 1)
    def _():
        halo_copy(z + 1).wait_send()


def middle(
    tok, frm, cq_ref, after_ref, cot_ref, w_ref, ib_ref, gain, shift, cross_offset, outer_offset,
    ck_in, cv_in, mem_in, wi_in, wo_in,
    out_ref, grad_ref, small_ref, mgrad_out, dw_out, dwi_out, dwo_out,
    ck_ref, cv_ref, mem_ref, wi_ref, wo_ref, mgrad_ref, dw_ref, dwb_ref, dwi_ref, dwo_ref,
    qbig, gbig, lse_ref, dot_ref, acc, dq_ref, dk_ref, dv_ref,
    in_sems, out_sems, chunk_sems,
):
    loads = [
        pltpu.make_async_copy(a, b, in_sems.at[i])
        for i, (a, b) in enumerate(
            ((ck_in, ck_ref), (cv_in, cv_ref), (wi_in, wi_ref), (wo_in, wo_ref), (mem_in, mem_ref))
        )
    ]
    for load in loads:
        load.start()
    rows, width = cq_ref.shape
    heads = width // HEAD
    blocks = rows // BLOCK
    frames = mem_ref.shape[0]

    def weight(i):
        return w_ref[i * width : (i + 1) * width]

    base = lax.axis_index("mp") * rows
    _, _, first_frame, end_frame = token_rows(tok, frm, base, rows)
    low, high = block_frames(tok, frm, base, rows)
    small_ref[...] = jnp.zeros_like(small_ref)

    def chunk_mask(c, b):
        frame = lax.broadcasted_iota(jnp.int32, (CHUNK, BLOCK), 0) + c * CHUNK
        here = slice(b * BLOCK, (b + 1) * BLOCK)
        return (frame >= first_frame[:, here]) & (frame < end_frame[:, here])

    loads[0].wait()
    loads[1].wait()
    attended = []
    for b in range(blocks):
        qbig[b] = head_stack(cq_ref[b * BLOCK : (b + 1) * BLOCK])
        acc[...] = jnp.zeros_like(acc)

        def step(c, carry):
            largest, total = carry
            here = pl.ds(pl.multiple_of(c * CHUNK, CHUNK), CHUNK)
            scores = mm(ck_ref[here], qbig[b], 1, 1)
            mask = chunk_mask(c, b)
            scores = jnp.where(jnp.concatenate([mask] * heads, axis=1), scores, NEGATIVE)
            now = jnp.maximum(largest, jnp.max(scores, axis=0, keepdims=True))
            fade = jnp.exp(largest - now)
            raised = jnp.exp(scores - now)
            total = total * fade + jnp.sum(raised, axis=0, keepdims=True)
            part = mm(cv_ref[here], raised.astype(BF16), 0, 0)
            for r, h in head_rows(heads):
                l = slice(h * BLOCK, (h + 1) * BLOCK)
                acc[r] = acc[r] * fade[:, l] + part[r, l]
            return now, total

        start = (jnp.full((1, heads * BLOCK), NEGATIVE, F32), jnp.zeros((1, heads * BLOCK), F32))
        largest, total = lax.fori_loop(low[b] // CHUNK, (high[b] + CHUNK - 1) // CHUNK, step, start)
        lse_ref[b] = largest + jnp.log(total)
        share = 1.0 / total
        for r, h in head_rows(heads):
            l = slice(h * BLOCK, (h + 1) * BLOCK)
            acc[r] = acc[r] * share[:, l]
        attended.append(acc[...])
    att_t = jnp.concatenate(attended, axis=1)
    att = att_t.T.astype(BF16)
    after_self = after_ref[...]
    after_cross = after_self + mm(att, weight(3)) + cross_offset[...]
    xhat3, scale3 = normed(after_cross)
    n3 = (xhat3 * gain[2:3] + shift[2:3]).astype(BF16)
    sent = cot_ref[...]
    small_ref[8:9] = column_sums(sent.astype(F32))
    hidden = wi_ref.shape[0]
    tile = hidden // SLICES
    loads[2].wait()
    loads[3].wait()
    out = after_cross + outer_offset[...]
    dn3 = jnp.zeros((rows, width), F32)
    for f in range(hidden // tile):
        here = slice(f * tile, (f + 1) * tile)
        before = mm(n3, wi_ref[here], 1, 1) + ib_ref[f : f + 1]
        square = before * before
        inner = jnp.tanh(GELU_A * (before + GELU_B * (before * square)))
        half = 0.5 * (1.0 + inner)
        active = (before * half).astype(BF16)
        slope = half + 0.5 * before * (1.0 - inner * inner) * (
            GELU_A + (3.0 * GELU_A * GELU_B) * square
        )
        out = out + mm(active, wo_ref[here])
        back = (slope * mm(sent, wo_ref[here], 1, 1)).astype(BF16)
        dn3 = dn3 + mm(back, wi_ref[here])
        dwo_ref[here] = mm(active, sent, 0, 0).astype(BF16)
        dwi_ref[here] = mm(back, n3, 0, 0).astype(BF16)
        small_ref[16 + f : 17 + f] = column_sums(back.astype(F32))
    stores = [
        pltpu.make_async_copy(a, b, out_sems.at[i])
        for i, (a, b) in enumerate(((dwi_ref, dwi_out), (dwo_ref, dwo_out), (dwb_ref, dw_out)))
    ]
    stores[0].start()
    stores[1].start()
    out_ref[...] = out
    small_ref[2:3] = column_sums(dn3 * xhat3)
    small_ref[5:6] = column_sums(dn3)
    grad = sent.astype(F32) + norm_back(dn3, gain[2:3], xhat3, scale3)
    sent2 = grad.astype(BF16)
    small_ref[7:8] = column_sums(sent2.astype(F32))
    dw_ref[3] = mm(att, sent2, 0, 0)
    go = mm(sent2, weight(3), 1, 1).astype(BF16)
    got = mm(weight(3), sent2, 1, 1).astype(BF16).astype(F32)
    prod = got * att_t
    for b in range(blocks):
        gbig[b] = head_stack(go[b * BLOCK : (b + 1) * BLOCK])
        sums = [column_sums(prod[r, b * BLOCK : (b + 1) * BLOCK]) for r, _ in head_rows(heads)]
        for h in range(heads):
            dot_ref[b, :, h * BLOCK : (h + 1) * BLOCK] = sums[h] + sums[heads + h]
    dq_ref[...] = jnp.zeros_like(dq_ref)
    dw_ref[1] = jnp.zeros((width, width), F32)
    dw_ref[2] = jnp.zeros((width, width), F32)

    loads[4].wait()

    def chunk_store(c):
        here = pl.ds(pl.multiple_of(c * CHUNK, CHUNK), CHUNK)
        return pltpu.make_async_copy(mgrad_ref.at[here], mgrad_out.at[here], chunk_sems.at[c])

    def frame_step(c, carry):
        here = pl.ds(pl.multiple_of(c * CHUNK, CHUNK), CHUNK)
        meets = [(low[b] < (c + 1) * CHUNK) & (high[b] > c * CHUNK) for b in range(blocks)]
        some = functools.reduce(jnp.logical_or, meets)

        @pl.when(some)
        def _():
            dk_ref[...] = jnp.zeros_like(dk_ref)
            dv_ref[...] = jnp.zeros_like(dv_ref)
            for b in range(blocks):

                @pl.when(meets[b])
                def _():
                    keys, values = ck_ref[here], cv_ref[here]
                    scores = mm(keys, qbig[b], 1, 1)
                    mask = chunk_mask(c, b)
                    mask = jnp.concatenate([mask] * heads, axis=1)
                    shares = jnp.where(mask, jnp.exp(scores - lse_ref[b]), 0.0)
                    dp = mm(values, gbig[b], 1, 1)
                    ds = (shares * (dp - dot_ref[b])).astype(BF16)
                    dv_ref[...] += mm(shares.astype(BF16), gbig[b])
                    dk_ref[...] += mm(ds, qbig[b])
                    l = slice(b * BLOCK, (b + 1) * BLOCK)
                    dq_ref[:, l] += head_diagonal(mm(keys, ds, 0, 0), heads)

            dk, dv = dk_ref[...].astype(BF16), dv_ref[...].astype(BF16)
            mgrad_ref[here] = (mm(dk, weight(1)) + mm(dv, weight(2))).astype(BF16)
            frame_rows = mem_ref[here]
            dw_ref[1] += mm(dk, frame_rows, 0, 0)
            dw_ref[2] += mm(dv, frame_rows, 0, 0)
            small_ref[12:13] += column_sums(dv.astype(F32))

        @pl.when(jnp.logical_not(some))
        def _():
            mgrad_ref[here] = jnp.zeros((CHUNK, width), BF16)

        chunk_store(c).start()
        return carry

    lax.fori_loop(0, frames // CHUNK, frame_step, 0)
    dq = (dq_ref[...] * 0.125).T.astype(BF16)
    small_ref[11:12] = column_sums(dq.astype(F32))
    xhat2, scale2 = normed(after_self)
    n2 = (xhat2 * gain[1:2] + shift[1:2]).astype(BF16)
    dw_ref[0] = mm(dq, n2, 0, 0)
    dn2 = mm(dq, weight(0))
    small_ref[1:2] = column_sums(dn2 * xhat2)
    small_ref[4:5] = column_sums(dn2)
    grad_ref[...] = grad + norm_back(dn2, gain[1:2], xhat2, scale2)
    for i in range(4):
        dwb_ref[i * width : (i + 1) * width] = dw_ref[i].astype(BF16)
    stores[2].start()

    def finish(c, carry):
        chunk_store(c).wait()
        return carry

    lax.fori_loop(0, frames // CHUNK, finish, 0)
    for store in stores:
        store.wait()


def epilogue(
    tok, frm, n1_ref, q_ref, k_ref, v_ref, att_ref, grad_ref, w_ref, small_in,
    dn_ref, halo_ref, dw_ref, small_ref,
    dk_ref, dv_ref, dq_ref,
):
    rows, width = q_ref.shape
    heads = width // HEAD
    base = lax.axis_index("mp") * rows
    place, first_row, _, _ = token_rows(tok, frm, base, rows)
    small_ref[...] = small_in[...]

    def weight(i):
        return w_ref[i * width : (i + 1) * width]

    sent = grad_ref[...].astype(BF16)
    small_ref[6:7] = column_sums(sent.astype(F32))
    dw_ref[3] = mm(att_ref[...], sent, 0, 0)
    go = mm(sent, weight(3), 1, 1).astype(BF16)
    dk_ref[...] = jnp.zeros_like(dk_ref)
    dv_ref[...] = jnp.zeros_like(dv_ref)
    count = HALO + BLOCK
    for b in range(rows // BLOCK):
        here = slice(b * BLOCK, (b + 1) * BLOCK)
        window = slice(b * BLOCK, b * BLOCK + count)
        queries, grads = head_stack(q_ref[here]), head_stack(go[here])
        mask = window_mask(place, first_row, base, b, count)
        shares = self_probs(queries, k_ref[window], mask, heads)
        dp = mm(v_ref[window], grads, 1, 1)
        ds = (shares * (dp - jnp.sum(shares * dp, axis=0, keepdims=True))).astype(BF16)
        dv_ref[window] += mm(shares.astype(BF16), grads)
        dk_ref[window] += mm(ds, queries)
        dq_ref[here] = (head_diagonal(mm(k_ref[window], ds, 0, 0), heads) * 0.125).T.astype(BF16)
    dq = dq_ref[...]
    dk, dv = dk_ref[...].astype(BF16), dv_ref[...].astype(BF16)
    n1 = n1_ref[...]
    dw_ref[0] = mm(dq, n1[HALO:], 0, 0)
    dw_ref[1] = mm(dk, n1, 0, 0)
    dw_ref[2] = mm(dv, n1, 0, 0)
    small_ref[9:10] = column_sums(dq.astype(F32))
    small_ref[10:11] = column_sums(dv.astype(F32))
    dn = mm(dk, weight(1)) + mm(dv, weight(2))
    halo_ref[...] = dn[:HALO].astype(BF16)
    dn_ref[...] = dn[HALO:] + mm(dq, weight(0))


def call(body, outs, ins, scratch, **params):
    places = {"s": pltpu.SMEM, "v": pltpu.VMEM, "h": pl.ANY}

    def spec(place):
        return pl.BlockSpec(memory_space=places[place])

    def run(*args):
        return pl.pallas_call(
            body,
            out_shape=[jax.ShapeDtypeStruct(shape, kind) for shape, kind, _ in outs],
            in_specs=[spec(place) for place in ins],
            out_specs=[spec(place) for _, _, place in outs],
            scratch_shapes=[pltpu.VMEM(*x) if isinstance(x, tuple) else x for x in scratch],
            compiler_params=pltpu.CompilerParams(vmem_limit_bytes=56 << 20, **params),
        )(*args)

    return run


def shards(
    block_input,
    memory,
    tok_lengths,
    frame_lengths,
    cotangent,
    norm_gain,
    norm_shift,
    self_weights,
    self_biases,
    self_output,
    self_offset,
    cross_weights,
    cross_biases,
    cross_output,
    cross_offset,
    inner_weight,
    inner_bias,
    outer_weight,
    outer_offset,
):
    rows, width = block_input.shape
    parts = lax.axis_size("mp")
    frames = memory.shape[0] * parts
    heads = width // HEAD
    blocks = rows // BLOCK
    own_hidden = inner_weight.shape[1]
    hidden = own_hidden * parts
    own = width // parts
    dma = pltpu.SemaphoreType.DMA
    wide = heads * BLOCK

    (
        wself, wcross, inner, outer, inner_row, memory_rows, ck, cv, n1, q, k, v, att, after, cq
    ) = call(
        gather,
        [
            ((4 * width, width), BF16, "h"),
            ((4 * width, width), BF16, "h"),
            ((hidden, width), BF16, "h"),
            ((hidden, width), BF16, "h"),
            ((SLICES, hidden // SLICES), F32, "v"),
            ((frames, width), BF16, "h"),
            ((frames, width), BF16, "h"),
            ((frames, width), BF16, "h"),
            ((rows + HALO, width), BF16, "v"),
            ((rows, width), BF16, "v"),
            ((rows + HALO, width), BF16, "v"),
            ((rows + HALO, width), BF16, "v"),
            ((rows, width), BF16, "v"),
            ((rows, width), F32, "v"),
            ((rows, width), BF16, "v"),
        ],
        "ssvhvvvvvvvvvvvv",
        [
            ((4 * width, width), BF16),
            ((4 * width, width), BF16),
            ((hidden, width), BF16),
            ((hidden, width), BF16),
            ((frames, width), BF16),
            ((frames, width), BF16),
            ((frames, width), BF16),
            ((4 * own, width), BF16),
            ((4 * own, width), BF16),
            ((own_hidden, width), BF16),
            ((HALO, width), BF16),
            ((8, own_hidden), F32),
            ((parts, 8, own_hidden), F32),
            dma((4, 4, parts - 1)),
            dma((PIECES, 4, parts - 1)),
            dma((4, 2, 3)),
            dma((2, parts)),
            dma((2,)),
            dma,
            dma((parts, 3)),
            dma((4,)),
        ],
        collective_id=0,
        has_side_effects=True,
    )(
        tok_lengths, frame_lengths, block_input, memory, self_weights, self_output, cross_weights,
        cross_output, inner_weight, outer_weight, self_biases, cross_biases,
        inner_bias.reshape(1, own_hidden), norm_gain, norm_shift, self_offset.reshape(1, width),
    )

    small_rows = 16 + SLICES
    block_output, grad, small, mgrad, dw_cross, dwi, dwo = call(
        middle,
        [
            ((rows, width), F32, "v"),
            ((rows, width), F32, "v"),
            ((small_rows, width), F32, "v"),
            ((frames, width), BF16, "h"),
            ((4 * width, width), BF16, "h"),
            ((hidden, width), BF16, "h"),
            ((hidden, width), BF16, "h"),
        ],
        "ssvvvvvvvvvhhhhh",
        [
            ((frames, width), BF16),
            ((frames, width), BF16),
            ((frames, width), BF16),
            ((hidden, width), BF16),
            ((hidden, width), BF16),
            ((frames, width), BF16),
            ((4, width, width), F32),
            ((4 * width, width), BF16),
            ((hidden, width), BF16),
            ((hidden, width), BF16),
            ((blocks, wide, width), BF16),
            ((blocks, wide, width), BF16),
            ((blocks, 1, wide), F32),
            ((blocks, 1, wide), F32),
            ((width, BLOCK), F32),
            ((width, rows), F32),
            ((CHUNK, width), F32),
            ((CHUNK, width), F32),
            dma((5,)),
            dma((3,)),
            dma((frames // CHUNK,)),
        ],
    )(
        tok_lengths, frame_lengths, cq, after, cotangent, wcross, inner_row, norm_gain, norm_shift,
        cross_offset.reshape(1, width), outer_offset.reshape(1, width),
        ck, cv, memory_rows, inner, outer,
    )

    memory_grad = lax.psum_scatter(mgrad, "mp", scatter_dimension=0, tiled=True).astype(F32)

    dn, halo_grad, dw_self, small = call(
        epilogue,
        [
            ((rows, width), F32, "v"),
            ((HALO, width), BF16, "v"),
            ((4, width, width), F32, "v"),
            ((small_rows, width), F32, "v"),
        ],
        "ssvvvvvvvv",
        [
            ((rows + HALO, width), F32),
            ((rows + HALO, width), F32),
            ((rows, width), BF16),
        ],
    )(tok_lengths, frame_lengths, n1, q, k, v, att, grad, wself, small)
    arrived = lax.ppermute(halo_grad, "mp", [(i + 1, i) for i in range(parts - 1)])
    dn = dn + jnp.pad(arrived.astype(F32), ((rows - HALO, 0), (0, 0)))
    xhat, scale = normed(block_input.astype(F32))
    input_grad = grad + norm_back(dn, norm_gain[0], xhat, scale)
    small = small.at[0].set(jnp.sum(dn * xhat, axis=0)).at[3].set(jnp.sum(dn, axis=0))

    small = lax.psum(small, ("dp", "mp"))

    def collected(values):
        values = values.reshape(SLICES, parts, values.shape[0] // SLICES // parts, width)
        mine = lax.psum_scatter(values, "mp", scatter_dimension=1, tiled=True)
        mine = lax.psum(mine.astype(F32), "dp")
        return mine.reshape(mine.shape[0] * mine.shape[2], width)

    dself = collected(dw_self.astype(BF16).reshape(4 * width, width)).reshape(4, own, width)
    dcross = collected(dw_cross).reshape(4, own, width)
    dinner, douter = collected(dwi), collected(dwo)
    me = lax.axis_index("mp")

    def turned(weights):
        return jnp.swapaxes(weights, 1, 2)

    def own_heads(values):
        count = values.shape[0]
        pieces = values.reshape(count, 2, parts, own // 2)
        return lax.dynamic_slice_in_dim(pieces, me, 1, axis=2).reshape(count, own)

    inner_bias_grad = lax.dynamic_slice_in_dim(
        small[16:].reshape(SLICES, parts, own_hidden // SLICES), me, 1, axis=1
    ).reshape(own_hidden)
    return (
        block_output,
        input_grad,
        memory_grad,
        small[0:3],
        small[3:6],
        turned(dself[0:3]),
        own_heads(small[9:11]),
        dself[3],
        small[6],
        turned(dcross[0:3]),
        own_heads(small[11:13]),
        dcross[3],
        small[7],
        dinner.T,
        inner_bias_grad,
        douter,
        small[8],
    )


def solution(mesh):
    in_specs = (
        P(("dp", "mp"), None),
        P(("dp", "mp"), None),
        P("dp", None),
        P("dp", None),
        P(("dp", "mp"), None),
        P(),
        P(),
        P(None, None, "mp"),
        P(None, "mp"),
        P("mp", None),
        P(),
        P(None, None, "mp"),
        P(None, "mp"),
        P("mp", None),
        P(),
        P(None, "mp"),
        P("mp"),
        P("mp", None),
        P(),
    )
    out_specs = (
        P(("dp", "mp"), None),
        P(("dp", "mp"), None),
        P(("dp", "mp"), None),
        P(),
        P(),
        P(None, None, "mp"),
        P(None, "mp"),
        P("mp", None),
        P(),
        P(None, None, "mp"),
        P(None, "mp"),
        P("mp", None),
        P(),
        P(None, "mp"),
        P("mp"),
        P("mp", None),
        P(),
    )
    return jax.shard_map(shards, mesh=mesh, in_specs=in_specs, out_specs=out_specs, check_vma=False)
```

```python
import functools
import math

import jax
import jax.numpy as jnp
from jax import lax
from jax.experimental import pallas as pl
from jax.experimental.pallas import tpu as pltpu
from jax.sharding import PartitionSpec as P

HEAD = 64
NEGATIVE = -1e30
EPSILON = 1e-05
BLOCK = 128
CHUNK = 256
HALO = 256
F32 = jnp.float32
BF16 = jnp.bfloat16
MESH = pl.DeviceIdType.MESH
HALF = HEAD // 2
SLICES = 8
PIECES = 4
GELU_A = math.sqrt(2.0 / math.pi)
GELU_B = 0.044715


def mm(a, b, ca=1, cb=0):
    return lax.dot_general(a, b, (((ca,), (cb,)), ((), ())), preferred_element_type=F32)


def normed(values):
    center = values - jnp.mean(values, axis=-1, keepdims=True)
    spread = jnp.mean(center * center, axis=-1, keepdims=True)
    scale = lax.rsqrt(spread + EPSILON)
    return center * scale, scale


def norm_back(grad, gain, xhat, scale):
    gn = grad * gain
    first = jnp.mean(gn, axis=-1, keepdims=True)
    second = jnp.mean(gn * xhat, axis=-1, keepdims=True)
    return (gn - first - xhat * second) * scale


def column_sums(values):
    return jnp.sum(values, axis=0, keepdims=True)


def head_stack(values):
    rows, width = values.shape
    heads = width // HEAD
    lane = lax.broadcasted_iota(jnp.int32, (rows, width), 1) // HALF % heads
    zero = jnp.zeros_like(values)
    return jnp.concatenate([jnp.where(lane == h, values, zero) for h in range(heads)], axis=0)


def head_rows(heads):
    return [
        (slice((i * heads + h) * HALF, (i * heads + h + 1) * HALF), h)
        for i in range(2)
        for h in range(heads)
    ]


def head_diagonal(values, heads):
    rows = values.shape[1] // heads
    return jnp.concatenate(
        [values[r, h * rows : (h + 1) * rows] for r, h in head_rows(heads)], axis=0
    )


def token_rows(tok_ref, frm_ref, base, count):
    place = lax.broadcasted_iota(jnp.int32, (1, count), 1) + base
    zero = jnp.zeros((1, count), jnp.int32)

    def step(u, carry):
        start, first_row, first_frame, end_frame = carry
        tokens, frames = tok_ref[0, u], frm_ref[0, u]
        end = start + tokens
        done = place >= end
        first_row = first_row + jnp.where(done, tokens, 0)
        first_frame = first_frame + jnp.where(done, frames, 0)
        end_frame = end_frame + jnp.where(place >= start, frames, 0)
        return end, first_row, first_frame, end_frame

    _, first_row, first_frame, end_frame = lax.fori_loop(
        0, tok_ref.shape[1], step, (jnp.int32(0), zero, zero, zero)
    )
    return place, first_row, first_frame, end_frame


def block_frames(tok_ref, frm_ref, base, count):
    blocks = count // BLOCK

    def step(u, carry):
        start, low, high = carry
        tokens, frames = tok_ref[0, u], frm_ref[0, u]
        end = start + tokens
        low = tuple(
            v + jnp.where(base + b * BLOCK >= end, frames, 0) for b, v in enumerate(low)
        )
        high = tuple(
            v + jnp.where(base + (b + 1) * BLOCK - 1 >= start, frames, 0) for b, v in enumerate(high)
        )
        return end, low, high

    zeros = (jnp.int32(0),) * blocks
    _, low, high = lax.fori_loop(0, tok_ref.shape[1], step, (jnp.int32(0), zeros, zeros))
    return low, high


def window_mask(place, first_row, base, block, count):
    keys = lax.broadcasted_iota(jnp.int32, (count, BLOCK), 0) + (base - HALO + block * BLOCK)
    here = slice(block * BLOCK, (block + 1) * BLOCK)
    return (keys >= first_row[:, here]) & (keys <= place[:, here])


def self_probs(queries, key_window, mask, heads):
    scores = mm(key_window, queries, 1, 1)
    parts = []
    for h in range(heads):
        part = jnp.where(mask, scores[:, h * BLOCK : (h + 1) * BLOCK], NEGATIVE)
        raised = jnp.exp(part - jnp.max(part, axis=0, keepdims=True))
        parts.append(raised * (1.0 / jnp.sum(raised, axis=0, keepdims=True)))
    return jnp.concatenate(parts, axis=1)


def rcopy(src, dst, send, recv, **device):
    return pltpu.make_async_remote_copy(
        src_ref=src, dst_ref=dst, send_sem=send, recv_sem=recv, device_id=device, device_id_type=MESH
    )


def at_rows(start, count):
    return pl.ds(pl.multiple_of(start, 16), count)


def flipped(index, bit):
    return index + bit - 2 * bit * (index // bit % 2)


def greet(z, parts, d, bits):
    barrier = pltpu.get_barrier_semaphore()
    for step in range(1, parts):
        device = {"mp": (z + step) % parts}
        pl.semaphore_signal(barrier, inc=1, device_id=device, device_id_type=MESH)
    for bit in bits:
        device = {"dp": flipped(d, bit)}
        pl.semaphore_signal(barrier, inc=1, device_id=device, device_id_type=MESH)
    return barrier, parts - 1 + len(bits)


class Line:
    def __init__(self, z, parts, own, place, sems):
        self.z, self.parts, self.own, self.place, self.sems = z, parts, own, place, sems

    def copy(self, k, up):
        shard = self.z - k if up else self.z + k
        kind = 0 if up else 2
        return rcopy(
            self.own if k == 0 else self.place(shard),
            self.place(shard),
            self.sems.at[kind, k],
            self.sems.at[kind + 1, k],
            mp=self.z + 1 if up else self.z - 1,
        )

    def sends(self, k, up):
        if up:
            return (self.z >= k) & (self.z < self.parts - 1)
        return (self.z + k < self.parts) & (self.z > 0)

    def send(self, k):
        for up in (True, False):

            @pl.when(self.sends(k, up))
            def _():
                self.copy(k, up).start()

    def arrive(self, k, up):
        shard = self.z - 1 - k if up else self.z + 1 + k
        kind = 0 if up else 2
        rcopy(
            self.place(shard),
            self.place(shard),
            self.sems.at[kind, k],
            self.sems.at[kind + 1, k],
            mp=self.z - 1 if up else self.z + 1,
        ).wait_recv()

    def comes(self, k, up):
        return self.z >= k + 1 if up else self.z + 1 + k < self.parts

    def arrived(self, k):
        for up in (True, False):

            @pl.when(self.comes(k, up))
            def _():
                self.arrive(k, up)

    def close(self):
        for k in range(self.parts - 1):
            for up in (True, False):

                @pl.when(self.sends(k, up))
                def _():
                    self.copy(k, up).wait_send()


class Direct:
    def __init__(self, z, parts, own, place, sems):
        self.z, self.parts, self.own, self.place, self.sems = z, parts, own, place, sems

    def copy(self, step):
        device = (self.z + step) % self.parts
        sems = self.sems
        return rcopy(self.own, self.place(self.z), sems.at[0, step], sems.at[1, step], mp=device)

    def send(self):
        for step in range(1, self.parts):
            self.copy(step).start()

    def arrived(self):
        for step in range(1, self.parts):
            other = (self.z - step + self.parts) % self.parts
            place, sems = self.place(other), self.sems
            rcopy(place, place, sems.at[0, step], sems.at[1, step], mp=other).wait_recv()

    def close(self):
        for step in range(1, self.parts):
            self.copy(step).wait_send()


DP_BITS = (2, 4, 1)
SLICE_BITS = (1, 2, 4)


class Plane:
    def __init__(self, d, s, buffer, rows, sems):
        self.d, self.s, self.buffer, self.rows, self.sems = d, s, buffer, rows, sems

    def block(self, s, p):
        bit = SLICE_BITS[p]
        return self.buffer.at[at_rows((s - s % bit) * self.rows, bit * self.rows)]

    def copy(self, p, s):
        block = self.block(s, p)
        device = flipped(self.d, DP_BITS[p])
        return rcopy(block, block, self.sems.at[0, p], self.sems.at[1, p], dp=device)

    def send(self, p):
        self.copy(p, self.s).start()

    def arrived(self, p):
        self.copy(p, flipped(self.s, SLICE_BITS[p])).wait_recv()

    def close(self):
        for p in range(3):
            self.copy(p, self.s).wait_send()


def gather(
    tok, frm, x_ref, mem, sw, so, cw, co, inner, outer, sb, cb, ib, gain, shift, offset,
    wself_out, wcross_out, inner_out, outer_out, ib_out, mem_out, ck_out, cv_out,
    n1_ref, q_ref, k_ref, v_ref, att_ref, after_ref, cq_ref,
    gself, gcross, ginner, gouter, gmem, sck, scv, pself, pcross, pinner, halo, pbias, gbias,
    line_sems, mem_sems, plane_sems, bias_sems, halo_sems, own_sem, out_sems, weight_sems,
):
    rows, width = x_ref.shape
    heads = width // HEAD
    parts = width // sw.shape[2]
    own = sw.shape[2]
    shard_rows = mem.shape[0]
    piece = shard_rows // PIECES
    z, d = lax.axis_index("mp"), lax.axis_index("dp")
    s = d % 2 * 4 + d // 2 % 4
    barrier, greetings = greet(z, parts, d, DP_BITS)

    for source, last, packed in ((sw, so, pself), (cw, co, pcross)):
        for i in range(3):
            packed[i * own : (i + 1) * own] = source[i].T
        packed[3 * own :] = last[...]
    pbias[...] = jnp.zeros_like(pbias)
    pbias[0:1] = ib[...]
    for i in range(2):
        pbias[1:2, i * own : (i + 1) * own] = sb[i : i + 1]
        pbias[1:2, (2 + i) * own : (3 + i) * own] = cb[i : i + 1]
    pinner[...] = inner[...].T
    groups = []
    for i, (packed, buffer) in enumerate(
        ((pself, gself), (pcross, gcross), (pinner, ginner), (outer, gouter))
    ):
        n = packed.shape[0] // SLICES
        mine = packed.at[at_rows(s * n, n)]

        def place(shard, buffer=buffer, n=n):
            return buffer.at[at_rows((s * parts + shard) * n, n)]

        line = Direct(z, parts, mine, place, line_sems.at[i])
        plane = Plane(d, s, buffer, parts * n, plane_sems.at[i])
        groups.append((line, plane))
        buffer[at_rows((s * parts + z) * n, n)] = packed[at_rows(s * n, n)]
    memory = []
    for c in range(PIECES):

        def place(shard, c=c):
            return gmem.at[at_rows(shard * shard_rows + c * piece, piece)]

        memory.append(Line(z, parts, mem.at[c * piece : (c + 1) * piece], place, mem_sems.at[c]))

    def bias_copy(step):
        return rcopy(
            pbias, gbias.at[z], bias_sems.at[0, step], bias_sems.at[1, step], mp=(z + step) % parts
        )

    def bias_arrival(step):
        other = (z - step + parts) % parts
        return rcopy(pbias, gbias.at[other], bias_sems.at[0, step], bias_sems.at[1, step], mp=other)

    def halo_copy(other):
        return rcopy(x_ref.at[rows - HALO :], halo, halo_sems.at[0], halo_sems.at[1], mp=other)

    def forward(c, k):
        memory[c].arrived(k)
        memory[c].send(k + 1)

    pl.semaphore_wait(barrier, greetings)
    for line, _ in groups[:2]:
        line.send()
    for step in range(1, parts):
        bias_copy(step).start()

    @pl.when(z < parts - 1)
    def _():
        halo_copy(z + 1).start()

    for line, _ in groups[2:]:
        line.send()
    for line in memory:
        line.send(0)
    own_rows = gmem.at[at_rows(z * shard_rows, shard_rows)]
    own_copy = pltpu.make_async_copy(mem, own_rows, own_sem)
    own_copy.start()
    gbias[z] = pbias[...]
    for line, plane in groups[:2]:
        line.arrived()
        plane.send(0)
    for _, plane in groups[:2]:
        plane.arrived(0)
        plane.send(1)
    for line, plane in groups[2:]:
        line.arrived()
        plane.send(0)
    for _, plane in groups[:2]:
        plane.arrived(1)
        plane.send(2)
    groups[0][1].arrived(2)

    for step in range(1, parts):
        bias_arrival(step).wait_recv()

    def head_bias(i):
        return jnp.concatenate(
            [
                gbias[o, 1:2, i * own + half * HALF : i * own + (half + 1) * HALF]
                for half in range(2)
                for o in range(parts)
            ],
            axis=1,
        )

    n = ginner.shape[0] // SLICES // parts
    for i in range(SLICES):
        ib_out[i : i + 1] = jnp.concatenate(
            [gbias[o, 0:1, i * n : (i + 1) * n] for o in range(parts)], axis=1
        )

    @pl.when(z > 0)
    def _():
        halo_copy(z - 1).wait_recv()

    @pl.when(z == 0)
    def _():
        halo[...] = jnp.zeros_like(halo)

    def weight(buffer, i):
        return buffer[i * width : (i + 1) * width]

    base = z * rows
    place_row, first_row, _, _ = token_rows(tok, frm, base, rows)
    for src, dst in ((halo, slice(0, HALO)), (x_ref, slice(HALO, HALO + rows))):
        xhat, _ = normed(src[...].astype(F32))
        n1_ref[dst] = (xhat * gain[0:1] + shift[0:1]).astype(BF16)
    n1 = n1_ref[...]
    query = mm(n1[HALO:], weight(gself, 0), 1, 1) + head_bias(0)
    q_ref[...] = query.astype(BF16) * jnp.asarray(0.125, BF16)
    k_ref[...] = mm(n1, weight(gself, 1), 1, 1).astype(BF16)
    v_ref[...] = (mm(n1, weight(gself, 2), 1, 1) + head_bias(1)).astype(BF16)
    count = HALO + BLOCK
    for b in range(rows // BLOCK):
        queries = head_stack(q_ref[b * BLOCK : (b + 1) * BLOCK])
        window = slice(b * BLOCK, b * BLOCK + count)
        mask = window_mask(place_row, first_row, base, b, count)
        probs = self_probs(queries, k_ref[window], mask, heads).astype(BF16)
        out = head_diagonal(mm(v_ref[window], probs, 0, 0), heads)
        att_ref[b * BLOCK : (b + 1) * BLOCK] = out.T.astype(BF16)
        if b == 0:
            for _, plane in groups[2:]:
                plane.arrived(0)
                plane.send(1)
    forward(0, 0)
    after = x_ref[...].astype(F32) + mm(att_ref[...], weight(gself, 3)) + offset[...]
    after_ref[...] = after
    xhat, _ = normed(after)
    groups[1][1].arrived(2)
    n2 = (xhat * gain[1:2] + shift[1:2]).astype(BF16)
    query = mm(n2, weight(gcross, 0), 1, 1) + head_bias(2)
    cq_ref[...] = query.astype(BF16) * jnp.asarray(0.125, BF16)
    value_bias = head_bias(3)
    forward(1, 0)

    def project(start, size):
        here = at_rows(start, size)
        block = gmem[here]
        sck[here] = mm(block, weight(gcross, 1), 1, 1).astype(BF16)
        scv[here] = (mm(block, weight(gcross, 2), 1, 1) + value_bias).astype(BF16)

    def copies_out(shard):
        here = at_rows(shard * shard_rows, shard_rows)
        return [
            pltpu.make_async_copy(a.at[here], b.at[here], out_sems.at[shard, i])
            for i, (a, b) in enumerate(((gmem, mem_out), (sck, ck_out), (scv, cv_out)))
        ]

    def project_shard(shard):
        lax.fori_loop(
            0, PIECES, lambda c, _: (project(shard * shard_rows + c * piece, piece), 0)[1], 0
        )
        for copy in copies_out(shard):
            copy.start()

    own_copy.wait()
    project_shard(z)
    forward(2, 0)
    for _, plane in groups[2:]:
        plane.arrived(1)
        plane.send(2)
    forward(3, 0)
    for up in (True, False):

        @pl.when(memory[0].comes(0, up))
        def _():
            project_shard(z - 1 if up else z + 1)

    for _, plane in groups[2:]:
        plane.arrived(2)
    outs = [
        pltpu.make_async_copy(a, b, weight_sems.at[i])
        for i, (a, b) in enumerate(
            ((gself, wself_out), (gcross, wcross_out), (ginner, inner_out), (gouter, outer_out))
        )
    ]
    for copy in outs:
        copy.start()
    for k in range(1, parts - 1):
        for c in range(PIECES):
            memory[c].arrived(k)
            if k < parts - 2:
                memory[c].send(k + 1)
            for up in (True, False):

                @pl.when(memory[c].comes(k, up))
                def _():
                    shard = z - 1 - k if up else z + 1 + k
                    project(shard * shard_rows + c * piece, piece)
                    if c == PIECES - 1:
                        for copy in copies_out(shard):
                            copy.start()

    for copy in outs:
        copy.wait()

    def finish(shard, carry):
        for copy in copies_out(shard):
            copy.wait()
        return carry

    lax.fori_loop(0, parts, finish, 0)
    for line, plane in groups:
        line.close()
        plane.close()
    for line in memory:
        line.close()
    for step in range(1, parts):
        bias_copy(step).wait_send()

    @pl.when(z < parts - 1)
    def _():
        halo_copy(z + 1).wait_send()


def middle(
    tok, frm, cq_ref, after_ref, cot_ref, w_ref, ib_ref, gain, shift, cross_offset, outer_offset,
    ck_in, cv_in, mem_in, wi_in, wo_in,
    out_ref, grad_ref, small_ref, mgrad_out, dw_out, dwi_out, dwo_out,
    ck_ref, cv_ref, mem_ref, wi_ref, wo_ref, mgrad_ref, dw_ref, dwb_ref, dwi_ref, dwo_ref,
    qbig, gbig, lse_ref, dot_ref, acc, dq_ref, dk_ref, dv_ref,
    in_sems, out_sems, chunk_sems,
):
    loads = [
        pltpu.make_async_copy(a, b, in_sems.at[i])
        for i, (a, b) in enumerate(
            ((ck_in, ck_ref), (cv_in, cv_ref), (wi_in, wi_ref), (wo_in, wo_ref), (mem_in, mem_ref))
        )
    ]
    for load in loads:
        load.start()
    rows, width = cq_ref.shape
    heads = width // HEAD
    blocks = rows // BLOCK
    frames = mem_ref.shape[0]

    def weight(i):
        return w_ref[i * width : (i + 1) * width]

    base = lax.axis_index("mp") * rows
    _, _, first_frame, end_frame = token_rows(tok, frm, base, rows)
    low, high = block_frames(tok, frm, base, rows)
    small_ref[...] = jnp.zeros_like(small_ref)

    def chunk_mask(c, b):
        frame = lax.broadcasted_iota(jnp.int32, (CHUNK, BLOCK), 0) + c * CHUNK
        here = slice(b * BLOCK, (b + 1) * BLOCK)
        return (frame >= first_frame[:, here]) & (frame < end_frame[:, here])

    loads[0].wait()
    loads[1].wait()
    attended = []
    for b in range(blocks):
        qbig[b] = head_stack(cq_ref[b * BLOCK : (b + 1) * BLOCK])
        acc[...] = jnp.zeros_like(acc)

        def step(c, carry):
            largest, total = carry
            here = pl.ds(pl.multiple_of(c * CHUNK, CHUNK), CHUNK)
            scores = mm(ck_ref[here], qbig[b], 1, 1)
            mask = chunk_mask(c, b)
            scores = jnp.where(jnp.concatenate([mask] * heads, axis=1), scores, NEGATIVE)
            now = jnp.maximum(largest, jnp.max(scores, axis=0, keepdims=True))
            fade = jnp.exp(largest - now)
            raised = jnp.exp(scores - now)
            total = total * fade + jnp.sum(raised, axis=0, keepdims=True)
            part = mm(cv_ref[here], raised.astype(BF16), 0, 0)
            for r, h in head_rows(heads):
                l = slice(h * BLOCK, (h + 1) * BLOCK)
                acc[r] = acc[r] * fade[:, l] + part[r, l]
            return now, total

        start = (jnp.full((1, heads * BLOCK), NEGATIVE, F32), jnp.zeros((1, heads * BLOCK), F32))
        largest, total = lax.fori_loop(low[b] // CHUNK, (high[b] + CHUNK - 1) // CHUNK, step, start)
        lse_ref[b] = largest + jnp.log(total)
        share = 1.0 / total
        for r, h in head_rows(heads):
            l = slice(h * BLOCK, (h + 1) * BLOCK)
            acc[r] = acc[r] * share[:, l]
        attended.append(acc[...])
    att_t = jnp.concatenate(attended, axis=1)
    att = att_t.T.astype(BF16)
    after_self = after_ref[...]
    after_cross = after_self + mm(att, weight(3)) + cross_offset[...]
    xhat3, scale3 = normed(after_cross)
    n3 = (xhat3 * gain[2:3] + shift[2:3]).astype(BF16)
    sent = cot_ref[...]
    small_ref[8:9] = column_sums(sent.astype(F32))
    hidden = wi_ref.shape[0]
    tile = hidden // SLICES
    loads[2].wait()
    loads[3].wait()
    out = after_cross + outer_offset[...]
    dn3 = jnp.zeros((rows, width), F32)
    for f in range(hidden // tile):
        here = slice(f * tile, (f + 1) * tile)
        before = mm(n3, wi_ref[here], 1, 1) + ib_ref[f : f + 1]
        square = before * before
        inner = jnp.tanh(GELU_A * (before + GELU_B * (before * square)))
        half = 0.5 * (1.0 + inner)
        active = (before * half).astype(BF16)
        slope = half + 0.5 * before * (1.0 - inner * inner) * (
            GELU_A + (3.0 * GELU_A * GELU_B) * square
        )
        out = out + mm(active, wo_ref[here])
        back = (slope * mm(sent, wo_ref[here], 1, 1)).astype(BF16)
        dn3 = dn3 + mm(back, wi_ref[here])
        dwo_ref[here] = mm(active, sent, 0, 0).astype(BF16)
        dwi_ref[here] = mm(back, n3, 0, 0).astype(BF16)
        small_ref[16 + f : 17 + f] = column_sums(back.astype(F32))
    stores = [
        pltpu.make_async_copy(a, b, out_sems.at[i])
        for i, (a, b) in enumerate(((dwi_ref, dwi_out), (dwo_ref, dwo_out), (dwb_ref, dw_out)))
    ]
    stores[0].start()
    stores[1].start()
    out_ref[...] = out
    small_ref[2:3] = column_sums(dn3 * xhat3)
    small_ref[5:6] = column_sums(dn3)
    grad = sent.astype(F32) + norm_back(dn3, gain[2:3], xhat3, scale3)
    sent2 = grad.astype(BF16)
    small_ref[7:8] = column_sums(sent2.astype(F32))
    dw_ref[3] = mm(att, sent2, 0, 0)
    go = mm(sent2, weight(3), 1, 1).astype(BF16)
    got = mm(weight(3), sent2, 1, 1).astype(BF16).astype(F32)
    prod = got * att_t
    for b in range(blocks):
        gbig[b] = head_stack(go[b * BLOCK : (b + 1) * BLOCK])
        sums = [column_sums(prod[r, b * BLOCK : (b + 1) * BLOCK]) for r, _ in head_rows(heads)]
        for h in range(heads):
            dot_ref[b, :, h * BLOCK : (h + 1) * BLOCK] = sums[h] + sums[heads + h]
    dq_ref[...] = jnp.zeros_like(dq_ref)
    dw_ref[1] = jnp.zeros((width, width), F32)
    dw_ref[2] = jnp.zeros((width, width), F32)

    loads[4].wait()

    def chunk_store(c):
        here = pl.ds(pl.multiple_of(c * CHUNK, CHUNK), CHUNK)
        return pltpu.make_async_copy(mgrad_ref.at[here], mgrad_out.at[here], chunk_sems.at[c])

    def frame_step(c, carry):
        here = pl.ds(pl.multiple_of(c * CHUNK, CHUNK), CHUNK)
        meets = [(low[b] < (c + 1) * CHUNK) & (high[b] > c * CHUNK) for b in range(blocks)]
        some = functools.reduce(jnp.logical_or, meets)

        @pl.when(some)
        def _():
            dk_ref[...] = jnp.zeros_like(dk_ref)
            dv_ref[...] = jnp.zeros_like(dv_ref)
            for b in range(blocks):

                @pl.when(meets[b])
                def _():
                    keys, values = ck_ref[here], cv_ref[here]
                    scores = mm(keys, qbig[b], 1, 1)
                    mask = chunk_mask(c, b)
                    mask = jnp.concatenate([mask] * heads, axis=1)
                    shares = jnp.where(mask, jnp.exp(scores - lse_ref[b]), 0.0)
                    dp = mm(values, gbig[b], 1, 1)
                    ds = (shares * (dp - dot_ref[b])).astype(BF16)
                    dv_ref[...] += mm(shares.astype(BF16), gbig[b])
                    dk_ref[...] += mm(ds, qbig[b])
                    l = slice(b * BLOCK, (b + 1) * BLOCK)
                    dq_ref[:, l] += head_diagonal(mm(keys, ds, 0, 0), heads)

            dk, dv = dk_ref[...].astype(BF16), dv_ref[...].astype(BF16)
            mgrad_ref[here] = (mm(dk, weight(1)) + mm(dv, weight(2))).astype(BF16)
            frame_rows = mem_ref[here]
            dw_ref[1] += mm(dk, frame_rows, 0, 0)
            dw_ref[2] += mm(dv, frame_rows, 0, 0)
            small_ref[12:13] += column_sums(dv.astype(F32))

        @pl.when(jnp.logical_not(some))
        def _():
            mgrad_ref[here] = jnp.zeros((CHUNK, width), BF16)

        chunk_store(c).start()
        return carry

    lax.fori_loop(0, frames // CHUNK, frame_step, 0)
    dq = (dq_ref[...] * 0.125).T.astype(BF16)
    small_ref[11:12] = column_sums(dq.astype(F32))
    xhat2, scale2 = normed(after_self)
    n2 = (xhat2 * gain[1:2] + shift[1:2]).astype(BF16)
    dw_ref[0] = mm(dq, n2, 0, 0)
    dn2 = mm(dq, weight(0))
    small_ref[1:2] = column_sums(dn2 * xhat2)
    small_ref[4:5] = column_sums(dn2)
    grad_ref[...] = grad + norm_back(dn2, gain[1:2], xhat2, scale2)
    for i in range(4):
        dwb_ref[i * width : (i + 1) * width] = dw_ref[i].astype(BF16)
    stores[2].start()

    def finish(c, carry):
        chunk_store(c).wait()
        return carry

    lax.fori_loop(0, frames // CHUNK, finish, 0)
    for store in stores:
        store.wait()


class Reduce:
    def __init__(self, d, z, parts, dp, local, first_x, buffers, sems):
        self.d, self.z, self.parts, self.dp = d, z, parts, dp
        self.local, self.first_x = local, first_x
        self.r1, self.a1, self.r2, self.a2, self.r3, self.a3, self.rz, self.wide, self.fin = buffers
        self.sems, self.extra_sems, self.plane_sems = sems
        self.c, self.y, self.x = d % 2, d // 4 % 2, d // 2 % 2
        n = self.rz.shape[1]
        self.s = self.c * 4 + self.y * 2 + self.x
        self.plane = Plane(d, self.s, self.fin, n, self.plane_sems)
        self.n = n
        self.bits = [8 << i for i in range(dp.bit_length() - 4)]

    def copy(self, p):
        if p == 0:
            src, dst, bit = self.local.at[1 - self.c], self.r1, 1
        elif p == 1:
            if self.first_x:
                src, dst, bit = self.a1.at[:, 1 - self.x], self.r2, 2
            else:
                src, dst, bit = self.a1.at[1 - self.y], self.r2, 4
        elif self.first_x:
            src, dst, bit = self.a2.at[1 - self.y], self.r3, 4
        else:
            src, dst, bit = self.a2.at[1 - self.x], self.r3, 2
        return rcopy(src, dst, self.sems.at[0, p], self.sems.at[1, p], dp=flipped(self.d, bit))

    def z_copy(self, step, other):
        sems = self.sems
        return rcopy(
            self.a3.at[other], self.rz.at[self.z], sems.at[0, 2 + step], sems.at[1, 2 + step], mp=other
        )

    def z_arrival(self, step, other):
        sems = self.sems
        return rcopy(
            self.a3.at[other], self.rz.at[other], sems.at[0, 2 + step], sems.at[1, 2 + step], mp=other
        )

    def extra(self, i):
        sems = self.extra_sems
        device = flipped(self.d, self.bits[i])
        return rcopy(self.wide.at[2 * i], self.wide.at[2 * i + 1], sems.at[0, i], sems.at[1, i], dp=device)

    def run(self, p):
        if p == 0:
            self.copy(0).start()
        elif p == 1:
            self.copy(0).wait_recv()
            self.a1[...] = (self.local[self.c].astype(F32) + self.r1[...].astype(F32)).astype(BF16)
            self.copy(1).start()
        elif p == 2:
            self.copy(1).wait_recv()
            mine = self.a1[:, self.x] if self.first_x else self.a1[self.y]
            self.a2[...] = (mine.astype(F32) + self.r2[...].astype(F32)).astype(BF16)
            self.copy(2).start()
        elif p == 3:
            self.copy(2).wait_recv()
            mine = self.a2[self.y] if self.first_x else self.a2[self.x]
            mine = mine.astype(F32) + self.r3[...].astype(F32)
            self.a3[...] = mine.astype(BF16).reshape(self.a3.shape)
            for step in range(1, self.parts):
                self.z_copy(step, (self.z + step) % self.parts).start()
        elif p == 4:
            self.rz[self.z] = self.a3[self.z]
            for step in range(1, self.parts):
                self.z_arrival(step, (self.z - step + self.parts) % self.parts).wait_recv()
            total = self.rz[0].astype(F32)
            for other in range(1, self.parts):
                total = total + self.rz[other].astype(F32)
            for i in range(len(self.bits)):
                self.wide[2 * i] = total
                self.extra(i).start()
                self.extra(i).wait_recv()
                total = total + self.wide[2 * i + 1]
            self.fin[at_rows(self.s * self.n, self.n)] = total.astype(BF16)
            self.plane.send(0)
        elif p in (5, 6):
            self.plane.arrived(p - 5)
            self.plane.send(p - 4)
        else:
            self.plane.arrived(2)

    def close(self):
        for p in range(3):
            self.copy(p).wait_send()
        for step in range(1, self.parts):
            self.z_copy(step, (self.z + step) % self.parts).wait_send()
        for i in range(len(self.bits)):
            self.extra(i).wait_send()
        self.plane.close()


class Total:
    def __init__(self, d, z, parts, bits, buffers, landing, line, sems, line_sems):
        self.d, self.z, self.parts, self.bits = d, z, parts, bits
        self.buffers, self.landing, self.line = buffers, landing, line
        self.sems, self.line_sems = sems, line_sems

    def copy(self, i):
        device = flipped(self.d, self.bits[i])
        sems = self.sems
        return rcopy(self.buffers.at[i], self.landing.at[i], sems.at[0, i], sems.at[1, i], dp=device)

    def z_copy(self, step, source):
        sems, last = self.line_sems, self.buffers.at[len(self.bits)]
        if source:
            other = (self.z - step + self.parts) % self.parts
            return rcopy(last, self.line.at[other], sems.at[0, step], sems.at[1, step], mp=other)
        other = (self.z + step) % self.parts
        return rcopy(last, self.line.at[self.z], sems.at[0, step], sems.at[1, step], mp=other)

    def run(self, p):
        if p > 0:
            self.copy(p - 1).wait_recv()
            self.buffers[p] = self.buffers[p - 1] + self.landing[p - 1]
        if p < len(self.bits):
            self.copy(p).start()
        else:
            for step in range(1, self.parts):
                self.z_copy(step, False).start()

    def finish(self, out):
        self.line[self.z] = self.buffers[len(self.bits)]
        for step in range(1, self.parts):
            self.z_copy(step, True).wait_recv()
        total = self.line[0]
        for other in range(1, self.parts):
            total = total + self.line[other]
        out[...] = total
        for i in range(len(self.bits)):
            self.copy(i).wait_send()
        for step in range(1, self.parts):
            self.z_copy(step, False).wait_send()


def give_back(
    window,
    tok, frm, x_ref, n1_ref, q_ref, k_ref, v_ref, att_ref, grad_ref, w_ref, small_in, gain,
    mgrad_in, dwc_in, dwi_in, dwo_in,
    input_out, mgrad_out, fself, fcross, finner, fouter, small_out,
    own, up_land, down_land, local_self, local_cross, local_inner, local_outer,
    dk_ref, dv_ref, dq_ref, halo_out, halo_land, total_buffers, total_land, total_line,
    self_bufs, cross_bufs, inner_bufs, outer_bufs,
    load_sems, flow_sems, reduce_sems, extra_sems, plane_sems, halo_sems, total_sems, line_sems,
):
    rows, width = q_ref.shape
    heads = width // HEAD
    parts = total_line.shape[0]
    shard_rows = mgrad_out.shape[0]
    piece = shard_rows // PIECES
    last = parts * PIECES
    z, d = lax.axis_index("mp"), lax.axis_index("dp")
    dp = lax.axis_size("dp")
    bits = [1 << i for i in range(dp.bit_length() - 1)]
    barrier, greetings = greet(z, parts, d, bits)
    loads = [
        pltpu.make_async_copy(a, b, load_sems.at[i])
        for i, (a, b) in enumerate(
            (
                (dwi_in, local_inner),
                (dwo_in, local_outer),
                (dwc_in, local_cross),
                (mgrad_in, own),
            )
        )
    ]
    for load in loads:
        load.start()
    chains = []
    for i, (local, first_x, bufs, fin) in enumerate(
        (
            (local_inner, False, inner_bufs, finner),
            (local_outer, True, outer_bufs, fouter),
            (local_cross, False, cross_bufs, fcross),
            (local_self, True, self_bufs, fself),
        )
    ):
        sems = (reduce_sems.at[i], extra_sems.at[i], plane_sems.at[i])
        chains.append(Reduce(d, z, parts, dp, local, first_x, (*bufs, fin), sems))
    inner, outer, cross, own_chain = chains

    def rows_of(number):
        return at_rows(number * piece, piece)

    def crosses(j, up):
        if up:
            return (z < parts - 1) & ((z + 1) * PIECES + j < last)
        return (z > 0) & (z * PIECES - 1 - j >= 0)

    def number(j, up):
        return (z + 1) * PIECES + j if up else z * PIECES - 1 - j

    def flow(j, up, summed):
        land = up_land if up else down_land
        kind = 0 if up else 2
        src = land.at[j + PIECES] if summed else mgrad_in.at[rows_of(number(j, up))]
        device = z + 1 if up else z - 1
        return rcopy(src, land.at[j], flow_sems.at[kind, j], flow_sems.at[kind + 1, j], mp=device)

    def comes(j, up):
        if up:
            return (z > 0) & (z * PIECES + j < last)
        return (z < parts - 1) & ((z + 1) * PIECES - 1 - j >= 0)

    def flow_arrival(j, up):
        land = up_land if up else down_land
        kind = 0 if up else 2
        device = z - 1 if up else z + 1
        return rcopy(
            land.at[j], land.at[j], flow_sems.at[kind, j], flow_sems.at[kind + 1, j], mp=device
        )

    def first_flows():
        for j in reversed(range(max(window - PIECES, 0), window)):
            for up in (True, False):

                @pl.when(crosses(j, up))
                def _():
                    flow(j, up, False).start()

    def next_flow(j):
        for up in (True, False):
            land = up_land if up else down_land

            @pl.when(crosses(j, up) & comes(j + PIECES, up))
            def _():
                flow_arrival(j + PIECES, up).wait_recv()
                mine = own[rows_of(number(j, up))]
                land[j + PIECES] = (land[j + PIECES].astype(F32) + mine.astype(F32)).astype(BF16)
                flow(j, up, True).start()

            @pl.when(crosses(j, up) & jnp.logical_not(comes(j + PIECES, up)))
            def _():
                flow(j, up, False).start()

    base = z * rows
    place, first_row, _, _ = token_rows(tok, frm, base, rows)

    def weight(i):
        return w_ref[i * width : (i + 1) * width]

    def halo_copy(other):
        return rcopy(halo_out, halo_land, halo_sems.at[0], halo_sems.at[1], mp=other)

    pl.semaphore_wait(barrier, greetings)
    first_flows()
    for load, chain in zip(loads[:3], chains[:3]):
        load.wait()
        chain.run(0)
    small = total_buffers.at[0]
    small[...] = small_in[...]
    grad = grad_ref[...]
    sent = grad.astype(BF16)
    small[6:7] = column_sums(sent.astype(F32))
    n = local_self.shape[3]

    def keep(i, values):
        for half in range(2):
            s = 2 * i + half
            local_self[s // 4, s // 2 % 2, s % 2] = values[half * n : (half + 1) * n].astype(BF16)

    keep(3, mm(att_ref[...], sent, 0, 0))
    go = mm(sent, weight(3), 1, 1).astype(BF16)
    dk_ref[...] = jnp.zeros_like(dk_ref)
    dv_ref[...] = jnp.zeros_like(dv_ref)
    for chain in chains[:3]:
        chain.run(1)
    count = HALO + BLOCK
    blocks = rows // BLOCK
    for b in range(blocks):
        here = slice(b * BLOCK, (b + 1) * BLOCK)
        span = slice(b * BLOCK, b * BLOCK + count)
        queries, grads = head_stack(q_ref[here]), head_stack(go[here])
        mask = window_mask(place, first_row, base, b, count)
        shares = self_probs(queries, k_ref[span], mask, heads)
        dp_ = mm(v_ref[span], grads, 1, 1)
        ds = (shares * (dp_ - jnp.sum(shares * dp_, axis=0, keepdims=True))).astype(BF16)
        dv_ref[span] += mm(shares.astype(BF16), grads)
        dk_ref[span] += mm(ds, queries)
        dq_ref[here] = (head_diagonal(mm(k_ref[span], ds, 0, 0), heads) * 0.125).T.astype(BF16)
    dq = dq_ref[...]
    dk, dv = dk_ref[...].astype(BF16), dv_ref[...].astype(BF16)
    n1 = n1_ref[...]
    dn = mm(dk, weight(1)) + mm(dv, weight(2))
    halo_out[...] = dn[:HALO].astype(BF16)

    @pl.when(z > 0)
    def _():
        halo_copy(z - 1).start()

    keep(0, mm(dq, n1[HALO:], 0, 0))
    keep(1, mm(dk, n1, 0, 0))
    keep(2, mm(dv, n1, 0, 0))
    own_chain.run(0)
    small[9:10] = column_sums(dq.astype(F32))
    small[10:11] = column_sums(dv.astype(F32))
    dn = dn[HALO:] + mm(dq, weight(0))
    for chain in chains[:3]:
        chain.run(2)
    own_chain.run(1)
    xhat, scale = normed(x_ref[...].astype(F32))

    @pl.when(z < parts - 1)
    def _():
        halo_copy(z + 1).wait_recv()

    @pl.when(z == parts - 1)
    def _():
        halo_land[...] = jnp.zeros_like(halo_land)

    dn = jnp.concatenate([dn[: rows - HALO], dn[rows - HALO :] + halo_land[...].astype(F32)], axis=0)
    input_out[...] = grad + norm_back(dn, gain[0:1], xhat, scale)
    small[0:1] = column_sums(dn * xhat)
    small[3:4] = column_sums(dn)
    total = Total(d, z, parts, bits, total_buffers, total_land, total_line, total_sems, line_sems)
    total.run(0)
    own_chain.run(2)
    for chain in chains[:3]:
        chain.run(3)
    loads[3].wait()
    total.run(1)
    own_chain.run(3)
    total.run(2)
    for j in reversed(range(max(window - PIECES, 0))):
        next_flow(j)
    for p in range(3, len(bits) + 1):
        total.run(p)
    for p in range(4, 8):
        for chain in chains:
            chain.run(p)

    @pl.when(z == 0)
    def _():
        up_land[:PIECES] = jnp.zeros((PIECES, piece, width), BF16)

    @pl.when(z == parts - 1)
    def _():
        down_land[:PIECES] = jnp.zeros((PIECES, piece, width), BF16)

    for i in range(PIECES):
        for up in (True, False):
            j = i if up else PIECES - 1 - i

            @pl.when(comes(j, up))
            def _():
                flow_arrival(j, up).wait_recv()

        mine = own[rows_of(z * PIECES + i)].astype(F32)
        sides = up_land[i].astype(F32) + down_land[PIECES - 1 - i].astype(F32)
        mgrad_out[i * piece : (i + 1) * piece] = (mine + sides).astype(BF16)
    total.finish(small_out)
    for chain in chains:
        chain.close()

    @pl.when(z > 0)
    def _():
        halo_copy(z - 1).wait_send()

    for j in range(window):
        for up in (True, False):
            @pl.when(crosses(j, up))
            def _():
                flow(j, up, False).wait_send()


def finals(
    mgrad, input_grad, fself, fcross, finner, fouter, small,
    out_mgrad, out_input, out_gain, out_shift, out_sw, out_sb, out_so, out_soff,
    out_cw, out_cb, out_co, out_coff, out_inner, out_ib, out_outer, out_ooff,
):
    z = lax.axis_index("mp")
    own = out_so.shape[0]
    parts = out_so.shape[1] // own
    out_mgrad[...] = mgrad[...].astype(F32)
    out_input[...] = input_grad[...]
    out_gain[...] = small[0:3]
    out_shift[...] = small[3:6]
    out_soff[...] = small[6:7]
    out_coff[...] = small[7:8]
    out_ooff[...] = small[8:9]

    def chosen(row, size, offset):
        pieces = [small[row : row + 1, offset + o * size : offset + (o + 1) * size] for o in range(parts)]
        result = pieces[0]
        for o in range(1, parts):
            result = jnp.where(z == o, pieces[o], result)
        return result

    for fin, weights, last, biases, first in (
        (fself, out_sw, out_so, out_sb, 9),
        (fcross, out_cw, out_co, out_cb, 11),
    ):
        for i in range(3):
            weights[i] = fin[i * own : (i + 1) * own].astype(F32).T
        last[...] = fin[3 * own :].astype(F32)
        for i in range(2):
            for half in range(2):
                lanes = slice(half * HALF, (half + 1) * HALF)
                biases[i : i + 1, lanes] = chosen(first + i, HALF, half * parts * HALF)
    out_inner[...] = finner[...].astype(F32).T
    out_outer[...] = fouter[...].astype(F32)
    size = out_ib.shape[1] // SLICES
    for s in range(SLICES):
        out_ib[0:1, s * size : (s + 1) * size] = chosen(16 + s, size, 0)


def call(body, outs, ins, scratch, **params):
    places = {"s": pltpu.SMEM, "v": pltpu.VMEM, "h": pl.ANY}

    def spec(place):
        return pl.BlockSpec(memory_space=places[place])

    def run(*args):
        return pl.pallas_call(
            body,
            out_shape=[jax.ShapeDtypeStruct(shape, kind) for shape, kind, _ in outs],
            in_specs=[spec(place) for place in ins],
            out_specs=[spec(place) for _, _, place in outs],
            scratch_shapes=[pltpu.VMEM(*x) if isinstance(x, tuple) else x for x in scratch],
            compiler_params=pltpu.CompilerParams(vmem_limit_bytes=56 << 20, **params),
        )(*args)

    return run


def shards(
    block_input,
    memory,
    tok_lengths,
    frame_lengths,
    cotangent,
    norm_gain,
    norm_shift,
    self_weights,
    self_biases,
    self_output,
    self_offset,
    cross_weights,
    cross_biases,
    cross_output,
    cross_offset,
    inner_weight,
    inner_bias,
    outer_weight,
    outer_offset,
):
    rows, width = block_input.shape
    parts = lax.axis_size("mp")
    frames = memory.shape[0] * parts
    heads = width // HEAD
    blocks = rows // BLOCK
    own_hidden = inner_weight.shape[1]
    hidden = own_hidden * parts
    own = width // parts
    dma = pltpu.SemaphoreType.DMA
    wide = heads * BLOCK

    (
        wself, wcross, inner, outer, inner_row, memory_rows, ck, cv, n1, q, k, v, att, after, cq
    ) = call(
        gather,
        [
            ((4 * width, width), BF16, "h"),
            ((4 * width, width), BF16, "h"),
            ((hidden, width), BF16, "h"),
            ((hidden, width), BF16, "h"),
            ((SLICES, hidden // SLICES), F32, "v"),
            ((frames, width), BF16, "h"),
            ((frames, width), BF16, "h"),
            ((frames, width), BF16, "h"),
            ((rows + HALO, width), BF16, "v"),
            ((rows, width), BF16, "v"),
            ((rows + HALO, width), BF16, "v"),
            ((rows + HALO, width), BF16, "v"),
            ((rows, width), BF16, "v"),
            ((rows, width), F32, "v"),
            ((rows, width), BF16, "v"),
        ],
        "ssvhvvvvvvvvvvvv",
        [
            ((4 * width, width), BF16),
            ((4 * width, width), BF16),
            ((hidden, width), BF16),
            ((hidden, width), BF16),
            ((frames, width), BF16),
            ((frames, width), BF16),
            ((frames, width), BF16),
            ((4 * own, width), BF16),
            ((4 * own, width), BF16),
            ((own_hidden, width), BF16),
            ((HALO, width), BF16),
            ((8, own_hidden), F32),
            ((parts, 8, own_hidden), F32),
            dma((4, 2, parts)),
            dma((PIECES, 4, parts - 1)),
            dma((4, 2, 3)),
            dma((2, parts)),
            dma((2,)),
            dma,
            dma((parts, 3)),
            dma((4,)),
        ],
        collective_id=0,
        has_side_effects=True,
    )(
        tok_lengths, frame_lengths, block_input, memory, self_weights, self_output, cross_weights,
        cross_output, inner_weight, outer_weight, self_biases, cross_biases,
        inner_bias.reshape(1, own_hidden), norm_gain, norm_shift, self_offset.reshape(1, width),
    )

    small_rows = 16 + SLICES
    block_output, grad, small, mgrad, dw_cross, dwi, dwo = call(
        middle,
        [
            ((rows, width), F32, "v"),
            ((rows, width), F32, "v"),
            ((small_rows, width), F32, "v"),
            ((frames, width), BF16, "h"),
            ((4 * width, width), BF16, "h"),
            ((hidden, width), BF16, "h"),
            ((hidden, width), BF16, "h"),
        ],
        "ssvvvvvvvvvhhhhh",
        [
            ((frames, width), BF16),
            ((frames, width), BF16),
            ((frames, width), BF16),
            ((hidden, width), BF16),
            ((hidden, width), BF16),
            ((frames, width), BF16),
            ((4, width, width), F32),
            ((4 * width, width), BF16),
            ((hidden, width), BF16),
            ((hidden, width), BF16),
            ((blocks, wide, width), BF16),
            ((blocks, wide, width), BF16),
            ((blocks, 1, wide), F32),
            ((blocks, 1, wide), F32),
            ((width, BLOCK), F32),
            ((width, rows), F32),
            ((CHUNK, width), F32),
            ((CHUNK, width), F32),
            dma((5,)),
            dma((3,)),
            dma((frames // CHUNK,)),
        ],
    )(
        tok_lengths, frame_lengths, cq, after, cotangent, wcross, inner_row, norm_gain, norm_shift,
        cross_offset.reshape(1, width), outer_offset.reshape(1, width),
        ck, cv, memory_rows, inner, outer,
    )

    n_att, n_ffn = own * 4 // SLICES, own_hidden // SLICES
    dp = lax.axis_size("dp")
    n_bits = dp.bit_length() - 1
    window = PIECES * (parts - 1)
    piece = memory.shape[0] // PIECES

    def sliced(n):
        return (2, 2, 2, parts * n, width)

    def reduce_buffers(n):
        full = parts * n
        return [
            pltpu.VMEM((2, 2, full, width), BF16),
            pltpu.VMEM((2, 2, full, width), BF16),
            pltpu.VMEM((2, full, width), BF16),
            pltpu.VMEM((2, full, width), BF16),
            pltpu.VMEM((full, width), BF16),
            pltpu.VMEM((parts, n, width), BF16),
            pltpu.VMEM((parts, n, width), BF16),
            pltpu.VMEM((2 * max(n_bits - 3, 1), n, width), F32),
        ]

    input_grad, mgrad_sum, fself, fcross, finner, fouter, small = call(
        functools.partial(give_back, window),
        [
            ((rows, width), F32, "v"),
            ((frames // parts, width), BF16, "v"),
            ((4 * own, width), BF16, "v"),
            ((4 * own, width), BF16, "v"),
            ((own_hidden, width), BF16, "v"),
            ((own_hidden, width), BF16, "v"),
            ((small_rows, width), F32, "v"),
        ],
        "ssvvvvvvvvvvhhhh",
        [
            ((frames, width), BF16),
            ((window, piece, width), BF16),
            ((window, piece, width), BF16),
            (sliced(n_att), BF16),
            (sliced(n_att), BF16),
            (sliced(n_ffn), BF16),
            (sliced(n_ffn), BF16),
            ((rows + HALO, width), F32),
            ((rows + HALO, width), F32),
            ((rows, width), BF16),
            ((HALO, width), BF16),
            ((HALO, width), BF16),
            ((n_bits + 1, small_rows, width), F32),
            ((n_bits, small_rows, width), F32),
            ((parts, small_rows, width), F32),
            reduce_buffers(n_att),
            reduce_buffers(n_att),
            reduce_buffers(n_ffn),
            reduce_buffers(n_ffn),
            dma((4,)),
            dma((4, window)),
            dma((4, 2, 2 + parts)),
            dma((4, 2, max(n_bits - 3, 1))),
            dma((4, 2, 3)),
            dma((2,)),
            dma((2, n_bits)),
            dma((2, parts)),
        ],
        collective_id=1,
        has_side_effects=True,
    )(
        tok_lengths, frame_lengths, block_input, n1, q, k, v, att, grad, wself, small, norm_gain,
        mgrad, dw_cross.reshape(sliced(n_att)), dwi.reshape(sliced(n_ffn)), dwo.reshape(sliced(n_ffn)),
    )
    results = call(
        finals,
        [
            ((frames // parts, width), F32, "v"),
            ((rows, width), F32, "v"),
            ((3, width), F32, "v"),
            ((3, width), F32, "v"),
            ((3, width, own), F32, "v"),
            ((2, own), F32, "v"),
            ((own, width), F32, "v"),
            ((1, width), F32, "v"),
            ((3, width, own), F32, "v"),
            ((2, own), F32, "v"),
            ((own, width), F32, "v"),
            ((1, width), F32, "v"),
            ((width, own_hidden), F32, "v"),
            ((1, own_hidden), F32, "v"),
            ((own_hidden, width), F32, "v"),
            ((1, width), F32, "v"),
        ],
        "vvvvvvv",
        [],
    )(mgrad_sum, input_grad, fself, fcross, finner, fouter, small)
    memory_grad, input_grad, *others = results
    others = [r.reshape(-1) if r.shape[0] == 1 else r for r in others]
    return (block_output, input_grad, memory_grad, *others)


def solution(mesh):
    in_specs = (
        P(("dp", "mp"), None),
        P(("dp", "mp"), None),
        P("dp", None),
        P("dp", None),
        P(("dp", "mp"), None),
        P(),
        P(),
        P(None, None, "mp"),
        P(None, "mp"),
        P("mp", None),
        P(),
        P(None, None, "mp"),
        P(None, "mp"),
        P("mp", None),
        P(),
        P(None, "mp"),
        P("mp"),
        P("mp", None),
        P(),
    )
    out_specs = (
        P(("dp", "mp"), None),
        P(("dp", "mp"), None),
        P(("dp", "mp"), None),
        P(),
        P(),
        P(None, None, "mp"),
        P(None, "mp"),
        P("mp", None),
        P(),
        P(None, None, "mp"),
        P(None, "mp"),
        P("mp", None),
        P(),
        P(None, "mp"),
        P("mp"),
        P("mp", None),
        P(),
    )
    return jax.shard_map(shards, mesh=mesh, in_specs=in_specs, out_specs=out_specs, check_vma=False)
```

```python
import functools
import math

import jax
import jax.numpy as jnp
from jax import lax
from jax.experimental import pallas as pl
from jax.experimental.pallas import tpu as pltpu
from jax.sharding import PartitionSpec as P

HEAD = 64
NEGATIVE = -1e30
EPSILON = 1e-05
BLOCK = 128
CHUNK = 256
HALO = 256
F32 = jnp.float32
BF16 = jnp.bfloat16
MESH = pl.DeviceIdType.MESH
HALF = HEAD // 2
SLICES = 8
PIECES = 4
NEAR = 6
GELU_A = math.sqrt(2.0 / math.pi)
GELU_B = 0.044715


def mm(a, b, ca=1, cb=0):
    return lax.dot_general(a, b, (((ca,), (cb,)), ((), ())), preferred_element_type=F32)


def normed(values):
    center = values - jnp.mean(values, axis=-1, keepdims=True)
    spread = jnp.mean(center * center, axis=-1, keepdims=True)
    scale = lax.rsqrt(spread + EPSILON)
    return center * scale, scale


def norm_back(grad, gain, xhat, scale):
    gn = grad * gain
    first = jnp.mean(gn, axis=-1, keepdims=True)
    second = jnp.mean(gn * xhat, axis=-1, keepdims=True)
    return (gn - first - xhat * second) * scale


def column_sums(values):
    return jnp.sum(values, axis=0, keepdims=True)


def head_stack(values):
    rows, width = values.shape
    heads = width // HEAD
    lane = lax.broadcasted_iota(jnp.int32, (rows, width), 1) // HALF % heads
    zero = jnp.zeros_like(values)
    return jnp.concatenate([jnp.where(lane == h, values, zero) for h in range(heads)], axis=0)


def head_rows(heads):
    return [
        (slice((i * heads + h) * HALF, (i * heads + h + 1) * HALF), h)
        for i in range(2)
        for h in range(heads)
    ]


def head_diagonal(values, heads):
    rows = values.shape[1] // heads
    return jnp.concatenate(
        [values[r, h * rows : (h + 1) * rows] for r, h in head_rows(heads)], axis=0
    )


def token_rows(tok_ref, frm_ref, base, count):
    place = lax.broadcasted_iota(jnp.int32, (1, count), 1) + base
    zero = jnp.zeros((1, count), jnp.int32)

    def step(u, carry):
        start, first_row, first_frame, end_frame = carry
        tokens, frames = tok_ref[0, u], frm_ref[0, u]
        end = start + tokens
        done = place >= end
        first_row = first_row + jnp.where(done, tokens, 0)
        first_frame = first_frame + jnp.where(done, frames, 0)
        end_frame = end_frame + jnp.where(place >= start, frames, 0)
        return end, first_row, first_frame, end_frame

    _, first_row, first_frame, end_frame = lax.fori_loop(
        0, tok_ref.shape[1], step, (jnp.int32(0), zero, zero, zero)
    )
    return place, first_row, first_frame, end_frame


def excursion(tok_ref, frm_ref, rows, frames, parts):
    lane = lax.broadcasted_iota(jnp.int32, (1, 128), 1)
    zero = jnp.zeros((1, 128), jnp.int32)

    def step(u, carry):
        start, low, high = carry
        tokens, count = tok_ref[0, u], frm_ref[0, u]
        end = start + tokens
        low = low + jnp.where(lane * rows >= end, count, 0)
        high = high + jnp.where((lane + 1) * rows - 1 >= start, count, 0)
        return end, low, high

    _, low, high = lax.fori_loop(0, tok_ref.shape[1], step, (jnp.int32(0), zero, zero))
    beyond = jnp.maximum(high - (lane + 1) * frames, lane * frames - low)
    return jnp.max(jnp.where(lane < parts, beyond, 0), axis=1, keepdims=True).astype(F32)


def block_frames(tok_ref, frm_ref, base, count):
    blocks = count // BLOCK

    def step(u, carry):
        start, low, high = carry
        tokens, frames = tok_ref[0, u], frm_ref[0, u]
        end = start + tokens
        low = tuple(
            v + jnp.where(base + b * BLOCK >= end, frames, 0) for b, v in enumerate(low)
        )
        high = tuple(
            v + jnp.where(base + (b + 1) * BLOCK - 1 >= start, frames, 0) for b, v in enumerate(high)
        )
        return end, low, high

    zeros = (jnp.int32(0),) * blocks
    _, low, high = lax.fori_loop(0, tok_ref.shape[1], step, (jnp.int32(0), zeros, zeros))
    return low, high


def window_mask(place, first_row, base, block, count):
    keys = lax.broadcasted_iota(jnp.int32, (count, BLOCK), 0) + (base - HALO + block * BLOCK)
    here = slice(block * BLOCK, (block + 1) * BLOCK)
    return (keys >= first_row[:, here]) & (keys <= place[:, here])


def self_probs(queries, key_window, mask, heads):
    scores = mm(key_window, queries, 1, 1)
    parts = []
    for h in range(heads):
        part = jnp.where(mask, scores[:, h * BLOCK : (h + 1) * BLOCK], NEGATIVE)
        raised = jnp.exp(part - jnp.max(part, axis=0, keepdims=True))
        parts.append(raised * (1.0 / jnp.sum(raised, axis=0, keepdims=True)))
    return jnp.concatenate(parts, axis=1)


def rcopy(src, dst, send, recv, **device):
    return pltpu.make_async_remote_copy(
        src_ref=src, dst_ref=dst, send_sem=send, recv_sem=recv, device_id=device, device_id_type=MESH
    )


def at_rows(start, count):
    return pl.ds(pl.multiple_of(start, 16), count)


def flipped(index, bit):
    return index + bit - 2 * bit * (index // bit % 2)


def greet(z, parts, d, bits):
    barrier = pltpu.get_barrier_semaphore()
    for step in range(1, parts):
        device = {"mp": (z + step) % parts}
        pl.semaphore_signal(barrier, inc=1, device_id=device, device_id_type=MESH)
    for bit in bits:
        device = {"dp": flipped(d, bit)}
        pl.semaphore_signal(barrier, inc=1, device_id=device, device_id_type=MESH)
    return barrier, parts - 1 + len(bits)


class Direct:
    def __init__(self, z, parts, own, place, sems):
        self.z, self.parts, self.own, self.place, self.sems = z, parts, own, place, sems

    def copy(self, step):
        device = (self.z + step) % self.parts
        sems = self.sems
        return rcopy(self.own, self.place(self.z), sems.at[0, step], sems.at[1, step], mp=device)

    def send(self):
        for step in range(1, self.parts):
            self.copy(step).start()

    def arrived(self):
        for step in range(1, self.parts):
            other = (self.z - step + self.parts) % self.parts
            place, sems = self.place(other), self.sems
            rcopy(place, place, sems.at[0, step], sems.at[1, step], mp=other).wait_recv()

    def close(self):
        for step in range(1, self.parts):
            self.copy(step).wait_send()


DP_BITS = (2, 4, 1)


def corner(d):
    return d % 2, d // 4 % 2, d // 2 % 2


class Plane:
    def __init__(self, d, buffer, first_y, sems):
        self.d, self.buffer, self.first_y, self.sems = d, buffer, first_y, sems

    def block(self, p, c, y, x):
        if p == 0:
            return self.buffer.at[c, y, x]
        if p == 2:
            return self.buffer.at[c]
        return self.buffer.at[c, :, x] if self.first_y else self.buffer.at[c, y]

    def copy(self, p, other):
        c, y, x = corner(self.d)
        over_y = p == (0 if self.first_y else 1)
        if other:
            if p == 2:
                c = 1 - c
            elif over_y:
                y = 1 - y
            else:
                x = 1 - x
        block = self.block(p, c, y, x)
        device = flipped(self.d, 1 if p == 2 else 4 if over_y else 2)
        return rcopy(block, block, self.sems.at[0, p], self.sems.at[1, p], dp=device)

    def send(self, p):
        self.copy(p, False).start()

    def arrived(self, p):
        self.copy(p, True).wait_recv()

    def close(self):
        for p in range(3):
            self.copy(p, False).wait_send()


class Window:
    def __init__(self, z, parts, source, place, sems):
        self.z, self.parts, self.source, self.place, self.sems = z, parts, source, place, sems

    def number(self, z, j, up):
        return (z + 1) * PIECES - 1 - j if up else z * PIECES + j

    def there(self, number):
        return (number >= 0) & (number < self.parts * PIECES)

    def copy(self, j, up):
        number = self.number(self.z, j, up)
        place, kind = self.place(number, j, up), 0 if up else 2
        return rcopy(
            self.source(number, j, up),
            place,
            self.sems.at[kind, j],
            self.sems.at[kind + 1, j],
            mp=self.z + 1 if up else self.z - 1,
        )

    def sends(self, j, up):
        edge = self.z < self.parts - 1 if up else self.z > 0
        return edge & self.there(self.number(self.z, j, up))

    def send(self, j):
        for up in (True, False):

            @pl.when(self.sends(j, up))
            def _():
                self.copy(j, up).start()

    def comes(self, j, up):
        edge = self.z > 0 if up else self.z < self.parts - 1
        return edge & self.there(self.arrival(j, up))

    def arrival(self, j, up):
        return self.number(self.z - 1 if up else self.z + 1, j, up)

    def arrived(self, j):
        for up in (True, False):

            @pl.when(self.comes(j, up))
            def _():
                number = self.arrival(j, up)
                place, kind = self.place(number, j, up), 0 if up else 2
                rcopy(
                    place,
                    place,
                    self.sems.at[kind, j],
                    self.sems.at[kind + 1, j],
                    mp=self.z - 1 if up else self.z + 1,
                ).wait_recv()

    def each(self, j, use):
        for up in (True, False):

            @pl.when(self.comes(j, up))
            def _():
                use(self.arrival(j, up), j, up)

    def close(self, pieces):
        for j in pieces:
            for up in (True, False):

                @pl.when(self.sends(j, up))
                def _():
                    self.copy(j, up).wait_send()


def gather(
    tok, frm, x_ref, mem, sw, so, cw, co, inner, outer, sb, cb, ib, gain, shift, offset,
    wself_out, wcross_out, inner_out, outer_out, ib_out, vb_out, far_out, mem_out, ck_out, cv_out,
    n1_ref, q_ref, k_ref, v_ref, att_ref, after_ref, cq_ref,
    gself, gcross, ginner, gouter, gmem, sck, scv, pself, pcross, pinner, halo, pbias, gbias,
    far, far_land, line_sems, mem_sems, plane_sems, bias_sems, halo_sems, far_sems, own_sem, out_sems, weight_sems,
):
    rows, width = x_ref.shape
    heads = width // HEAD
    own = sw.shape[1]
    parts = width // own
    shard_rows = mem.shape[0]
    piece = shard_rows // PIECES
    z, d = lax.axis_index("mp"), lax.axis_index("dp")
    dp = lax.axis_size("dp")
    bits = [1 << i for i in range(dp.bit_length() - 1)]
    c, y, x = corner(d)
    s = c * 4 + y * 2 + x
    barrier, greetings = greet(z, parts, d, bits)

    for source, last, packed in ((sw, so, pself), (cw, co, pcross)):
        for i in range(3):
            packed[i * own : (i + 1) * own] = source[i]
        packed[3 * own :] = last[...]
    pbias[...] = jnp.zeros_like(pbias)
    pbias[0:1] = ib[...]
    for i in range(2):
        pbias[1:2, i * own : (i + 1) * own] = sb[i : i + 1]
        pbias[1:2, (2 + i) * own : (3 + i) * own] = cb[i : i + 1]
    pinner[...] = inner[...].T
    groups = []
    for i, (packed, buffer) in enumerate(
        ((pself, gself), (pcross, gcross), (pinner, ginner), (outer, gouter))
    ):
        n = packed.shape[0] // SLICES
        mine = packed.at[at_rows(s * n, n)]

        def place(shard, buffer=buffer, n=n):
            return buffer.at[c, y, x, at_rows(shard * n, n)]

        line = Direct(z, parts, mine, place, line_sems.at[i])
        plane = Plane(d, buffer, i % 2 == 1, plane_sems.at[i])
        groups.append((line, plane))
        buffer[c, y, x, at_rows(z * n, n)] = packed[at_rows(s * n, n)]

    def piece_place(number, j, up):
        return gmem.at[at_rows(number * piece, piece)]

    def piece_source(number, j, up):
        if j < PIECES:
            return mem.at[at_rows((number - z * PIECES) * piece, piece)]
        return piece_place(number, j, up)

    memory = Window(z, parts, piece_source, piece_place, mem_sems)

    def bias_copy(step):
        return rcopy(
            pbias, gbias.at[z], bias_sems.at[0, step], bias_sems.at[1, step], mp=(z + step) % parts
        )

    def bias_arrival(step):
        other = (z - step + parts) % parts
        return rcopy(pbias, gbias.at[other], bias_sems.at[0, step], bias_sems.at[1, step], mp=other)

    def halo_copy(other):
        return rcopy(x_ref.at[rows - HALO :], halo, halo_sems.at[0], halo_sems.at[1], mp=other)

    def far_copy(i):
        device = flipped(d, bits[i])
        return rcopy(far.at[i], far_land.at[i], far_sems.at[0, i], far_sems.at[1, i], dp=device)

    def far_step(i):
        if i > 0:
            far_copy(i - 1).wait_recv()
            far[i] = jnp.maximum(far[i - 1], far_land[i - 1])
        if i < len(bits):
            far_copy(i).start()
        else:
            far_out[...] = far[i]

    def forward(j):
        memory.arrived(j - PIECES)
        memory.send(j)

    far[0] = jnp.broadcast_to(excursion(tok, frm, rows, shard_rows, parts), far.shape[1:])
    pl.semaphore_wait(barrier, greetings)
    for line, _ in groups[:2]:
        line.send()
    for step in range(1, parts):
        bias_copy(step).start()

    @pl.when(z < parts - 1)
    def _():
        halo_copy(z + 1).start()

    for line, _ in groups[2:]:
        line.send()
    for j in range(PIECES):
        memory.send(j)
    far_step(0)
    own_rows = gmem.at[at_rows(z * shard_rows, shard_rows)]
    own_copy = pltpu.make_async_copy(mem, own_rows, own_sem)
    own_copy.start()
    gbias[z] = pbias[...]
    for line, plane in groups[:2]:
        line.arrived()
        plane.send(0)
    for _, plane in groups[:2]:
        plane.arrived(0)
        plane.send(1)
    for line, plane in groups[2:]:
        line.arrived()
        plane.send(0)
    far_step(1)
    for _, plane in groups[:2]:
        plane.arrived(1)
        plane.send(2)
    far_step(2)
    groups[0][1].arrived(2)

    for step in range(1, parts):
        bias_arrival(step).wait_recv()

    def head_bias(i):
        return jnp.concatenate(
            [
                gbias[o, 1:2, i * own + half * HALF : i * own + (half + 1) * HALF]
                for half in range(2)
                for o in range(parts)
            ],
            axis=1,
        )

    n = ginner.shape[3] // parts
    for i in range(SLICES):
        ib_out[i : i + 1] = jnp.concatenate(
            [gbias[o, 0:1, i * n : (i + 1) * n] for o in range(parts)], axis=1
        )

    @pl.when(z > 0)
    def _():
        halo_copy(z - 1).wait_recv()

    @pl.when(z == 0)
    def _():
        halo[...] = jnp.zeros_like(halo)

    def weight(buffer, i):
        return buffer[i // 2, i % 2].reshape(width, width)

    base = z * rows
    place_row, first_row, _, _ = token_rows(tok, frm, base, rows)
    for src, dst in ((halo, slice(0, HALO)), (x_ref, slice(HALO, HALO + rows))):
        xhat, _ = normed(src[...].astype(F32))
        n1_ref[dst] = (xhat * gain[0:1] + shift[0:1]).astype(BF16)
    n1 = n1_ref[...]
    query = mm(n1[HALO:], weight(gself, 0), 1, 1) + head_bias(0)
    q_ref[...] = query.astype(BF16) * jnp.asarray(0.125, BF16)
    k_ref[...] = mm(n1, weight(gself, 1), 1, 1).astype(BF16)
    v_ref[...] = (mm(n1, weight(gself, 2), 1, 1) + head_bias(1)).astype(BF16)
    count = HALO + BLOCK
    for b in range(rows // BLOCK):
        queries = head_stack(q_ref[b * BLOCK : (b + 1) * BLOCK])
        window = slice(b * BLOCK, b * BLOCK + count)
        mask = window_mask(place_row, first_row, base, b, count)
        probs = self_probs(queries, k_ref[window], mask, heads).astype(BF16)
        out = head_diagonal(mm(v_ref[window], probs, 0, 0), heads)
        att_ref[b * BLOCK : (b + 1) * BLOCK] = out.T.astype(BF16)
        if b == 0:
            for _, plane in groups[2:]:
                plane.arrived(0)
                plane.send(1)
    forward(PIECES)
    after = x_ref[...].astype(F32) + mm(att_ref[...], weight(gself, 3)) + offset[...]
    after_ref[...] = after
    xhat, _ = normed(after)
    groups[1][1].arrived(2)
    n2 = (xhat * gain[1:2] + shift[1:2]).astype(BF16)
    query = mm(n2, weight(gcross, 0), 1, 1) + head_bias(2)
    cq_ref[...] = query.astype(BF16) * jnp.asarray(0.125, BF16)
    value_bias = head_bias(3)
    forward(PIECES + 1)

    def project(start, size):
        here = at_rows(start, size)
        block = gmem[here]
        sck[here] = mm(block, weight(gcross, 1), 1, 1).astype(BF16)
        scv[here] = (mm(block, weight(gcross, 2), 1, 1) + value_bias).astype(BF16)

    def copies_out(number):
        here = at_rows(number * piece, piece)
        return [
            pltpu.make_async_copy(a.at[here], b.at[here], out_sems.at[number, i])
            for i, (a, b) in enumerate(((gmem, mem_out), (sck, ck_out), (scv, cv_out)))
        ]

    def project_piece(number, j=0, up=True):
        project(number * piece, piece)
        for copy in copies_out(number):
            copy.start()

    own_copy.wait()
    lax.fori_loop(0, PIECES, lambda i, _: (project_piece(z * PIECES + i), 0)[1], 0)
    for _, plane in groups[2:]:
        plane.arrived(1)
        plane.send(2)
    for j in range(PIECES):
        if j >= 2:
            memory.arrived(j)
        memory.each(j, project_piece)
    for i in range(3, len(bits) + 1):
        far_step(i)
    for _, plane in groups[2:]:
        plane.arrived(2)
    outs = [
        pltpu.make_async_copy(a, b, weight_sems.at[i])
        for i, (a, b) in enumerate(
            ((gself, wself_out), (gcross, wcross_out), (ginner, inner_out), (gouter, outer_out))
        )
    ]
    for copy in outs:
        copy.start()
    vb_out[...] = value_bias
    for j in range(PIECES, NEAR):
        memory.arrived(j)
        memory.each(j, project_piece)
    for copy in outs:
        copy.wait()

    def finish(number, *_):
        for copy in copies_out(number):
            copy.wait()

    for i in range(PIECES):
        finish(z * PIECES + i)
    for j in range(NEAR):
        memory.each(j, finish)
    for line, plane in groups:
        line.close()
        plane.close()
    memory.close(range(NEAR))
    for i in range(len(bits)):
        far_copy(i).wait_send()
    for step in range(1, parts):
        bias_copy(step).wait_send()

    @pl.when(z < parts - 1)
    def _():
        halo_copy(z + 1).wait_send()


def gather_far(mem, wcross, vb, far_mem, far_ck, far_cv, block, keys, values, sems, load_sem, out_sems):
    pieces, piece = far_mem.shape[1:3]
    width = mem.shape[1]
    parts = mem.shape[0] // piece // PIECES
    z, d = lax.axis_index("mp"), lax.axis_index("dp")
    barrier, greetings = greet(z, parts, d, ())

    def place(number, j, up):
        return far_mem.at[0 if up else 1, j - NEAR]

    def source(number, j, up):
        if j - PIECES < NEAR:
            return mem.at[at_rows(number * piece, piece)]
        return place(number, j - PIECES, up)

    memory = Window(z, parts, source, place, sems)
    pl.semaphore_wait(barrier, greetings)

    def project(number, j, up):
        side, i = 0 if up else 1, j - NEAR
        load = pltpu.make_async_copy(far_mem.at[side, i], block, load_sem)
        load.start()
        load.wait()
        rows = block[...]
        weights = [wcross[i // 2, i % 2].reshape(width, width) for i in (1, 2)]
        keys[...] = mm(rows, weights[0], 1, 1).astype(BF16)
        values[...] = (mm(rows, weights[1], 1, 1) + vb[...]).astype(BF16)
        stores = [
            pltpu.make_async_copy(keys, far_ck.at[side, i], out_sems.at[0]),
            pltpu.make_async_copy(values, far_cv.at[side, i], out_sems.at[1]),
        ]
        for store in stores:
            store.start()
        for store in stores:
            store.wait()

    last = NEAR + pieces
    for j in range(NEAR, last):
        if j - PIECES >= NEAR:
            memory.arrived(j - PIECES)
        memory.send(j)
    for j in range(NEAR, last):
        if j + PIECES >= last:
            memory.arrived(j)
        memory.each(j, project)
    memory.close(range(NEAR, last))


def middle(
    window, tok, frm, cq_ref, after_ref, cot_ref, w_ref, ib_ref, gain, shift, cross_offset, outer_offset,
    ck_in, cv_in, mem_in, wi_in, wo_in, *refs,
):
    if window > NEAR:
        far_ck, far_cv, far_mem, *refs = refs
    (
    out_ref, grad_ref, small_ref, mgrad_out, dw_out, dwi_out, dwo_out,
    ck_ref, cv_ref, mem_ref, wi_ref, wo_ref, mgrad_ref, dw_ref, dwb_ref, dwi_ref, dwo_ref,
    qbig, gbig, lse_ref, dot_ref, acc, dq_ref, dk_ref, dv_ref,
    in_sems, out_sems, chunk_sems, piece_sems,
    ) = refs
    rows, width = cq_ref.shape
    heads = width // HEAD
    blocks = rows // BLOCK
    frames = mem_ref.shape[0]
    z = lax.axis_index("mp")
    parts = lax.axis_size("mp")
    last = parts * PIECES
    piece = frames // last

    def piece_loads(i, near, full, far):
        def at(number):
            return full.at[at_rows(number * piece, piece)]

        loads = [(None, near.at[at_rows((z * PIECES + j) * piece, piece)], at(z * PIECES + j), j) for j in range(PIECES)]
        for j in range(window):
            for up in (True, False):
                number = z * PIECES - 1 - j if up else (z + 1) * PIECES + j
                there = number >= 0 if up else number < last
                if j < NEAR:
                    source = near.at[at_rows(jnp.clip(number, 0, last - 1) * piece, piece)]
                else:
                    source = far.at[0 if up else 1, j - NEAR]
                place = at(jnp.clip(number, 0, last - 1))
                loads.append((there, source, place, PIECES + 2 * j + (0 if up else 1)))
        return [
            (there, pltpu.make_async_copy(source, place, piece_sems.at[i, sem]))
            for there, source, place, sem in loads
        ]

    def clear(full):
        for up in (True, False):
            number = z * PIECES - 1 - window if up else (z + 1) * PIECES + window

            @pl.when((number >= 0) & (number < last))
            def _():
                full[at_rows(number * piece, piece)] = jnp.zeros((piece, width), BF16)

    def act(pieces, name):
        for there, copy in pieces:
            if there is None:
                getattr(copy, name)()
            else:
                pl.when(there)(getattr(copy, name))

    far = (far_ck, far_cv, far_mem) if window > NEAR else (None, None, None)
    arrays = ((ck_in, ck_ref), (cv_in, cv_ref), (mem_in, mem_ref))
    frame_loads = [piece_loads(i, a, b, far[i]) for i, (a, b) in enumerate(arrays)]
    for pieces in frame_loads[:2]:
        act(pieces, "start")
    loads = [
        pltpu.make_async_copy(a, b, in_sems.at[i])
        for i, (a, b) in enumerate(((wi_in, wi_ref), (wo_in, wo_ref)))
    ]
    for load in loads:
        load.start()
    act(frame_loads[2], "start")
    for _, full in arrays:
        clear(full)

    def weight(i):
        return w_ref[i * width : (i + 1) * width]

    base = z * rows
    _, _, first_frame, end_frame = token_rows(tok, frm, base, rows)
    low, high = block_frames(tok, frm, base, rows)
    small_ref[...] = jnp.zeros_like(small_ref)

    def chunk_mask(c, b):
        frame = lax.broadcasted_iota(jnp.int32, (CHUNK, BLOCK), 0) + c * CHUNK
        here = slice(b * BLOCK, (b + 1) * BLOCK)
        return (frame >= first_frame[:, here]) & (frame < end_frame[:, here])

    act(frame_loads[0], "wait")
    act(frame_loads[1], "wait")
    attended = []
    for b in range(blocks):
        qbig[b] = head_stack(cq_ref[b * BLOCK : (b + 1) * BLOCK])
        acc[...] = jnp.zeros_like(acc)

        def step(c, carry):
            largest, total = carry
            here = pl.ds(pl.multiple_of(c * CHUNK, CHUNK), CHUNK)
            scores = mm(ck_ref[here], qbig[b], 1, 1)
            mask = chunk_mask(c, b)
            scores = jnp.where(jnp.concatenate([mask] * heads, axis=1), scores, NEGATIVE)
            now = jnp.maximum(largest, jnp.max(scores, axis=0, keepdims=True))
            fade = jnp.exp(largest - now)
            raised = jnp.exp(scores - now)
            total = total * fade + jnp.sum(raised, axis=0, keepdims=True)
            part = mm(cv_ref[here], raised.astype(BF16), 0, 0)
            for r, h in head_rows(heads):
                l = slice(h * BLOCK, (h + 1) * BLOCK)
                acc[r] = acc[r] * fade[:, l] + part[r, l]
            return now, total

        start = (jnp.full((1, heads * BLOCK), NEGATIVE, F32), jnp.zeros((1, heads * BLOCK), F32))
        largest, total = lax.fori_loop(low[b] // CHUNK, (high[b] + CHUNK - 1) // CHUNK, step, start)
        lse_ref[b] = largest + jnp.log(total)
        share = 1.0 / total
        for r, h in head_rows(heads):
            l = slice(h * BLOCK, (h + 1) * BLOCK)
            acc[r] = acc[r] * share[:, l]
        attended.append(acc[...])
    att_t = jnp.concatenate(attended, axis=1)
    att = att_t.T.astype(BF16)
    after_self = after_ref[...]
    after_cross = after_self + mm(att, weight(3)) + cross_offset[...]
    xhat3, scale3 = normed(after_cross)
    n3 = (xhat3 * gain[2:3] + shift[2:3]).astype(BF16)
    sent = cot_ref[...]
    small_ref[8:9] = column_sums(sent.astype(F32))
    hidden = wi_ref.shape[0]
    tile = hidden // SLICES
    loads[0].wait()
    loads[1].wait()
    out = after_cross + outer_offset[...]
    dn3 = jnp.zeros((rows, width), F32)
    for f in range(hidden // tile):
        here = slice(f * tile, (f + 1) * tile)
        before = mm(n3, wi_ref[here], 1, 1) + ib_ref[f : f + 1]
        square = before * before
        inner = jnp.tanh(GELU_A * (before + GELU_B * (before * square)))
        half = 0.5 * (1.0 + inner)
        active = (before * half).astype(BF16)
        slope = half + 0.5 * before * (1.0 - inner * inner) * (
            GELU_A + (3.0 * GELU_A * GELU_B) * square
        )
        out = out + mm(active, wo_ref[here])
        back = (slope * mm(sent, wo_ref[here], 1, 1)).astype(BF16)
        dn3 = dn3 + mm(back, wi_ref[here])
        dwo_ref[here] = mm(active, sent, 0, 0).astype(BF16)
        dwi_ref[here] = mm(back, n3, 0, 0).astype(BF16)
        small_ref[16 + f : 17 + f] = column_sums(back.astype(F32))
    stores = [
        pltpu.make_async_copy(a, b, out_sems.at[i])
        for i, (a, b) in enumerate(((dwi_ref, dwi_out), (dwo_ref, dwo_out), (dwb_ref, dw_out)))
    ]
    stores[0].start()
    stores[1].start()
    out_ref[...] = out
    small_ref[2:3] = column_sums(dn3 * xhat3)
    small_ref[5:6] = column_sums(dn3)
    grad = sent.astype(F32) + norm_back(dn3, gain[2:3], xhat3, scale3)
    sent2 = grad.astype(BF16)
    small_ref[7:8] = column_sums(sent2.astype(F32))
    dw_ref[3] = mm(att, sent2, 0, 0)
    go = mm(sent2, weight(3), 1, 1).astype(BF16)
    got = mm(weight(3), sent2, 1, 1).astype(BF16).astype(F32)
    prod = got * att_t
    for b in range(blocks):
        gbig[b] = head_stack(go[b * BLOCK : (b + 1) * BLOCK])
        sums = [column_sums(prod[r, b * BLOCK : (b + 1) * BLOCK]) for r, _ in head_rows(heads)]
        for h in range(heads):
            dot_ref[b, :, h * BLOCK : (h + 1) * BLOCK] = sums[h] + sums[heads + h]
    dq_ref[...] = jnp.zeros_like(dq_ref)
    dw_ref[1] = jnp.zeros((width, width), F32)
    dw_ref[2] = jnp.zeros((width, width), F32)

    act(frame_loads[2], "wait")

    def chunk_store(c):
        here = pl.ds(pl.multiple_of(c * CHUNK, CHUNK), CHUNK)
        return pltpu.make_async_copy(mgrad_ref.at[here], mgrad_out.at[here], chunk_sems.at[c])

    def frame_step(c, carry):
        here = pl.ds(pl.multiple_of(c * CHUNK, CHUNK), CHUNK)
        meets = [(low[b] < (c + 1) * CHUNK) & (high[b] > c * CHUNK) for b in range(blocks)]
        some = functools.reduce(jnp.logical_or, meets)

        @pl.when(some)
        def _():
            dk_ref[...] = jnp.zeros_like(dk_ref)
            dv_ref[...] = jnp.zeros_like(dv_ref)
            for b in range(blocks):

                @pl.when(meets[b])
                def _():
                    keys, values = ck_ref[here], cv_ref[here]
                    scores = mm(keys, qbig[b], 1, 1)
                    mask = chunk_mask(c, b)
                    mask = jnp.concatenate([mask] * heads, axis=1)
                    shares = jnp.where(mask, jnp.exp(scores - lse_ref[b]), 0.0)
                    dp = mm(values, gbig[b], 1, 1)
                    ds = (shares * (dp - dot_ref[b])).astype(BF16)
                    dv_ref[...] += mm(shares.astype(BF16), gbig[b])
                    dk_ref[...] += mm(ds, qbig[b])
                    l = slice(b * BLOCK, (b + 1) * BLOCK)
                    dq_ref[:, l] += head_diagonal(mm(keys, ds, 0, 0), heads)

            dk, dv = dk_ref[...].astype(BF16), dv_ref[...].astype(BF16)
            mgrad_ref[here] = (mm(dk, weight(1)) + mm(dv, weight(2))).astype(BF16)
            frame_rows = mem_ref[here]
            dw_ref[1] += mm(dk, frame_rows, 0, 0)
            dw_ref[2] += mm(dv, frame_rows, 0, 0)
            small_ref[12:13] += column_sums(dv.astype(F32))

        @pl.when(jnp.logical_not(some))
        def _():
            mgrad_ref[here] = jnp.zeros((CHUNK, width), BF16)

        chunk_store(c).start()
        return carry

    lax.fori_loop(0, frames // CHUNK, frame_step, 0)
    dq = (dq_ref[...] * 0.125).T.astype(BF16)
    small_ref[11:12] = column_sums(dq.astype(F32))
    xhat2, scale2 = normed(after_self)
    n2 = (xhat2 * gain[1:2] + shift[1:2]).astype(BF16)
    dw_ref[0] = mm(dq, n2, 0, 0)
    dn2 = mm(dq, weight(0))
    small_ref[1:2] = column_sums(dn2 * xhat2)
    small_ref[4:5] = column_sums(dn2)
    grad_ref[...] = grad + norm_back(dn2, gain[1:2], xhat2, scale2)
    for i in range(4):
        dwb_ref[i * width : (i + 1) * width] = dw_ref[i].astype(BF16)
    stores[2].start()

    def finish(c, carry):
        chunk_store(c).wait()
        return carry

    lax.fori_loop(0, frames // CHUNK, finish, 0)
    for store in stores:
        store.wait()


class Reduce:
    def __init__(self, d, z, parts, dp, local, first_x, buffers, sems):
        self.d, self.z, self.parts, self.dp = d, z, parts, dp
        self.local, self.first_x = local, first_x
        self.r1, self.a1, self.r2, self.a2, self.r3, self.a3, self.rz, self.wide, self.fin = buffers
        self.sems, self.extra_sems, self.plane_sems = sems
        self.c, self.y, self.x = d % 2, d // 4 % 2, d // 2 % 2
        self.plane = Plane(d, self.fin, first_x, self.plane_sems)
        self.bits = [8 << i for i in range(dp.bit_length() - 4)]

    def copy(self, p):
        if p == 0:
            src, dst, bit = self.local.at[1 - self.c], self.r1, 1
        elif p == 1:
            if self.first_x:
                src, dst, bit = self.a1.at[:, 1 - self.x], self.r2, 2
            else:
                src, dst, bit = self.a1.at[1 - self.y], self.r2, 4
        elif self.first_x:
            src, dst, bit = self.a2.at[1 - self.y], self.r3, 4
        else:
            src, dst, bit = self.a2.at[1 - self.x], self.r3, 2
        return rcopy(src, dst, self.sems.at[0, p], self.sems.at[1, p], dp=flipped(self.d, bit))

    def z_copy(self, step, other):
        sems = self.sems
        return rcopy(
            self.a3.at[other], self.rz.at[self.z], sems.at[0, 2 + step], sems.at[1, 2 + step], mp=other
        )

    def z_arrival(self, step, other):
        sems = self.sems
        return rcopy(
            self.a3.at[other], self.rz.at[other], sems.at[0, 2 + step], sems.at[1, 2 + step], mp=other
        )

    def extra(self, i):
        sems = self.extra_sems
        device = flipped(self.d, self.bits[i])
        return rcopy(self.wide.at[2 * i], self.wide.at[2 * i + 1], sems.at[0, i], sems.at[1, i], dp=device)

    def run(self, p):
        if p == 0:
            self.copy(0).start()
        elif p == 1:
            self.copy(0).wait_recv()
            self.a1[...] = (self.local[self.c].astype(F32) + self.r1[...].astype(F32)).astype(BF16)
            self.copy(1).start()
        elif p == 2:
            self.copy(1).wait_recv()
            mine = self.a1[:, self.x] if self.first_x else self.a1[self.y]
            self.a2[...] = (mine.astype(F32) + self.r2[...].astype(F32)).astype(BF16)
            self.copy(2).start()
        elif p == 3:
            self.copy(2).wait_recv()
            mine = self.a2[self.y] if self.first_x else self.a2[self.x]
            mine = mine.astype(F32) + self.r3[...].astype(F32)
            self.a3[...] = mine.astype(BF16).reshape(self.a3.shape)
            for step in range(1, self.parts):
                self.z_copy(step, (self.z + step) % self.parts).start()
        elif p == 4:
            self.rz[self.z] = self.a3[self.z]
            for step in range(1, self.parts):
                self.z_arrival(step, (self.z - step + self.parts) % self.parts).wait_recv()
            total = self.rz[0].astype(F32)
            for other in range(1, self.parts):
                total = total + self.rz[other].astype(F32)
            for i in range(len(self.bits)):
                self.wide[2 * i] = total
                self.extra(i).start()
                self.extra(i).wait_recv()
                total = total + self.wide[2 * i + 1]
            self.fin[self.c, self.y, self.x] = total.astype(BF16)
            self.plane.send(0)
        elif p in (5, 6):
            self.plane.arrived(p - 5)
            self.plane.send(p - 4)
        else:
            self.plane.arrived(2)

    def close(self):
        for p in range(3):
            self.copy(p).wait_send()
        for step in range(1, self.parts):
            self.z_copy(step, (self.z + step) % self.parts).wait_send()
        for i in range(len(self.bits)):
            self.extra(i).wait_send()
        self.plane.close()


class Total:
    def __init__(self, d, z, parts, bits, buffers, landing, line, sems, line_sems):
        self.d, self.z, self.parts, self.bits = d, z, parts, bits
        self.buffers, self.landing, self.line = buffers, landing, line
        self.sems, self.line_sems = sems, line_sems

    def copy(self, i):
        device = flipped(self.d, self.bits[i])
        sems = self.sems
        return rcopy(self.buffers.at[i], self.landing.at[i], sems.at[0, i], sems.at[1, i], dp=device)

    def z_copy(self, step, source):
        sems, last = self.line_sems, self.buffers.at[len(self.bits)]
        if source:
            other = (self.z - step + self.parts) % self.parts
            return rcopy(last, self.line.at[other], sems.at[0, step], sems.at[1, step], mp=other)
        other = (self.z + step) % self.parts
        return rcopy(last, self.line.at[self.z], sems.at[0, step], sems.at[1, step], mp=other)

    def run(self, p):
        if p > 0:
            self.copy(p - 1).wait_recv()
            self.buffers[p] = self.buffers[p - 1] + self.landing[p - 1]
        if p < len(self.bits):
            self.copy(p).start()
        else:
            for step in range(1, self.parts):
                self.z_copy(step, False).start()

    def finish(self, out):
        self.line[self.z] = self.buffers[len(self.bits)]
        for step in range(1, self.parts):
            self.z_copy(step, True).wait_recv()
        total = self.line[0]
        for other in range(1, self.parts):
            total = total + self.line[other]
        out[...] = total
        for i in range(len(self.bits)):
            self.copy(i).wait_send()
        for step in range(1, self.parts):
            self.z_copy(step, False).wait_send()


def give_back(
    window,
    tok, frm, x_ref, n1_ref, q_ref, k_ref, v_ref, att_ref, grad_ref, w_ref, small_in, gain,
    mgrad_in, dwc_in, dwi_in, dwo_in,
    input_out, mgrad_out, fself, fcross, finner, fouter, small_out,
    own, up_land, down_land, local_self, local_cross, local_inner, local_outer,
    dk_ref, dv_ref, dq_ref, halo_out, halo_land, total_buffers, total_land, total_line,
    self_bufs, cross_bufs, inner_bufs, outer_bufs,
    load_sems, flow_sems, reduce_sems, extra_sems, plane_sems, halo_sems, total_sems, line_sems,
):
    rows, width = q_ref.shape
    heads = width // HEAD
    parts = total_line.shape[0]
    shard_rows = mgrad_out.shape[0]
    piece = shard_rows // PIECES
    last = parts * PIECES
    z, d = lax.axis_index("mp"), lax.axis_index("dp")
    dp = lax.axis_size("dp")
    bits = [1 << i for i in range(dp.bit_length() - 1)]
    barrier, greetings = greet(z, parts, d, bits)
    loads = [
        pltpu.make_async_copy(a, b, load_sems.at[i])
        for i, (a, b) in enumerate(
            (
                (dwi_in, local_inner),
                (dwo_in, local_outer),
                (dwc_in, local_cross),
                (mgrad_in, own),
            )
        )
    ]
    for load in loads:
        load.start()
    chains = []
    for i, (local, first_x, bufs, fin) in enumerate(
        (
            (local_inner, False, inner_bufs, finner),
            (local_outer, True, outer_bufs, fouter),
            (local_cross, False, cross_bufs, fcross),
            (local_self, True, self_bufs, fself),
        )
    ):
        sems = (reduce_sems.at[i], extra_sems.at[i], plane_sems.at[i])
        chains.append(Reduce(d, z, parts, dp, local, first_x, (*bufs, fin), sems))
    inner, outer, cross, own_chain = chains

    def rows_of(number):
        return at_rows(number * piece, piece)

    def crosses(j, up):
        if up:
            return (z < parts - 1) & ((z + 1) * PIECES + j < last)
        return (z > 0) & (z * PIECES - 1 - j >= 0)

    def number(j, up):
        return (z + 1) * PIECES + j if up else z * PIECES - 1 - j

    def flow(j, up, summed):
        land = up_land if up else down_land
        kind = 0 if up else 2
        src = land.at[j + PIECES] if summed else mgrad_in.at[rows_of(number(j, up))]
        device = z + 1 if up else z - 1
        return rcopy(src, land.at[j], flow_sems.at[kind, j], flow_sems.at[kind + 1, j], mp=device)

    def comes(j, up):
        if up:
            return (z > 0) & (z * PIECES + j < last)
        return (z < parts - 1) & ((z + 1) * PIECES - 1 - j >= 0)

    def flow_arrival(j, up):
        land = up_land if up else down_land
        kind = 0 if up else 2
        device = z - 1 if up else z + 1
        return rcopy(
            land.at[j], land.at[j], flow_sems.at[kind, j], flow_sems.at[kind + 1, j], mp=device
        )

    def first_flows():
        for j in reversed(range(max(window - PIECES, 0), window)):
            for up in (True, False):

                @pl.when(crosses(j, up))
                def _():
                    flow(j, up, False).start()

    def next_flow(j):
        for up in (True, False):
            land = up_land if up else down_land

            @pl.when(crosses(j, up) & comes(j + PIECES, up))
            def _():
                flow_arrival(j + PIECES, up).wait_recv()
                mine = own[rows_of(number(j, up))]
                land[j + PIECES] = (land[j + PIECES].astype(F32) + mine.astype(F32)).astype(BF16)
                flow(j, up, True).start()

            @pl.when(crosses(j, up) & jnp.logical_not(comes(j + PIECES, up)))
            def _():
                flow(j, up, False).start()

    base = z * rows
    place, first_row, _, _ = token_rows(tok, frm, base, rows)

    def weight(i):
        return w_ref[i * width : (i + 1) * width]

    def halo_copy(other):
        return rcopy(halo_out, halo_land, halo_sems.at[0], halo_sems.at[1], mp=other)

    pl.semaphore_wait(barrier, greetings)
    first_flows()
    for load, chain in zip(loads[:3], chains[:3]):
        load.wait()
        chain.run(0)
    small = total_buffers.at[0]
    small[...] = small_in[...]
    grad = grad_ref[...]
    sent = grad.astype(BF16)
    small[6:7] = column_sums(sent.astype(F32))
    n = local_self.shape[3]

    def keep(i, values):
        for half in range(2):
            s = 2 * i + half
            local_self[s // 4, s // 2 % 2, s % 2] = values[half * n : (half + 1) * n].astype(BF16)

    keep(3, mm(att_ref[...], sent, 0, 0))
    go = mm(sent, weight(3), 1, 1).astype(BF16)
    dk_ref[...] = jnp.zeros_like(dk_ref)
    dv_ref[...] = jnp.zeros_like(dv_ref)
    for chain in chains[:3]:
        chain.run(1)
    count = HALO + BLOCK
    blocks = rows // BLOCK
    for b in range(blocks):
        here = slice(b * BLOCK, (b + 1) * BLOCK)
        span = slice(b * BLOCK, b * BLOCK + count)
        queries, grads = head_stack(q_ref[here]), head_stack(go[here])
        mask = window_mask(place, first_row, base, b, count)
        shares = self_probs(queries, k_ref[span], mask, heads)
        dp_ = mm(v_ref[span], grads, 1, 1)
        ds = (shares * (dp_ - jnp.sum(shares * dp_, axis=0, keepdims=True))).astype(BF16)
        dv_ref[span] += mm(shares.astype(BF16), grads)
        dk_ref[span] += mm(ds, queries)
        dq_ref[here] = (head_diagonal(mm(k_ref[span], ds, 0, 0), heads) * 0.125).T.astype(BF16)
    dq = dq_ref[...]
    dk, dv = dk_ref[...].astype(BF16), dv_ref[...].astype(BF16)
    n1 = n1_ref[...]
    dn = mm(dk, weight(1)) + mm(dv, weight(2))
    halo_out[...] = dn[:HALO].astype(BF16)

    @pl.when(z > 0)
    def _():
        halo_copy(z - 1).start()

    keep(0, mm(dq, n1[HALO:], 0, 0))
    keep(1, mm(dk, n1, 0, 0))
    keep(2, mm(dv, n1, 0, 0))
    own_chain.run(0)
    small[9:10] = column_sums(dq.astype(F32))
    small[10:11] = column_sums(dv.astype(F32))
    dn = dn[HALO:] + mm(dq, weight(0))
    for chain in chains[:3]:
        chain.run(2)
    own_chain.run(1)
    xhat, scale = normed(x_ref[...].astype(F32))

    @pl.when(z < parts - 1)
    def _():
        halo_copy(z + 1).wait_recv()

    @pl.when(z == parts - 1)
    def _():
        halo_land[...] = jnp.zeros_like(halo_land)

    dn = jnp.concatenate([dn[: rows - HALO], dn[rows - HALO :] + halo_land[...].astype(F32)], axis=0)
    input_out[...] = grad + norm_back(dn, gain[0:1], xhat, scale)
    small[0:1] = column_sums(dn * xhat)
    small[3:4] = column_sums(dn)
    total = Total(d, z, parts, bits, total_buffers, total_land, total_line, total_sems, line_sems)
    total.run(0)
    own_chain.run(2)
    for chain in chains[:3]:
        chain.run(3)
    loads[3].wait()
    total.run(1)
    own_chain.run(3)
    total.run(2)
    for j in reversed(range(max(window - PIECES, 0))):
        next_flow(j)
    for p in range(3, len(bits) + 1):
        total.run(p)
    for p in range(4, 8):
        for chain in chains:
            chain.run(p)

    @pl.when(z == 0)
    def _():
        up_land[:PIECES] = jnp.zeros((PIECES, piece, width), BF16)

    @pl.when(z == parts - 1)
    def _():
        down_land[:PIECES] = jnp.zeros((PIECES, piece, width), BF16)

    for i in range(PIECES):
        for up in (True, False):
            j = i if up else PIECES - 1 - i

            @pl.when(comes(j, up))
            def _():
                flow_arrival(j, up).wait_recv()

        mine = own[rows_of(z * PIECES + i)].astype(F32)
        sides = up_land[i].astype(F32) + down_land[PIECES - 1 - i].astype(F32)
        mgrad_out[i * piece : (i + 1) * piece] = (mine + sides).astype(BF16)
    total.finish(small_out)
    for chain in chains:
        chain.close()

    @pl.when(z > 0)
    def _():
        halo_copy(z - 1).wait_send()

    for j in range(window):
        for up in (True, False):
            @pl.when(crosses(j, up))
            def _():
                flow(j, up, False).wait_send()


def finals(
    mgrad, input_grad, fself, fcross, finner, fouter, small,
    out_mgrad, out_input, out_gain, out_shift, out_sw, out_sb, out_so, out_soff,
    out_cw, out_cb, out_co, out_coff, out_inner, out_ib, out_outer, out_ooff,
):
    z = lax.axis_index("mp")
    own = out_so.shape[0]
    parts = out_so.shape[1] // own
    out_mgrad[...] = mgrad[...].astype(F32)
    out_input[...] = input_grad[...]
    out_gain[...] = small[0:3]
    out_shift[...] = small[3:6]
    out_soff[...] = small[6:7]
    out_coff[...] = small[7:8]
    out_ooff[...] = small[8:9]

    def chosen(row, size, offset):
        pieces = [small[row : row + 1, offset + o * size : offset + (o + 1) * size] for o in range(parts)]
        result = pieces[0]
        for o in range(1, parts):
            result = jnp.where(z == o, pieces[o], result)
        return result

    for fin, weights, last, biases, first in (
        (fself, out_sw, out_so, out_sb, 9),
        (fcross, out_cw, out_co, out_cb, 11),
    ):
        for i in range(3):
            weights[i] = fin[i // 2, i % 2].reshape(own, -1).astype(F32)
        last[...] = fin[1, 1].reshape(own, -1).astype(F32)
        for i in range(2):
            for half in range(2):
                lanes = slice(half * HALF, (half + 1) * HALF)
                biases[i : i + 1, lanes] = chosen(first + i, HALF, half * parts * HALF)
    out_inner[...] = finner[...].reshape(out_outer.shape).astype(F32).T
    out_outer[...] = fouter[...].reshape(out_outer.shape).astype(F32)
    size = out_ib.shape[1] // SLICES
    for s in range(SLICES):
        out_ib[0:1, s * size : (s + 1) * size] = chosen(16 + s, size, 0)


def call(body, outs, ins, scratch, **params):
    places = {"s": pltpu.SMEM, "v": pltpu.VMEM, "h": pl.ANY}

    def spec(place):
        return pl.BlockSpec(memory_space=places[place])

    def run(*args):
        return pl.pallas_call(
            body,
            out_shape=[jax.ShapeDtypeStruct(shape, kind) for shape, kind, _ in outs],
            in_specs=[spec(place) for place in ins],
            out_specs=[spec(place) for _, _, place in outs],
            scratch_shapes=[pltpu.VMEM(*x) if isinstance(x, tuple) else x for x in scratch],
            compiler_params=pltpu.CompilerParams(vmem_limit_bytes=56 << 20, **params),
        )(*args)

    return run


def shards(
    block_input,
    memory,
    tok_lengths,
    frame_lengths,
    cotangent,
    norm_gain,
    norm_shift,
    self_weights,
    self_biases,
    self_output,
    self_offset,
    cross_weights,
    cross_biases,
    cross_output,
    cross_offset,
    inner_weight,
    inner_bias,
    outer_weight,
    outer_offset,
):
    rows, width = block_input.shape
    parts = lax.axis_size("mp")
    frames = memory.shape[0] * parts
    heads = width // HEAD
    blocks = rows // BLOCK
    own_hidden = inner_weight.shape[1]
    hidden = own_hidden * parts
    own = width // parts
    dma = pltpu.SemaphoreType.DMA
    wide = heads * BLOCK

    n_att, n_ffn = own * 4 // SLICES, own_hidden // SLICES
    n_bits = lax.axis_size("dp").bit_length() - 1
    piece = memory.shape[0] // PIECES
    small_rows = 16 + SLICES
    own_rows = (rows, width)
    halo_rows = (rows + HALO, width)

    def sliced(n):
        return (2, 2, 2, n, width)

    def turned(weights):
        return jnp.swapaxes(weights, 1, 2)

    (
        wself, wcross, inner, outer, inner_row, value_row, far, memory_rows, ck, cv, n1, q, k, v, att, after, cq
    ) = call(
        gather,
        [
            (sliced(parts * n_att), BF16, "h"),
            (sliced(parts * n_att), BF16, "h"),
            (sliced(parts * n_ffn), BF16, "h"),
            (sliced(parts * n_ffn), BF16, "h"),
            ((SLICES, hidden // SLICES), F32, "v"),
            ((1, width), F32, "v"),
            ((8, 128), F32, "v"),
            ((frames, width), BF16, "h"),
            ((frames, width), BF16, "h"),
            ((frames, width), BF16, "h"),
            (halo_rows, BF16, "v"),
            (own_rows, BF16, "v"),
            (halo_rows, BF16, "v"),
            (halo_rows, BF16, "v"),
            (own_rows, BF16, "v"),
            (own_rows, F32, "v"),
            (own_rows, BF16, "v"),
        ],
        "ssvhvvvvvvvvvvvv",
        [
            (sliced(parts * n_att), BF16),
            (sliced(parts * n_att), BF16),
            (sliced(parts * n_ffn), BF16),
            (sliced(parts * n_ffn), BF16),
            ((frames, width), BF16),
            ((frames, width), BF16),
            ((frames, width), BF16),
            ((4 * own, width), BF16),
            ((4 * own, width), BF16),
            ((own_hidden, width), BF16),
            ((HALO, width), BF16),
            ((8, own_hidden), F32),
            ((parts, 8, own_hidden), F32),
            ((n_bits + 1, 8, 128), F32),
            ((n_bits, 8, 128), F32),
            dma((4, 2, parts)),
            dma((4, NEAR)),
            dma((4, 2, 3)),
            dma((2, parts)),
            dma((2,)),
            dma((2, n_bits)),
            dma,
            dma((parts * PIECES, 3)),
            dma((4,)),
        ],
        collective_id=0,
        has_side_effects=True,
    )(
        tok_lengths, frame_lengths, block_input, memory, turned(self_weights), self_output,
        turned(cross_weights), cross_output, inner_weight, outer_weight, self_biases, cross_biases,
        inner_bias.reshape(1, own_hidden), norm_gain, norm_shift, self_offset.reshape(1, width),
    )
    wcross_rows = wcross.reshape(4 * width, width)
    wself_rows = wself.reshape(4 * width, width)
    inner_rows, outer_rows = inner.reshape(hidden, width), outer.reshape(hidden, width)

    def reduce_buffers(n):
        full = parts * n
        return [
            pltpu.VMEM((2, 2, full, width), BF16),
            pltpu.VMEM((2, 2, full, width), BF16),
            pltpu.VMEM((2, full, width), BF16),
            pltpu.VMEM((2, full, width), BF16),
            pltpu.VMEM((full, width), BF16),
            pltpu.VMEM((parts, n, width), BF16),
            pltpu.VMEM((parts, n, width), BF16),
            pltpu.VMEM((2 * max(n_bits - 3, 1), n, width), F32),
        ]

    def rest(window, first_id):
        extra = ()
        if window > NEAR:
            count = window - NEAR
            pieces = (2, count, piece, width)
            far_mem, far_ck, far_cv = call(
                gather_far,
                [(pieces, BF16, "h")] * 3,
                "hvv",
                [((piece, width), BF16)] * 3 + [dma((4, window)), dma, dma((2,))],
                collective_id=first_id + 1,
                has_side_effects=True,
            )(memory_rows, wcross, value_row)
            extra = (far_ck, far_cv, far_mem)
        block_output, grad, small, mgrad, dw_cross, dwi, dwo = call(
            functools.partial(middle, window),
            [
                (own_rows, F32, "v"),
                (own_rows, F32, "v"),
                ((small_rows, width), F32, "v"),
                ((frames, width), BF16, "h"),
                ((4 * width, width), BF16, "h"),
                ((hidden, width), BF16, "h"),
                ((hidden, width), BF16, "h"),
            ],
            "ssvvvvvvvvvhhhhh" + "h" * len(extra),
            [
                ((frames, width), BF16),
                ((frames, width), BF16),
                ((frames, width), BF16),
                ((hidden, width), BF16),
                ((hidden, width), BF16),
                ((frames, width), BF16),
                ((4, width, width), F32),
                ((4 * width, width), BF16),
                ((hidden, width), BF16),
                ((hidden, width), BF16),
                ((blocks, wide, width), BF16),
                ((blocks, wide, width), BF16),
                ((blocks, 1, wide), F32),
                ((blocks, 1, wide), F32),
                ((width, BLOCK), F32),
                ((width, rows), F32),
                ((CHUNK, width), F32),
                ((CHUNK, width), F32),
                dma((2,)),
                dma((3,)),
                dma((frames // CHUNK,)),
                dma((3, PIECES + 2 * window)),
            ],
        )(
            tok_lengths, frame_lengths, cq, after, cotangent, wcross_rows, inner_row, norm_gain,
            norm_shift, cross_offset.reshape(1, width), outer_offset.reshape(1, width),
            ck, cv, memory_rows, inner_rows, outer_rows, *extra,
        )
        input_grad, *sums = call(
            functools.partial(give_back, window),
            [
                (own_rows, F32, "v"),
                ((frames // parts, width), BF16, "v"),
                (sliced(n_att), BF16, "v"),
                (sliced(n_att), BF16, "v"),
                (sliced(n_ffn), BF16, "v"),
                (sliced(n_ffn), BF16, "v"),
                ((small_rows, width), F32, "v"),
            ],
            "ssvvvvvvvvvvhhhh",
            [
                ((frames, width), BF16),
                ((window, piece, width), BF16),
                ((window, piece, width), BF16),
                (sliced(parts * n_att), BF16),
                (sliced(parts * n_att), BF16),
                (sliced(parts * n_ffn), BF16),
                (sliced(parts * n_ffn), BF16),
                (halo_rows, F32),
                (halo_rows, F32),
                (own_rows, BF16),
                ((HALO, width), BF16),
                ((HALO, width), BF16),
                ((n_bits + 1, small_rows, width), F32),
                ((n_bits, small_rows, width), F32),
                ((parts, small_rows, width), F32),
                reduce_buffers(n_att),
                reduce_buffers(n_att),
                reduce_buffers(n_ffn),
                reduce_buffers(n_ffn),
                dma((4,)),
                dma((4, window)),
                dma((4, 2, 2 + parts)),
                dma((4, 2, max(n_bits - 3, 1))),
                dma((4, 2, 3)),
                dma((2,)),
                dma((2, n_bits)),
                dma((2, parts)),
            ],
            collective_id=first_id,
            has_side_effects=True,
        )(
            tok_lengths, frame_lengths, block_input, n1, q, k, v, att, grad, wself_rows, small, norm_gain,
            mgrad, dw_cross.reshape(sliced(parts * n_att)), dwi.reshape(sliced(parts * n_ffn)),
            dwo.reshape(sliced(parts * n_ffn)),
        )
        return (block_output, input_grad, *sums)

    block_output, *partial_results = lax.cond(
        far[0, 0] > NEAR * piece,
        lambda: rest(PIECES * (parts - 1), 2),
        lambda: rest(NEAR, 1),
    )
    input_grad, mgrad_sum, fself, fcross, finner, fouter, small = partial_results
    results = call(
        finals,
        [
            ((frames // parts, width), F32, "v"),
            (own_rows, F32, "v"),
            ((3, width), F32, "v"),
            ((3, width), F32, "v"),
            ((3, own, width), F32, "v"),
            ((2, own), F32, "v"),
            ((own, width), F32, "v"),
            ((1, width), F32, "v"),
            ((3, own, width), F32, "v"),
            ((2, own), F32, "v"),
            ((own, width), F32, "v"),
            ((1, width), F32, "v"),
            ((width, own_hidden), F32, "v"),
            ((1, own_hidden), F32, "v"),
            ((own_hidden, width), F32, "v"),
            ((1, width), F32, "v"),
        ],
        "vvvvvvv",
        [],
    )(mgrad_sum, input_grad, fself, fcross, finner, fouter, small)
    memory_grad, input_grad, *others = results
    others = [r.reshape(-1) if r.shape[0] == 1 else r for r in others]
    others[2], others[6] = turned(others[2]), turned(others[6])
    return (block_output, input_grad, memory_grad, *others)


def solution(mesh):
    in_specs = (
        P(("dp", "mp"), None),
        P(("dp", "mp"), None),
        P("dp", None),
        P("dp", None),
        P(("dp", "mp"), None),
        P(),
        P(),
        P(None, None, "mp"),
        P(None, "mp"),
        P("mp", None),
        P(),
        P(None, None, "mp"),
        P(None, "mp"),
        P("mp", None),
        P(),
        P(None, "mp"),
        P("mp"),
        P("mp", None),
        P(),
    )
    out_specs = (
        P(("dp", "mp"), None),
        P(("dp", "mp"), None),
        P(("dp", "mp"), None),
        P(),
        P(),
        P(None, None, "mp"),
        P(None, "mp"),
        P("mp", None),
        P(),
        P(None, None, "mp"),
        P(None, "mp"),
        P("mp", None),
        P(),
        P(None, "mp"),
        P("mp"),
        P("mp", None),
        P(),
    )
    return jax.shard_map(shards, mesh=mesh, in_specs=in_specs, out_specs=out_specs, check_vma=False)
```

```python
import functools
import math

import jax
import jax.numpy as jnp
from jax import lax
from jax.experimental import pallas as pl
from jax.experimental.pallas import tpu as pltpu
from jax.sharding import PartitionSpec as P

HEAD = 64
NEGATIVE = -1e30
EPSILON = 1e-05
BLOCK = 128
TILE = 512
HALO = 256
F32 = jnp.float32
BF16 = jnp.bfloat16
MESH = pl.DeviceIdType.MESH
HALF = HEAD // 2
SLICES = 8
PIECES = 4
NEAR = 6
GELU_A = math.sqrt(2.0 / math.pi)
GELU_B = 0.044715


def mm(a, b, ca=1, cb=0):
    return lax.dot_general(a, b, (((ca,), (cb,)), ((), ())), preferred_element_type=F32)


def normed(values):
    center = values - jnp.mean(values, axis=-1, keepdims=True)
    spread = jnp.mean(center * center, axis=-1, keepdims=True)
    scale = lax.rsqrt(spread + EPSILON)
    return center * scale, scale


def norm_back(grad, gain, xhat, scale):
    gn = grad * gain
    first = jnp.mean(gn, axis=-1, keepdims=True)
    second = jnp.mean(gn * xhat, axis=-1, keepdims=True)
    return (gn - first - xhat * second) * scale


def column_sums(values):
    return jnp.sum(values, axis=0, keepdims=True)


def head_stack(values):
    rows, width = values.shape
    heads = width // HEAD
    lane = lax.broadcasted_iota(jnp.int32, (rows, width), 1) // HALF % heads
    zero = jnp.zeros_like(values)
    return jnp.concatenate([jnp.where(lane == h, values, zero) for h in range(heads)], axis=0)


def head_rows(heads):
    return [
        (slice((i * heads + h) * HALF, (i * heads + h + 1) * HALF), h)
        for i in range(2)
        for h in range(heads)
    ]


def head_diagonal(values, heads):
    rows = values.shape[1] // heads
    return jnp.concatenate(
        [values[r, h * rows : (h + 1) * rows] for r, h in head_rows(heads)], axis=0
    )


def token_rows(tok_ref, frm_ref, base, count):
    place = lax.broadcasted_iota(jnp.int32, (1, count), 1) + base
    zero = jnp.zeros((1, count), jnp.int32)

    def step(u, carry):
        start, first_row, first_frame, end_frame = carry
        tokens, frames = tok_ref[0, u], frm_ref[0, u]
        end = start + tokens
        done = place >= end
        first_row = first_row + jnp.where(done, tokens, 0)
        first_frame = first_frame + jnp.where(done, frames, 0)
        end_frame = end_frame + jnp.where(place >= start, frames, 0)
        return end, first_row, first_frame, end_frame

    _, first_row, first_frame, end_frame = lax.fori_loop(
        0, tok_ref.shape[1], step, (jnp.int32(0), zero, zero, zero)
    )
    return place, first_row, first_frame, end_frame


def excursion(tok_ref, frm_ref, rows, frames, parts):
    lane = lax.broadcasted_iota(jnp.int32, (1, 128), 1)
    zero = jnp.zeros((1, 128), jnp.int32)

    def step(u, carry):
        start, low, high = carry
        tokens, count = tok_ref[0, u], frm_ref[0, u]
        end = start + tokens
        low = low + jnp.where(lane * rows >= end, count, 0)
        high = high + jnp.where((lane + 1) * rows - 1 >= start, count, 0)
        return end, low, high

    _, low, high = lax.fori_loop(0, tok_ref.shape[1], step, (jnp.int32(0), zero, zero))
    beyond = jnp.maximum(high - (lane + 1) * frames, lane * frames - low)
    return jnp.max(jnp.where(lane < parts, beyond, 0), axis=1, keepdims=True).astype(F32)


def block_frames(tok_ref, frm_ref, base, count):
    blocks = count // BLOCK

    def step(u, carry):
        start, low, high = carry
        tokens, frames = tok_ref[0, u], frm_ref[0, u]
        end = start + tokens
        low = tuple(
            v + jnp.where(base + b * BLOCK >= end, frames, 0) for b, v in enumerate(low)
        )
        high = tuple(
            v + jnp.where(base + (b + 1) * BLOCK - 1 >= start, frames, 0) for b, v in enumerate(high)
        )
        return end, low, high

    zeros = (jnp.int32(0),) * blocks
    _, low, high = lax.fori_loop(0, tok_ref.shape[1], step, (jnp.int32(0), zeros, zeros))
    return low, high


def window_mask(place, first_row, base, block, count):
    keys = lax.broadcasted_iota(jnp.int32, (count, BLOCK), 0) + (base - HALO + block * BLOCK)
    here = slice(block * BLOCK, (block + 1) * BLOCK)
    return (keys >= first_row[:, here]) & (keys <= place[:, here])


def self_probs(queries, key_window, mask, heads):
    scores = mm(key_window, queries, 1, 1)
    parts = []
    for h in range(heads):
        part = jnp.where(mask, scores[:, h * BLOCK : (h + 1) * BLOCK], NEGATIVE)
        raised = jnp.exp(part - jnp.max(part, axis=0, keepdims=True))
        parts.append(raised * (1.0 / jnp.sum(raised, axis=0, keepdims=True)))
    return jnp.concatenate(parts, axis=1)


def rcopy(src, dst, send, recv, **device):
    return pltpu.make_async_remote_copy(
        src_ref=src, dst_ref=dst, send_sem=send, recv_sem=recv, device_id=device, device_id_type=MESH
    )


def at_rows(start, count):
    return pl.ds(pl.multiple_of(start, 16), count)


def flipped(index, bit):
    return index + bit - 2 * bit * (index // bit % 2)


def greet(z, parts, d, bits, masks=()):
    barrier = pltpu.get_barrier_semaphore()
    for mask in masks:
        device = d
        for bit in (1, 2, 4):
            if mask & bit:
                device = flipped(device, bit)
        pl.semaphore_signal(barrier, inc=1, device_id={"dp": device}, device_id_type=MESH)
    for step in range(1, parts):
        device = {"mp": (z + step) % parts}
        pl.semaphore_signal(barrier, inc=1, device_id=device, device_id_type=MESH)
    for bit in bits:
        device = {"dp": flipped(d, bit)}
        pl.semaphore_signal(barrier, inc=1, device_id=device, device_id_type=MESH)
    return barrier, parts - 1 + len(bits) + len(masks)


class Direct:
    def __init__(self, z, parts, own, place, sems):
        self.z, self.parts, self.own, self.place, self.sems = z, parts, own, place, sems

    def copy(self, step):
        device = (self.z + step) % self.parts
        sems = self.sems
        return rcopy(self.own, self.place(self.z), sems.at[0, step], sems.at[1, step], mp=device)

    def send(self):
        for step in range(1, self.parts):
            self.copy(step).start()

    def arrived(self):
        for step in range(1, self.parts):
            other = (self.z - step + self.parts) % self.parts
            place, sems = self.place(other), self.sems
            rcopy(place, place, sems.at[0, step], sems.at[1, step], mp=other).wait_recv()

    def close(self):
        for step in range(1, self.parts):
            self.copy(step).wait_send()


DP_BITS = (2, 4, 1)


def corner(d):
    return d % 2, d // 4 % 2, d // 2 % 2


class Plane:
    def __init__(self, d, buffer, first_y, sems):
        self.d, self.buffer, self.first_y, self.sems = d, buffer, first_y, sems

    def block(self, p, c, y, x):
        if p == 0:
            return self.buffer.at[c, y, x]
        if p == 2:
            return self.buffer.at[c]
        return self.buffer.at[c, :, x] if self.first_y else self.buffer.at[c, y]

    def copy(self, p, other):
        c, y, x = corner(self.d)
        over_y = p == (0 if self.first_y else 1)
        if other:
            if p == 2:
                c = 1 - c
            elif over_y:
                y = 1 - y
            else:
                x = 1 - x
        block = self.block(p, c, y, x)
        device = flipped(self.d, 1 if p == 2 else 4 if over_y else 2)
        return rcopy(block, block, self.sems.at[0, p], self.sems.at[1, p], dp=device)

    def send(self, p):
        self.copy(p, False).start()

    def arrived(self, p):
        self.copy(p, True).wait_recv()

    def close(self):
        for p in range(3):
            self.copy(p, False).wait_send()


class Window:
    def __init__(self, z, parts, source, place, sems):
        self.z, self.parts, self.source, self.place, self.sems = z, parts, source, place, sems

    def number(self, z, j, up):
        return (z + 1) * PIECES - 1 - j if up else z * PIECES + j

    def there(self, number):
        return (number >= 0) & (number < self.parts * PIECES)

    def copy(self, j, up):
        number = self.number(self.z, j, up)
        place, kind = self.place(number, j, up), 0 if up else 2
        return rcopy(
            self.source(number, j, up),
            place,
            self.sems.at[kind, j],
            self.sems.at[kind + 1, j],
            mp=self.z + 1 if up else self.z - 1,
        )

    def sends(self, j, up):
        edge = self.z < self.parts - 1 if up else self.z > 0
        return edge & self.there(self.number(self.z, j, up))

    def send(self, j):
        for up in (True, False):

            @pl.when(self.sends(j, up))
            def _():
                self.copy(j, up).start()

    def comes(self, j, up):
        edge = self.z > 0 if up else self.z < self.parts - 1
        return edge & self.there(self.arrival(j, up))

    def arrival(self, j, up):
        return self.number(self.z - 1 if up else self.z + 1, j, up)

    def arrived(self, j):
        for up in (True, False):

            @pl.when(self.comes(j, up))
            def _():
                number = self.arrival(j, up)
                place, kind = self.place(number, j, up), 0 if up else 2
                rcopy(
                    place,
                    place,
                    self.sems.at[kind, j],
                    self.sems.at[kind + 1, j],
                    mp=self.z - 1 if up else self.z + 1,
                ).wait_recv()

    def each(self, j, use):
        for up in (True, False):

            @pl.when(self.comes(j, up))
            def _():
                use(self.arrival(j, up), j, up)

    def close(self, pieces):
        for j in pieces:
            for up in (True, False):

                @pl.when(self.sends(j, up))
                def _():
                    self.copy(j, up).wait_send()


def gather(
    tok, frm, x_ref, mem, sw, so, cw, co, inner, outer, sb, cb, ib, gain, shift, offset,
    wself_out, wcross_out, inner_out, outer_out, ib_out, vb_out, far_out, mem_out, ck_out, cv_out, spare,
    n1_ref, q_ref, k_ref, v_ref, att_ref, after_ref, cq_ref,
    gself, gcross, ginner, gouter, gmem, sck, scv, pself, pcross, pinner, halo, pbias, gbias,
    far, far_land, line_sems, mem_sems, plane_sems, bias_sems, halo_sems, far_sems, own_sem, out_sems, weight_sems,
):
    rows, width = x_ref.shape
    heads = width // HEAD
    own = sw.shape[1]
    parts = width // own
    shard_rows = mem.shape[0]
    piece = shard_rows // PIECES
    z, d = lax.axis_index("mp"), lax.axis_index("dp")
    dp = lax.axis_size("dp")
    bits = [1 << i for i in range(dp.bit_length() - 1)]
    c, y, x = corner(d)
    s = c * 4 + y * 2 + x
    barrier, greetings = greet(z, parts, d, bits)

    for source, last, packed in ((sw, so, pself), (cw, co, pcross)):
        for i in range(3):
            packed[i * own : (i + 1) * own] = source[i]
        packed[3 * own :] = last[...]
    pbias[...] = jnp.zeros_like(pbias)
    pbias[0:1] = ib[...]
    for i in range(2):
        pbias[1:2, i * own : (i + 1) * own] = sb[i : i + 1]
        pbias[1:2, (2 + i) * own : (3 + i) * own] = cb[i : i + 1]
    pinner[...] = inner[...].T
    groups = []
    for i, (packed, buffer) in enumerate(
        ((pself, gself), (pcross, gcross), (pinner, ginner), (outer, gouter))
    ):
        n = packed.shape[0] // SLICES
        mine = packed.at[at_rows(s * n, n)]

        def place(shard, buffer=buffer, n=n):
            return buffer.at[c, y, x, at_rows(shard * n, n)]

        line = Direct(z, parts, mine, place, line_sems.at[i])
        plane = Plane(d, buffer, i % 2 == 1, plane_sems.at[i])
        groups.append((line, plane))
        buffer[c, y, x, at_rows(z * n, n)] = packed[at_rows(s * n, n)]

    def piece_place(number, j, up):
        return gmem.at[at_rows(number * piece, piece)]

    def piece_source(number, j, up):
        if j < PIECES:
            return mem.at[at_rows((number - z * PIECES) * piece, piece)]
        return piece_place(number, j, up)

    memory = Window(z, parts, piece_source, piece_place, mem_sems)

    def bias_copy(step):
        return rcopy(
            pbias, gbias.at[z], bias_sems.at[0, step], bias_sems.at[1, step], mp=(z + step) % parts
        )

    def bias_arrival(step):
        other = (z - step + parts) % parts
        return rcopy(pbias, gbias.at[other], bias_sems.at[0, step], bias_sems.at[1, step], mp=other)

    def halo_copy(other):
        return rcopy(x_ref.at[rows - HALO :], halo, halo_sems.at[0], halo_sems.at[1], mp=other)

    def far_copy(i):
        device = flipped(d, bits[i])
        return rcopy(far.at[i], far_land.at[i], far_sems.at[0, i], far_sems.at[1, i], dp=device)

    def far_step(i):
        if i > 0:
            far_copy(i - 1).wait_recv()
            far[i] = jnp.maximum(far[i - 1], far_land[i - 1])
        if i < len(bits):
            far_copy(i).start()
        else:
            far_out[...] = far[i, 0:1, 0:1]

    def forward(j):
        memory.arrived(j - PIECES)
        memory.send(j)

    far[0] = jnp.broadcast_to(excursion(tok, frm, rows, shard_rows, parts), far.shape[1:])
    pl.semaphore_wait(barrier, greetings)
    for line, _ in groups[:2]:
        line.send()
    for step in range(1, parts):
        bias_copy(step).start()

    @pl.when(z < parts - 1)
    def _():
        halo_copy(z + 1).start()

    for line, _ in groups[2:]:
        line.send()
    for j in range(PIECES):
        memory.send(j)
    far_step(0)
    own_rows = gmem.at[at_rows(z * shard_rows, shard_rows)]
    own_copy = pltpu.make_async_copy(mem, own_rows, own_sem)
    own_copy.start()
    gbias[z] = pbias[...]
    for line, plane in groups[:2]:
        line.arrived()
        plane.send(0)
    for _, plane in groups[:2]:
        plane.arrived(0)
        plane.send(1)
    for line, plane in groups[2:]:
        line.arrived()
        plane.send(0)
    far_step(1)
    for _, plane in groups[:2]:
        plane.arrived(1)
        plane.send(2)
    far_step(2)
    groups[0][1].arrived(2)

    for step in range(1, parts):
        bias_arrival(step).wait_recv()

    def head_bias(i):
        return jnp.concatenate(
            [
                gbias[o, 1:2, i * own + half * HALF : i * own + (half + 1) * HALF]
                for half in range(2)
                for o in range(parts)
            ],
            axis=1,
        )

    n = ginner.shape[3] // parts
    for i in range(SLICES):
        ib_out[i : i + 1] = jnp.concatenate(
            [gbias[o, 0:1, i * n : (i + 1) * n] for o in range(parts)], axis=1
        )

    @pl.when(z > 0)
    def _():
        halo_copy(z - 1).wait_recv()

    @pl.when(z == 0)
    def _():
        halo[...] = jnp.zeros_like(halo)

    def weight(buffer, i):
        return buffer[i // 2, i % 2].reshape(width, width)

    base = z * rows
    place_row, first_row, _, _ = token_rows(tok, frm, base, rows)
    for src, dst in ((halo, slice(0, HALO)), (x_ref, slice(HALO, HALO + rows))):
        xhat, _ = normed(src[...].astype(F32))
        n1_ref[dst] = (xhat * gain[0:1] + shift[0:1]).astype(BF16)
    n1 = n1_ref[...]
    query = mm(n1[HALO:], weight(gself, 0), 1, 1) + head_bias(0)
    q_ref[...] = query.astype(BF16) * jnp.asarray(0.125, BF16)
    k_ref[...] = mm(n1, weight(gself, 1), 1, 1).astype(BF16)
    v_ref[...] = (mm(n1, weight(gself, 2), 1, 1) + head_bias(1)).astype(BF16)
    count = HALO + BLOCK
    for b in range(rows // BLOCK):
        queries = head_stack(q_ref[b * BLOCK : (b + 1) * BLOCK])
        window = slice(b * BLOCK, b * BLOCK + count)
        mask = window_mask(place_row, first_row, base, b, count)
        probs = self_probs(queries, k_ref[window], mask, heads).astype(BF16)
        out = head_diagonal(mm(v_ref[window], probs, 0, 0), heads)
        att_ref[b * BLOCK : (b + 1) * BLOCK] = out.T.astype(BF16)
        if b == 0:
            for _, plane in groups[2:]:
                plane.arrived(0)
                plane.send(1)
    forward(PIECES)
    after = x_ref[...].astype(F32) + mm(att_ref[...], weight(gself, 3)) + offset[...]
    after_ref[...] = after
    xhat, _ = normed(after)
    groups[1][1].arrived(2)
    n2 = (xhat * gain[1:2] + shift[1:2]).astype(BF16)
    query = mm(n2, weight(gcross, 0), 1, 1) + head_bias(2)
    cq_ref[...] = query.astype(BF16) * jnp.asarray(0.125, BF16)
    value_bias = head_bias(3)
    forward(PIECES + 1)

    def project(start, size):
        here = at_rows(start, size)
        block = gmem[here]
        sck[here] = mm(block, weight(gcross, 1), 1, 1).astype(BF16)
        scv[here] = (mm(block, weight(gcross, 2), 1, 1) + value_bias).astype(BF16)

    def copies_out(number):
        here = at_rows(number * piece, piece)
        return [
            pltpu.make_async_copy(a.at[here], b.at[here], out_sems.at[number, i])
            for i, (a, b) in enumerate(((gmem, mem_out), (sck, ck_out), (scv, cv_out)))
        ]

    def project_piece(number, j=0, up=True):
        project(number * piece, piece)
        for copy in copies_out(number):
            copy.start()

    own_copy.wait()
    lax.fori_loop(0, PIECES, lambda i, _: (project_piece(z * PIECES + i), 0)[1], 0)
    for _, plane in groups[2:]:
        plane.arrived(1)
        plane.send(2)
    for j in range(PIECES):
        if j >= 2:
            memory.arrived(j)
        memory.each(j, project_piece)
    for i in range(3, len(bits) + 1):
        far_step(i)
    for _, plane in groups[2:]:
        plane.arrived(2)
    outs = [
        pltpu.make_async_copy(a, b, weight_sems.at[i])
        for i, (a, b) in enumerate(
            ((gself, wself_out), (gcross, wcross_out), (ginner, inner_out), (gouter, outer_out))
        )
    ]
    for copy in outs:
        copy.start()
    vb_out[...] = value_bias
    for j in range(PIECES, NEAR):
        memory.arrived(j)
        memory.each(j, project_piece)
    for copy in outs:
        copy.wait()

    def finish(number, *_):
        for copy in copies_out(number):
            copy.wait()

    for i in range(PIECES):
        finish(z * PIECES + i)
    for j in range(NEAR):
        memory.each(j, finish)
    for line, plane in groups:
        line.close()
        plane.close()
    memory.close(range(NEAR))
    for i in range(len(bits)):
        far_copy(i).wait_send()
    for step in range(1, parts):
        bias_copy(step).wait_send()

    @pl.when(z < parts - 1)
    def _():
        halo_copy(z + 1).wait_send()


def gather_far(mem, far_mem, sems):
    z, d = lax.axis_index("mp"), lax.axis_index("dp")
    parts = lax.axis_size("mp")
    last = PIECES * (parts - 1)
    piece = mem.shape[0] // parts // PIECES
    barrier, greetings = greet(z, parts, d, ())

    def place(number, j, up):
        return far_mem.at[at_rows(number * piece, piece)]

    def source(number, j, up):
        return (mem if j - PIECES < NEAR else far_mem).at[at_rows(number * piece, piece)]

    memory = Window(z, parts, source, place, sems)
    pl.semaphore_wait(barrier, greetings)
    for j in range(NEAR, last):
        if j - PIECES >= NEAR:
            memory.arrived(j - PIECES)
        memory.send(j)
    for j in range(max(NEAR, last - PIECES), last):
        memory.arrived(j)
    memory.close(range(NEAR, last))


def middle(
    far, tok, frm, cq_ref, after_ref, cot_ref, w_ref, ib_ref, vb_ref, gain, shift, cross_offset, outer_offset,
    ck_in, cv_in, mem_in, far_in, wi_in, wo_in,
    out_ref, grad_ref, small_ref, mgrad_out, dw_out, dwi_out, dwo_out,
    ck_ref, cv_ref, mem_ref, wi_ref, wo_ref, mgrad_ref, dw_ref, dwb_ref, dwi_ref, dwo_ref,
    qbig, gbig, lse_ref, dot_ref, att_ref, dq_ref, dk_ref, dv_ref, first_ref, end_ref, bounds,
    in_sems, out_sems, piece_sems,
):
    rows, width = cq_ref.shape
    heads = width // HEAD
    blocks = rows // BLOCK
    z = lax.axis_index("mp")
    parts = lax.axis_size("mp")
    last = parts * PIECES
    frames = mem_in.shape[0]
    piece = frames // last
    beyond = far[0, 0] > NEAR * piece

    def weight(i):
        return w_ref[i * width : (i + 1) * width]

    def rows_of(number):
        return at_rows(jnp.clip(number, 0, last - 1) * piece, piece)

    def number(j, up):
        return z * PIECES - 1 - j if up else (z + 1) * PIECES + j

    def there(j, up):
        return number(j, up) >= 0 if up else number(j, up) < last

    def near_loads(i, source, full):
        own = at_rows(z * PIECES * piece, PIECES * piece)
        loads = [(None, pltpu.make_async_copy(source.at[own], full.at[own], piece_sems.at[i, 0]))]
        for j in range(NEAR):
            for up in (True, False):
                here = rows_of(number(j, up))
                sem = piece_sems.at[i, 1 + 2 * j + (0 if up else 1)]
                loads.append((there(j, up), pltpu.make_async_copy(source.at[here], full.at[here], sem)))
        return loads

    def act(loads, name):
        for present, copy in loads:
            if present is None:
                getattr(copy, name)()
            else:
                pl.when(present)(getattr(copy, name))

    arrays = ((ck_in, ck_ref), (cv_in, cv_ref), (mem_in, mem_ref))
    frame_loads = [near_loads(i, a, b) for i, (a, b) in enumerate(arrays)]
    act(frame_loads[0], "start")
    act(frame_loads[1], "start")
    loads = [
        pltpu.make_async_copy(a, b, in_sems.at[i])
        for i, (a, b) in enumerate(((wi_in, wi_ref), (wo_in, wo_ref)))
    ]
    for load in loads:
        load.start()
    act(frame_loads[2], "start")
    for _, full in arrays:
        full[frames:] = jnp.zeros((TILE, width), BF16)

        @pl.when(jnp.logical_not(beyond))
        def _():
            for j, up in ((NEAR, True), (NEAR, False), (NEAR + 1, False)):

                @pl.when(there(j, up))
                def _():
                    full[rows_of(number(j, up))] = jnp.zeros((piece, width), BF16)

    @pl.when(beyond)
    def _():
        act(frame_loads[2], "wait")

        def fetch(i, carry):
            for up in (True, False):
                j = NEAR + i

                @pl.when(there(j, up))
                def _():
                    here = rows_of(number(j, up))
                    copy = pltpu.make_async_copy(far_in.at[here], mem_ref.at[here], in_sems.at[2])
                    copy.start()
                    copy.wait()
                    block = mem_ref[here]
                    ck_ref[here] = mm(block, weight(1), 1, 1).astype(BF16)
                    cv_ref[here] = (mm(block, weight(2), 1, 1) + vb_ref[...]).astype(BF16)

            return carry

        lax.fori_loop(0, last - PIECES - NEAR, fetch, 0)

    base = z * rows
    _, _, first_frame, end_frame = token_rows(tok, frm, base, rows)
    for b in range(blocks):
        first_ref[b] = first_frame[:, b * BLOCK : (b + 1) * BLOCK]
        end_ref[b] = end_frame[:, b * BLOCK : (b + 1) * BLOCK]
        qbig[b] = head_stack(cq_ref[b * BLOCK : (b + 1) * BLOCK])
    low, high = block_frames(tok, frm, base, rows)
    for b in range(blocks):
        bounds[0, b] = low[b] // 128 * 128
        bounds[1, b] = high[b]
    small_ref[...] = jnp.zeros_like(small_ref)
    mgrad_ref[...] = jnp.zeros_like(mgrad_ref)

    def tiles(b):
        return (bounds[1, b] - bounds[0, b] + TILE - 1) // TILE

    def tile_mask(start, b):
        frame = lax.broadcasted_iota(jnp.int32, (TILE, BLOCK), 0) + start
        return (frame >= first_ref[b]) & (frame < end_ref[b])

    def columns(h):
        return slice(h * BLOCK, (h + 1) * BLOCK)

    act(frame_loads[0], "wait")
    act(frame_loads[1], "wait")

    def attend(b, carry):
        att_ref[b] = jnp.zeros((width, BLOCK), F32)

        def step(i, carry):
            start = bounds[0, b] + i * TILE
            here = pl.ds(pl.multiple_of(start, 128), TILE)
            scores = mm(ck_ref[here], qbig[b], 1, 1)
            mask = tile_mask(start, b)
            values = cv_ref[here].T
            news = []
            for h in range(heads):
                largest, total = carry[h]
                part = jnp.where(mask, scores[:, columns(h)], NEGATIVE)
                now = jnp.maximum(largest, jnp.max(part, axis=0, keepdims=True))
                fade = jnp.exp(largest - now)
                raised = jnp.exp(part - now)
                news.append((now, total * fade + jnp.sum(raised, axis=0, keepdims=True)))
                pieces = [r for r, o in head_rows(heads) if o == h]
                own = jnp.concatenate([values[r] for r in pieces], axis=0)
                out = mm(own, raised.astype(BF16))
                for i, r in enumerate(pieces):
                    att_ref[b, r] = att_ref[b, r] * fade + out[i * HALF : (i + 1) * HALF]
            return tuple(news)

        start = (jnp.full((1, BLOCK), NEGATIVE, F32), jnp.zeros((1, BLOCK), F32))
        done = lax.fori_loop(0, tiles(b), step, (start,) * heads)
        for h, (largest, total) in enumerate(done):
            lse_ref[b, :, columns(h)] = largest + jnp.log(total)
            share = 1.0 / total
            for r, o in head_rows(heads):
                if o == h:
                    att_ref[b, r] = att_ref[b, r] * share
        return carry

    lax.fori_loop(0, blocks, attend, 0)
    att = jnp.concatenate([att_ref[b].T for b in range(blocks)], axis=0).astype(BF16)
    after_self = after_ref[...]
    after_cross = after_self + mm(att, weight(3)) + cross_offset[...]
    xhat3, scale3 = normed(after_cross)
    n3 = (xhat3 * gain[2:3] + shift[2:3]).astype(BF16)
    sent = cot_ref[...]
    small_ref[8:9] = column_sums(sent.astype(F32))
    hidden = wi_ref.shape[0]
    tile = hidden // SLICES
    loads[0].wait()
    loads[1].wait()
    out_ref[...] = after_cross + outer_offset[...]
    grad_ref[...] = jnp.zeros((rows, width), F32)

    def feed(f, carry):
        here = pl.ds(pl.multiple_of(f * tile, tile), tile)
        before = mm(n3, wi_ref[here], 1, 1) + ib_ref[pl.ds(f, 1)]
        square = before * before
        inner = jnp.tanh(before * (GELU_A + (GELU_A * GELU_B) * square))
        half = 0.5 + 0.5 * inner
        active = (before * half).astype(BF16)
        slope = half + (0.5 * before) * (1.0 - inner * inner) * (
            GELU_A + (3.0 * GELU_A * GELU_B) * square
        )
        out_ref[...] += mm(active, wo_ref[here])
        back = (slope * mm(sent, wo_ref[here], 1, 1)).astype(BF16)
        grad_ref[...] += mm(back, wi_ref[here])
        dwo_ref[here] = mm(active, sent, 0, 0).astype(BF16)
        dwi_ref[here] = mm(back, n3, 0, 0).astype(BF16)
        small_ref[pl.ds(16 + f, 1)] = column_sums(back.astype(F32))
        return carry

    lax.fori_loop(0, SLICES, feed, 0)
    stores = [
        pltpu.make_async_copy(a, b, out_sems.at[i])
        for i, (a, b) in enumerate(
            ((dwi_ref, dwi_out), (dwo_ref, dwo_out), (dwb_ref, dw_out), (mgrad_ref.at[:frames], mgrad_out))
        )
    ]
    stores[0].start()
    stores[1].start()
    dn3 = grad_ref[...]
    small_ref[2:3] = column_sums(dn3 * xhat3)
    small_ref[5:6] = column_sums(dn3)
    grad = sent.astype(F32) + norm_back(dn3, gain[2:3], xhat3, scale3)
    sent2 = grad.astype(BF16)
    small_ref[7:8] = column_sums(sent2.astype(F32))
    dwb_ref[3 * width :] = mm(att, sent2, 0, 0).astype(BF16)
    go = mm(sent2, weight(3), 1, 1).astype(BF16)
    got = mm(weight(3), sent2, 1, 1).astype(BF16).astype(F32)
    for b in range(blocks):
        gbig[b] = head_stack(go[b * BLOCK : (b + 1) * BLOCK])
        prod = got[:, b * BLOCK : (b + 1) * BLOCK] * att_ref[b]
        sums = [column_sums(prod[r]) for r, _ in head_rows(heads)]
        for h in range(heads):
            dot_ref[b, :, columns(h)] = sums[h] + sums[heads + h]
    origin = bounds[0, 0]
    count = (bounds[1, blocks - 1] - origin + TILE - 1) // TILE

    def span(i):
        return pl.ds(pl.multiple_of(origin + i * TILE, 128), TILE)

    def clear(i, carry):
        dk_ref[span(i)] = jnp.zeros((TILE, width), F32)
        dv_ref[span(i)] = jnp.zeros((TILE, width), F32)
        return carry

    lax.fori_loop(0, count, clear, 0)

    def attend_back(b, carry):
        dq_ref[b] = jnp.zeros((width, BLOCK), F32)

        def step(i, carry):
            start = bounds[0, b] + i * TILE
            here = pl.ds(pl.multiple_of(start, 128), TILE)
            keys, values = ck_ref[here], cv_ref[here]
            scores = mm(keys, qbig[b], 1, 1)
            dp = mm(values, gbig[b], 1, 1)
            mask = tile_mask(start, b)
            shares, scaled = [], []
            for h in range(heads):
                part = jnp.exp(scores[:, columns(h)] - lse_ref[b, :, columns(h)])
                part = jnp.where(mask, part, 0.0)
                shares.append(part.astype(BF16))
                scaled.append((part * (dp[:, columns(h)] - dot_ref[b, :, columns(h)])).astype(BF16))
            shares, scaled = jnp.concatenate(shares, axis=1), jnp.concatenate(scaled, axis=1)
            dv_ref[here] += mm(shares, gbig[b])
            dk_ref[here] += mm(scaled, qbig[b])
            dq_ref[b] += head_diagonal(mm(keys, scaled, 0, 0), heads)
            return carry

        return lax.fori_loop(0, tiles(b), step, carry)

    lax.fori_loop(0, blocks, attend_back, 0)

    @pl.when(jnp.logical_not(beyond))
    def _():
        act(frame_loads[2], "wait")

    dw_ref[...] = jnp.zeros_like(dw_ref)

    def frame_step(i, carry):
        here = span(i)
        dk, dv = dk_ref[here].astype(BF16), dv_ref[here].astype(BF16)
        mgrad_ref[here] = (mm(dk, weight(1)) + mm(dv, weight(2))).astype(BF16)
        frame_rows = mem_ref[here]
        dw_ref[0] += mm(dk, frame_rows, 0, 0)
        dw_ref[1] += mm(dv, frame_rows, 0, 0)
        small_ref[12:13] += column_sums(dv.astype(F32))
        return carry

    lax.fori_loop(0, count, frame_step, 0)
    stores[3].start()
    dq = jnp.concatenate([(dq_ref[b] * 0.125).T for b in range(blocks)], axis=0).astype(BF16)
    small_ref[11:12] = column_sums(dq.astype(F32))
    xhat2, scale2 = normed(after_self)
    n2 = (xhat2 * gain[1:2] + shift[1:2]).astype(BF16)
    dwb_ref[:width] = mm(dq, n2, 0, 0).astype(BF16)
    dwb_ref[width : 2 * width] = dw_ref[0].astype(BF16)
    dwb_ref[2 * width : 3 * width] = dw_ref[1].astype(BF16)
    stores[2].start()
    dn2 = mm(dq, weight(0))
    small_ref[1:2] = column_sums(dn2 * xhat2)
    small_ref[4:5] = column_sums(dn2)
    grad_ref[...] = grad + norm_back(dn2, gain[1:2], xhat2, scale2)
    for store in stores:
        store.wait()


def sum_far(mgrad_in, mgrad_out, own, land, flow_sems, load_sem):
    pieces, piece = land.shape[1:3]
    frames = own.shape[0]
    parts = frames // piece // PIECES
    last = NEAR + pieces
    z, d = lax.axis_index("mp"), lax.axis_index("dp")
    barrier, greetings = greet(z, parts, d, ())
    load = pltpu.make_async_copy(mgrad_in, own, load_sem)
    load.start()

    def rows_of(number):
        return at_rows(number * piece, piece)

    def there(number):
        return (number >= 0) & (number < parts * PIECES)

    def sent(j, up):
        return (z + 1) * PIECES + j if up else z * PIECES - 1 - j

    def comes(j, up):
        return z * PIECES + j if up else (z + 1) * PIECES - 1 - j

    def flow(j, up, number, device):
        kind = 0 if up else 2
        place = land.at[0 if up else 1, j - NEAR]
        sems = flow_sems.at[kind, j - NEAR], flow_sems.at[kind + 1, j - NEAR]
        return rcopy(own.at[rows_of(number)], place, *sems, mp=device)

    def arrive(j):
        for up in (True, False):

            @pl.when(there(comes(j, up)) & (z > 0 if up else z < parts - 1))
            def _():
                number = comes(j, up)
                flow(j, up, number, z - 1 if up else z + 1).wait_recv()
                here = rows_of(number)
                more = land[0 if up else 1, j - NEAR].astype(F32)
                own[here] = (own[here].astype(F32) + more).astype(BF16)

    def each(j, name):
        for up in (True, False):

            @pl.when(there(sent(j, up)) & (z < parts - 1 if up else z > 0))
            def _():
                getattr(flow(j, up, sent(j, up), z + 1 if up else z - 1), name)()

    load.wait()
    pl.semaphore_wait(barrier, greetings)
    for j in reversed(range(NEAR, last)):
        if j + PIECES < last:
            arrive(j + PIECES)
        each(j, "start")
    for j in range(NEAR, min(NEAR + PIECES, last)):
        arrive(j)
    for j in range(NEAR, last):
        each(j, "wait_send")
    store = pltpu.make_async_copy(own, mgrad_out, load_sem)
    store.start()
    store.wait()


class Reduce:
    def __init__(self, d, z, parts, dp, local, first_x, buffers, sems):
        self.d, self.z, self.parts, self.dp = d, z, parts, dp
        self.local, self.first_x = local, first_x
        self.r1, self.a1, self.r2, self.a2, self.r3, self.a3, self.rz, self.wide, self.fin = buffers
        self.sems, self.extra_sems, self.plane_sems = sems
        self.c, self.y, self.x = d % 2, d // 4 % 2, d // 2 % 2
        self.spread = Spread(d, self.fin, self.plane_sems)
        self.bits = [8 << i for i in range(dp.bit_length() - 4)]

    def copy(self, p):
        if p == 0:
            src, dst, bit = self.local.at[1 - self.c], self.r1, 1
        elif p == 1:
            if self.first_x:
                src, dst, bit = self.a1.at[:, 1 - self.x], self.r2, 2
            else:
                src, dst, bit = self.a1.at[1 - self.y], self.r2, 4
        elif self.first_x:
            src, dst, bit = self.a2.at[1 - self.y], self.r3, 4
        else:
            src, dst, bit = self.a2.at[1 - self.x], self.r3, 2
        return rcopy(src, dst, self.sems.at[0, p], self.sems.at[1, p], dp=flipped(self.d, bit))

    def z_copy(self, step, other):
        sems = self.sems
        return rcopy(
            self.a3.at[other], self.rz.at[self.z], sems.at[0, 2 + step], sems.at[1, 2 + step], mp=other
        )

    def z_arrival(self, step, other):
        sems = self.sems
        return rcopy(
            self.a3.at[other], self.rz.at[other], sems.at[0, 2 + step], sems.at[1, 2 + step], mp=other
        )

    def extra(self, i):
        sems = self.extra_sems
        device = flipped(self.d, self.bits[i])
        return rcopy(self.wide.at[2 * i], self.wide.at[2 * i + 1], sems.at[0, i], sems.at[1, i], dp=device)

    def run(self, p):
        if p == 0:
            self.copy(0).start()
        elif p == 1:
            self.copy(0).wait_recv()
            self.a1[...] = (self.local[self.c].astype(F32) + self.r1[...].astype(F32)).astype(BF16)
            self.copy(1).start()
        elif p == 2:
            self.copy(1).wait_recv()
            mine = self.a1[:, self.x] if self.first_x else self.a1[self.y]
            self.a2[...] = (mine.astype(F32) + self.r2[...].astype(F32)).astype(BF16)
            self.copy(2).start()
        elif p == 3:
            self.copy(2).wait_recv()
            mine = self.a2[self.y] if self.first_x else self.a2[self.x]
            mine = mine.astype(F32) + self.r3[...].astype(F32)
            self.a3[...] = mine.astype(BF16).reshape(self.a3.shape)
            for step in range(1, self.parts):
                self.z_copy(step, (self.z + step) % self.parts).start()
        elif p == 4:
            self.rz[self.z] = self.a3[self.z]
            for step in range(1, self.parts):
                self.z_arrival(step, (self.z - step + self.parts) % self.parts).wait_recv()
            total = self.rz[0].astype(F32)
            for other in range(1, self.parts):
                total = total + self.rz[other].astype(F32)
            for i in range(len(self.bits)):
                self.wide[2 * i] = total
                self.extra(i).start()
                self.extra(i).wait_recv()
                total = total + self.wide[2 * i + 1]
            self.fin[self.c, self.y, self.x] = total.astype(BF16)
            self.spread.send()
        else:
            self.spread.arrived()

    def close(self):
        for p in range(3):
            self.copy(p).wait_send()
        for step in range(1, self.parts):
            self.z_copy(step, (self.z + step) % self.parts).wait_send()
        for i in range(len(self.bits)):
            self.extra(i).wait_send()
        self.spread.close()


class Spread:
    def __init__(self, d, buffer, sems):
        self.d, self.buffer, self.sems = d, buffer, sems

    def neighbour(self, m):
        d = self.d
        for bit in (1, 2, 4):
            if m & bit:
                d = flipped(d, bit)
        return d

    def copy(self, m, own):
        neighbour = self.neighbour(m)
        c, y, x = corner(self.d if own else neighbour)
        block = self.buffer.at[c, y, x]
        return rcopy(block, block, self.sems.at[0, m], self.sems.at[1, m], dp=neighbour)

    def send(self):
        for m in range(1, 8):
            self.copy(m, True).start()

    def arrived(self):
        for m in range(1, 8):
            self.copy(m, False).wait_recv()

    def close(self):
        for m in range(1, 8):
            self.copy(m, True).wait_send()


class Total:
    def __init__(self, d, z, parts, bits, buffer, wide, line, sems, wide_sems, line_sems):
        self.d, self.z, self.parts, self.bits = d, z, parts, bits
        self.wide, self.line = wide, line
        self.wide_sems, self.line_sems = wide_sems, line_sems
        self.buffer = buffer
        self.spread = Spread(d, buffer, sems)

    def extra(self, i):
        sems = self.wide_sems
        device = flipped(self.d, self.bits[i])
        return rcopy(self.wide.at[2 * i], self.wide.at[2 * i + 1], sems.at[0, i], sems.at[1, i], dp=device)

    def z_copy(self, step, source):
        sems, last = self.line_sems, self.wide.at[2 * len(self.bits)]
        if source:
            other = (self.z - step + self.parts) % self.parts
            return rcopy(last, self.line.at[other], sems.at[0, step], sems.at[1, step], mp=other)
        other = (self.z + step) % self.parts
        return rcopy(last, self.line.at[self.z], sems.at[0, step], sems.at[1, step], mp=other)

    def run(self, p):
        if p == 0:
            self.spread.send()
            return
        self.spread.arrived()
        total = self.buffer[0, 0, 0]
        for c, y, x in [(i // 4, i // 2 % 2, i % 2) for i in range(1, 8)]:
            total = total + self.buffer[c, y, x]
        for i in range(len(self.bits)):
            self.wide[2 * i] = total
            self.extra(i).start()
            self.extra(i).wait_recv()
            total = total + self.wide[2 * i + 1]
        self.wide[2 * len(self.bits)] = total
        for step in range(1, self.parts):
            self.z_copy(step, False).start()

    def finish(self, out):
        self.line[self.z] = self.wide[2 * len(self.bits)]
        for step in range(1, self.parts):
            self.z_copy(step, True).wait_recv()
        total = self.line[0]
        for other in range(1, self.parts):
            total = total + self.line[other]
        out[...] = total
        self.spread.close()
        for i in range(len(self.bits)):
            self.extra(i).wait_send()
        for step in range(1, self.parts):
            self.z_copy(step, False).wait_send()


def give_back(
    window,
    tok, frm, x_ref, n1_ref, q_ref, k_ref, v_ref, att_ref, grad_ref, w_ref, small_in, gain,
    mgrad_in, dwc_in, dwi_in, dwo_in,
    input_out, mgrad_out, fself, fcross, finner, fouter, small_out,
    own, up_land, down_land, local_self, local_cross, local_inner, local_outer,
    dk_ref, dv_ref, dq_ref, halo_out, halo_land, total_buffer, total_wide, total_line,
    self_bufs, cross_bufs, inner_bufs, outer_bufs,
    load_sems, flow_sems, reduce_sems, extra_sems, plane_sems, halo_sems, total_sems, wide_sems, line_sems,
):
    rows, width = q_ref.shape
    heads = width // HEAD
    parts = total_line.shape[0]
    shard_rows = mgrad_out.shape[0]
    piece = shard_rows // PIECES
    last = parts * PIECES
    z, d = lax.axis_index("mp"), lax.axis_index("dp")
    dp = lax.axis_size("dp")
    bits = [8 << i for i in range(dp.bit_length() - 4)]
    barrier, greetings = greet(z, parts, d, bits, range(1, 8))
    loads = [
        pltpu.make_async_copy(a, b, load_sems.at[i])
        for i, (a, b) in enumerate(
            (
                (dwi_in, local_inner),
                (dwo_in, local_outer),
                (dwc_in, local_cross),
                (mgrad_in, own),
            )
        )
    ]
    for load in loads:
        load.start()
    chains = []
    for i, (local, first_x, bufs, fin) in enumerate(
        (
            (local_inner, False, inner_bufs, finner),
            (local_outer, True, outer_bufs, fouter),
            (local_cross, False, cross_bufs, fcross),
            (local_self, True, self_bufs, fself),
        )
    ):
        sems = (reduce_sems.at[i], extra_sems.at[i], plane_sems.at[i])
        chains.append(Reduce(d, z, parts, dp, local, first_x, (*bufs, fin), sems))
    inner, outer, cross, own_chain = chains

    def rows_of(number):
        return at_rows(number * piece, piece)

    def crosses(j, up):
        if up:
            return (z < parts - 1) & ((z + 1) * PIECES + j < last)
        return (z > 0) & (z * PIECES - 1 - j >= 0)

    def number(j, up):
        return (z + 1) * PIECES + j if up else z * PIECES - 1 - j

    def flow(j, up, summed):
        land = up_land if up else down_land
        kind = 0 if up else 2
        src = land.at[j + PIECES] if summed else mgrad_in.at[rows_of(number(j, up))]
        device = z + 1 if up else z - 1
        return rcopy(src, land.at[j], flow_sems.at[kind, j], flow_sems.at[kind + 1, j], mp=device)

    def comes(j, up):
        if up:
            return (z > 0) & (z * PIECES + j < last)
        return (z < parts - 1) & ((z + 1) * PIECES - 1 - j >= 0)

    def flow_arrival(j, up):
        land = up_land if up else down_land
        kind = 0 if up else 2
        device = z - 1 if up else z + 1
        return rcopy(
            land.at[j], land.at[j], flow_sems.at[kind, j], flow_sems.at[kind + 1, j], mp=device
        )

    def first_flows(pieces):
        for j in pieces:
            for up in (True, False):

                @pl.when(crosses(j, up))
                def _():
                    flow(j, up, False).start()

    def next_flow(j):
        for up in (True, False):
            land = up_land if up else down_land

            @pl.when(crosses(j, up) & comes(j + PIECES, up))
            def _():
                flow_arrival(j + PIECES, up).wait_recv()
                mine = own[rows_of(number(j, up))]
                land[j + PIECES] = (land[j + PIECES].astype(F32) + mine.astype(F32)).astype(BF16)
                flow(j, up, True).start()

            @pl.when(crosses(j, up) & jnp.logical_not(comes(j + PIECES, up)))
            def _():
                flow(j, up, False).start()

    base = z * rows
    place, first_row, _, _ = token_rows(tok, frm, base, rows)

    def weight(i):
        return w_ref[i * width : (i + 1) * width]

    def halo_copy(other):
        return rcopy(halo_out, halo_land, halo_sems.at[0], halo_sems.at[1], mp=other)

    pl.semaphore_wait(barrier, greetings)
    first_flows((5, 4))
    for load, chain in zip(loads[:3], chains[:3]):
        load.wait()
        chain.run(0)
    c, y, x = corner(d)
    small = total_buffer.at[c, y, x]
    small[...] = small_in[...]
    grad = grad_ref[...]
    sent = grad.astype(BF16)
    small[6:7] = column_sums(sent.astype(F32))
    n = local_self.shape[3]

    def keep(i, values):
        for half in range(2):
            s = 2 * i + half
            local_self[s // 4, s // 2 % 2, s % 2] = values[half * n : (half + 1) * n].astype(BF16)

    go = mm(sent, weight(3), 1, 1).astype(BF16)
    dk_ref[...] = jnp.zeros_like(dk_ref)
    dv_ref[...] = jnp.zeros_like(dv_ref)
    count = HALO + BLOCK
    blocks = rows // BLOCK

    def attend_back(b):
        here = slice(b * BLOCK, (b + 1) * BLOCK)
        span = slice(b * BLOCK, b * BLOCK + count)
        queries, grads = head_stack(q_ref[here]), head_stack(go[here])
        mask = window_mask(place, first_row, base, b, count)
        shares = self_probs(queries, k_ref[span], mask, heads)
        dp_ = mm(v_ref[span], grads, 1, 1)
        ds = (shares * (dp_ - jnp.sum(shares * dp_, axis=0, keepdims=True))).astype(BF16)
        dv_ref[span] += mm(shares.astype(BF16), grads)
        dk_ref[span] += mm(ds, queries)
        dq_ref[here] = (head_diagonal(mm(k_ref[span], ds, 0, 0), heads) * 0.125).T.astype(BF16)

    def to_norm(here):
        return mm(dk_ref[here].astype(BF16), weight(1)) + mm(dv_ref[here].astype(BF16), weight(2))

    reaching = HALO // BLOCK
    for b in range(reaching):
        attend_back(b)
    halo_out[...] = to_norm(slice(0, HALO)).astype(BF16)

    @pl.when(z > 0)
    def _():
        halo_copy(z - 1).start()

    first_flows((3, 2))
    for chain in chains[:3]:
        chain.run(1)
    for b in range(reaching, blocks):
        attend_back(b)
    dq = dq_ref[...]
    dk, dv = dk_ref[...].astype(BF16), dv_ref[...].astype(BF16)
    n1 = n1_ref[...]
    keep(0, mm(dq, n1[HALO:], 0, 0))
    keep(1, mm(dk, n1, 0, 0))
    keep(2, mm(dv, n1, 0, 0))
    keep(3, mm(att_ref[...], sent, 0, 0))
    own_chain.run(0)
    small[9:10] = column_sums(dq.astype(F32))
    small[10:11] = column_sums(dv.astype(F32))
    for chain in chains[:3]:
        chain.run(2)
    dn = to_norm(slice(HALO, HALO + rows)) + mm(dq, weight(0))
    xhat, scale = normed(x_ref[...].astype(F32))

    @pl.when(z < parts - 1)
    def _():
        halo_copy(z + 1).wait_recv()

    @pl.when(z == parts - 1)
    def _():
        halo_land[...] = jnp.zeros_like(halo_land)

    dn = jnp.concatenate([dn[: rows - HALO], dn[rows - HALO :] + halo_land[...].astype(F32)], axis=0)
    input_out[...] = grad + norm_back(dn, gain[0:1], xhat, scale)
    small[0:1] = column_sums(dn * xhat)
    small[3:4] = column_sums(dn)
    total = Total(
        d, z, parts, bits, total_buffer, total_wide, total_line, total_sems, wide_sems, line_sems
    )
    total.run(0)
    own_chain.run(1)
    loads[3].wait()
    for chain in chains[:3]:
        chain.run(3)
    total.run(1)
    own_chain.run(2)
    next_flow(1)
    next_flow(0)
    own_chain.run(3)
    for p in range(4, 6):
        for chain in chains:
            chain.run(p)

    @pl.when(z == 0)
    def _():
        up_land[:PIECES] = jnp.zeros((PIECES, piece, width), BF16)

    @pl.when(z == parts - 1)
    def _():
        down_land[:PIECES] = jnp.zeros((PIECES, piece, width), BF16)

    for i in range(PIECES):
        for up in (True, False):
            j = i if up else PIECES - 1 - i

            @pl.when(comes(j, up))
            def _():
                flow_arrival(j, up).wait_recv()

        mine = own[rows_of(z * PIECES + i)].astype(F32)
        sides = up_land[i].astype(F32) + down_land[PIECES - 1 - i].astype(F32)
        mgrad_out[i * piece : (i + 1) * piece] = (mine + sides).astype(BF16)
    total.finish(small_out)
    for chain in chains:
        chain.close()

    @pl.when(z > 0)
    def _():
        halo_copy(z - 1).wait_send()

    for j in range(window):
        for up in (True, False):
            @pl.when(crosses(j, up))
            def _():
                flow(j, up, False).wait_send()


def finals(
    mgrad, input_grad, fself, fcross, finner, fouter, small,
    out_mgrad, out_input, out_gain, out_shift, out_sw, out_sb, out_so, out_soff,
    out_cw, out_cb, out_co, out_coff, out_inner, out_ib, out_outer, out_ooff,
):
    z = lax.axis_index("mp")
    own = out_so.shape[0]
    parts = out_so.shape[1] // own
    out_mgrad[...] = mgrad[...].astype(F32)
    out_input[...] = input_grad[...]
    out_gain[...] = small[0:3]
    out_shift[...] = small[3:6]
    out_soff[...] = small[6:7]
    out_coff[...] = small[7:8]
    out_ooff[...] = small[8:9]

    def chosen(row, size, offset):
        pieces = [small[row : row + 1, offset + o * size : offset + (o + 1) * size] for o in range(parts)]
        result = pieces[0]
        for o in range(1, parts):
            result = jnp.where(z == o, pieces[o], result)
        return result

    for fin, weights, last, biases, first in (
        (fself, out_sw, out_so, out_sb, 9),
        (fcross, out_cw, out_co, out_cb, 11),
    ):
        for i in range(3):
            weights[i] = fin[i // 2, i % 2].reshape(own, -1).astype(F32)
        last[...] = fin[1, 1].reshape(own, -1).astype(F32)
        for i in range(2):
            for half in range(2):
                lanes = slice(half * HALF, (half + 1) * HALF)
                biases[i : i + 1, lanes] = chosen(first + i, HALF, half * parts * HALF)
    out_inner[...] = finner[...].reshape(out_outer.shape).astype(F32).T
    out_outer[...] = fouter[...].reshape(out_outer.shape).astype(F32)
    size = out_ib.shape[1] // SLICES
    for s in range(SLICES):
        out_ib[0:1, s * size : (s + 1) * size] = chosen(16 + s, size, 0)


def call(body, outs, ins, scratch, limit, **params):
    places = {"s": pltpu.SMEM, "v": pltpu.VMEM, "h": pl.ANY}

    def spec(place):
        return pl.BlockSpec(memory_space=places[place])

    def run(*args):
        return pl.pallas_call(
            body,
            out_shape=[jax.ShapeDtypeStruct(shape, kind) for shape, kind, _ in outs],
            in_specs=[spec(place) for place in ins],
            out_specs=[spec(place) for _, _, place in outs],
            scratch_shapes=[pltpu.VMEM(*x) if isinstance(x, tuple) else x for x in scratch],
            compiler_params=pltpu.CompilerParams(vmem_limit_bytes=limit << 20, **params),
        )(*args)

    return run


def shards(
    block_input,
    memory,
    tok_lengths,
    frame_lengths,
    cotangent,
    norm_gain,
    norm_shift,
    self_weights,
    self_biases,
    self_output,
    self_offset,
    cross_weights,
    cross_biases,
    cross_output,
    cross_offset,
    inner_weight,
    inner_bias,
    outer_weight,
    outer_offset,
):
    rows, width = block_input.shape
    parts = lax.axis_size("mp")
    frames = memory.shape[0] * parts
    heads = width // HEAD
    blocks = rows // BLOCK
    own_hidden = inner_weight.shape[1]
    hidden = own_hidden * parts
    own = width // parts
    dma = pltpu.SemaphoreType.DMA
    wide = heads * BLOCK

    n_att, n_ffn = own * 4 // SLICES, own_hidden // SLICES
    n_bits = lax.axis_size("dp").bit_length() - 1
    piece = memory.shape[0] // PIECES
    small_rows = 16 + SLICES
    own_rows = (rows, width)
    halo_rows = (rows + HALO, width)

    def sliced(n):
        return (2, 2, 2, n, width)

    def turned(weights):
        return jnp.swapaxes(weights, 1, 2)

    (
        wself, wcross, inner, outer, inner_row, value_row, far, memory_rows, ck, cv, spare, n1, q, k, v, att, after, cq
    ) = call(
        gather,
        [
            (sliced(parts * n_att), BF16, "h"),
            (sliced(parts * n_att), BF16, "h"),
            (sliced(parts * n_ffn), BF16, "h"),
            (sliced(parts * n_ffn), BF16, "h"),
            ((SLICES, hidden // SLICES), F32, "v"),
            ((1, width), F32, "v"),
            ((1, 1), F32, "v"),
            ((frames, width), BF16, "h"),
            ((frames, width), BF16, "h"),
            ((frames, width), BF16, "h"),
            ((parts * frames, width), BF16, "h"),
            (halo_rows, BF16, "v"),
            (own_rows, BF16, "v"),
            (halo_rows, BF16, "v"),
            (halo_rows, BF16, "v"),
            (own_rows, BF16, "v"),
            (own_rows, F32, "v"),
            (own_rows, BF16, "v"),
        ],
        "ssvhvvvvvvvvvvvv",
        [
            (sliced(parts * n_att), BF16),
            (sliced(parts * n_att), BF16),
            (sliced(parts * n_ffn), BF16),
            (sliced(parts * n_ffn), BF16),
            ((frames, width), BF16),
            ((frames, width), BF16),
            ((frames, width), BF16),
            ((4 * own, width), BF16),
            ((4 * own, width), BF16),
            ((own_hidden, width), BF16),
            ((HALO, width), BF16),
            ((8, own_hidden), F32),
            ((parts, 8, own_hidden), F32),
            ((n_bits + 1, 8, 128), F32),
            ((n_bits, 8, 128), F32),
            dma((4, 2, parts)),
            dma((4, NEAR)),
            dma((4, 2, 3)),
            dma((2, parts)),
            dma((2,)),
            dma((2, n_bits)),
            dma,
            dma((parts * PIECES, 3)),
            dma((4,)),
        ],
        56,
        collective_id=0,
        has_side_effects=True,
    )(
        tok_lengths, frame_lengths, block_input, memory, turned(self_weights), self_output,
        turned(cross_weights), cross_output, inner_weight, outer_weight, self_biases, cross_biases,
        inner_bias.reshape(1, own_hidden), norm_gain, norm_shift, self_offset.reshape(1, width),
    )
    wcross_rows = wcross.reshape(4 * width, width)
    wself_rows = wself.reshape(4 * width, width)
    inner_rows, outer_rows = inner.reshape(hidden, width), outer.reshape(hidden, width)

    def reduce_buffers(n):
        full = parts * n
        return [
            pltpu.VMEM((2, 2, full, width), BF16),
            pltpu.VMEM((2, 2, full, width), BF16),
            pltpu.VMEM((2, full, width), BF16),
            pltpu.VMEM((2, full, width), BF16),
            pltpu.VMEM((full, width), BF16),
            pltpu.VMEM((parts, n, width), BF16),
            pltpu.VMEM((parts, n, width), BF16),
            pltpu.VMEM((2 * max(n_bits - 3, 1), n, width), F32),
        ]

    window = PIECES * (parts - 1)
    far_shape = (2, window - NEAR, piece, width)
    beyond = far[0, 0] > NEAR * piece

    def fetch_far():
        (far_memory,) = call(
            gather_far,
            [((parts * frames, width), BF16, "h")],
            "h",
            [dma((4, window))],
            8,
            collective_id=2,
            has_side_effects=True,
        )(memory_rows)
        return far_memory

    far_memory = lax.cond(beyond, fetch_far, lambda: spare)
    padded = (frames + TILE, width)
    block_output, grad, small, mgrad, dw_cross, dwi, dwo = call(
        middle,
        [
            (own_rows, F32, "v"),
            (own_rows, F32, "v"),
            ((small_rows, width), F32, "v"),
            ((frames, width), BF16, "h"),
            ((4 * width, width), BF16, "h"),
            ((hidden, width), BF16, "h"),
            ((hidden, width), BF16, "h"),
        ],
        "sssvvvvvvvvvvhhhhhh",
        [
            (padded, BF16),
            (padded, BF16),
            (padded, BF16),
            ((hidden, width), BF16),
            ((hidden, width), BF16),
            (padded, BF16),
            ((2, width, width), F32),
            ((4 * width, width), BF16),
            ((hidden, width), BF16),
            ((hidden, width), BF16),
            ((blocks, wide, width), BF16),
            ((blocks, wide, width), BF16),
            ((blocks, 1, wide), F32),
            ((blocks, 1, wide), F32),
            ((blocks, width, BLOCK), F32),
            ((blocks, width, BLOCK), F32),
            (padded, F32),
            (padded, F32),
            ((blocks, 1, BLOCK), jnp.int32),
            ((blocks, 1, BLOCK), jnp.int32),
            pltpu.SMEM((2, blocks), jnp.int32),
            dma((3,)),
            dma((4,)),
            dma((3, 1 + 2 * NEAR)),
        ],
        56,
    )(
        far, tok_lengths, frame_lengths, cq, after, cotangent, wcross_rows, inner_row, value_row, norm_gain,
        norm_shift, cross_offset.reshape(1, width), outer_offset.reshape(1, width),
        ck, cv, memory_rows, far_memory, inner_rows, outer_rows,
    )

    def return_far():
        (summed,) = call(
            sum_far,
            [((frames, width), BF16, "h")],
            "h",
            [((frames, width), BF16), (far_shape, BF16), dma((4, window - NEAR)), dma],
            16,
            collective_id=3,
            has_side_effects=True,
        )(mgrad)
        return summed

    mgrad = lax.cond(beyond, return_far, lambda: mgrad)
    partial_results = call(
        functools.partial(give_back, NEAR),
        [
            (own_rows, F32, "v"),
            ((frames // parts, width), BF16, "v"),
            (sliced(n_att), BF16, "v"),
            (sliced(n_att), BF16, "v"),
            (sliced(n_ffn), BF16, "v"),
            (sliced(n_ffn), BF16, "v"),
            ((small_rows, width), F32, "v"),
        ],
        "ssvvvvvvvvvvhhhh",
        [
            ((frames, width), BF16),
            ((NEAR, piece, width), BF16),
            ((NEAR, piece, width), BF16),
            (sliced(parts * n_att), BF16),
            (sliced(parts * n_att), BF16),
            (sliced(parts * n_ffn), BF16),
            (sliced(parts * n_ffn), BF16),
            (halo_rows, F32),
            (halo_rows, F32),
            (own_rows, BF16),
            ((HALO, width), BF16),
            ((HALO, width), BF16),
            ((2, 2, 2, small_rows, width), F32),
            ((2 * (n_bits - 3) + 1, small_rows, width), F32),
            ((parts, small_rows, width), F32),
            reduce_buffers(n_att),
            reduce_buffers(n_att),
            reduce_buffers(n_ffn),
            reduce_buffers(n_ffn),
            dma((4,)),
            dma((4, NEAR)),
            dma((4, 2, 2 + parts)),
            dma((4, 2, max(n_bits - 3, 1))),
            dma((4, 2, 8)),
            dma((2,)),
            dma((2, 8)),
            dma((2, max(n_bits - 3, 1))),
            dma((2, parts)),
        ],
        56,
        collective_id=1,
        has_side_effects=True,
    )(
        tok_lengths, frame_lengths, block_input, n1, q, k, v, att, grad, wself_rows, small, norm_gain,
        mgrad, dw_cross.reshape(sliced(parts * n_att)), dwi.reshape(sliced(parts * n_ffn)),
        dwo.reshape(sliced(parts * n_ffn)),
    )
    input_grad, mgrad_sum, fself, fcross, finner, fouter, small = partial_results
    results = call(
        finals,
        [
            ((frames // parts, width), F32, "v"),
            (own_rows, F32, "v"),
            ((3, width), F32, "v"),
            ((3, width), F32, "v"),
            ((3, own, width), F32, "v"),
            ((2, own), F32, "v"),
            ((own, width), F32, "v"),
            ((1, width), F32, "v"),
            ((3, own, width), F32, "v"),
            ((2, own), F32, "v"),
            ((own, width), F32, "v"),
            ((1, width), F32, "v"),
            ((width, own_hidden), F32, "v"),
            ((1, own_hidden), F32, "v"),
            ((own_hidden, width), F32, "v"),
            ((1, width), F32, "v"),
        ],
        "vvvvvvv",
        [],
        56,
    )(mgrad_sum, input_grad, fself, fcross, finner, fouter, small)
    memory_grad, input_grad, *others = results
    others = [r.reshape(-1) if r.shape[0] == 1 else r for r in others]
    others[2], others[6] = turned(others[2]), turned(others[6])
    return (block_output, input_grad, memory_grad, *others)


def solution(mesh):
    in_specs = (
        P(("dp", "mp"), None),
        P(("dp", "mp"), None),
        P("dp", None),
        P("dp", None),
        P(("dp", "mp"), None),
        P(),
        P(),
        P(None, None, "mp"),
        P(None, "mp"),
        P("mp", None),
        P(),
        P(None, None, "mp"),
        P(None, "mp"),
        P("mp", None),
        P(),
        P(None, "mp"),
        P("mp"),
        P("mp", None),
        P(),
    )
    out_specs = (
        P(("dp", "mp"), None),
        P(("dp", "mp"), None),
        P(("dp", "mp"), None),
        P(),
        P(),
        P(None, None, "mp"),
        P(None, "mp"),
        P("mp", None),
        P(),
        P(None, None, "mp"),
        P(None, "mp"),
        P("mp", None),
        P(),
        P(None, "mp"),
        P("mp"),
        P("mp", None),
        P(),
    )
    return jax.shard_map(shards, mesh=mesh, in_specs=in_specs, out_specs=out_specs, check_vma=False)
```

```python
import functools
import math

import jax
import jax.numpy as jnp
from jax import lax
from jax.experimental import pallas as pl
from jax.experimental.pallas import tpu as pltpu
from jax.sharding import PartitionSpec as P

HEAD = 64
NEGATIVE = -1e30
EPSILON = 1e-05
BLOCK = 128
TILE = 512
UNIT = 128
HALO = 256
F32 = jnp.float32
BF16 = jnp.bfloat16
MESH = pl.DeviceIdType.MESH
HALF = HEAD // 2
SLICES = 8
PIECES = 4
NEAR = 6
GELU_A = math.sqrt(2.0 / math.pi)
GELU_B = 0.044715


def mm(a, b, ca=1, cb=0):
    return lax.dot_general(a, b, (((ca,), (cb,)), ((), ())), preferred_element_type=F32)


def normed(values):
    center = values - jnp.mean(values, axis=-1, keepdims=True)
    spread = jnp.mean(center * center, axis=-1, keepdims=True)
    scale = lax.rsqrt(spread + EPSILON)
    return center * scale, scale


def norm_back(grad, gain, xhat, scale):
    gn = grad * gain
    first = jnp.mean(gn, axis=-1, keepdims=True)
    second = jnp.mean(gn * xhat, axis=-1, keepdims=True)
    return (gn - first - xhat * second) * scale


def column_sums(values):
    return jnp.sum(values, axis=0, keepdims=True)


def head_stack(values):
    rows, width = values.shape
    heads = width // HEAD
    lane = lax.broadcasted_iota(jnp.int32, (rows, width), 1) // HALF % heads
    zero = jnp.zeros_like(values)
    return jnp.concatenate([jnp.where(lane == h, values, zero) for h in range(heads)], axis=0)


def head_rows(heads):
    return [
        (slice((i * heads + h) * HALF, (i * heads + h + 1) * HALF), h)
        for i in range(2)
        for h in range(heads)
    ]


def head_diagonal(values, heads):
    rows = values.shape[1] // heads
    return jnp.concatenate(
        [values[r, h * rows : (h + 1) * rows] for r, h in head_rows(heads)], axis=0
    )


def token_rows(tok_ref, frm_ref, base, count):
    place = lax.broadcasted_iota(jnp.int32, (1, count), 1) + base
    zero = jnp.zeros((1, count), jnp.int32)

    def step(u, carry):
        start, first_row, first_frame, end_frame = carry
        tokens, frames = tok_ref[0, u], frm_ref[0, u]
        end = start + tokens
        done = place >= end
        first_row = first_row + jnp.where(done, tokens, 0)
        first_frame = first_frame + jnp.where(done, frames, 0)
        end_frame = end_frame + jnp.where(place >= start, frames, 0)
        return end, first_row, first_frame, end_frame

    _, first_row, first_frame, end_frame = lax.fori_loop(
        0, tok_ref.shape[1], step, (jnp.int32(0), zero, zero, zero)
    )
    return place, first_row, first_frame, end_frame


def excursion(tok_ref, frm_ref, rows, frames, parts):
    lane = lax.broadcasted_iota(jnp.int32, (1, 128), 1)
    zero = jnp.zeros((1, 128), jnp.int32)

    def step(u, carry):
        start, low, high = carry
        tokens, count = tok_ref[0, u], frm_ref[0, u]
        end = start + tokens
        low = low + jnp.where(lane * rows >= end, count, 0)
        high = high + jnp.where((lane + 1) * rows - 1 >= start, count, 0)
        return end, low, high

    _, low, high = lax.fori_loop(0, tok_ref.shape[1], step, (jnp.int32(0), zero, zero))
    beyond = jnp.maximum(high - (lane + 1) * frames, lane * frames - low)
    return jnp.max(jnp.where(lane < parts, beyond, 0), axis=1, keepdims=True).astype(F32)


def block_frames(tok_ref, frm_ref, base, count):
    blocks = count // BLOCK

    def step(u, carry):
        start, low, high = carry
        tokens, frames = tok_ref[0, u], frm_ref[0, u]
        end = start + tokens
        low = tuple(
            v + jnp.where(base + b * BLOCK >= end, frames, 0) for b, v in enumerate(low)
        )
        high = tuple(
            v + jnp.where(base + (b + 1) * BLOCK - 1 >= start, frames, 0) for b, v in enumerate(high)
        )
        return end, low, high

    zeros = (jnp.int32(0),) * blocks
    _, low, high = lax.fori_loop(0, tok_ref.shape[1], step, (jnp.int32(0), zeros, zeros))
    return low, high


def window_mask(place, first_row, base, block, count):
    keys = lax.broadcasted_iota(jnp.int32, (count, BLOCK), 0) + (base - HALO + block * BLOCK)
    here = slice(block * BLOCK, (block + 1) * BLOCK)
    return (keys >= first_row[:, here]) & (keys <= place[:, here])


def self_probs(queries, key_window, mask, heads):
    scores = mm(key_window, queries, 1, 1)
    parts = []
    for h in range(heads):
        part = jnp.where(mask, scores[:, h * BLOCK : (h + 1) * BLOCK], NEGATIVE)
        raised = jnp.exp(part - jnp.max(part, axis=0, keepdims=True))
        parts.append(raised * (1.0 / jnp.sum(raised, axis=0, keepdims=True)))
    return jnp.concatenate(parts, axis=1)


def rcopy(src, dst, send, recv, **device):
    return pltpu.make_async_remote_copy(
        src_ref=src, dst_ref=dst, send_sem=send, recv_sem=recv, device_id=device, device_id_type=MESH
    )


def at_rows(start, count):
    return pl.ds(pl.multiple_of(start, 16), count)


def flipped(index, bit):
    return index + bit - 2 * bit * (index // bit % 2)


def greet(z, parts, d, bits, masks=()):
    barrier = pltpu.get_barrier_semaphore()
    for mask in masks:
        device = {"dp": masked(d, mask)}
        pl.semaphore_signal(barrier, inc=1, device_id=device, device_id_type=MESH)
    for step in range(1, parts):
        device = {"mp": (z + step) % parts}
        pl.semaphore_signal(barrier, inc=1, device_id=device, device_id_type=MESH)
    for bit in bits:
        device = {"dp": flipped(d, bit)}
        pl.semaphore_signal(barrier, inc=1, device_id=device, device_id_type=MESH)
    return barrier, parts - 1 + len(bits) + len(masks)


class Direct:
    def __init__(self, z, parts, own, place, sems):
        self.z, self.parts, self.own, self.place, self.sems = z, parts, own, place, sems

    def copy(self, step):
        device = (self.z + step) % self.parts
        sems = self.sems
        return rcopy(self.own, self.place(self.z), sems.at[0, step], sems.at[1, step], mp=device)

    def send(self):
        for step in range(1, self.parts):
            self.copy(step).start()

    def arrived(self):
        for step in range(1, self.parts):
            other = (self.z - step + self.parts) % self.parts
            place, sems = self.place(other), self.sems
            rcopy(place, place, sems.at[0, step], sems.at[1, step], mp=other).wait_recv()

    def close(self):
        for step in range(1, self.parts):
            self.copy(step).wait_send()


DP_BITS = (2, 4, 1)


def corner(d):
    return d % 2, d // 4 % 2, d // 2 % 2


class Plane:
    def __init__(self, d, buffer, first_y, sems):
        self.d, self.buffer, self.first_y, self.sems = d, buffer, first_y, sems

    def block(self, p, c, y, x):
        if p == 0:
            return self.buffer.at[c, y, x]
        if p == 2:
            return self.buffer.at[c]
        return self.buffer.at[c, :, x] if self.first_y else self.buffer.at[c, y]

    def copy(self, p, other):
        c, y, x = corner(self.d)
        over_y = p == (0 if self.first_y else 1)
        if other:
            if p == 2:
                c = 1 - c
            elif over_y:
                y = 1 - y
            else:
                x = 1 - x
        block = self.block(p, c, y, x)
        device = flipped(self.d, 1 if p == 2 else 4 if over_y else 2)
        return rcopy(block, block, self.sems.at[0, p], self.sems.at[1, p], dp=device)

    def send(self, p):
        self.copy(p, False).start()

    def arrived(self, p):
        self.copy(p, True).wait_recv()

    def close(self):
        for p in range(3):
            self.copy(p, False).wait_send()


class Window:
    def __init__(self, z, parts, source, place, sems):
        self.z, self.parts, self.source, self.place, self.sems = z, parts, source, place, sems

    def number(self, z, j, up):
        return (z + 1) * PIECES - 1 - j if up else z * PIECES + j

    def there(self, number):
        return (number >= 0) & (number < self.parts * PIECES)

    def copy(self, j, up):
        number = self.number(self.z, j, up)
        place, kind = self.place(number, j, up), 0 if up else 2
        return rcopy(
            self.source(number, j, up),
            place,
            self.sems.at[kind, j],
            self.sems.at[kind + 1, j],
            mp=self.z + 1 if up else self.z - 1,
        )

    def sends(self, j, up):
        edge = self.z < self.parts - 1 if up else self.z > 0
        return edge & self.there(self.number(self.z, j, up))

    def send(self, j):
        for up in (True, False):

            @pl.when(self.sends(j, up))
            def _():
                self.copy(j, up).start()

    def comes(self, j, up):
        edge = self.z > 0 if up else self.z < self.parts - 1
        return edge & self.there(self.arrival(j, up))

    def arrival(self, j, up):
        return self.number(self.z - 1 if up else self.z + 1, j, up)

    def arrived(self, j):
        for up in (True, False):

            @pl.when(self.comes(j, up))
            def _():
                number = self.arrival(j, up)
                place, kind = self.place(number, j, up), 0 if up else 2
                rcopy(
                    place,
                    place,
                    self.sems.at[kind, j],
                    self.sems.at[kind + 1, j],
                    mp=self.z - 1 if up else self.z + 1,
                ).wait_recv()

    def each(self, j, use):
        for up in (True, False):

            @pl.when(self.comes(j, up))
            def _():
                use(self.arrival(j, up), j, up)

    def close(self, pieces):
        for j in pieces:
            for up in (True, False):

                @pl.when(self.sends(j, up))
                def _():
                    self.copy(j, up).wait_send()


def gather(
    tok, frm, x_ref, mem, sw, so, cw, co, inner, outer, sb, cb, ib, gain, shift, offset,
    wself_out, wcross_out, inner_out, outer_out, ib_out, vb_out, far_out, mem_out, ck_out, cv_out, spare,
    n1_ref, q_ref, k_ref, v_ref, att_ref, after_ref, cq_ref,
    gself, gcross, ginner, gouter, gmem, sck, scv, pself, pcross, pinner, halo, pbias, gbias,
    far, far_land, line_sems, mem_sems, plane_sems, bias_sems, halo_sems, far_sems, own_sem, out_sems, weight_sems,
):
    rows, width = x_ref.shape
    heads = width // HEAD
    own = sw.shape[1]
    parts = width // own
    shard_rows = mem.shape[0]
    piece = shard_rows // PIECES
    z, d = lax.axis_index("mp"), lax.axis_index("dp")
    dp = lax.axis_size("dp")
    bits = [1 << i for i in range(dp.bit_length() - 1)]
    c, y, x = corner(d)
    s = c * 4 + y * 2 + x
    barrier, greetings = greet(z, parts, d, bits)

    for source, last, packed in ((sw, so, pself), (cw, co, pcross)):
        for i in range(3):
            packed[i * own : (i + 1) * own] = source[i]
        packed[3 * own :] = last[...]
    pbias[...] = jnp.zeros_like(pbias)
    pbias[0:1] = ib[...]
    for i in range(2):
        pbias[1:2, i * own : (i + 1) * own] = sb[i : i + 1]
        pbias[1:2, (2 + i) * own : (3 + i) * own] = cb[i : i + 1]
    pinner[...] = inner[...].T
    groups = []
    for i, (packed, buffer) in enumerate(
        ((pself, gself), (pcross, gcross), (pinner, ginner), (outer, gouter))
    ):
        n = packed.shape[0] // SLICES
        mine = packed.at[at_rows(s * n, n)]

        def place(shard, buffer=buffer, n=n):
            return buffer.at[c, y, x, at_rows(shard * n, n)]

        line = Direct(z, parts, mine, place, line_sems.at[i])
        plane = Plane(d, buffer, i % 2 == 1, plane_sems.at[i])
        groups.append((line, plane))
        buffer[c, y, x, at_rows(z * n, n)] = packed[at_rows(s * n, n)]

    def piece_place(number, j, up):
        return gmem.at[at_rows(number * piece, piece)]

    def piece_source(number, j, up):
        if j < PIECES:
            return mem.at[at_rows((number - z * PIECES) * piece, piece)]
        return piece_place(number, j, up)

    memory = Window(z, parts, piece_source, piece_place, mem_sems)

    def bias_copy(step):
        return rcopy(
            pbias, gbias.at[z], bias_sems.at[0, step], bias_sems.at[1, step], mp=(z + step) % parts
        )

    def bias_arrival(step):
        other = (z - step + parts) % parts
        return rcopy(pbias, gbias.at[other], bias_sems.at[0, step], bias_sems.at[1, step], mp=other)

    def halo_copy(other):
        return rcopy(x_ref.at[rows - HALO :], halo, halo_sems.at[0], halo_sems.at[1], mp=other)

    def far_copy(i):
        device = flipped(d, bits[i])
        return rcopy(far.at[i], far_land.at[i], far_sems.at[0, i], far_sems.at[1, i], dp=device)

    def far_step(i):
        if i > 0:
            far_copy(i - 1).wait_recv()
            far[i] = jnp.maximum(far[i - 1], far_land[i - 1])
        if i < len(bits):
            far_copy(i).start()
        else:
            far_out[...] = far[i, 0:1, 0:1]

    def forward(j):
        memory.arrived(j - PIECES)
        memory.send(j)

    far[0] = jnp.broadcast_to(excursion(tok, frm, rows, shard_rows, parts), far.shape[1:])
    pl.semaphore_wait(barrier, greetings)
    for line, _ in groups[:2]:
        line.send()
    for step in range(1, parts):
        bias_copy(step).start()

    @pl.when(z < parts - 1)
    def _():
        halo_copy(z + 1).start()

    for line, _ in groups[2:]:
        line.send()
    for j in range(PIECES):
        memory.send(j)
    far_step(0)
    own_rows = gmem.at[at_rows(z * shard_rows, shard_rows)]
    own_copy = pltpu.make_async_copy(mem, own_rows, own_sem)
    own_copy.start()
    gbias[z] = pbias[...]
    for line, plane in groups[:2]:
        line.arrived()
        plane.send(0)
    for _, plane in groups[:2]:
        plane.arrived(0)
        plane.send(1)
    for line, plane in groups[2:]:
        line.arrived()
        plane.send(0)
    far_step(1)
    for _, plane in groups[:2]:
        plane.arrived(1)
        plane.send(2)
    far_step(2)
    groups[0][1].arrived(2)

    for step in range(1, parts):
        bias_arrival(step).wait_recv()

    def head_bias(i):
        return jnp.concatenate(
            [
                gbias[o, 1:2, i * own + half * HALF : i * own + (half + 1) * HALF]
                for half in range(2)
                for o in range(parts)
            ],
            axis=1,
        )

    n = ginner.shape[3] // parts
    for i in range(SLICES):
        ib_out[i : i + 1] = jnp.concatenate(
            [gbias[o, 0:1, i * n : (i + 1) * n] for o in range(parts)], axis=1
        )

    @pl.when(z > 0)
    def _():
        halo_copy(z - 1).wait_recv()

    @pl.when(z == 0)
    def _():
        halo[...] = jnp.zeros_like(halo)

    def weight(buffer, i):
        return buffer[i // 2, i % 2].reshape(width, width)

    base = z * rows
    place_row, first_row, _, _ = token_rows(tok, frm, base, rows)
    for src, dst in ((halo, slice(0, HALO)), (x_ref, slice(HALO, HALO + rows))):
        xhat, _ = normed(src[...].astype(F32))
        n1_ref[dst] = (xhat * gain[0:1] + shift[0:1]).astype(BF16)
    n1 = n1_ref[...]
    query = mm(n1[HALO:], weight(gself, 0), 1, 1) + head_bias(0)
    q_ref[...] = query.astype(BF16) * jnp.asarray(0.125, BF16)
    k_ref[...] = mm(n1, weight(gself, 1), 1, 1).astype(BF16)
    v_ref[...] = (mm(n1, weight(gself, 2), 1, 1) + head_bias(1)).astype(BF16)
    count = HALO + BLOCK
    for b in range(rows // BLOCK):
        queries = head_stack(q_ref[b * BLOCK : (b + 1) * BLOCK])
        window = slice(b * BLOCK, b * BLOCK + count)
        mask = window_mask(place_row, first_row, base, b, count)
        probs = self_probs(queries, k_ref[window], mask, heads).astype(BF16)
        out = head_diagonal(mm(v_ref[window], probs, 0, 0), heads)
        att_ref[b * BLOCK : (b + 1) * BLOCK] = out.T.astype(BF16)
        if b == 0:
            for _, plane in groups[2:]:
                plane.arrived(0)
                plane.send(1)
    forward(PIECES)
    after = x_ref[...].astype(F32) + mm(att_ref[...], weight(gself, 3)) + offset[...]
    after_ref[...] = after
    xhat, _ = normed(after)
    groups[1][1].arrived(2)
    n2 = (xhat * gain[1:2] + shift[1:2]).astype(BF16)
    query = mm(n2, weight(gcross, 0), 1, 1) + head_bias(2)
    cq_ref[...] = query.astype(BF16) * jnp.asarray(0.125, BF16)
    value_bias = head_bias(3)
    forward(PIECES + 1)

    def project(start, size):
        here = at_rows(start, size)
        block = gmem[here]
        sck[here] = mm(block, weight(gcross, 1), 1, 1).astype(BF16)
        scv[here] = (mm(block, weight(gcross, 2), 1, 1) + value_bias).astype(BF16)

    def copies_out(number):
        here = at_rows(number * piece, piece)
        return [
            pltpu.make_async_copy(a.at[here], b.at[here], out_sems.at[number, i])
            for i, (a, b) in enumerate(((gmem, mem_out), (sck, ck_out), (scv, cv_out)))
        ]

    def project_piece(number, j=0, up=True):
        project(number * piece, piece)
        for copy in copies_out(number):
            copy.start()

    own_copy.wait()
    lax.fori_loop(0, PIECES, lambda i, _: (project_piece(z * PIECES + i), 0)[1], 0)
    for _, plane in groups[2:]:
        plane.arrived(1)
        plane.send(2)
    for j in range(PIECES):
        if j >= 2:
            memory.arrived(j)
        memory.each(j, project_piece)
    for i in range(3, len(bits) + 1):
        far_step(i)
    for _, plane in groups[2:]:
        plane.arrived(2)
    outs = [
        pltpu.make_async_copy(a, b, weight_sems.at[i])
        for i, (a, b) in enumerate(
            ((gself, wself_out), (gcross, wcross_out), (ginner, inner_out), (gouter, outer_out))
        )
    ]
    for copy in outs:
        copy.start()
    vb_out[...] = value_bias
    for j in range(PIECES, NEAR):
        memory.arrived(j)
        memory.each(j, project_piece)
    for copy in outs:
        copy.wait()

    def finish(number, *_):
        for copy in copies_out(number):
            copy.wait()

    for i in range(PIECES):
        finish(z * PIECES + i)
    for j in range(NEAR):
        memory.each(j, finish)
    for line, plane in groups:
        line.close()
        plane.close()
    memory.close(range(NEAR))
    for i in range(len(bits)):
        far_copy(i).wait_send()
    for step in range(1, parts):
        bias_copy(step).wait_send()

    @pl.when(z < parts - 1)
    def _():
        halo_copy(z + 1).wait_send()


def gather_far(mem, far_mem, sems):
    z, d = lax.axis_index("mp"), lax.axis_index("dp")
    parts = lax.axis_size("mp")
    last = PIECES * (parts - 1)
    piece = mem.shape[0] // parts // PIECES
    barrier, greetings = greet(z, parts, d, ())

    def place(number, j, up):
        return far_mem.at[at_rows(number * piece, piece)]

    def source(number, j, up):
        return (mem if j - PIECES < NEAR else far_mem).at[at_rows(number * piece, piece)]

    memory = Window(z, parts, source, place, sems)
    pl.semaphore_wait(barrier, greetings)
    for j in range(NEAR, last):
        if j - PIECES >= NEAR:
            memory.arrived(j - PIECES)
        memory.send(j)
    for j in range(max(NEAR, last - PIECES), last):
        memory.arrived(j)
    memory.close(range(NEAR, last))


def middle(
    far, tok, frm, cq_ref, ib_ref, vb_ref, gain, shift, cross_offset, outer_offset,
    after_in, cot_in, w_in, ck_in, cv_in, mem_in, far_in, wi_in, wo_in,
    grad_ref, small_ref, block_out, mgrad_out, dw_out, dwi_out, dwo_out,
    after_ref, cot_ref, w_ref, out_ref,
    ck_ref, cv_ref, mem_ref, wi_ref, wo_ref, mgrad_ref, dw_ref, dwb_ref, dwi_ref, dwo_ref,
    qbig, gbig, lse_ref, dot_ref, att_ref, dq_ref, dk_ref, dv_ref, first_ref, end_ref, bounds,
    in_sems, out_sems, unit_sems, far_sems,
):
    rows, width = cq_ref.shape
    heads = width // HEAD
    blocks = rows // BLOCK
    z = lax.axis_index("mp")
    parts = lax.axis_size("mp")
    last = parts * PIECES
    frames = mem_in.shape[0]
    piece = frames // last
    beyond = far[0, 0] > NEAR * piece

    def weight(i):
        return w_ref[i * width : (i + 1) * width]

    def rows_of(number):
        return at_rows(jnp.clip(number, 0, last - 1) * piece, piece)

    def spans(i, unit):
        here = pl.ds(pl.multiple_of(origin + unit * UNIT, UNIT), UNIT)
        source, full = arrays[i]
        return pltpu.make_async_copy(source.at[here], full.at[here], unit_sems.at[i, unit])

    def units(i, name):
        def one(unit, carry):
            getattr(spans(i, unit), name)()
            return carry

        lax.fori_loop(0, unit_count, one, 0)

    arrays = ((ck_in, ck_ref), (cv_in, cv_ref), (mem_in, mem_ref))
    base = z * rows
    _, _, first_frame, end_frame = token_rows(tok, frm, base, rows)
    for b in range(blocks):
        first_ref[b] = first_frame[:, b * BLOCK : (b + 1) * BLOCK]
        end_ref[b] = end_frame[:, b * BLOCK : (b + 1) * BLOCK]
        qbig[b] = head_stack(cq_ref[b * BLOCK : (b + 1) * BLOCK])
    low, high = block_frames(tok, frm, base, rows)
    for b in range(blocks):
        bounds[0, b] = low[b] // UNIT * UNIT
        bounds[1, b] = high[b]
    origin = bounds[0, 0]
    unit_count = (bounds[1, blocks - 1] - origin + UNIT - 1) // UNIT
    count = (unit_count * UNIT + TILE - 1) // TILE
    loads = [
        pltpu.make_async_copy(a, b, in_sems.at[i])
        for i, (a, b) in enumerate(
            ((wi_in, wi_ref), (wo_in, wo_ref), (after_in, after_ref), (cot_in, cot_ref), (w_in, w_ref))
        )
    ]

    @pl.when(jnp.logical_not(beyond))
    def _():
        units(0, "start")
        units(1, "start")

    for load in loads:
        load.start()

    @pl.when(jnp.logical_not(beyond))
    def _():
        units(2, "start")

    @pl.when(beyond)
    def _():
        loads[4].wait()

        def fetch(i, carry):
            number = i
            here = rows_of(number)
            distance = jnp.maximum(z * PIECES - 1 - number, number - (z + 1) * PIECES)

            @pl.when(distance < NEAR)
            def _():
                copies = [
                    pltpu.make_async_copy(a.at[here], b.at[here], far_sems.at[k])
                    for k, (a, b) in enumerate(arrays)
                ]
                for copy in copies:
                    copy.start()
                for copy in copies:
                    copy.wait()

            @pl.when(distance >= NEAR)
            def _():
                copy = pltpu.make_async_copy(far_in.at[here], mem_ref.at[here], far_sems.at[0])
                copy.start()
                copy.wait()
                block = mem_ref[here]
                ck_ref[here] = mm(block, weight(1), 1, 1).astype(BF16)
                cv_ref[here] = (mm(block, weight(2), 1, 1) + vb_ref[...]).astype(BF16)

            return carry

        lax.fori_loop(0, last, fetch, 0)

    tail = pl.ds(pl.multiple_of(origin + unit_count * UNIT, UNIT), TILE)
    for _, full in arrays:
        full[tail] = jnp.zeros((TILE, width), BF16)
    small_ref[...] = jnp.zeros_like(small_ref)
    mgrad_ref[...] = jnp.zeros_like(mgrad_ref)

    def tiles(b):
        return (bounds[1, b] - bounds[0, b] + TILE - 1) // TILE

    def tile_mask(start, b):
        frame = lax.broadcasted_iota(jnp.int32, (TILE, BLOCK), 0) + start
        return (frame >= first_ref[b]) & (frame < end_ref[b])

    def columns(h):
        return slice(h * BLOCK, (h + 1) * BLOCK)

    @pl.when(jnp.logical_not(beyond))
    def _():
        units(0, "wait")
        units(1, "wait")

    def attend(b, carry):
        att_ref[b] = jnp.zeros((width, BLOCK), F32)

        def step(i, carry):
            start = bounds[0, b] + i * TILE
            here = pl.ds(pl.multiple_of(start, 128), TILE)
            scores = mm(ck_ref[here], qbig[b], 1, 1)
            mask = tile_mask(start, b)
            values = cv_ref[here].T
            news = []
            for h in range(heads):
                largest, total = carry[h]
                part = jnp.where(mask, scores[:, columns(h)], NEGATIVE)
                now = jnp.maximum(largest, jnp.max(part, axis=0, keepdims=True))
                fade = jnp.exp(largest - now)
                raised = jnp.exp(part - now)
                news.append((now, total * fade + jnp.sum(raised, axis=0, keepdims=True)))
                pieces = [r for r, o in head_rows(heads) if o == h]
                own = jnp.concatenate([values[r] for r in pieces], axis=0)
                out = mm(own, raised.astype(BF16))
                for i, r in enumerate(pieces):
                    att_ref[b, r] = att_ref[b, r] * fade + out[i * HALF : (i + 1) * HALF]
            return tuple(news)

        start = (jnp.full((1, BLOCK), NEGATIVE, F32), jnp.zeros((1, BLOCK), F32))
        done = lax.fori_loop(0, tiles(b), step, (start,) * heads)
        for h, (largest, total) in enumerate(done):
            lse_ref[b, :, columns(h)] = largest + jnp.log(total)
            share = 1.0 / total
            for r, o in head_rows(heads):
                if o == h:
                    att_ref[b, r] = att_ref[b, r] * share
        return carry

    lax.fori_loop(0, blocks, attend, 0)
    att = jnp.concatenate([att_ref[b].T for b in range(blocks)], axis=0).astype(BF16)
    loads[2].wait()
    loads[3].wait()

    @pl.when(jnp.logical_not(beyond))
    def _():
        loads[4].wait()

    after_self = after_ref[...]
    after_cross = after_self + mm(att, weight(3)) + cross_offset[...]
    xhat3, scale3 = normed(after_cross)
    n3 = (xhat3 * gain[2:3] + shift[2:3]).astype(BF16)
    sent = cot_ref[...]
    small_ref[8:9] = column_sums(sent.astype(F32))
    hidden = wi_ref.shape[0]
    group = 4
    tile = hidden // SLICES * group
    loads[0].wait()
    loads[1].wait()
    out_ref[...] = after_cross + outer_offset[...]
    grad_ref[...] = jnp.zeros((rows, width), F32)

    def feed(f, carry):
        here = pl.ds(pl.multiple_of(f * tile, tile), tile)
        bias = jnp.concatenate([ib_ref[pl.ds(f * group + i, 1)] for i in range(group)], axis=1)
        before = mm(n3, wi_ref[here], 1, 1) + bias
        square = before * before
        inner = jnp.tanh(before * (GELU_A + (GELU_A * GELU_B) * square))
        half = 0.5 + 0.5 * inner
        active = (before * half).astype(BF16)
        slope = half + (0.5 * before) * (1.0 - inner * inner) * (
            GELU_A + (3.0 * GELU_A * GELU_B) * square
        )
        out_ref[...] += mm(active, wo_ref[here])
        back = (slope * mm(sent, wo_ref[here], 1, 1)).astype(BF16)
        grad_ref[...] += mm(back, wi_ref[here])
        dwo_ref[here] = mm(active, sent, 0, 0).astype(BF16)
        dwi_ref[here] = mm(back, n3, 0, 0).astype(BF16)
        sums = column_sums(back.astype(F32))
        for i in range(group):
            small_ref[pl.ds(16 + f * group + i, 1)] = sums[:, i * tile // group : (i + 1) * tile // group]
        return carry

    lax.fori_loop(0, SLICES // group, feed, 0)
    stores = [
        pltpu.make_async_copy(a, b, out_sems.at[i])
        for i, (a, b) in enumerate(
            (
                (dwi_ref, dwi_out),
                (dwo_ref, dwo_out),
                (dwb_ref, dw_out),
                (mgrad_ref.at[:frames], mgrad_out),
                (out_ref, block_out),
            )
        )
    ]
    stores[0].start()
    stores[1].start()
    stores[4].start()
    dn3 = grad_ref[...]
    small_ref[2:3] = column_sums(dn3 * xhat3)
    small_ref[5:6] = column_sums(dn3)
    grad = sent.astype(F32) + norm_back(dn3, gain[2:3], xhat3, scale3)
    sent2 = grad.astype(BF16)
    small_ref[7:8] = column_sums(sent2.astype(F32))
    dwb_ref[3 * width :] = mm(att, sent2, 0, 0).astype(BF16)
    go = mm(sent2, weight(3), 1, 1).astype(BF16)
    got = mm(weight(3), sent2, 1, 1).astype(BF16).astype(F32)
    for b in range(blocks):
        gbig[b] = head_stack(go[b * BLOCK : (b + 1) * BLOCK])
        prod = got[:, b * BLOCK : (b + 1) * BLOCK] * att_ref[b]
        sums = [column_sums(prod[r]) for r, _ in head_rows(heads)]
        for h in range(heads):
            dot_ref[b, :, columns(h)] = sums[h] + sums[heads + h]
    def span(i):
        return pl.ds(pl.multiple_of(origin + i * TILE, 128), TILE)

    def clear(i, carry):
        dk_ref[span(i)] = jnp.zeros((TILE, width), F32)
        dv_ref[span(i)] = jnp.zeros((TILE, width), F32)
        return carry

    lax.fori_loop(0, count, clear, 0)

    def attend_back(b, carry):
        dq_ref[b] = jnp.zeros((width, BLOCK), F32)

        def step(i, carry):
            start = bounds[0, b] + i * TILE
            here = pl.ds(pl.multiple_of(start, 128), TILE)
            keys, values = ck_ref[here], cv_ref[here]
            scores = mm(keys, qbig[b], 1, 1)
            dp = mm(values, gbig[b], 1, 1)
            mask = tile_mask(start, b)
            shares, scaled = [], []
            for h in range(heads):
                part = jnp.exp(scores[:, columns(h)] - lse_ref[b, :, columns(h)])
                part = jnp.where(mask, part, 0.0)
                shares.append(part.astype(BF16))
                scaled.append((part * (dp[:, columns(h)] - dot_ref[b, :, columns(h)])).astype(BF16))
            shares, scaled = jnp.concatenate(shares, axis=1), jnp.concatenate(scaled, axis=1)
            dv_ref[here] += mm(shares, gbig[b])
            dk_ref[here] += mm(scaled, qbig[b])
            dq_ref[b] += head_diagonal(mm(keys, scaled, 0, 0), heads)
            return carry

        return lax.fori_loop(0, tiles(b), step, carry)

    lax.fori_loop(0, blocks, attend_back, 0)

    @pl.when(jnp.logical_not(beyond))
    def _():
        units(2, "wait")

    dw_ref[...] = jnp.zeros_like(dw_ref)

    def frame_step(i, carry):
        here = span(i)
        dk, dv = dk_ref[here].astype(BF16), dv_ref[here].astype(BF16)
        mgrad_ref[here] = (mm(dk, weight(1)) + mm(dv, weight(2))).astype(BF16)
        frame_rows = mem_ref[here]
        dw_ref[0] += mm(dk, frame_rows, 0, 0)
        dw_ref[1] += mm(dv, frame_rows, 0, 0)
        small_ref[12:13] += column_sums(dv.astype(F32))
        return carry

    lax.fori_loop(0, count, frame_step, 0)
    stores[3].start()
    dq = jnp.concatenate([(dq_ref[b] * 0.125).T for b in range(blocks)], axis=0).astype(BF16)
    small_ref[11:12] = column_sums(dq.astype(F32))
    xhat2, scale2 = normed(after_self)
    n2 = (xhat2 * gain[1:2] + shift[1:2]).astype(BF16)
    dwb_ref[:width] = mm(dq, n2, 0, 0).astype(BF16)
    dwb_ref[width : 2 * width] = dw_ref[0].astype(BF16)
    dwb_ref[2 * width : 3 * width] = dw_ref[1].astype(BF16)
    stores[2].start()
    dn2 = mm(dq, weight(0))
    small_ref[1:2] = column_sums(dn2 * xhat2)
    small_ref[4:5] = column_sums(dn2)
    grad_ref[...] = grad + norm_back(dn2, gain[1:2], xhat2, scale2)
    for store in stores:
        store.wait()


def sum_far(mgrad_in, mgrad_out, own, land, flow_sems, load_sem):
    pieces, piece = land.shape[1:3]
    frames = own.shape[0]
    parts = frames // piece // PIECES
    last = NEAR + pieces
    z, d = lax.axis_index("mp"), lax.axis_index("dp")
    barrier, greetings = greet(z, parts, d, ())
    load = pltpu.make_async_copy(mgrad_in, own, load_sem)
    load.start()

    def rows_of(number):
        return at_rows(number * piece, piece)

    def there(number):
        return (number >= 0) & (number < parts * PIECES)

    def sent(j, up):
        return (z + 1) * PIECES + j if up else z * PIECES - 1 - j

    def comes(j, up):
        return z * PIECES + j if up else (z + 1) * PIECES - 1 - j

    def flow(j, up, number, device):
        kind = 0 if up else 2
        place = land.at[0 if up else 1, j - NEAR]
        sems = flow_sems.at[kind, j - NEAR], flow_sems.at[kind + 1, j - NEAR]
        return rcopy(own.at[rows_of(number)], place, *sems, mp=device)

    def arrive(j):
        for up in (True, False):

            @pl.when(there(comes(j, up)) & (z > 0 if up else z < parts - 1))
            def _():
                number = comes(j, up)
                flow(j, up, number, z - 1 if up else z + 1).wait_recv()
                here = rows_of(number)
                more = land[0 if up else 1, j - NEAR].astype(F32)
                own[here] = (own[here].astype(F32) + more).astype(BF16)

    def each(j, name):
        for up in (True, False):

            @pl.when(there(sent(j, up)) & (z < parts - 1 if up else z > 0))
            def _():
                getattr(flow(j, up, sent(j, up), z + 1 if up else z - 1), name)()

    load.wait()
    pl.semaphore_wait(barrier, greetings)
    for j in reversed(range(NEAR, last)):
        if j + PIECES < last:
            arrive(j + PIECES)
        each(j, "start")
    for j in range(NEAR, min(NEAR + PIECES, last)):
        arrive(j)
    for j in range(NEAR, last):
        each(j, "wait_send")
    store = pltpu.make_async_copy(own, mgrad_out, load_sem)
    store.start()
    store.wait()


def masked(d, mask):
    for bit in (1, 2, 4):
        if mask & bit:
            d = flipped(d, bit)
    return d


CHIPS = (2, 4, 6)


class Reduce:
    def __init__(self, d, z, parts, dp, local, buffers, sems):
        self.d, self.z, self.parts, self.dp, self.local = d, z, parts, dp, local
        self.r1, self.a1, self.r2, self.a3, self.rz, self.wide, self.fin = buffers
        self.sems, self.extra_sems, self.plane_sems = sems
        self.c, self.y, self.x = corner(d)
        self.spread = Chips(d, self.fin, self.plane_sems)
        self.bits = [8 << i for i in range(dp.bit_length() - 4)]

    def to_core(self):
        sems = self.sems
        return rcopy(
            self.local.at[1 - self.c], self.r1, sems.at[0, 0], sems.at[1, 0], dp=flipped(self.d, 1)
        )

    def to_chip(self, i):
        sems, other = self.sems, masked(self.d, CHIPS[i])
        _, y, x = corner(other)
        return rcopy(self.a1.at[y, x], self.r2.at[i], sems.at[0, 1 + i], sems.at[1, 1 + i], dp=other)

    def z_copy(self, step, other):
        sems = self.sems
        return rcopy(
            self.a3.at[other], self.rz.at[self.z], sems.at[0, 3 + step], sems.at[1, 3 + step], mp=other
        )

    def z_arrival(self, step, other):
        sems = self.sems
        return rcopy(
            self.a3.at[other], self.rz.at[other], sems.at[0, 3 + step], sems.at[1, 3 + step], mp=other
        )

    def extra(self, i):
        sems = self.extra_sems
        device = flipped(self.d, self.bits[i])
        return rcopy(self.wide.at[2 * i], self.wide.at[2 * i + 1], sems.at[0, i], sems.at[1, i], dp=device)

    def run(self, p):
        if p == 0:
            self.to_core().start()
        elif p == 1:
            self.to_core().wait_recv()
            self.a1[...] = (self.local[self.c].astype(F32) + self.r1[...].astype(F32)).astype(BF16)
            for i in range(3):
                self.to_chip(i).start()
        elif p == 2:
            total = self.a1[self.y, self.x].astype(F32)
            for i in range(3):
                self.to_chip(i).wait_recv()
                total = total + self.r2[i].astype(F32)
            self.a3[...] = total.astype(BF16).reshape(self.a3.shape)
            for step in range(1, self.parts):
                self.z_copy(step, (self.z + step) % self.parts).start()
        elif p == 3:
            self.rz[self.z] = self.a3[self.z]
            for step in range(1, self.parts):
                self.z_arrival(step, (self.z - step + self.parts) % self.parts).wait_recv()
            total = self.rz[0].astype(F32)
            for other in range(1, self.parts):
                total = total + self.rz[other].astype(F32)
            for i in range(len(self.bits)):
                self.wide[2 * i] = total
                self.extra(i).start()
                self.extra(i).wait_recv()
                total = total + self.wide[2 * i + 1]
            self.fin[self.c, self.y, self.x] = total.astype(BF16)
            self.spread.send(0)
        elif p == 4:
            self.spread.arrived(0)
            self.spread.send(1)
        else:
            self.spread.arrived(1)

    def close(self):
        self.to_core().wait_send()
        for i in range(3):
            self.to_chip(i).wait_send()
        for step in range(1, self.parts):
            self.z_copy(step, (self.z + step) % self.parts).wait_send()
        for i in range(len(self.bits)):
            self.extra(i).wait_send()
        self.spread.close()


class Spread:
    def __init__(self, d, buffer, sems):
        self.d, self.buffer, self.sems = d, buffer, sems

    def copy(self, m, own):
        neighbour = masked(self.d, m)
        c, y, x = corner(self.d if own else neighbour)
        block = self.buffer.at[c, y, x]
        return rcopy(block, block, self.sems.at[0, m], self.sems.at[1, m], dp=neighbour)

    def send(self):
        for m in range(1, 8):
            self.copy(m, True).start()

    def arrived(self):
        for m in range(1, 8):
            self.copy(m, False).wait_recv()

    def close(self):
        for m in range(1, 8):
            self.copy(m, True).wait_send()


class Chips:
    def __init__(self, d, buffer, sems):
        self.d, self.buffer, self.sems = d, buffer, sems

    def copy(self, m, own):
        neighbour = masked(self.d, m)
        c, y, x = corner(self.d if own else neighbour)
        block = self.buffer.at[c] if m == 1 else self.buffer.at[c, y, x]
        return rcopy(block, block, self.sems.at[0, m], self.sems.at[1, m], dp=neighbour)

    def send(self, p):
        for m in (CHIPS, (1,))[p]:
            self.copy(m, True).start()

    def arrived(self, p):
        for m in (CHIPS, (1,))[p]:
            self.copy(m, False).wait_recv()

    def close(self):
        for m in (1, 2, 4, 6):
            self.copy(m, True).wait_send()


class Total:
    def __init__(self, d, z, parts, bits, buffer, wide, line, sems, wide_sems, line_sems):
        self.d, self.z, self.parts, self.bits = d, z, parts, bits
        self.wide, self.line = wide, line
        self.wide_sems, self.line_sems = wide_sems, line_sems
        self.buffer = buffer
        self.spread = Spread(d, buffer, sems)

    def extra(self, i):
        sems = self.wide_sems
        device = flipped(self.d, self.bits[i])
        return rcopy(self.wide.at[2 * i], self.wide.at[2 * i + 1], sems.at[0, i], sems.at[1, i], dp=device)

    def z_copy(self, step, source):
        sems, last = self.line_sems, self.wide.at[2 * len(self.bits)]
        if source:
            other = (self.z - step + self.parts) % self.parts
            return rcopy(last, self.line.at[other], sems.at[0, step], sems.at[1, step], mp=other)
        other = (self.z + step) % self.parts
        return rcopy(last, self.line.at[self.z], sems.at[0, step], sems.at[1, step], mp=other)

    def run(self, p):
        if p == 0:
            self.spread.send()
            return
        self.spread.arrived()
        total = self.buffer[0, 0, 0]
        for c, y, x in [(i // 4, i // 2 % 2, i % 2) for i in range(1, 8)]:
            total = total + self.buffer[c, y, x]
        for i in range(len(self.bits)):
            self.wide[2 * i] = total
            self.extra(i).start()
            self.extra(i).wait_recv()
            total = total + self.wide[2 * i + 1]
        self.wide[2 * len(self.bits)] = total
        for step in range(1, self.parts):
            self.z_copy(step, False).start()

    def finish(self, out):
        self.line[self.z] = self.wide[2 * len(self.bits)]
        for step in range(1, self.parts):
            self.z_copy(step, True).wait_recv()
        total = self.line[0]
        for other in range(1, self.parts):
            total = total + self.line[other]
        out[...] = total
        self.spread.close()
        for i in range(len(self.bits)):
            self.extra(i).wait_send()
        for step in range(1, self.parts):
            self.z_copy(step, False).wait_send()


def give_back(
    window,
    tok, frm, small_in, gain,
    x_in, n1_in, q_in, k_in, v_in, att_in, grad_in, w_in, mgrad_in, dwc_in, dwi_in, dwo_in,
    input_out, mgrad_out, fself, fcross, finner, fouter, small_out,
    x_ref, n1_ref, q_ref, k_ref, v_ref, att_ref, grad_ref, w_ref,
    own, up_land, down_land, local_self, local_cross, local_inner, local_outer,
    dk_ref, dv_ref, dq_ref, halo_out, halo_land, total_buffer, total_wide, total_line,
    self_bufs, cross_bufs, inner_bufs, outer_bufs,
    load_sems, flow_sems, reduce_sems, extra_sems, plane_sems, halo_sems, total_sems, wide_sems, line_sems,
):
    rows, width = q_ref.shape
    heads = width // HEAD
    parts = total_line.shape[0]
    shard_rows = mgrad_out.shape[0]
    piece = shard_rows // PIECES
    last = parts * PIECES
    z, d = lax.axis_index("mp"), lax.axis_index("dp")
    dp = lax.axis_size("dp")
    bits = [8 << i for i in range(dp.bit_length() - 4)]
    barrier, greetings = greet(z, parts, d, bits, range(1, 8))
    loads = [
        pltpu.make_async_copy(a, b, load_sems.at[i])
        for i, (a, b) in enumerate(
            (
                (dwi_in, local_inner),
                (dwo_in, local_outer),
                (dwc_in, local_cross),
                (grad_in, grad_ref),
                (w_in, w_ref),
                (q_in, q_ref),
                (k_in, k_ref),
                (v_in, v_ref),
                (n1_in, n1_ref),
                (att_in, att_ref),
                (x_in, x_ref),
                (mgrad_in, own),
            )
        )
    ]
    for load in loads:
        load.start()
    chains = []
    for i, (local, bufs, fin) in enumerate(
        (
            (local_inner, inner_bufs, finner),
            (local_outer, outer_bufs, fouter),
            (local_cross, cross_bufs, fcross),
            (local_self, self_bufs, fself),
        )
    ):
        sems = (reduce_sems.at[i], extra_sems.at[i], plane_sems.at[i])
        chains.append(Reduce(d, z, parts, dp, local, (*bufs, fin), sems))
    inner, outer, cross, own_chain = chains

    def rows_of(number):
        return at_rows(number * piece, piece)

    def crosses(j, up):
        if up:
            return (z < parts - 1) & ((z + 1) * PIECES + j < last)
        return (z > 0) & (z * PIECES - 1 - j >= 0)

    def number(j, up):
        return (z + 1) * PIECES + j if up else z * PIECES - 1 - j

    def flow(j, up, summed):
        land = up_land if up else down_land
        kind = 0 if up else 2
        src = land.at[j + PIECES] if summed else mgrad_in.at[rows_of(number(j, up))]
        device = z + 1 if up else z - 1
        return rcopy(src, land.at[j], flow_sems.at[kind, j], flow_sems.at[kind + 1, j], mp=device)

    def comes(j, up):
        if up:
            return (z > 0) & (z * PIECES + j < last)
        return (z < parts - 1) & ((z + 1) * PIECES - 1 - j >= 0)

    def flow_arrival(j, up):
        land = up_land if up else down_land
        kind = 0 if up else 2
        device = z - 1 if up else z + 1
        return rcopy(
            land.at[j], land.at[j], flow_sems.at[kind, j], flow_sems.at[kind + 1, j], mp=device
        )

    def first_flows(pieces):
        for j in pieces:
            for up in (True, False):

                @pl.when(crosses(j, up))
                def _():
                    flow(j, up, False).start()

    def next_flow(j):
        for up in (True, False):
            land = up_land if up else down_land

            @pl.when(crosses(j, up) & comes(j + PIECES, up))
            def _():
                flow_arrival(j + PIECES, up).wait_recv()
                mine = own[rows_of(number(j, up))]
                land[j + PIECES] = (land[j + PIECES].astype(F32) + mine.astype(F32)).astype(BF16)
                flow(j, up, True).start()

            @pl.when(crosses(j, up) & jnp.logical_not(comes(j + PIECES, up)))
            def _():
                flow(j, up, False).start()

    base = z * rows
    place, first_row, _, _ = token_rows(tok, frm, base, rows)

    def weight(i):
        return w_ref[i * width : (i + 1) * width]

    def halo_copy(other):
        return rcopy(halo_out, halo_land, halo_sems.at[0], halo_sems.at[1], mp=other)

    pl.semaphore_wait(barrier, greetings)
    first_flows((5, 4))
    for load, chain in zip(loads[:3], chains[:3]):
        load.wait()
        chain.run(0)
    c, y, x = corner(d)
    small = total_buffer.at[c, y, x]
    small[...] = small_in[...]
    loads[3].wait()
    loads[4].wait()
    grad = grad_ref[...]
    sent = grad.astype(BF16)
    small[6:7] = column_sums(sent.astype(F32))
    n = local_self.shape[3]

    def keep(i, values):
        for half in range(2):
            s = 2 * i + half
            local_self[s // 4, s // 2 % 2, s % 2] = values[half * n : (half + 1) * n].astype(BF16)

    go = mm(sent, weight(3), 1, 1).astype(BF16)
    dk_ref[...] = jnp.zeros_like(dk_ref)
    dv_ref[...] = jnp.zeros_like(dv_ref)
    count = HALO + BLOCK
    blocks = rows // BLOCK

    def attend_back(b):
        here = slice(b * BLOCK, (b + 1) * BLOCK)
        span = slice(b * BLOCK, b * BLOCK + count)
        queries, grads = head_stack(q_ref[here]), head_stack(go[here])
        mask = window_mask(place, first_row, base, b, count)
        shares = self_probs(queries, k_ref[span], mask, heads)
        dp_ = mm(v_ref[span], grads, 1, 1)
        ds = (shares * (dp_ - jnp.sum(shares * dp_, axis=0, keepdims=True))).astype(BF16)
        dv_ref[span] += mm(shares.astype(BF16), grads)
        dk_ref[span] += mm(ds, queries)
        dq_ref[here] = (head_diagonal(mm(k_ref[span], ds, 0, 0), heads) * 0.125).T.astype(BF16)

    def to_norm(here):
        return mm(dk_ref[here].astype(BF16), weight(1)) + mm(dv_ref[here].astype(BF16), weight(2))

    for chain in chains[:3]:
        chain.run(1)
    for load in loads[5:8]:
        load.wait()
    reaching = HALO // BLOCK
    for b in range(reaching):
        attend_back(b)
    halo_out[...] = to_norm(slice(0, HALO)).astype(BF16)

    @pl.when(z > 0)
    def _():
        halo_copy(z - 1).start()

    first_flows((3, 2))
    for b in range(reaching, blocks):
        attend_back(b)
    dq = dq_ref[...]
    dk, dv = dk_ref[...].astype(BF16), dv_ref[...].astype(BF16)
    for load in loads[8:]:
        load.wait()
    n1 = n1_ref[...]
    keep(0, mm(dq, n1[HALO:], 0, 0))
    keep(1, mm(dk, n1, 0, 0))
    keep(2, mm(dv, n1, 0, 0))
    keep(3, mm(att_ref[...], sent, 0, 0))
    own_chain.run(0)
    small[9:10] = column_sums(dq.astype(F32))
    small[10:11] = column_sums(dv.astype(F32))
    dn = to_norm(slice(HALO, HALO + rows)) + mm(dq, weight(0))
    xhat, scale = normed(x_ref[...].astype(F32))
    own_chain.run(1)

    @pl.when(z < parts - 1)
    def _():
        halo_copy(z + 1).wait_recv()

    @pl.when(z == parts - 1)
    def _():
        halo_land[...] = jnp.zeros_like(halo_land)

    dn = jnp.concatenate([dn[: rows - HALO], dn[rows - HALO :] + halo_land[...].astype(F32)], axis=0)
    small[0:1] = column_sums(dn * xhat)
    small[3:4] = column_sums(dn)
    total = Total(
        d, z, parts, bits, total_buffer, total_wide, total_line, total_sems, wide_sems, line_sems
    )
    total.run(0)
    input_out[...] = grad + norm_back(dn, gain[0:1], xhat, scale)
    for chain in chains[:3]:
        chain.run(2)
    own_chain.run(2)
    total.run(1)
    next_flow(1)
    next_flow(0)
    for p in range(3, 6):
        for chain in chains:
            chain.run(p)

    @pl.when(z == 0)
    def _():
        up_land[:PIECES] = jnp.zeros((PIECES, piece, width), BF16)

    @pl.when(z == parts - 1)
    def _():
        down_land[:PIECES] = jnp.zeros((PIECES, piece, width), BF16)

    for i in range(PIECES):
        for up in (True, False):
            j = i if up else PIECES - 1 - i

            @pl.when(comes(j, up))
            def _():
                flow_arrival(j, up).wait_recv()

        mine = own[rows_of(z * PIECES + i)].astype(F32)
        sides = up_land[i].astype(F32) + down_land[PIECES - 1 - i].astype(F32)
        mgrad_out[i * piece : (i + 1) * piece] = (mine + sides).astype(BF16)
    total.finish(small_out)
    for chain in chains:
        chain.close()

    @pl.when(z > 0)
    def _():
        halo_copy(z - 1).wait_send()

    for j in range(window):
        for up in (True, False):
            @pl.when(crosses(j, up))
            def _():
                flow(j, up, False).wait_send()


def finals(
    mgrad, input_grad, fself, fcross, finner, fouter, small,
    out_mgrad, out_input, out_gain, out_shift, out_sw, out_sb, out_so, out_soff,
    out_cw, out_cb, out_co, out_coff, out_inner, out_ib, out_outer, out_ooff,
):
    z = lax.axis_index("mp")
    own = out_so.shape[0]
    parts = out_so.shape[1] // own
    out_mgrad[...] = mgrad[...].astype(F32)
    out_input[...] = input_grad[...]
    out_gain[...] = small[0:3]
    out_shift[...] = small[3:6]
    out_soff[...] = small[6:7]
    out_coff[...] = small[7:8]
    out_ooff[...] = small[8:9]

    def chosen(row, size, offset):
        pieces = [small[row : row + 1, offset + o * size : offset + (o + 1) * size] for o in range(parts)]
        result = pieces[0]
        for o in range(1, parts):
            result = jnp.where(z == o, pieces[o], result)
        return result

    for fin, weights, last, biases, first in (
        (fself, out_sw, out_so, out_sb, 9),
        (fcross, out_cw, out_co, out_cb, 11),
    ):
        for i in range(3):
            weights[i] = fin[i // 2, i % 2].reshape(own, -1).astype(F32)
        last[...] = fin[1, 1].reshape(own, -1).astype(F32)
        for i in range(2):
            for half in range(2):
                lanes = slice(half * HALF, (half + 1) * HALF)
                biases[i : i + 1, lanes] = chosen(first + i, HALF, half * parts * HALF)
    out_inner[...] = finner[...].reshape(out_outer.shape).astype(F32).T
    out_outer[...] = fouter[...].reshape(out_outer.shape).astype(F32)
    size = out_ib.shape[1] // SLICES
    for s in range(SLICES):
        out_ib[0:1, s * size : (s + 1) * size] = chosen(16 + s, size, 0)


def call(body, outs, ins, scratch, limit, **params):
    places = {"s": pltpu.SMEM, "v": pltpu.VMEM, "h": pl.ANY}

    def spec(place):
        return pl.BlockSpec(memory_space=places[place])

    def run(*args):
        return pl.pallas_call(
            body,
            out_shape=[jax.ShapeDtypeStruct(shape, kind) for shape, kind, _ in outs],
            in_specs=[spec(place) for place in ins],
            out_specs=[spec(place) for _, _, place in outs],
            scratch_shapes=[pltpu.VMEM(*x) if isinstance(x, tuple) else x for x in scratch],
            compiler_params=pltpu.CompilerParams(vmem_limit_bytes=limit << 20, **params),
        )(*args)

    return run


def shards(
    block_input,
    memory,
    tok_lengths,
    frame_lengths,
    cotangent,
    norm_gain,
    norm_shift,
    self_weights,
    self_biases,
    self_output,
    self_offset,
    cross_weights,
    cross_biases,
    cross_output,
    cross_offset,
    inner_weight,
    inner_bias,
    outer_weight,
    outer_offset,
):
    rows, width = block_input.shape
    parts = lax.axis_size("mp")
    frames = memory.shape[0] * parts
    heads = width // HEAD
    blocks = rows // BLOCK
    own_hidden = inner_weight.shape[1]
    hidden = own_hidden * parts
    own = width // parts
    dma = pltpu.SemaphoreType.DMA
    wide = heads * BLOCK

    n_att, n_ffn = own * 4 // SLICES, own_hidden // SLICES
    n_bits = lax.axis_size("dp").bit_length() - 1
    piece = memory.shape[0] // PIECES
    small_rows = 16 + SLICES
    own_rows = (rows, width)
    halo_rows = (rows + HALO, width)

    def sliced(n):
        return (2, 2, 2, n, width)

    def turned(weights):
        return jnp.swapaxes(weights, 1, 2)

    (
        wself, wcross, inner, outer, inner_row, value_row, far, memory_rows, ck, cv, spare, n1, q, k, v, att, after, cq
    ) = call(
        gather,
        [
            (sliced(parts * n_att), BF16, "h"),
            (sliced(parts * n_att), BF16, "h"),
            (sliced(parts * n_ffn), BF16, "h"),
            (sliced(parts * n_ffn), BF16, "h"),
            ((SLICES, hidden // SLICES), F32, "v"),
            ((1, width), F32, "v"),
            ((1, 1), F32, "v"),
            ((frames, width), BF16, "h"),
            ((frames, width), BF16, "h"),
            ((frames, width), BF16, "h"),
            ((parts * frames, width), BF16, "h"),
            (halo_rows, BF16, "v"),
            (own_rows, BF16, "v"),
            (halo_rows, BF16, "v"),
            (halo_rows, BF16, "v"),
            (own_rows, BF16, "v"),
            (own_rows, F32, "v"),
            (own_rows, BF16, "v"),
        ],
        "ssvhvvvvvvvvvvvv",
        [
            (sliced(parts * n_att), BF16),
            (sliced(parts * n_att), BF16),
            (sliced(parts * n_ffn), BF16),
            (sliced(parts * n_ffn), BF16),
            ((frames, width), BF16),
            ((frames, width), BF16),
            ((frames, width), BF16),
            ((4 * own, width), BF16),
            ((4 * own, width), BF16),
            ((own_hidden, width), BF16),
            ((HALO, width), BF16),
            ((8, own_hidden), F32),
            ((parts, 8, own_hidden), F32),
            ((n_bits + 1, 8, 128), F32),
            ((n_bits, 8, 128), F32),
            dma((4, 2, parts)),
            dma((4, NEAR)),
            dma((4, 2, 3)),
            dma((2, parts)),
            dma((2,)),
            dma((2, n_bits)),
            dma,
            dma((parts * PIECES, 3)),
            dma((4,)),
        ],
        56,
        collective_id=0,
        has_side_effects=True,
    )(
        tok_lengths, frame_lengths, block_input, memory, turned(self_weights), self_output,
        turned(cross_weights), cross_output, inner_weight, outer_weight, self_biases, cross_biases,
        inner_bias.reshape(1, own_hidden), norm_gain, norm_shift, self_offset.reshape(1, width),
    )
    wcross_rows = wcross.reshape(4 * width, width)
    wself_rows = wself.reshape(4 * width, width)
    inner_rows, outer_rows = inner.reshape(hidden, width), outer.reshape(hidden, width)

    def reduce_buffers(n):
        full = parts * n
        return [
            pltpu.VMEM((2, 2, full, width), BF16),
            pltpu.VMEM((2, 2, full, width), BF16),
            pltpu.VMEM((3, full, width), BF16),
            pltpu.VMEM((parts, n, width), BF16),
            pltpu.VMEM((parts, n, width), BF16),
            pltpu.VMEM((2 * max(n_bits - 3, 1), n, width), F32),
        ]

    window = PIECES * (parts - 1)
    far_shape = (2, window - NEAR, piece, width)
    beyond = far[0, 0] > NEAR * piece

    def fetch_far():
        (far_memory,) = call(
            gather_far,
            [((parts * frames, width), BF16, "h")],
            "h",
            [dma((4, window))],
            8,
            collective_id=2,
            has_side_effects=True,
        )(memory_rows)
        return far_memory

    far_memory = lax.cond(beyond, fetch_far, lambda: spare)
    padded = (frames + TILE, width)
    grad, small, block_output, mgrad, dw_cross, dwi, dwo = call(
        middle,
        [
            (own_rows, F32, "v"),
            ((small_rows, width), F32, "v"),
            (own_rows, F32, "h"),
            ((frames, width), BF16, "h"),
            ((4 * width, width), BF16, "h"),
            ((hidden, width), BF16, "h"),
            ((hidden, width), BF16, "h"),
        ],
        "sssvvvvvvvhhhhhhhhh",
        [
            (own_rows, F32),
            (own_rows, BF16),
            ((4 * width, width), BF16),
            (own_rows, F32),
            (padded, BF16),
            (padded, BF16),
            (padded, BF16),
            ((hidden, width), BF16),
            ((hidden, width), BF16),
            (padded, BF16),
            ((2, width, width), F32),
            ((4 * width, width), BF16),
            ((hidden, width), BF16),
            ((hidden, width), BF16),
            ((blocks, wide, width), BF16),
            ((blocks, wide, width), BF16),
            ((blocks, 1, wide), F32),
            ((blocks, 1, wide), F32),
            ((blocks, width, BLOCK), F32),
            ((blocks, width, BLOCK), F32),
            (padded, F32),
            (padded, F32),
            ((blocks, 1, BLOCK), jnp.int32),
            ((blocks, 1, BLOCK), jnp.int32),
            pltpu.SMEM((2, blocks), jnp.int32),
            dma((5,)),
            dma((5,)),
            dma((3, frames // UNIT)),
            dma((3,)),
        ],
        56,
    )(
        far, tok_lengths, frame_lengths, cq, inner_row, value_row, norm_gain,
        norm_shift, cross_offset.reshape(1, width), outer_offset.reshape(1, width),
        after, cotangent, wcross_rows, ck, cv, memory_rows, far_memory, inner_rows, outer_rows,
    )

    def return_far():
        (summed,) = call(
            sum_far,
            [((frames, width), BF16, "h")],
            "h",
            [((frames, width), BF16), (far_shape, BF16), dma((4, window - NEAR)), dma],
            16,
            collective_id=3,
            has_side_effects=True,
        )(mgrad)
        return summed

    mgrad = lax.cond(beyond, return_far, lambda: mgrad)
    partial_results = call(
        functools.partial(give_back, NEAR),
        [
            (own_rows, F32, "v"),
            ((frames // parts, width), BF16, "v"),
            (sliced(n_att), BF16, "v"),
            (sliced(n_att), BF16, "v"),
            (sliced(n_ffn), BF16, "v"),
            (sliced(n_ffn), BF16, "v"),
            ((small_rows, width), F32, "v"),
        ],
        "ssvvhhhhhhhhhhhh",
        [
            (own_rows, BF16),
            (halo_rows, BF16),
            (own_rows, BF16),
            (halo_rows, BF16),
            (halo_rows, BF16),
            (own_rows, BF16),
            (own_rows, F32),
            ((4 * width, width), BF16),
            ((frames, width), BF16),
            ((NEAR, piece, width), BF16),
            ((NEAR, piece, width), BF16),
            (sliced(parts * n_att), BF16),
            (sliced(parts * n_att), BF16),
            (sliced(parts * n_ffn), BF16),
            (sliced(parts * n_ffn), BF16),
            (halo_rows, F32),
            (halo_rows, F32),
            (own_rows, BF16),
            ((HALO, width), BF16),
            ((HALO, width), BF16),
            ((2, 2, 2, small_rows, width), F32),
            ((2 * (n_bits - 3) + 1, small_rows, width), F32),
            ((parts, small_rows, width), F32),
            reduce_buffers(n_att),
            reduce_buffers(n_att),
            reduce_buffers(n_ffn),
            reduce_buffers(n_ffn),
            dma((12,)),
            dma((4, NEAR)),
            dma((4, 2, 3 + parts)),
            dma((4, 2, max(n_bits - 3, 1))),
            dma((4, 2, 8)),
            dma((2,)),
            dma((2, 8)),
            dma((2, max(n_bits - 3, 1))),
            dma((2, parts)),
        ],
        56,
        collective_id=1,
        has_side_effects=True,
    )(
        tok_lengths, frame_lengths, small, norm_gain, block_input, n1, q, k, v, att, grad, wself_rows,
        mgrad, dw_cross.reshape(sliced(parts * n_att)), dwi.reshape(sliced(parts * n_ffn)),
        dwo.reshape(sliced(parts * n_ffn)),
    )
    input_grad, mgrad_sum, fself, fcross, finner, fouter, small = partial_results
    results = call(
        finals,
        [
            ((frames // parts, width), F32, "v"),
            (own_rows, F32, "v"),
            ((3, width), F32, "v"),
            ((3, width), F32, "v"),
            ((3, own, width), F32, "v"),
            ((2, own), F32, "v"),
            ((own, width), F32, "v"),
            ((1, width), F32, "v"),
            ((3, own, width), F32, "v"),
            ((2, own), F32, "v"),
            ((own, width), F32, "v"),
            ((1, width), F32, "v"),
            ((width, own_hidden), F32, "v"),
            ((1, own_hidden), F32, "v"),
            ((own_hidden, width), F32, "v"),
            ((1, width), F32, "v"),
        ],
        "vvvvvvv",
        [],
        56,
    )(mgrad_sum, input_grad, fself, fcross, finner, fouter, small)
    memory_grad, input_grad, *others = results
    others = [r.reshape(-1) if r.shape[0] == 1 else r for r in others]
    others[2], others[6] = turned(others[2]), turned(others[6])
    return (block_output, input_grad, memory_grad, *others)


def solution(mesh):
    in_specs = (
        P(("dp", "mp"), None),
        P(("dp", "mp"), None),
        P("dp", None),
        P("dp", None),
        P(("dp", "mp"), None),
        P(),
        P(),
        P(None, None, "mp"),
        P(None, "mp"),
        P("mp", None),
        P(),
        P(None, None, "mp"),
        P(None, "mp"),
        P("mp", None),
        P(),
        P(None, "mp"),
        P("mp"),
        P("mp", None),
        P(),
    )
    out_specs = (
        P(("dp", "mp"), None),
        P(("dp", "mp"), None),
        P(("dp", "mp"), None),
        P(),
        P(),
        P(None, None, "mp"),
        P(None, "mp"),
        P("mp", None),
        P(),
        P(None, None, "mp"),
        P(None, "mp"),
        P("mp", None),
        P(),
        P(None, "mp"),
        P("mp"),
        P("mp", None),
        P(),
    )
    return jax.shard_map(shards, mesh=mesh, in_specs=in_specs, out_specs=out_specs, check_vma=False)
```

```python
import functools
import math

import jax
import jax.numpy as jnp
from jax import lax
from jax.experimental import pallas as pl
from jax.experimental.pallas import tpu as pltpu
from jax.sharding import PartitionSpec as P

HEAD = 64
NEGATIVE = -1e30
EPSILON = 1e-05
BLOCK = 128
TILE = 512
UNIT = 128
HALO = 256
F32 = jnp.float32
BF16 = jnp.bfloat16
MESH = pl.DeviceIdType.MESH
HALF = HEAD // 2
SLICES = 8
PIECES = 4
NEAR = 6
GELU_A = math.sqrt(2.0 / math.pi)
GELU_B = 0.044715


def mm(a, b, ca=1, cb=0):
    return lax.dot_general(a, b, (((ca,), (cb,)), ((), ())), preferred_element_type=F32)


def normed(values):
    center = values - jnp.mean(values, axis=-1, keepdims=True)
    spread = jnp.mean(center * center, axis=-1, keepdims=True)
    scale = lax.rsqrt(spread + EPSILON)
    return center * scale, scale


def norm_back(grad, gain, xhat, scale):
    gn = grad * gain
    first = jnp.mean(gn, axis=-1, keepdims=True)
    second = jnp.mean(gn * xhat, axis=-1, keepdims=True)
    return (gn - first - xhat * second) * scale


def column_sums(values):
    return jnp.sum(values, axis=0, keepdims=True)


def head_stack(values):
    rows, width = values.shape
    heads = width // HEAD
    lane = lax.broadcasted_iota(jnp.int32, (rows, width), 1) // HALF % heads
    zero = jnp.zeros_like(values)
    return jnp.concatenate([jnp.where(lane == h, values, zero) for h in range(heads)], axis=0)


def head_rows(heads):
    return [
        (slice((i * heads + h) * HALF, (i * heads + h + 1) * HALF), h)
        for i in range(2)
        for h in range(heads)
    ]


def head_diagonal(values, heads):
    rows = values.shape[1] // heads
    return jnp.concatenate(
        [values[r, h * rows : (h + 1) * rows] for r, h in head_rows(heads)], axis=0
    )


def token_rows(tok_ref, frm_ref, base, count):
    place = lax.broadcasted_iota(jnp.int32, (1, count), 1) + base
    zero = jnp.zeros((1, count), jnp.int32)

    def step(u, carry):
        start, first_row, first_frame, end_frame = carry
        tokens, frames = tok_ref[0, u], frm_ref[0, u]
        end = start + tokens
        done = place >= end
        first_row = first_row + jnp.where(done, tokens, 0)
        first_frame = first_frame + jnp.where(done, frames, 0)
        end_frame = end_frame + jnp.where(place >= start, frames, 0)
        return end, first_row, first_frame, end_frame

    _, first_row, first_frame, end_frame = lax.fori_loop(
        0, tok_ref.shape[1], step, (jnp.int32(0), zero, zero, zero)
    )
    return place, first_row, first_frame, end_frame


def excursion(tok_ref, frm_ref, rows, frames, parts):
    lane = lax.broadcasted_iota(jnp.int32, (1, 128), 1)
    zero = jnp.zeros((1, 128), jnp.int32)

    def step(u, carry):
        start, low, high = carry
        tokens, count = tok_ref[0, u], frm_ref[0, u]
        end = start + tokens
        low = low + jnp.where(lane * rows >= end, count, 0)
        high = high + jnp.where((lane + 1) * rows - 1 >= start, count, 0)
        return end, low, high

    _, low, high = lax.fori_loop(0, tok_ref.shape[1], step, (jnp.int32(0), zero, zero))
    beyond = jnp.maximum(high - (lane + 1) * frames, lane * frames - low)
    return jnp.max(jnp.where(lane < parts, beyond, 0), axis=1, keepdims=True).astype(F32)


def block_frames(tok_ref, frm_ref, base, count):
    blocks = count // BLOCK

    def step(u, carry):
        start, low, high = carry
        tokens, frames = tok_ref[0, u], frm_ref[0, u]
        end = start + tokens
        low = tuple(
            v + jnp.where(base + b * BLOCK >= end, frames, 0) for b, v in enumerate(low)
        )
        high = tuple(
            v + jnp.where(base + (b + 1) * BLOCK - 1 >= start, frames, 0) for b, v in enumerate(high)
        )
        return end, low, high

    zeros = (jnp.int32(0),) * blocks
    _, low, high = lax.fori_loop(0, tok_ref.shape[1], step, (jnp.int32(0), zeros, zeros))
    return low, high


def window_mask(place, first_row, base, block, count):
    keys = lax.broadcasted_iota(jnp.int32, (count, BLOCK), 0) + (base - HALO + block * BLOCK)
    here = slice(block * BLOCK, (block + 1) * BLOCK)
    return (keys >= first_row[:, here]) & (keys <= place[:, here])


def self_probs(queries, key_window, mask, heads):
    scores = mm(key_window, queries, 1, 1)
    parts = []
    for h in range(heads):
        part = jnp.where(mask, scores[:, h * BLOCK : (h + 1) * BLOCK], NEGATIVE)
        raised = jnp.exp(part - jnp.max(part, axis=0, keepdims=True))
        parts.append(raised * (1.0 / jnp.sum(raised, axis=0, keepdims=True)))
    return jnp.concatenate(parts, axis=1)


def rcopy(src, dst, send, recv, **device):
    return pltpu.make_async_remote_copy(
        src_ref=src, dst_ref=dst, send_sem=send, recv_sem=recv, device_id=device, device_id_type=MESH
    )


def at_rows(start, count):
    return pl.ds(pl.multiple_of(start, 16), count)


def flipped(index, bit):
    return index + bit - 2 * bit * (index // bit % 2)


def greet(z, parts, d, bits, masks=()):
    barrier = pltpu.get_barrier_semaphore()
    for mask in masks:
        device = {"dp": masked(d, mask)}
        pl.semaphore_signal(barrier, inc=1, device_id=device, device_id_type=MESH)
    for step in range(1, parts):
        device = {"mp": (z + step) % parts}
        pl.semaphore_signal(barrier, inc=1, device_id=device, device_id_type=MESH)
    for bit in bits:
        device = {"dp": flipped(d, bit)}
        pl.semaphore_signal(barrier, inc=1, device_id=device, device_id_type=MESH)
    return barrier, parts - 1 + len(bits) + len(masks)


class Double:
    def __init__(self, z, own, place, sems):
        self.z, self.own, self.place, self.sems = z, own, place, sems

    def copies(self, step, other):
        z = self.z
        if step == 0:
            far = flipped(z, 2)
            blocks = [(self.place(far) if other else self.own, self.place(far if other else z), 0)]
            device = far
        else:
            device = flipped(z, 1)
            first = device if other else z
            blocks = [(self.place(i), self.place(i), k) for k, i in ((1, first), (2, flipped(first, 2)))]
        sems = self.sems
        return [rcopy(src, dst, sems.at[0, k], sems.at[1, k], mp=device) for src, dst, k in blocks]

    def send(self, step):
        for copy in self.copies(step, False):
            copy.start()

    def arrived(self, step):
        for copy in self.copies(step, True):
            copy.wait_recv()

    def close(self):
        for step in range(2):
            for copy in self.copies(step, False):
                copy.wait_send()


DP_BITS = (2, 4, 1)


def corner(d):
    return d % 2, d // 4 % 2, d // 2 % 2


class Plane:
    def __init__(self, d, buffer, first_y, sems):
        self.d, self.buffer, self.first_y, self.sems = d, buffer, first_y, sems

    def block(self, p, c, y, x):
        if p == 0:
            return self.buffer.at[c, y, x]
        if p == 2:
            return self.buffer.at[c]
        return self.buffer.at[c, :, x] if self.first_y else self.buffer.at[c, y]

    def copy(self, p, other):
        c, y, x = corner(self.d)
        over_y = p == (0 if self.first_y else 1)
        if other:
            if p == 2:
                c = 1 - c
            elif over_y:
                y = 1 - y
            else:
                x = 1 - x
        block = self.block(p, c, y, x)
        device = flipped(self.d, 1 if p == 2 else 4 if over_y else 2)
        return rcopy(block, block, self.sems.at[0, p], self.sems.at[1, p], dp=device)

    def send(self, p):
        self.copy(p, False).start()

    def arrived(self, p):
        self.copy(p, True).wait_recv()

    def close(self):
        for p in range(3):
            self.copy(p, False).wait_send()


class Window:
    def __init__(self, z, parts, source, place, sems):
        self.z, self.parts, self.source, self.place, self.sems = z, parts, source, place, sems

    def number(self, z, j, up):
        return (z + 1) * PIECES - 1 - j if up else z * PIECES + j

    def there(self, number):
        return (number >= 0) & (number < self.parts * PIECES)

    def copy(self, j, up):
        number = self.number(self.z, j, up)
        place, kind = self.place(number, j, up), 0 if up else 2
        return rcopy(
            self.source(number, j, up),
            place,
            self.sems.at[kind, j],
            self.sems.at[kind + 1, j],
            mp=self.z + 1 if up else self.z - 1,
        )

    def sends(self, j, up):
        edge = self.z < self.parts - 1 if up else self.z > 0
        return edge & self.there(self.number(self.z, j, up))

    def send(self, j):
        for up in (True, False):

            @pl.when(self.sends(j, up))
            def _():
                self.copy(j, up).start()

    def comes(self, j, up):
        edge = self.z > 0 if up else self.z < self.parts - 1
        return edge & self.there(self.arrival(j, up))

    def arrival(self, j, up):
        return self.number(self.z - 1 if up else self.z + 1, j, up)

    def arrived(self, j):
        for up in (True, False):

            @pl.when(self.comes(j, up))
            def _():
                number = self.arrival(j, up)
                place, kind = self.place(number, j, up), 0 if up else 2
                rcopy(
                    place,
                    place,
                    self.sems.at[kind, j],
                    self.sems.at[kind + 1, j],
                    mp=self.z - 1 if up else self.z + 1,
                ).wait_recv()

    def each(self, j, use):
        for up in (True, False):

            @pl.when(self.comes(j, up))
            def _():
                use(self.arrival(j, up), j, up)

    def close(self, pieces):
        for j in pieces:
            for up in (True, False):

                @pl.when(self.sends(j, up))
                def _():
                    self.copy(j, up).wait_send()


def gather(
    tok, frm, x_ref, mem, sw, so, cw, co, inner, outer, sb, cb, ib, gain, shift, offset,
    wself_out, wcross_out, inner_out, outer_out, ib_out, vb_out, far_out, mem_out, ck_out, cv_out, spare,
    n1_ref, q_ref, k_ref, v_ref, att_ref, after_ref, cq_ref,
    gself, gcross, ginner, gouter, gmem, sck, scv, pself, pcross, pinner, halo, pbias, gbias,
    far, far_land, line_sems, mem_sems, plane_sems, bias_sems, halo_sems, far_sems, own_sem, out_sems, weight_sems,
):
    rows, width = x_ref.shape
    heads = width // HEAD
    own = sw.shape[1]
    parts = width // own
    shard_rows = mem.shape[0]
    piece = shard_rows // PIECES
    z, d = lax.axis_index("mp"), lax.axis_index("dp")
    dp = lax.axis_size("dp")
    bits = [1 << i for i in range(dp.bit_length() - 1)]
    c, y, x = corner(d)
    s = c * 4 + y * 2 + x
    barrier, greetings = greet(z, parts, d, bits)

    for source, last, packed in ((sw, so, pself), (cw, co, pcross)):
        for i in range(3):
            packed[i * own : (i + 1) * own] = source[i]
        packed[3 * own :] = last[...]
    pbias[...] = jnp.zeros_like(pbias)
    pbias[0:1] = ib[...]
    for i in range(2):
        pbias[1:2, i * own : (i + 1) * own] = sb[i : i + 1]
        pbias[1:2, (2 + i) * own : (3 + i) * own] = cb[i : i + 1]
    pinner[...] = inner[...].T
    groups = []
    for i, (packed, buffer) in enumerate(
        ((pself, gself), (pcross, gcross), (pinner, ginner), (outer, gouter))
    ):
        n = packed.shape[0] // SLICES
        mine = packed.at[at_rows(s * n, n)]

        def place(shard, buffer=buffer, n=n):
            return buffer.at[c, y, x, at_rows(shard * n, n)]

        line = Double(z, mine, place, line_sems.at[i])
        plane = Plane(d, buffer, i % 2 == 1, plane_sems.at[i])
        groups.append((line, plane))
        buffer[c, y, x, at_rows(z * n, n)] = packed[at_rows(s * n, n)]

    def piece_place(number, j, up):
        return gmem.at[at_rows(number * piece, piece)]

    def piece_source(number, j, up):
        if j < PIECES:
            return mem.at[at_rows((number - z * PIECES) * piece, piece)]
        return piece_place(number, j, up)

    memory = Window(z, parts, piece_source, piece_place, mem_sems)

    bias_line = Double(z, pbias, lambda shard: gbias.at[shard], bias_sems)

    def halo_copy(other):
        return rcopy(x_ref.at[rows - HALO :], halo, halo_sems.at[0], halo_sems.at[1], mp=other)

    def far_copy(i):
        device = flipped(d, bits[i])
        return rcopy(far.at[i], far_land.at[i], far_sems.at[0, i], far_sems.at[1, i], dp=device)

    def far_step(i):
        if i > 0:
            far_copy(i - 1).wait_recv()
            far[i] = jnp.maximum(far[i - 1], far_land[i - 1])
        if i < len(bits):
            far_copy(i).start()
        else:
            far_out[...] = far[i, 0:1, 0:1]

    def forward(j):
        memory.arrived(j - PIECES)
        memory.send(j)

    far[0] = jnp.broadcast_to(excursion(tok, frm, rows, shard_rows, parts), far.shape[1:])
    gbias[z] = pbias[...]
    own_rows = gmem.at[at_rows(z * shard_rows, shard_rows)]
    own_copy = pltpu.make_async_copy(mem, own_rows, own_sem)
    own_copy.start()
    pl.semaphore_wait(barrier, greetings)
    for line, _ in groups[:2]:
        line.send(0)
    bias_line.send(0)

    @pl.when(z < parts - 1)
    def _():
        halo_copy(z + 1).start()

    for line, _ in groups[2:]:
        line.send(0)
    for line in (groups[0][0], groups[1][0], bias_line):
        line.arrived(0)
        line.send(1)
    memory.send(0)
    for line, _ in groups[2:]:
        line.arrived(0)
        line.send(1)
    for j in range(1, PIECES):
        memory.send(j)
    far_step(0)
    for line, plane in groups[:2]:
        line.arrived(1)
        plane.send(0)
    for _, plane in groups[:2]:
        plane.arrived(0)
        plane.send(1)
    for line, plane in groups[2:]:
        line.arrived(1)
        plane.send(0)
    far_step(1)
    for _, plane in groups[:2]:
        plane.arrived(1)
        plane.send(2)
    far_step(2)
    groups[0][1].arrived(2)

    bias_line.arrived(1)

    def head_bias(i):
        return jnp.concatenate(
            [
                gbias[o, 1:2, i * own + half * HALF : i * own + (half + 1) * HALF]
                for half in range(2)
                for o in range(parts)
            ],
            axis=1,
        )

    n = ginner.shape[3] // parts
    for i in range(SLICES):
        ib_out[i : i + 1] = jnp.concatenate(
            [gbias[o, 0:1, i * n : (i + 1) * n] for o in range(parts)], axis=1
        )

    @pl.when(z > 0)
    def _():
        halo_copy(z - 1).wait_recv()

    @pl.when(z == 0)
    def _():
        halo[...] = jnp.zeros_like(halo)

    def weight(buffer, i):
        return buffer[i // 2, i % 2].reshape(width, width)

    base = z * rows
    place_row, first_row, _, _ = token_rows(tok, frm, base, rows)
    for src, dst in ((halo, slice(0, HALO)), (x_ref, slice(HALO, HALO + rows))):
        xhat, _ = normed(src[...].astype(F32))
        n1_ref[dst] = (xhat * gain[0:1] + shift[0:1]).astype(BF16)
    n1 = n1_ref[...]
    query = mm(n1[HALO:], weight(gself, 0), 1, 1) + head_bias(0)
    q_ref[...] = query.astype(BF16) * jnp.asarray(0.125, BF16)
    k_ref[...] = mm(n1, weight(gself, 1), 1, 1).astype(BF16)
    v_ref[...] = (mm(n1, weight(gself, 2), 1, 1) + head_bias(1)).astype(BF16)
    count = HALO + BLOCK
    for b in range(rows // BLOCK):
        queries = head_stack(q_ref[b * BLOCK : (b + 1) * BLOCK])
        window = slice(b * BLOCK, b * BLOCK + count)
        mask = window_mask(place_row, first_row, base, b, count)
        probs = self_probs(queries, k_ref[window], mask, heads).astype(BF16)
        out = head_diagonal(mm(v_ref[window], probs, 0, 0), heads)
        att_ref[b * BLOCK : (b + 1) * BLOCK] = out.T.astype(BF16)
        if b == 0:
            for _, plane in groups[2:]:
                plane.arrived(0)
                plane.send(1)
    forward(PIECES)
    after = x_ref[...].astype(F32) + mm(att_ref[...], weight(gself, 3)) + offset[...]
    after_ref[...] = after
    xhat, _ = normed(after)
    groups[1][1].arrived(2)
    n2 = (xhat * gain[1:2] + shift[1:2]).astype(BF16)
    query = mm(n2, weight(gcross, 0), 1, 1) + head_bias(2)
    cq_ref[...] = query.astype(BF16) * jnp.asarray(0.125, BF16)
    value_bias = head_bias(3)
    forward(PIECES + 1)

    def project(start, size):
        here = at_rows(start, size)
        block = gmem[here]
        sck[here] = mm(block, weight(gcross, 1), 1, 1).astype(BF16)
        scv[here] = (mm(block, weight(gcross, 2), 1, 1) + value_bias).astype(BF16)

    def copies_out(number):
        here = at_rows(number * piece, piece)
        return [
            pltpu.make_async_copy(a.at[here], b.at[here], out_sems.at[number, i])
            for i, (a, b) in enumerate(((gmem, mem_out), (sck, ck_out), (scv, cv_out)))
        ]

    def project_piece(number, j=0, up=True):
        project(number * piece, piece)
        for copy in copies_out(number):
            copy.start()

    own_copy.wait()
    lax.fori_loop(0, PIECES, lambda i, _: (project_piece(z * PIECES + i), 0)[1], 0)
    for _, plane in groups[2:]:
        plane.arrived(1)
        plane.send(2)
    for j in range(PIECES):
        if j >= 2:
            memory.arrived(j)
        memory.each(j, project_piece)
    for i in range(3, len(bits) + 1):
        far_step(i)
    for _, plane in groups[2:]:
        plane.arrived(2)
    outs = [
        pltpu.make_async_copy(a, b, weight_sems.at[i])
        for i, (a, b) in enumerate(
            ((gself, wself_out), (gcross, wcross_out), (ginner, inner_out), (gouter, outer_out))
        )
    ]
    for copy in outs:
        copy.start()
    vb_out[...] = value_bias
    for j in range(PIECES, NEAR):
        memory.arrived(j)
        memory.each(j, project_piece)
    for copy in outs:
        copy.wait()

    def finish(number, *_):
        for copy in copies_out(number):
            copy.wait()

    for i in range(PIECES):
        finish(z * PIECES + i)
    for j in range(NEAR):
        memory.each(j, finish)
    for line, plane in groups:
        line.close()
        plane.close()
    memory.close(range(NEAR))
    for i in range(len(bits)):
        far_copy(i).wait_send()
    bias_line.close()

    @pl.when(z < parts - 1)
    def _():
        halo_copy(z + 1).wait_send()


def gather_far(mem, far_mem, sems):
    z, d = lax.axis_index("mp"), lax.axis_index("dp")
    parts = lax.axis_size("mp")
    last = PIECES * (parts - 1)
    piece = mem.shape[0] // parts // PIECES
    barrier, greetings = greet(z, parts, d, ())

    def place(number, j, up):
        return far_mem.at[at_rows(number * piece, piece)]

    def source(number, j, up):
        return (mem if j - PIECES < NEAR else far_mem).at[at_rows(number * piece, piece)]

    memory = Window(z, parts, source, place, sems)
    pl.semaphore_wait(barrier, greetings)
    for j in range(NEAR, last):
        if j - PIECES >= NEAR:
            memory.arrived(j - PIECES)
        memory.send(j)
    for j in range(max(NEAR, last - PIECES), last):
        memory.arrived(j)
    memory.close(range(NEAR, last))


def middle(
    far, tok, frm, cq_ref, ib_ref, vb_ref, gain, shift, cross_offset, outer_offset,
    after_in, cot_in, w_in, ck_in, cv_in, mem_in, far_in, wi_in, wo_in,
    grad_ref, small_ref, block_out, mgrad_out, dw_out, dwi_out, dwo_out,
    after_ref, cot_ref, w_ref, out_ref,
    ck_ref, cv_ref, mem_ref, wi_ref, wo_ref, mgrad_ref, dw_ref, dwb_ref, dwi_ref, dwo_ref,
    qbig, gbig, lse_ref, dot_ref, att_ref, dq_ref, dk_ref, dv_ref, first_ref, end_ref, bounds,
    in_sems, out_sems, unit_sems, far_sems,
):
    rows, width = cq_ref.shape
    heads = width // HEAD
    blocks = rows // BLOCK
    z = lax.axis_index("mp")
    parts = lax.axis_size("mp")
    last = parts * PIECES
    frames = mem_in.shape[0]
    piece = frames // last
    beyond = far[0, 0] > NEAR * piece

    def weight(i):
        return w_ref[i * width : (i + 1) * width]

    def rows_of(number):
        return at_rows(jnp.clip(number, 0, last - 1) * piece, piece)

    def spans(i, unit):
        here = pl.ds(pl.multiple_of(origin + unit * UNIT, UNIT), UNIT)
        source, full = arrays[i]
        return pltpu.make_async_copy(source.at[here], full.at[here], unit_sems.at[i, unit])

    def units(i, name):
        def one(unit, carry):
            getattr(spans(i, unit), name)()
            return carry

        lax.fori_loop(0, unit_count, one, 0)

    arrays = ((ck_in, ck_ref), (cv_in, cv_ref), (mem_in, mem_ref))
    base = z * rows
    _, _, first_frame, end_frame = token_rows(tok, frm, base, rows)
    for b in range(blocks):
        first_ref[b] = first_frame[:, b * BLOCK : (b + 1) * BLOCK]
        end_ref[b] = end_frame[:, b * BLOCK : (b + 1) * BLOCK]
        qbig[b] = head_stack(cq_ref[b * BLOCK : (b + 1) * BLOCK])
    low, high = block_frames(tok, frm, base, rows)
    for b in range(blocks):
        bounds[0, b] = low[b] // UNIT * UNIT
        bounds[1, b] = high[b]
    origin = bounds[0, 0]
    unit_count = (bounds[1, blocks - 1] - origin + UNIT - 1) // UNIT
    count = (unit_count * UNIT + TILE - 1) // TILE
    loads = [
        pltpu.make_async_copy(a, b, in_sems.at[i])
        for i, (a, b) in enumerate(
            ((wi_in, wi_ref), (wo_in, wo_ref), (after_in, after_ref), (cot_in, cot_ref), (w_in, w_ref))
        )
    ]

    @pl.when(jnp.logical_not(beyond))
    def _():
        units(0, "start")
        units(1, "start")

    for load in loads:
        load.start()

    @pl.when(jnp.logical_not(beyond))
    def _():
        units(2, "start")

    @pl.when(beyond)
    def _():
        loads[4].wait()

        def fetch(i, carry):
            number = i
            here = rows_of(number)
            distance = jnp.maximum(z * PIECES - 1 - number, number - (z + 1) * PIECES)

            @pl.when(distance < NEAR)
            def _():
                copies = [
                    pltpu.make_async_copy(a.at[here], b.at[here], far_sems.at[k])
                    for k, (a, b) in enumerate(arrays)
                ]
                for copy in copies:
                    copy.start()
                for copy in copies:
                    copy.wait()

            @pl.when(distance >= NEAR)
            def _():
                copy = pltpu.make_async_copy(far_in.at[here], mem_ref.at[here], far_sems.at[0])
                copy.start()
                copy.wait()
                block = mem_ref[here]
                ck_ref[here] = mm(block, weight(1), 1, 1).astype(BF16)
                cv_ref[here] = (mm(block, weight(2), 1, 1) + vb_ref[...]).astype(BF16)

            return carry

        lax.fori_loop(0, last, fetch, 0)

    tail = pl.ds(pl.multiple_of(origin + unit_count * UNIT, UNIT), TILE)
    for _, full in arrays:
        full[tail] = jnp.zeros((TILE, width), BF16)
    small_ref[...] = jnp.zeros_like(small_ref)
    mgrad_ref[...] = jnp.zeros_like(mgrad_ref)

    def tiles(b):
        return (bounds[1, b] - bounds[0, b] + TILE - 1) // TILE

    def tile_mask(start, b):
        frame = lax.broadcasted_iota(jnp.int32, (TILE, BLOCK), 0) + start
        return (frame >= first_ref[b]) & (frame < end_ref[b])

    def columns(h):
        return slice(h * BLOCK, (h + 1) * BLOCK)

    @pl.when(jnp.logical_not(beyond))
    def _():
        units(0, "wait")
        units(1, "wait")

    def attend(b, carry):
        att_ref[b] = jnp.zeros((width, BLOCK), F32)

        def step(i, carry):
            start = bounds[0, b] + i * TILE
            here = pl.ds(pl.multiple_of(start, 128), TILE)
            scores = mm(ck_ref[here], qbig[b], 1, 1)
            mask = tile_mask(start, b)
            values = cv_ref[here].T
            news = []
            for h in range(heads):
                largest, total = carry[h]
                part = jnp.where(mask, scores[:, columns(h)], NEGATIVE)
                now = jnp.maximum(largest, jnp.max(part, axis=0, keepdims=True))
                fade = jnp.exp(largest - now)
                raised = jnp.exp(part - now)
                news.append((now, total * fade + jnp.sum(raised, axis=0, keepdims=True)))
                pieces = [r for r, o in head_rows(heads) if o == h]
                own = jnp.concatenate([values[r] for r in pieces], axis=0)
                out = mm(own, raised.astype(BF16))
                for i, r in enumerate(pieces):
                    att_ref[b, r] = att_ref[b, r] * fade + out[i * HALF : (i + 1) * HALF]
            return tuple(news)

        start = (jnp.full((1, BLOCK), NEGATIVE, F32), jnp.zeros((1, BLOCK), F32))
        done = lax.fori_loop(0, tiles(b), step, (start,) * heads)
        for h, (largest, total) in enumerate(done):
            lse_ref[b, :, columns(h)] = largest + jnp.log(total)
            share = 1.0 / total
            for r, o in head_rows(heads):
                if o == h:
                    att_ref[b, r] = att_ref[b, r] * share
        return carry

    lax.fori_loop(0, blocks, attend, 0)
    att = jnp.concatenate([att_ref[b].T for b in range(blocks)], axis=0).astype(BF16)
    loads[2].wait()
    loads[3].wait()

    @pl.when(jnp.logical_not(beyond))
    def _():
        loads[4].wait()

    after_self = after_ref[...]
    after_cross = after_self + mm(att, weight(3)) + cross_offset[...]
    xhat3, scale3 = normed(after_cross)
    n3 = (xhat3 * gain[2:3] + shift[2:3]).astype(BF16)
    sent = cot_ref[...]
    small_ref[8:9] = column_sums(sent.astype(F32))
    hidden = wi_ref.shape[0]
    group = 4
    tile = hidden // SLICES * group
    loads[0].wait()
    loads[1].wait()
    out_ref[...] = after_cross + outer_offset[...]
    grad_ref[...] = jnp.zeros((rows, width), F32)

    def feed(f, carry):
        here = pl.ds(pl.multiple_of(f * tile, tile), tile)
        bias = jnp.concatenate([ib_ref[pl.ds(f * group + i, 1)] for i in range(group)], axis=1)
        before = mm(n3, wi_ref[here], 1, 1) + bias
        square = before * before
        inner = jnp.tanh(before * (GELU_A + (GELU_A * GELU_B) * square))
        half = 0.5 + 0.5 * inner
        active = (before * half).astype(BF16)
        slope = half + (0.5 * before) * (1.0 - inner * inner) * (
            GELU_A + (3.0 * GELU_A * GELU_B) * square
        )
        out_ref[...] += mm(active, wo_ref[here])
        back = (slope * mm(sent, wo_ref[here], 1, 1)).astype(BF16)
        grad_ref[...] += mm(back, wi_ref[here])
        dwo_ref[here] = mm(active, sent, 0, 0).astype(BF16)
        dwi_ref[here] = mm(back, n3, 0, 0).astype(BF16)
        sums = column_sums(back.astype(F32))
        for i in range(group):
            small_ref[pl.ds(16 + f * group + i, 1)] = sums[:, i * tile // group : (i + 1) * tile // group]
        return carry

    lax.fori_loop(0, SLICES // group, feed, 0)
    stores = [
        pltpu.make_async_copy(a, b, out_sems.at[i])
        for i, (a, b) in enumerate(
            (
                (dwi_ref, dwi_out),
                (dwo_ref, dwo_out),
                (dwb_ref, dw_out),
                (mgrad_ref.at[:frames], mgrad_out),
                (out_ref, block_out),
            )
        )
    ]
    stores[0].start()
    stores[1].start()
    stores[4].start()
    dn3 = grad_ref[...]
    small_ref[2:3] = column_sums(dn3 * xhat3)
    small_ref[5:6] = column_sums(dn3)
    grad = sent.astype(F32) + norm_back(dn3, gain[2:3], xhat3, scale3)
    sent2 = grad.astype(BF16)
    small_ref[7:8] = column_sums(sent2.astype(F32))
    dwb_ref[3 * width :] = mm(att, sent2, 0, 0).astype(BF16)
    go = mm(sent2, weight(3), 1, 1).astype(BF16)
    got = mm(weight(3), sent2, 1, 1).astype(BF16).astype(F32)
    for b in range(blocks):
        gbig[b] = head_stack(go[b * BLOCK : (b + 1) * BLOCK])
        prod = got[:, b * BLOCK : (b + 1) * BLOCK] * att_ref[b]
        sums = [column_sums(prod[r]) for r, _ in head_rows(heads)]
        for h in range(heads):
            dot_ref[b, :, columns(h)] = sums[h] + sums[heads + h]
    def span(i):
        return pl.ds(pl.multiple_of(origin + i * TILE, 128), TILE)

    def clear(i, carry):
        dk_ref[span(i)] = jnp.zeros((TILE, width), F32)
        dv_ref[span(i)] = jnp.zeros((TILE, width), F32)
        return carry

    lax.fori_loop(0, count, clear, 0)

    def attend_back(b, carry):
        dq_ref[b] = jnp.zeros((width, BLOCK), F32)

        def step(i, carry):
            start = bounds[0, b] + i * TILE
            here = pl.ds(pl.multiple_of(start, 128), TILE)
            keys, values = ck_ref[here], cv_ref[here]
            scores = mm(keys, qbig[b], 1, 1)
            dp = mm(values, gbig[b], 1, 1)
            mask = tile_mask(start, b)
            shares, scaled = [], []
            for h in range(heads):
                part = jnp.exp(scores[:, columns(h)] - lse_ref[b, :, columns(h)])
                part = jnp.where(mask, part, 0.0)
                shares.append(part.astype(BF16))
                scaled.append((part * (dp[:, columns(h)] - dot_ref[b, :, columns(h)])).astype(BF16))
            shares, scaled = jnp.concatenate(shares, axis=1), jnp.concatenate(scaled, axis=1)
            dv_ref[here] += mm(shares, gbig[b])
            dk_ref[here] += mm(scaled, qbig[b])
            dq_ref[b] += head_diagonal(mm(keys, scaled, 0, 0), heads)
            return carry

        return lax.fori_loop(0, tiles(b), step, carry)

    lax.fori_loop(0, blocks, attend_back, 0)

    @pl.when(jnp.logical_not(beyond))
    def _():
        units(2, "wait")

    dw_ref[...] = jnp.zeros_like(dw_ref)

    def frame_step(i, carry):
        here = span(i)
        dk, dv = dk_ref[here].astype(BF16), dv_ref[here].astype(BF16)
        mgrad_ref[here] = (mm(dk, weight(1)) + mm(dv, weight(2))).astype(BF16)
        frame_rows = mem_ref[here]
        dw_ref[0] += mm(dk, frame_rows, 0, 0)
        dw_ref[1] += mm(dv, frame_rows, 0, 0)
        small_ref[12:13] += column_sums(dv.astype(F32))
        return carry

    lax.fori_loop(0, count, frame_step, 0)
    stores[3].start()
    dq = jnp.concatenate([(dq_ref[b] * 0.125).T for b in range(blocks)], axis=0).astype(BF16)
    small_ref[11:12] = column_sums(dq.astype(F32))
    xhat2, scale2 = normed(after_self)
    n2 = (xhat2 * gain[1:2] + shift[1:2]).astype(BF16)
    dwb_ref[:width] = mm(dq, n2, 0, 0).astype(BF16)
    dwb_ref[width : 2 * width] = dw_ref[0].astype(BF16)
    dwb_ref[2 * width : 3 * width] = dw_ref[1].astype(BF16)
    stores[2].start()
    dn2 = mm(dq, weight(0))
    small_ref[1:2] = column_sums(dn2 * xhat2)
    small_ref[4:5] = column_sums(dn2)
    grad_ref[...] = grad + norm_back(dn2, gain[1:2], xhat2, scale2)
    for store in stores:
        store.wait()


def sum_far(mgrad_in, mgrad_out, own, land, flow_sems, load_sem):
    pieces, piece = land.shape[1:3]
    frames = own.shape[0]
    parts = frames // piece // PIECES
    last = NEAR + pieces
    z, d = lax.axis_index("mp"), lax.axis_index("dp")
    barrier, greetings = greet(z, parts, d, ())
    load = pltpu.make_async_copy(mgrad_in, own, load_sem)
    load.start()

    def rows_of(number):
        return at_rows(number * piece, piece)

    def there(number):
        return (number >= 0) & (number < parts * PIECES)

    def sent(j, up):
        return (z + 1) * PIECES + j if up else z * PIECES - 1 - j

    def comes(j, up):
        return z * PIECES + j if up else (z + 1) * PIECES - 1 - j

    def flow(j, up, number, device):
        kind = 0 if up else 2
        place = land.at[0 if up else 1, j - NEAR]
        sems = flow_sems.at[kind, j - NEAR], flow_sems.at[kind + 1, j - NEAR]
        return rcopy(own.at[rows_of(number)], place, *sems, mp=device)

    def arrive(j):
        for up in (True, False):

            @pl.when(there(comes(j, up)) & (z > 0 if up else z < parts - 1))
            def _():
                number = comes(j, up)
                flow(j, up, number, z - 1 if up else z + 1).wait_recv()
                here = rows_of(number)
                more = land[0 if up else 1, j - NEAR].astype(F32)
                own[here] = (own[here].astype(F32) + more).astype(BF16)

    def each(j, name):
        for up in (True, False):

            @pl.when(there(sent(j, up)) & (z < parts - 1 if up else z > 0))
            def _():
                getattr(flow(j, up, sent(j, up), z + 1 if up else z - 1), name)()

    load.wait()
    pl.semaphore_wait(barrier, greetings)
    for j in reversed(range(NEAR, last)):
        if j + PIECES < last:
            arrive(j + PIECES)
        each(j, "start")
    for j in range(NEAR, min(NEAR + PIECES, last)):
        arrive(j)
    for j in range(NEAR, last):
        each(j, "wait_send")
    store = pltpu.make_async_copy(own, mgrad_out, load_sem)
    store.start()
    store.wait()


def masked(d, mask):
    for bit in (1, 2, 4):
        if mask & bit:
            d = flipped(d, bit)
    return d


CHIPS = (2, 4, 6)


class Reduce:
    def __init__(self, d, z, parts, dp, local, buffers, sems):
        self.d, self.z, self.parts, self.dp, self.local = d, z, parts, dp, local
        self.r1, self.a1, self.r2, self.a3, self.rz, self.a4, self.wide, self.fin = buffers
        self.high, self.low = z // 2, z % 2
        self.sems, self.extra_sems, self.plane_sems = sems
        self.c, self.y, self.x = corner(d)
        self.spread = Chips(d, self.fin, self.plane_sems)
        self.bits = [8 << i for i in range(dp.bit_length() - 4)]

    def to_core(self):
        sems = self.sems
        return rcopy(
            self.local.at[1 - self.c], self.r1, sems.at[0, 0], sems.at[1, 0], dp=flipped(self.d, 1)
        )

    def to_chip(self, i):
        sems, other = self.sems, masked(self.d, CHIPS[i])
        _, y, x = corner(other)
        return rcopy(self.a1.at[y, x], self.r2.at[i], sems.at[0, 1 + i], sems.at[1, 1 + i], dp=other)

    def to_neighbour(self):
        sems = self.sems
        src = self.a3.at[:, 1 - self.low]
        return rcopy(src, self.rz.at[:2], sems.at[0, 4], sems.at[1, 4], mp=flipped(self.z, 1))

    def to_far(self):
        sems = self.sems
        src = self.a4.at[1 - self.high]
        return rcopy(src, self.rz.at[2], sems.at[0, 5], sems.at[1, 5], mp=flipped(self.z, 2))

    def extra(self, i):
        sems = self.extra_sems
        device = flipped(self.d, self.bits[i])
        return rcopy(self.wide.at[2 * i], self.wide.at[2 * i + 1], sems.at[0, i], sems.at[1, i], dp=device)

    def run(self, p):
        if p == 0:
            self.to_core().start()
        elif p == 1:
            self.to_core().wait_recv()
            self.a1[...] = (self.local[self.c].astype(F32) + self.r1[...].astype(F32)).astype(BF16)
            for i in range(3):
                self.to_chip(i).start()
        elif p == 2:
            total = self.a1[self.y, self.x].astype(F32)
            for i in range(3):
                self.to_chip(i).wait_recv()
                total = total + self.r2[i].astype(F32)
            self.a3[...] = total.astype(BF16).reshape(self.a3.shape)
            self.to_neighbour().start()
        elif p == 3:
            self.to_neighbour().wait_recv()
            mine = self.a3[:, self.low].astype(F32) + self.rz[:2].astype(F32)
            self.a4[...] = mine.astype(BF16)
            self.to_far().start()
        elif p == 4:
            self.to_far().wait_recv()
            total = self.a4[self.high].astype(F32) + self.rz[2].astype(F32)
            for i in range(len(self.bits)):
                self.wide[2 * i] = total
                self.extra(i).start()
                self.extra(i).wait_recv()
                total = total + self.wide[2 * i + 1]
            self.fin[self.c, self.y, self.x] = total.astype(BF16)
            self.spread.send(0)
        elif p == 5:
            self.spread.arrived(0)
            self.spread.send(1)
        else:
            self.spread.arrived(1)

    def close(self):
        self.to_core().wait_send()
        for i in range(3):
            self.to_chip(i).wait_send()
        self.to_neighbour().wait_send()
        self.to_far().wait_send()
        for i in range(len(self.bits)):
            self.extra(i).wait_send()
        self.spread.close()


class Spread:
    def __init__(self, d, buffer, sems):
        self.d, self.buffer, self.sems = d, buffer, sems

    def copy(self, m, own):
        neighbour = masked(self.d, m)
        c, y, x = corner(self.d if own else neighbour)
        block = self.buffer.at[c, y, x]
        return rcopy(block, block, self.sems.at[0, m], self.sems.at[1, m], dp=neighbour)

    def send(self):
        for m in range(1, 8):
            self.copy(m, True).start()

    def arrived(self):
        for m in range(1, 8):
            self.copy(m, False).wait_recv()

    def close(self):
        for m in range(1, 8):
            self.copy(m, True).wait_send()


class Chips:
    def __init__(self, d, buffer, sems):
        self.d, self.buffer, self.sems = d, buffer, sems

    def copy(self, m, own):
        neighbour = masked(self.d, m)
        c, y, x = corner(self.d if own else neighbour)
        block = self.buffer.at[c] if m == 1 else self.buffer.at[c, y, x]
        return rcopy(block, block, self.sems.at[0, m], self.sems.at[1, m], dp=neighbour)

    def send(self, p):
        for m in (CHIPS, (1,))[p]:
            self.copy(m, True).start()

    def arrived(self, p):
        for m in (CHIPS, (1,))[p]:
            self.copy(m, False).wait_recv()

    def close(self):
        for m in (1, 2, 4, 6):
            self.copy(m, True).wait_send()


class Total:
    def __init__(self, d, z, bits, buffer, wide, sems, wide_sems):
        self.d, self.z, self.bits, self.wide, self.wide_sems = d, z, bits, wide, wide_sems
        self.buffer = buffer
        self.spread = Spread(d, buffer, sems)

    def extra(self, i):
        sems, count = self.wide_sems, len(self.bits)
        if i < count:
            device = {"dp": flipped(self.d, self.bits[i])}
        else:
            device = {"mp": flipped(self.z, 1 if i == count else 2)}
        return rcopy(self.wide.at[2 * i], self.wide.at[2 * i + 1], sems.at[0, i], sems.at[1, i], **device)

    def run(self, p):
        count = len(self.bits)
        if p == 0:
            self.spread.send()
        elif p == 1:
            self.spread.arrived()
            total = self.buffer[0, 0, 0]
            for c, y, x in [(i // 4, i // 2 % 2, i % 2) for i in range(1, 8)]:
                total = total + self.buffer[c, y, x]
            for i in range(count):
                self.wide[2 * i] = total
                self.extra(i).start()
                self.extra(i).wait_recv()
                total = total + self.wide[2 * i + 1]
            self.wide[2 * count] = total
            self.extra(count).start()
        else:
            self.extra(count).wait_recv()
            self.wide[2 * count + 2] = self.wide[2 * count] + self.wide[2 * count + 1]
            self.extra(count + 1).start()

    def finish(self, out):
        last = len(self.bits) + 1
        self.extra(last).wait_recv()
        out[...] = self.wide[2 * last] + self.wide[2 * last + 1]
        self.spread.close()
        for i in range(last + 1):
            self.extra(i).wait_send()


def give_back(
    window,
    tok, frm, small_in, gain,
    x_in, n1_in, q_in, k_in, v_in, att_in, grad_in, w_in, mgrad_in, dwc_in, dwi_in, dwo_in,
    input_out, mgrad_out, fself, fcross, finner, fouter, small_out,
    x_ref, n1_ref, q_ref, k_ref, v_ref, att_ref, grad_ref, w_ref,
    own, up_land, down_land, local_self, local_cross, local_inner, local_outer,
    dk_ref, dv_ref, dq_ref, halo_out, halo_land, total_buffer, total_wide,
    self_bufs, cross_bufs, inner_bufs, outer_bufs,
    load_sems, flow_sems, reduce_sems, extra_sems, plane_sems, halo_sems, total_sems, wide_sems,
):
    rows, width = q_ref.shape
    heads = width // HEAD
    parts = lax.axis_size("mp")
    shard_rows = mgrad_out.shape[0]
    piece = shard_rows // PIECES
    last = parts * PIECES
    z, d = lax.axis_index("mp"), lax.axis_index("dp")
    dp = lax.axis_size("dp")
    bits = [8 << i for i in range(dp.bit_length() - 4)]
    barrier, greetings = greet(z, parts, d, bits, range(1, 8))
    loads = [
        pltpu.make_async_copy(a, b, load_sems.at[i])
        for i, (a, b) in enumerate(
            (
                (dwi_in, local_inner),
                (dwo_in, local_outer),
                (dwc_in, local_cross),
                (grad_in, grad_ref),
                (w_in, w_ref),
                (q_in, q_ref),
                (k_in, k_ref),
                (v_in, v_ref),
                (n1_in, n1_ref),
                (att_in, att_ref),
                (x_in, x_ref),
                (mgrad_in, own),
            )
        )
    ]
    for load in loads:
        load.start()
    chains = []
    for i, (local, bufs, fin) in enumerate(
        (
            (local_inner, inner_bufs, finner),
            (local_outer, outer_bufs, fouter),
            (local_cross, cross_bufs, fcross),
            (local_self, self_bufs, fself),
        )
    ):
        sems = (reduce_sems.at[i], extra_sems.at[i], plane_sems.at[i])
        chains.append(Reduce(d, z, parts, dp, local, (*bufs, fin), sems))
    inner, outer, cross, own_chain = chains

    def rows_of(number):
        return at_rows(number * piece, piece)

    def crosses(j, up):
        if up:
            return (z < parts - 1) & ((z + 1) * PIECES + j < last)
        return (z > 0) & (z * PIECES - 1 - j >= 0)

    def number(j, up):
        return (z + 1) * PIECES + j if up else z * PIECES - 1 - j

    def flow(j, up, summed):
        land = up_land if up else down_land
        kind = 0 if up else 2
        src = land.at[j + PIECES] if summed else mgrad_in.at[rows_of(number(j, up))]
        device = z + 1 if up else z - 1
        return rcopy(src, land.at[j], flow_sems.at[kind, j], flow_sems.at[kind + 1, j], mp=device)

    def comes(j, up):
        if up:
            return (z > 0) & (z * PIECES + j < last)
        return (z < parts - 1) & ((z + 1) * PIECES - 1 - j >= 0)

    def flow_arrival(j, up):
        land = up_land if up else down_land
        kind = 0 if up else 2
        device = z - 1 if up else z + 1
        return rcopy(
            land.at[j], land.at[j], flow_sems.at[kind, j], flow_sems.at[kind + 1, j], mp=device
        )

    def first_flows(pieces):
        for j in pieces:
            for up in (True, False):

                @pl.when(crosses(j, up))
                def _():
                    flow(j, up, False).start()

    def next_flow(j):
        for up in (True, False):
            land = up_land if up else down_land

            @pl.when(crosses(j, up) & comes(j + PIECES, up))
            def _():
                flow_arrival(j + PIECES, up).wait_recv()
                mine = own[rows_of(number(j, up))]
                land[j + PIECES] = (land[j + PIECES].astype(F32) + mine.astype(F32)).astype(BF16)
                flow(j, up, True).start()

            @pl.when(crosses(j, up) & jnp.logical_not(comes(j + PIECES, up)))
            def _():
                flow(j, up, False).start()

    base = z * rows
    place, first_row, _, _ = token_rows(tok, frm, base, rows)

    def weight(i):
        return w_ref[i * width : (i + 1) * width]

    def halo_copy(other):
        return rcopy(halo_out, halo_land, halo_sems.at[0], halo_sems.at[1], mp=other)

    pl.semaphore_wait(barrier, greetings)
    first_flows((5, 4))
    for load, chain in zip(loads[:3], chains[:3]):
        load.wait()
        chain.run(0)
    c, y, x = corner(d)
    small = total_buffer.at[c, y, x]
    small[...] = small_in[...]
    loads[3].wait()
    loads[4].wait()
    grad = grad_ref[...]
    sent = grad.astype(BF16)
    small[6:7] = column_sums(sent.astype(F32))
    n = local_self.shape[3]

    def keep(i, values):
        for half in range(2):
            s = 2 * i + half
            local_self[s // 4, s // 2 % 2, s % 2] = values[half * n : (half + 1) * n].astype(BF16)

    go = mm(sent, weight(3), 1, 1).astype(BF16)
    dk_ref[...] = jnp.zeros_like(dk_ref)
    dv_ref[...] = jnp.zeros_like(dv_ref)
    count = HALO + BLOCK
    blocks = rows // BLOCK

    def attend_back(b):
        here = slice(b * BLOCK, (b + 1) * BLOCK)
        span = slice(b * BLOCK, b * BLOCK + count)
        queries, grads = head_stack(q_ref[here]), head_stack(go[here])
        mask = window_mask(place, first_row, base, b, count)
        shares = self_probs(queries, k_ref[span], mask, heads)
        dp_ = mm(v_ref[span], grads, 1, 1)
        ds = (shares * (dp_ - jnp.sum(shares * dp_, axis=0, keepdims=True))).astype(BF16)
        dv_ref[span] += mm(shares.astype(BF16), grads)
        dk_ref[span] += mm(ds, queries)
        dq_ref[here] = (head_diagonal(mm(k_ref[span], ds, 0, 0), heads) * 0.125).T.astype(BF16)

    def to_norm(here):
        return mm(dk_ref[here].astype(BF16), weight(1)) + mm(dv_ref[here].astype(BF16), weight(2))

    for chain in chains[:3]:
        chain.run(1)
    for load in loads[5:8]:
        load.wait()
    reaching = HALO // BLOCK
    for b in range(reaching):
        attend_back(b)
    halo_out[...] = to_norm(slice(0, HALO)).astype(BF16)

    @pl.when(z > 0)
    def _():
        halo_copy(z - 1).start()

    first_flows((3, 2))
    for b in range(reaching, blocks):
        attend_back(b)
    dq = dq_ref[...]
    dk, dv = dk_ref[...].astype(BF16), dv_ref[...].astype(BF16)
    for load in loads[8:]:
        load.wait()
    n1 = n1_ref[...]
    keep(0, mm(dq, n1[HALO:], 0, 0))
    keep(1, mm(dk, n1, 0, 0))
    keep(2, mm(dv, n1, 0, 0))
    keep(3, mm(att_ref[...], sent, 0, 0))
    own_chain.run(0)
    small[9:10] = column_sums(dq.astype(F32))
    small[10:11] = column_sums(dv.astype(F32))
    dn = to_norm(slice(HALO, HALO + rows)) + mm(dq, weight(0))
    xhat, scale = normed(x_ref[...].astype(F32))
    own_chain.run(1)

    @pl.when(z < parts - 1)
    def _():
        halo_copy(z + 1).wait_recv()

    @pl.when(z == parts - 1)
    def _():
        halo_land[...] = jnp.zeros_like(halo_land)

    dn = jnp.concatenate([dn[: rows - HALO], dn[rows - HALO :] + halo_land[...].astype(F32)], axis=0)
    small[0:1] = column_sums(dn * xhat)
    small[3:4] = column_sums(dn)
    total = Total(d, z, bits, total_buffer, total_wide, total_sems, wide_sems)
    total.run(0)
    input_out[...] = grad + norm_back(dn, gain[0:1], xhat, scale)
    for chain in chains[:3]:
        chain.run(2)
    next_flow(1)
    own_chain.run(2)
    for chain in chains[:3]:
        chain.run(3)
    total.run(1)
    own_chain.run(3)
    next_flow(0)
    for chain in chains[:3]:
        chain.run(4)
    total.run(2)
    own_chain.run(4)
    for p in range(5, 7):
        for chain in chains:
            chain.run(p)

    @pl.when(z == 0)
    def _():
        up_land[:PIECES] = jnp.zeros((PIECES, piece, width), BF16)

    @pl.when(z == parts - 1)
    def _():
        down_land[:PIECES] = jnp.zeros((PIECES, piece, width), BF16)

    for i in range(PIECES):
        for up in (True, False):
            j = i if up else PIECES - 1 - i

            @pl.when(comes(j, up))
            def _():
                flow_arrival(j, up).wait_recv()

        mine = own[rows_of(z * PIECES + i)].astype(F32)
        sides = up_land[i].astype(F32) + down_land[PIECES - 1 - i].astype(F32)
        mgrad_out[i * piece : (i + 1) * piece] = (mine + sides).astype(BF16)
    total.finish(small_out)
    for chain in chains:
        chain.close()

    @pl.when(z > 0)
    def _():
        halo_copy(z - 1).wait_send()

    for j in range(window):
        for up in (True, False):
            @pl.when(crosses(j, up))
            def _():
                flow(j, up, False).wait_send()


def finals(
    mgrad, input_grad, fself, fcross, finner, fouter, small,
    out_mgrad, out_input, out_gain, out_shift, out_sw, out_sb, out_so, out_soff,
    out_cw, out_cb, out_co, out_coff, out_inner, out_ib, out_outer, out_ooff,
):
    z = lax.axis_index("mp")
    own = out_so.shape[0]
    parts = out_so.shape[1] // own
    out_mgrad[...] = mgrad[...].astype(F32)
    out_input[...] = input_grad[...]
    out_gain[...] = small[0:3]
    out_shift[...] = small[3:6]
    out_soff[...] = small[6:7]
    out_coff[...] = small[7:8]
    out_ooff[...] = small[8:9]

    def chosen(row, size, offset):
        pieces = [small[row : row + 1, offset + o * size : offset + (o + 1) * size] for o in range(parts)]
        result = pieces[0]
        for o in range(1, parts):
            result = jnp.where(z == o, pieces[o], result)
        return result

    for fin, weights, last, biases, first in (
        (fself, out_sw, out_so, out_sb, 9),
        (fcross, out_cw, out_co, out_cb, 11),
    ):
        for i in range(3):
            weights[i] = fin[i // 2, i % 2].reshape(own, -1).astype(F32)
        last[...] = fin[1, 1].reshape(own, -1).astype(F32)
        for i in range(2):
            for half in range(2):
                lanes = slice(half * HALF, (half + 1) * HALF)
                biases[i : i + 1, lanes] = chosen(first + i, HALF, half * parts * HALF)
    out_inner[...] = finner[...].reshape(out_outer.shape).astype(F32).T
    out_outer[...] = fouter[...].reshape(out_outer.shape).astype(F32)
    size = out_ib.shape[1] // SLICES
    for s in range(SLICES):
        out_ib[0:1, s * size : (s + 1) * size] = chosen(16 + s, size, 0)


def call(body, outs, ins, scratch, limit, **params):
    places = {"s": pltpu.SMEM, "v": pltpu.VMEM, "h": pl.ANY}

    def spec(place):
        return pl.BlockSpec(memory_space=places[place])

    def run(*args):
        return pl.pallas_call(
            body,
            out_shape=[jax.ShapeDtypeStruct(shape, kind) for shape, kind, _ in outs],
            in_specs=[spec(place) for place in ins],
            out_specs=[spec(place) for _, _, place in outs],
            scratch_shapes=[pltpu.VMEM(*x) if isinstance(x, tuple) else x for x in scratch],
            compiler_params=pltpu.CompilerParams(vmem_limit_bytes=limit << 20, **params),
        )(*args)

    return run


def shards(
    block_input,
    memory,
    tok_lengths,
    frame_lengths,
    cotangent,
    norm_gain,
    norm_shift,
    self_weights,
    self_biases,
    self_output,
    self_offset,
    cross_weights,
    cross_biases,
    cross_output,
    cross_offset,
    inner_weight,
    inner_bias,
    outer_weight,
    outer_offset,
):
    rows, width = block_input.shape
    parts = lax.axis_size("mp")
    frames = memory.shape[0] * parts
    heads = width // HEAD
    blocks = rows // BLOCK
    own_hidden = inner_weight.shape[1]
    hidden = own_hidden * parts
    own = width // parts
    dma = pltpu.SemaphoreType.DMA
    wide = heads * BLOCK

    n_att, n_ffn = own * 4 // SLICES, own_hidden // SLICES
    n_bits = lax.axis_size("dp").bit_length() - 1
    piece = memory.shape[0] // PIECES
    small_rows = 16 + SLICES
    own_rows = (rows, width)
    halo_rows = (rows + HALO, width)

    def sliced(n):
        return (2, 2, 2, n, width)

    def turned(weights):
        return jnp.swapaxes(weights, 1, 2)

    (
        wself, wcross, inner, outer, inner_row, value_row, far, memory_rows, ck, cv, spare, n1, q, k, v, att, after, cq
    ) = call(
        gather,
        [
            (sliced(parts * n_att), BF16, "h"),
            (sliced(parts * n_att), BF16, "h"),
            (sliced(parts * n_ffn), BF16, "h"),
            (sliced(parts * n_ffn), BF16, "h"),
            ((SLICES, hidden // SLICES), F32, "v"),
            ((1, width), F32, "v"),
            ((1, 1), F32, "v"),
            ((frames, width), BF16, "h"),
            ((frames, width), BF16, "h"),
            ((frames, width), BF16, "h"),
            ((parts * frames, width), BF16, "h"),
            (halo_rows, BF16, "v"),
            (own_rows, BF16, "v"),
            (halo_rows, BF16, "v"),
            (halo_rows, BF16, "v"),
            (own_rows, BF16, "v"),
            (own_rows, F32, "v"),
            (own_rows, BF16, "v"),
        ],
        "ssvhvvvvvvvvvvvv",
        [
            (sliced(parts * n_att), BF16),
            (sliced(parts * n_att), BF16),
            (sliced(parts * n_ffn), BF16),
            (sliced(parts * n_ffn), BF16),
            ((frames, width), BF16),
            ((frames, width), BF16),
            ((frames, width), BF16),
            ((4 * own, width), BF16),
            ((4 * own, width), BF16),
            ((own_hidden, width), BF16),
            ((HALO, width), BF16),
            ((8, own_hidden), F32),
            ((parts, 8, own_hidden), F32),
            ((n_bits + 1, 8, 128), F32),
            ((n_bits, 8, 128), F32),
            dma((4, 2, 3)),
            dma((4, NEAR)),
            dma((4, 2, 3)),
            dma((2, 3)),
            dma((2,)),
            dma((2, n_bits)),
            dma,
            dma((parts * PIECES, 3)),
            dma((4,)),
        ],
        56,
        collective_id=0,
        has_side_effects=True,
    )(
        tok_lengths, frame_lengths, block_input, memory, turned(self_weights), self_output,
        turned(cross_weights), cross_output, inner_weight, outer_weight, self_biases, cross_biases,
        inner_bias.reshape(1, own_hidden), norm_gain, norm_shift, self_offset.reshape(1, width),
    )
    wcross_rows = wcross.reshape(4 * width, width)
    wself_rows = wself.reshape(4 * width, width)
    inner_rows, outer_rows = inner.reshape(hidden, width), outer.reshape(hidden, width)

    def reduce_buffers(n):
        full = parts * n
        return [
            pltpu.VMEM((2, 2, full, width), BF16),
            pltpu.VMEM((2, 2, full, width), BF16),
            pltpu.VMEM((3, full, width), BF16),
            pltpu.VMEM((parts // 2, 2, n, width), BF16),
            pltpu.VMEM((3, n, width), BF16),
            pltpu.VMEM((2, n, width), BF16),
            pltpu.VMEM((2 * max(n_bits - 3, 1), n, width), F32),
        ]

    window = PIECES * (parts - 1)
    far_shape = (2, window - NEAR, piece, width)
    beyond = far[0, 0] > NEAR * piece

    def fetch_far():
        (far_memory,) = call(
            gather_far,
            [((parts * frames, width), BF16, "h")],
            "h",
            [dma((4, window))],
            8,
            collective_id=2,
            has_side_effects=True,
        )(memory_rows)
        return far_memory

    far_memory = lax.cond(beyond, fetch_far, lambda: spare)
    padded = (frames + TILE, width)
    grad, small, block_output, mgrad, dw_cross, dwi, dwo = call(
        middle,
        [
            (own_rows, F32, "v"),
            ((small_rows, width), F32, "v"),
            (own_rows, F32, "h"),
            ((frames, width), BF16, "h"),
            ((4 * width, width), BF16, "h"),
            ((hidden, width), BF16, "h"),
            ((hidden, width), BF16, "h"),
        ],
        "sssvvvvvvvhhhhhhhhh",
        [
            (own_rows, F32),
            (own_rows, BF16),
            ((4 * width, width), BF16),
            (own_rows, F32),
            (padded, BF16),
            (padded, BF16),
            (padded, BF16),
            ((hidden, width), BF16),
            ((hidden, width), BF16),
            (padded, BF16),
            ((2, width, width), F32),
            ((4 * width, width), BF16),
            ((hidden, width), BF16),
            ((hidden, width), BF16),
            ((blocks, wide, width), BF16),
            ((blocks, wide, width), BF16),
            ((blocks, 1, wide), F32),
            ((blocks, 1, wide), F32),
            ((blocks, width, BLOCK), F32),
            ((blocks, width, BLOCK), F32),
            (padded, F32),
            (padded, F32),
            ((blocks, 1, BLOCK), jnp.int32),
            ((blocks, 1, BLOCK), jnp.int32),
            pltpu.SMEM((2, blocks), jnp.int32),
            dma((5,)),
            dma((5,)),
            dma((3, frames // UNIT)),
            dma((3,)),
        ],
        56,
    )(
        far, tok_lengths, frame_lengths, cq, inner_row, value_row, norm_gain,
        norm_shift, cross_offset.reshape(1, width), outer_offset.reshape(1, width),
        after, cotangent, wcross_rows, ck, cv, memory_rows, far_memory, inner_rows, outer_rows,
    )

    def return_far():
        (summed,) = call(
            sum_far,
            [((frames, width), BF16, "h")],
            "h",
            [((frames, width), BF16), (far_shape, BF16), dma((4, window - NEAR)), dma],
            16,
            collective_id=3,
            has_side_effects=True,
        )(mgrad)
        return summed

    mgrad = lax.cond(beyond, return_far, lambda: mgrad)
    partial_results = call(
        functools.partial(give_back, NEAR),
        [
            (own_rows, F32, "v"),
            ((frames // parts, width), BF16, "v"),
            (sliced(n_att), BF16, "v"),
            (sliced(n_att), BF16, "v"),
            (sliced(n_ffn), BF16, "v"),
            (sliced(n_ffn), BF16, "v"),
            ((small_rows, width), F32, "v"),
        ],
        "ssvvhhhhhhhhhhhh",
        [
            (own_rows, BF16),
            (halo_rows, BF16),
            (own_rows, BF16),
            (halo_rows, BF16),
            (halo_rows, BF16),
            (own_rows, BF16),
            (own_rows, F32),
            ((4 * width, width), BF16),
            ((frames, width), BF16),
            ((NEAR, piece, width), BF16),
            ((NEAR, piece, width), BF16),
            (sliced(parts * n_att), BF16),
            (sliced(parts * n_att), BF16),
            (sliced(parts * n_ffn), BF16),
            (sliced(parts * n_ffn), BF16),
            (halo_rows, F32),
            (halo_rows, F32),
            (own_rows, BF16),
            ((HALO, width), BF16),
            ((HALO, width), BF16),
            ((2, 2, 2, small_rows, width), F32),
            ((2 * (n_bits - 1), small_rows, width), F32),
            reduce_buffers(n_att),
            reduce_buffers(n_att),
            reduce_buffers(n_ffn),
            reduce_buffers(n_ffn),
            dma((12,)),
            dma((4, NEAR)),
            dma((4, 2, 6)),
            dma((4, 2, max(n_bits - 3, 1))),
            dma((4, 2, 8)),
            dma((2,)),
            dma((2, 8)),
            dma((2, n_bits - 1)),
        ],
        56,
        collective_id=1,
        has_side_effects=True,
    )(
        tok_lengths, frame_lengths, small, norm_gain, block_input, n1, q, k, v, att, grad, wself_rows,
        mgrad, dw_cross.reshape(sliced(parts * n_att)), dwi.reshape(sliced(parts * n_ffn)),
        dwo.reshape(sliced(parts * n_ffn)),
    )
    input_grad, mgrad_sum, fself, fcross, finner, fouter, small = partial_results
    results = call(
        finals,
        [
            ((frames // parts, width), F32, "v"),
            (own_rows, F32, "v"),
            ((3, width), F32, "v"),
            ((3, width), F32, "v"),
            ((3, own, width), F32, "v"),
            ((2, own), F32, "v"),
            ((own, width), F32, "v"),
            ((1, width), F32, "v"),
            ((3, own, width), F32, "v"),
            ((2, own), F32, "v"),
            ((own, width), F32, "v"),
            ((1, width), F32, "v"),
            ((width, own_hidden), F32, "v"),
            ((1, own_hidden), F32, "v"),
            ((own_hidden, width), F32, "v"),
            ((1, width), F32, "v"),
        ],
        "vvvvvvv",
        [],
        56,
    )(mgrad_sum, input_grad, fself, fcross, finner, fouter, small)
    memory_grad, input_grad, *others = results
    others = [r.reshape(-1) if r.shape[0] == 1 else r for r in others]
    others[2], others[6] = turned(others[2]), turned(others[6])
    return (block_output, input_grad, memory_grad, *others)


def solution(mesh):
    in_specs = (
        P(("dp", "mp"), None),
        P(("dp", "mp"), None),
        P("dp", None),
        P("dp", None),
        P(("dp", "mp"), None),
        P(),
        P(),
        P(None, None, "mp"),
        P(None, "mp"),
        P("mp", None),
        P(),
        P(None, None, "mp"),
        P(None, "mp"),
        P("mp", None),
        P(),
        P(None, "mp"),
        P("mp"),
        P("mp", None),
        P(),
    )
    out_specs = (
        P(("dp", "mp"), None),
        P(("dp", "mp"), None),
        P(("dp", "mp"), None),
        P(),
        P(),
        P(None, None, "mp"),
        P(None, "mp"),
        P("mp", None),
        P(),
        P(None, None, "mp"),
        P(None, "mp"),
        P("mp", None),
        P(),
        P(None, "mp"),
        P("mp"),
        P("mp", None),
        P(),
    )
    return jax.shard_map(shards, mesh=mesh, in_specs=in_specs, out_specs=out_specs, check_vma=False)
```

```python
import functools
import math

import jax
import jax.numpy as jnp
from jax import lax
from jax.experimental import pallas as pl
from jax.experimental.pallas import tpu as pltpu
from jax.sharding import PartitionSpec as P

HEAD = 64
NEGATIVE = -1e30
EPSILON = 1e-05
BLOCK = 128
TILE = 512
UNIT = 128
SIZES = (1024, 512, 256)
HALO = 256
F32 = jnp.float32
BF16 = jnp.bfloat16
MESH = pl.DeviceIdType.MESH
HALF = HEAD // 2
SLICES = 8
PIECES = 4
NEAR = 6
GELU_A = math.sqrt(2.0 / math.pi)
GELU_B = 0.044715


def mm(a, b, ca=1, cb=0):
    return lax.dot_general(a, b, (((ca,), (cb,)), ((), ())), preferred_element_type=F32)


def normed(values):
    center = values - jnp.mean(values, axis=-1, keepdims=True)
    spread = jnp.mean(center * center, axis=-1, keepdims=True)
    scale = lax.rsqrt(spread + EPSILON)
    return center * scale, scale


def norm_back(grad, gain, xhat, scale):
    gn = grad * gain
    first = jnp.mean(gn, axis=-1, keepdims=True)
    second = jnp.mean(gn * xhat, axis=-1, keepdims=True)
    return (gn - first - xhat * second) * scale


def column_sums(values):
    return jnp.sum(values, axis=0, keepdims=True)


def head_stack(values):
    rows, width = values.shape
    heads = width // HEAD
    lane = lax.broadcasted_iota(jnp.int32, (rows, width), 1) // HALF % heads
    zero = jnp.zeros_like(values)
    return jnp.concatenate([jnp.where(lane == h, values, zero) for h in range(heads)], axis=0)


def head_rows(heads):
    return [
        (slice((i * heads + h) * HALF, (i * heads + h + 1) * HALF), h)
        for i in range(2)
        for h in range(heads)
    ]


def head_diagonal(values, heads):
    rows = values.shape[1] // heads
    return jnp.concatenate(
        [values[r, h * rows : (h + 1) * rows] for r, h in head_rows(heads)], axis=0
    )


def token_rows(tok_ref, frm_ref, base, count):
    place = lax.broadcasted_iota(jnp.int32, (1, count), 1) + base
    zero = jnp.zeros((1, count), jnp.int32)

    def step(u, carry):
        start, first_row, first_frame, end_frame = carry
        tokens, frames = tok_ref[0, u], frm_ref[0, u]
        end = start + tokens
        done = place >= end
        first_row = first_row + jnp.where(done, tokens, 0)
        first_frame = first_frame + jnp.where(done, frames, 0)
        end_frame = end_frame + jnp.where(place >= start, frames, 0)
        return end, first_row, first_frame, end_frame

    _, first_row, first_frame, end_frame = lax.fori_loop(
        0, tok_ref.shape[1], step, (jnp.int32(0), zero, zero, zero)
    )
    return place, first_row, first_frame, end_frame


def excursion(tok_ref, frm_ref, rows, frames, parts):
    lane = lax.broadcasted_iota(jnp.int32, (1, 128), 1)
    zero = jnp.zeros((1, 128), jnp.int32)

    def step(u, carry):
        start, low, high = carry
        tokens, count = tok_ref[0, u], frm_ref[0, u]
        end = start + tokens
        low = low + jnp.where(lane * rows >= end, count, 0)
        high = high + jnp.where((lane + 1) * rows - 1 >= start, count, 0)
        return end, low, high

    _, low, high = lax.fori_loop(0, tok_ref.shape[1], step, (jnp.int32(0), zero, zero))
    beyond = jnp.maximum(high - (lane + 1) * frames, lane * frames - low)
    return jnp.max(jnp.where(lane < parts, beyond, 0), axis=1, keepdims=True).astype(F32)


def block_frames(tok_ref, frm_ref, base):
    lane = lax.broadcasted_iota(jnp.int32, (1, 128), 1) * BLOCK + base
    zero = jnp.zeros((1, 128), jnp.int32)

    def step(u, carry):
        start, low, high = carry
        tokens, frames = tok_ref[0, u], frm_ref[0, u]
        end = start + tokens
        low = low + jnp.where(lane >= end, frames, 0)
        high = high + jnp.where(lane + (BLOCK - 1) >= start, frames, 0)
        return end, low, high

    _, low, high = lax.fori_loop(0, tok_ref.shape[1], step, (jnp.int32(0), zero, zero))
    return low // UNIT * UNIT, high


def window_mask(place, first_row, base, block, count):
    keys = lax.broadcasted_iota(jnp.int32, (count, BLOCK), 0) + (base - HALO + block * BLOCK)
    here = slice(block * BLOCK, (block + 1) * BLOCK)
    return (keys >= first_row[:, here]) & (keys <= place[:, here])


def self_probs(queries, key_window, mask, heads):
    scores = mm(key_window, queries, 1, 1)
    parts = []
    for h in range(heads):
        part = jnp.where(mask, scores[:, h * BLOCK : (h + 1) * BLOCK], NEGATIVE)
        raised = jnp.exp(part - jnp.max(part, axis=0, keepdims=True))
        parts.append(raised * (1.0 / jnp.sum(raised, axis=0, keepdims=True)))
    return jnp.concatenate(parts, axis=1)


def rcopy(src, dst, send, recv, **device):
    return pltpu.make_async_remote_copy(
        src_ref=src, dst_ref=dst, send_sem=send, recv_sem=recv, device_id=device, device_id_type=MESH
    )


def at_rows(start, count):
    return pl.ds(pl.multiple_of(start, 16), count)


def flipped(index, bit):
    return index + bit - 2 * bit * (index // bit % 2)


def greet(z, parts, d, bits, masks=()):
    barrier = pltpu.get_barrier_semaphore()
    for mask in masks:
        device = {"dp": masked(d, mask)}
        pl.semaphore_signal(barrier, inc=1, device_id=device, device_id_type=MESH)
    for step in range(1, parts):
        device = {"mp": (z + step) % parts}
        pl.semaphore_signal(barrier, inc=1, device_id=device, device_id_type=MESH)
    for bit in bits:
        device = {"dp": flipped(d, bit)}
        pl.semaphore_signal(barrier, inc=1, device_id=device, device_id_type=MESH)
    return barrier, parts - 1 + len(bits) + len(masks)


class Double:
    def __init__(self, z, own, place, sems):
        self.z, self.own, self.place, self.sems = z, own, place, sems

    def copies(self, step, other):
        z = self.z
        if step == 0:
            far = flipped(z, 2)
            blocks = [(self.place(far) if other else self.own, self.place(far if other else z), 0)]
            device = far
        else:
            device = flipped(z, 1)
            first = device if other else z
            blocks = [(self.place(i), self.place(i), k) for k, i in ((1, first), (2, flipped(first, 2)))]
        sems = self.sems
        return [rcopy(src, dst, sems.at[0, k], sems.at[1, k], mp=device) for src, dst, k in blocks]

    def send(self, step):
        for copy in self.copies(step, False):
            copy.start()

    def arrived(self, step):
        for copy in self.copies(step, True):
            copy.wait_recv()

    def close(self):
        for step in range(2):
            for copy in self.copies(step, False):
                copy.wait_send()


DP_BITS = (2, 4, 1)


def corner(d):
    return d % 2, d // 4 % 2, d // 2 % 2


class Plane:
    def __init__(self, d, buffer, first_y, sems):
        self.d, self.buffer, self.first_y, self.sems = d, buffer, first_y, sems

    def block(self, p, c, y, x):
        if p == 0:
            return self.buffer.at[c, y, x]
        if p == 2:
            return self.buffer.at[c]
        return self.buffer.at[c, :, x] if self.first_y else self.buffer.at[c, y]

    def copy(self, p, other):
        c, y, x = corner(self.d)
        over_y = p == (0 if self.first_y else 1)
        if other:
            if p == 2:
                c = 1 - c
            elif over_y:
                y = 1 - y
            else:
                x = 1 - x
        block = self.block(p, c, y, x)
        device = flipped(self.d, 1 if p == 2 else 4 if over_y else 2)
        return rcopy(block, block, self.sems.at[0, p], self.sems.at[1, p], dp=device)

    def send(self, p):
        self.copy(p, False).start()

    def arrived(self, p):
        self.copy(p, True).wait_recv()

    def close(self):
        for p in range(3):
            self.copy(p, False).wait_send()


class Window:
    def __init__(self, z, parts, source, place, sems):
        self.z, self.parts, self.source, self.place, self.sems = z, parts, source, place, sems

    def number(self, z, j, up):
        return (z + 1) * PIECES - 1 - j if up else z * PIECES + j

    def there(self, number):
        return (number >= 0) & (number < self.parts * PIECES)

    def copy(self, j, up):
        number = self.number(self.z, j, up)
        place, kind = self.place(number, j, up), 0 if up else 2
        return rcopy(
            self.source(number, j, up),
            place,
            self.sems.at[kind, j],
            self.sems.at[kind + 1, j],
            mp=self.z + 1 if up else self.z - 1,
        )

    def sends(self, j, up):
        edge = self.z < self.parts - 1 if up else self.z > 0
        return edge & self.there(self.number(self.z, j, up))

    def send(self, j):
        for up in (True, False):

            @pl.when(self.sends(j, up))
            def _():
                self.copy(j, up).start()

    def comes(self, j, up):
        edge = self.z > 0 if up else self.z < self.parts - 1
        return edge & self.there(self.arrival(j, up))

    def arrival(self, j, up):
        return self.number(self.z - 1 if up else self.z + 1, j, up)

    def arrived(self, j):
        for up in (True, False):

            @pl.when(self.comes(j, up))
            def _():
                number = self.arrival(j, up)
                place, kind = self.place(number, j, up), 0 if up else 2
                rcopy(
                    place,
                    place,
                    self.sems.at[kind, j],
                    self.sems.at[kind + 1, j],
                    mp=self.z - 1 if up else self.z + 1,
                ).wait_recv()

    def each(self, j, use):
        for up in (True, False):

            @pl.when(self.comes(j, up))
            def _():
                use(self.arrival(j, up), j, up)

    def close(self, pieces):
        for j in pieces:
            for up in (True, False):

                @pl.when(self.sends(j, up))
                def _():
                    self.copy(j, up).wait_send()


def gather(
    tok, frm, x_ref, mem, sw, so, cw, co, inner, outer, sb, cb, ib, gain, shift, offset,
    wself_out, wcross_out, inner_out, outer_out, ib_out, vb_out, segment_out, bounds_out, far_out, mem_out, ck_out, cv_out, spare,
    n1_out, q_out, k_out, v_out, att_out, after_out, cq_out,
    n1_ref, q_ref, k_ref, v_ref, att_ref, after_ref, cq_ref,
    gself, gcross, ginner, gouter, gmem, sck, scv, pself, pcross, pinner, halo, pbias, gbias,
    far, far_land, line_sems, mem_sems, plane_sems, bias_sems, halo_sems, far_sems, own_sem, out_sems, weight_sems, row_sems,
):
    rows, width = x_ref.shape
    heads = width // HEAD
    own = sw.shape[1]
    parts = width // own
    shard_rows = mem.shape[0]
    piece = shard_rows // PIECES
    z, d = lax.axis_index("mp"), lax.axis_index("dp")
    dp = lax.axis_size("dp")
    bits = [1 << i for i in range(dp.bit_length() - 1)]
    c, y, x = corner(d)
    s = c * 4 + y * 2 + x
    barrier, greetings = greet(z, parts, d, bits)

    for source, last, packed in ((sw, so, pself), (cw, co, pcross)):
        for i in range(3):
            packed[i * own : (i + 1) * own] = source[i]
        packed[3 * own :] = last[...]
    pbias[...] = jnp.zeros_like(pbias)
    pbias[0:1] = ib[...]
    for i in range(2):
        pbias[1:2, i * own : (i + 1) * own] = sb[i : i + 1]
        pbias[1:2, (2 + i) * own : (3 + i) * own] = cb[i : i + 1]
    pinner[...] = inner[...].T
    groups = []
    for i, (packed, buffer) in enumerate(
        ((pself, gself), (pcross, gcross), (pinner, ginner), (outer, gouter))
    ):
        n = packed.shape[0] // SLICES
        mine = packed.at[at_rows(s * n, n)]

        def place(shard, buffer=buffer, n=n):
            return buffer.at[c, y, x, at_rows(shard * n, n)]

        line = Double(z, mine, place, line_sems.at[i])
        plane = Plane(d, buffer, i % 2 == 1, plane_sems.at[i])
        groups.append((line, plane))
        buffer[c, y, x, at_rows(z * n, n)] = packed[at_rows(s * n, n)]

    def piece_place(number, j, up):
        return gmem.at[at_rows(number * piece, piece)]

    def piece_source(number, j, up):
        if j < PIECES:
            return mem.at[at_rows((number - z * PIECES) * piece, piece)]
        return piece_place(number, j, up)

    memory = Window(z, parts, piece_source, piece_place, mem_sems)

    bias_line = Double(z, pbias, lambda shard: gbias.at[shard], bias_sems)

    def halo_copy(other):
        return rcopy(x_ref.at[rows - HALO :], halo, halo_sems.at[0], halo_sems.at[1], mp=other)

    def far_copy(i):
        device = flipped(d, bits[i])
        return rcopy(far.at[i], far_land.at[i], far_sems.at[0, i], far_sems.at[1, i], dp=device)

    def far_step(i):
        if i > 0:
            far_copy(i - 1).wait_recv()
            far[i] = jnp.maximum(far[i - 1], far_land[i - 1])
        if i < len(bits):
            far_copy(i).start()
        else:
            far_out[...] = far[i, 0:1, 0:1]

    def forward(j):
        memory.arrived(j - PIECES)
        memory.send(j)

    far[0] = jnp.broadcast_to(excursion(tok, frm, rows, shard_rows, parts), far.shape[1:])
    gbias[z] = pbias[...]
    own_rows = gmem.at[at_rows(z * shard_rows, shard_rows)]
    own_copy = pltpu.make_async_copy(mem, own_rows, own_sem)
    own_copy.start()
    pl.semaphore_wait(barrier, greetings)
    for line, _ in groups[:2]:
        line.send(0)
    bias_line.send(0)

    @pl.when(z < parts - 1)
    def _():
        halo_copy(z + 1).start()

    for line, _ in groups[2:]:
        line.send(0)
    for line in (groups[0][0], groups[1][0], bias_line):
        line.arrived(0)
        line.send(1)
    memory.send(0)
    for line, _ in groups[2:]:
        line.arrived(0)
        line.send(1)
    for j in range(1, PIECES):
        memory.send(j)
    far_step(0)
    for line, plane in groups[:2]:
        line.arrived(1)
        plane.send(0)
    for _, plane in groups[:2]:
        plane.arrived(0)
        plane.send(1)
    for line, plane in groups[2:]:
        line.arrived(1)
        plane.send(0)
    far_step(1)
    for _, plane in groups[:2]:
        plane.arrived(1)
        plane.send(2)
    far_step(2)
    groups[0][1].arrived(2)

    bias_line.arrived(1)

    def head_bias(i):
        return jnp.concatenate(
            [
                gbias[o, 1:2, i * own + half * HALF : i * own + (half + 1) * HALF]
                for half in range(2)
                for o in range(parts)
            ],
            axis=1,
        )

    n = ginner.shape[3] // parts
    for i in range(SLICES):
        ib_out[i : i + 1] = jnp.concatenate(
            [gbias[o, 0:1, i * n : (i + 1) * n] for o in range(parts)], axis=1
        )

    @pl.when(z > 0)
    def _():
        halo_copy(z - 1).wait_recv()

    @pl.when(z == 0)
    def _():
        halo[...] = jnp.zeros_like(halo)

    def weight(buffer, i):
        return buffer[i // 2, i % 2].reshape(width, width)

    base = z * rows
    place_row, first_row, first_frame, end_frame = token_rows(tok, frm, base, rows)
    segment_out[0:1], segment_out[1:2] = first_frame, end_frame
    bounds_out[0:1], bounds_out[1:2] = block_frames(tok, frm, base)
    for src, dst in ((halo, slice(0, HALO)), (x_ref, slice(HALO, HALO + rows))):
        xhat, _ = normed(src[...].astype(F32))
        n1_ref[dst] = (xhat * gain[0:1] + shift[0:1]).astype(BF16)
    n1 = n1_ref[...]
    query = mm(n1[HALO:], weight(gself, 0), 1, 1) + head_bias(0)
    q_ref[...] = query.astype(BF16) * jnp.asarray(0.125, BF16)
    k_ref[...] = mm(n1, weight(gself, 1), 1, 1).astype(BF16)
    v_ref[...] = (mm(n1, weight(gself, 2), 1, 1) + head_bias(1)).astype(BF16)
    count = HALO + BLOCK
    for b in range(rows // BLOCK):
        queries = head_stack(q_ref[b * BLOCK : (b + 1) * BLOCK])
        window = slice(b * BLOCK, b * BLOCK + count)
        mask = window_mask(place_row, first_row, base, b, count)
        probs = self_probs(queries, k_ref[window], mask, heads).astype(BF16)
        out = head_diagonal(mm(v_ref[window], probs, 0, 0), heads)
        att_ref[b * BLOCK : (b + 1) * BLOCK] = out.T.astype(BF16)
        if b == 0:
            for _, plane in groups[2:]:
                plane.arrived(0)
                plane.send(1)
    forward(PIECES)
    after = x_ref[...].astype(F32) + mm(att_ref[...], weight(gself, 3)) + offset[...]
    after_ref[...] = after
    xhat, _ = normed(after)
    groups[1][1].arrived(2)
    n2 = (xhat * gain[1:2] + shift[1:2]).astype(BF16)
    query = mm(n2, weight(gcross, 0), 1, 1) + head_bias(2)
    cq_ref[...] = query.astype(BF16) * jnp.asarray(0.125, BF16)
    value_bias = head_bias(3)
    row_stores = [
        pltpu.make_async_copy(a, b, row_sems.at[i])
        for i, (a, b) in enumerate(
            (
                (n1_ref, n1_out),
                (q_ref, q_out),
                (k_ref, k_out),
                (v_ref, v_out),
                (att_ref, att_out),
                (after_ref, after_out),
                (cq_ref, cq_out),
            )
        )
    ]
    for store in row_stores:
        store.start()
    forward(PIECES + 1)

    def project(start, size):
        here = at_rows(start, size)
        block = gmem[here]
        sck[here] = mm(block, weight(gcross, 1), 1, 1).astype(BF16)
        scv[here] = (mm(block, weight(gcross, 2), 1, 1) + value_bias).astype(BF16)

    def copies_out(number):
        here = at_rows(number * piece, piece)
        return [
            pltpu.make_async_copy(a.at[here], b.at[here], out_sems.at[number, i])
            for i, (a, b) in enumerate(((gmem, mem_out), (sck, ck_out), (scv, cv_out)))
        ]

    def project_piece(number, j=0, up=True):
        project(number * piece, piece)
        for copy in copies_out(number):
            copy.start()

    own_copy.wait()
    lax.fori_loop(0, PIECES, lambda i, _: (project_piece(z * PIECES + i), 0)[1], 0)
    for _, plane in groups[2:]:
        plane.arrived(1)
        plane.send(2)
    for j in range(PIECES):
        if j >= 2:
            memory.arrived(j)
        memory.each(j, project_piece)
    for i in range(3, len(bits) + 1):
        far_step(i)
    for _, plane in groups[2:]:
        plane.arrived(2)
    outs = [
        pltpu.make_async_copy(a, b, weight_sems.at[i])
        for i, (a, b) in enumerate(
            ((gself, wself_out), (gcross, wcross_out), (ginner, inner_out), (gouter, outer_out))
        )
    ]
    for copy in outs:
        copy.start()
    vb_out[...] = value_bias
    for j in range(PIECES, NEAR):
        memory.arrived(j)
        memory.each(j, project_piece)
    for copy in outs + row_stores:
        copy.wait()

    def finish(number, *_):
        for copy in copies_out(number):
            copy.wait()

    for i in range(PIECES):
        finish(z * PIECES + i)
    for j in range(NEAR):
        memory.each(j, finish)
    for line, plane in groups:
        line.close()
        plane.close()
    memory.close(range(NEAR))
    for i in range(len(bits)):
        far_copy(i).wait_send()
    bias_line.close()

    @pl.when(z < parts - 1)
    def _():
        halo_copy(z + 1).wait_send()


def gather_far(mem, far_mem, sems):
    z, d = lax.axis_index("mp"), lax.axis_index("dp")
    parts = lax.axis_size("mp")
    last = PIECES * (parts - 1)
    piece = mem.shape[0] // parts // PIECES
    barrier, greetings = greet(z, parts, d, ())

    def place(number, j, up):
        return far_mem.at[at_rows(number * piece, piece)]

    def source(number, j, up):
        return (mem if j - PIECES < NEAR else far_mem).at[at_rows(number * piece, piece)]

    memory = Window(z, parts, source, place, sems)
    pl.semaphore_wait(barrier, greetings)
    for j in range(NEAR, last):
        if j - PIECES >= NEAR:
            memory.arrived(j - PIECES)
        memory.send(j)
    for j in range(max(NEAR, last - PIECES), last):
        memory.arrived(j)
    memory.close(range(NEAR, last))


def middle(
    far, bounds, cq_ref, segment_ref, ib_ref, vb_ref, gain, shift, cross_offset, outer_offset,
    after_in, cot_in, w_in, ck_in, cv_in, mem_in, far_in, wi_in, wo_in,
    grad_ref, small_ref, block_out, mgrad_out, dw_out, dwi_out, dwo_out,
    after_ref, cot_ref, w_ref, out_ref,
    ck_ref, cv_ref, mem_ref, wi_ref, wo_ref, mgrad_ref, dw_ref, dwb_ref, dwi_ref, dwo_ref,
    qbig, gbig, lse_ref, dot_ref, att_ref, dq_ref, dk_ref, dv_ref, first_ref, end_ref,
    in_sems, out_sems, unit_sems, far_sems,
):
    rows, width = cq_ref.shape
    heads = width // HEAD
    blocks = rows // BLOCK
    z = lax.axis_index("mp")
    parts = lax.axis_size("mp")
    last = parts * PIECES
    frames = mem_in.shape[0]
    piece = frames // last
    beyond = far[0, 0] > NEAR * piece

    def weight(i):
        return w_ref[i * width : (i + 1) * width]

    def rows_of(number):
        return at_rows(jnp.clip(number, 0, last - 1) * piece, piece)

    def spans(i, unit):
        here = pl.ds(pl.multiple_of(origin + unit * UNIT, UNIT), UNIT)
        source, full = arrays[i]
        return pltpu.make_async_copy(source.at[here], full.at[here], unit_sems.at[i, unit])

    def units(i, name):
        def one(unit, carry):
            getattr(spans(i, unit), name)()
            return carry

        lax.fori_loop(0, unit_count, one, 0)

    arrays = ((ck_in, ck_ref), (cv_in, cv_ref), (mem_in, mem_ref))
    for b in range(blocks):
        first_ref[b] = segment_ref[0:1, b * BLOCK : (b + 1) * BLOCK]
        end_ref[b] = segment_ref[1:2, b * BLOCK : (b + 1) * BLOCK]
        qbig[b] = head_stack(cq_ref[b * BLOCK : (b + 1) * BLOCK])
    origin = bounds[0, 0]
    unit_count = (bounds[1, blocks - 1] - origin + UNIT - 1) // UNIT
    count = (unit_count * UNIT + TILE - 1) // TILE
    loads = [
        pltpu.make_async_copy(a, b, in_sems.at[i])
        for i, (a, b) in enumerate(
            ((wi_in, wi_ref), (wo_in, wo_ref), (after_in, after_ref), (cot_in, cot_ref), (w_in, w_ref))
        )
    ]

    @pl.when(jnp.logical_not(beyond))
    def _():
        units(0, "start")
        units(1, "start")

    for load in loads:
        load.start()

    @pl.when(jnp.logical_not(beyond))
    def _():
        units(2, "start")

    @pl.when(beyond)
    def _():
        loads[4].wait()

        def fetch(i, carry):
            number = i
            here = rows_of(number)
            distance = jnp.maximum(z * PIECES - 1 - number, number - (z + 1) * PIECES)

            @pl.when(distance < NEAR)
            def _():
                copies = [
                    pltpu.make_async_copy(a.at[here], b.at[here], far_sems.at[k])
                    for k, (a, b) in enumerate(arrays)
                ]
                for copy in copies:
                    copy.start()
                for copy in copies:
                    copy.wait()

            @pl.when(distance >= NEAR)
            def _():
                copy = pltpu.make_async_copy(far_in.at[here], mem_ref.at[here], far_sems.at[0])
                copy.start()
                copy.wait()
                block = mem_ref[here]
                ck_ref[here] = mm(block, weight(1), 1, 1).astype(BF16)
                cv_ref[here] = (mm(block, weight(2), 1, 1) + vb_ref[...]).astype(BF16)

            return carry

        lax.fori_loop(0, last, fetch, 0)

    tail = pl.ds(pl.multiple_of(origin + unit_count * UNIT, UNIT), SIZES[0])
    for _, full in arrays:
        full[tail] = jnp.zeros((SIZES[0], width), BF16)
    small_ref[...] = jnp.zeros_like(small_ref)
    mgrad_ref[...] = jnp.zeros_like(mgrad_ref)

    def over_tiles(b, step, carry):
        large, medium, small = SIZES
        start = bounds[0, b]
        length = bounds[1, b] - start
        number = (length + medium - 1) // large
        left = length - number * large
        after = start + number * large
        carry = lax.fori_loop(0, number, lambda i, c: step(large, start + i * large, c), carry)
        one = (left > small).astype(jnp.int32)
        carry = lax.fori_loop(0, one, lambda i, c: step(medium, after, c), carry)
        one = ((left > 0) & (left <= small)).astype(jnp.int32)
        return lax.fori_loop(0, one, lambda i, c: step(small, after, c), carry)

    def tile_mask(size, start, b):
        frame = lax.broadcasted_iota(jnp.int32, (size, BLOCK), 0) + start
        return (frame >= first_ref[b]) & (frame < end_ref[b])

    def columns(h):
        return slice(h * BLOCK, (h + 1) * BLOCK)

    @pl.when(jnp.logical_not(beyond))
    def _():
        units(0, "wait")
        units(1, "wait")

    def attend(b, carry):
        att_ref[b] = jnp.zeros((width, BLOCK), F32)

        def step(size, start, carry):
            here = pl.ds(pl.multiple_of(start, UNIT), size)
            scores = mm(ck_ref[here], qbig[b], 1, 1)
            mask = tile_mask(size, start, b)
            values = cv_ref[here].T
            news = []
            for h in range(heads):
                largest, total = carry[h]
                part = jnp.where(mask, scores[:, columns(h)], NEGATIVE)
                now = jnp.maximum(largest, jnp.max(part, axis=0, keepdims=True))
                fade = jnp.exp(largest - now)
                raised = jnp.exp(part - now)
                news.append((now, total * fade + jnp.sum(raised, axis=0, keepdims=True)))
                pieces = [r for r, o in head_rows(heads) if o == h]
                own = jnp.concatenate([values[r] for r in pieces], axis=0)
                out = mm(own, raised.astype(BF16))
                for i, r in enumerate(pieces):
                    att_ref[b, r] = att_ref[b, r] * fade + out[i * HALF : (i + 1) * HALF]
            return tuple(news)

        start = (jnp.full((1, BLOCK), NEGATIVE, F32), jnp.zeros((1, BLOCK), F32))
        done = over_tiles(b, step, (start,) * heads)
        for h, (largest, total) in enumerate(done):
            lse_ref[b, :, columns(h)] = largest + jnp.log(total)
            share = 1.0 / total
            for r, o in head_rows(heads):
                if o == h:
                    att_ref[b, r] = att_ref[b, r] * share
        return carry

    lax.fori_loop(0, blocks, attend, 0)
    att = jnp.concatenate([att_ref[b].T for b in range(blocks)], axis=0).astype(BF16)
    loads[2].wait()
    loads[3].wait()

    @pl.when(jnp.logical_not(beyond))
    def _():
        loads[4].wait()

    after_self = after_ref[...]
    after_cross = after_self + mm(att, weight(3)) + cross_offset[...]
    xhat3, scale3 = normed(after_cross)
    n3 = (xhat3 * gain[2:3] + shift[2:3]).astype(BF16)
    sent = cot_ref[...]
    small_ref[8:9] = column_sums(sent.astype(F32))
    hidden = wi_ref.shape[0]
    group = 4
    tile = hidden // SLICES * group
    loads[0].wait()
    loads[1].wait()
    out_ref[...] = after_cross + outer_offset[...]
    grad_ref[...] = jnp.zeros((rows, width), F32)

    def feed(f, carry):
        here = pl.ds(pl.multiple_of(f * tile, tile), tile)
        bias = jnp.concatenate([ib_ref[pl.ds(f * group + i, 1)] for i in range(group)], axis=1)
        before = mm(n3, wi_ref[here], 1, 1) + bias
        square = before * before
        inner = jnp.tanh(before * (GELU_A + (GELU_A * GELU_B) * square))
        half = 0.5 + 0.5 * inner
        active = (before * half).astype(BF16)
        slope = half + (0.5 * before) * (1.0 - inner * inner) * (
            GELU_A + (3.0 * GELU_A * GELU_B) * square
        )
        out_ref[...] += mm(active, wo_ref[here])
        back = (slope * mm(sent, wo_ref[here], 1, 1)).astype(BF16)
        grad_ref[...] += mm(back, wi_ref[here])
        dwo_ref[here] = mm(active, sent, 0, 0).astype(BF16)
        dwi_ref[here] = mm(back, n3, 0, 0).astype(BF16)
        sums = column_sums(back.astype(F32))
        for i in range(group):
            small_ref[pl.ds(16 + f * group + i, 1)] = sums[:, i * tile // group : (i + 1) * tile // group]
        return carry

    lax.fori_loop(0, SLICES // group, feed, 0)
    stores = [
        pltpu.make_async_copy(a, b, out_sems.at[i])
        for i, (a, b) in enumerate(
            (
                (dwi_ref, dwi_out),
                (dwo_ref, dwo_out),
                (dwb_ref, dw_out),
                (mgrad_ref.at[:frames], mgrad_out),
                (out_ref, block_out),
            )
        )
    ]
    stores[0].start()
    stores[1].start()
    stores[4].start()
    dn3 = grad_ref[...]
    small_ref[2:3] = column_sums(dn3 * xhat3)
    small_ref[5:6] = column_sums(dn3)
    grad = sent.astype(F32) + norm_back(dn3, gain[2:3], xhat3, scale3)
    sent2 = grad.astype(BF16)
    small_ref[7:8] = column_sums(sent2.astype(F32))
    dwb_ref[3 * width :] = mm(att, sent2, 0, 0).astype(BF16)
    go = mm(sent2, weight(3), 1, 1).astype(BF16)
    got = mm(weight(3), sent2, 1, 1).astype(BF16).astype(F32)
    for b in range(blocks):
        gbig[b] = head_stack(go[b * BLOCK : (b + 1) * BLOCK])
        prod = got[:, b * BLOCK : (b + 1) * BLOCK] * att_ref[b]
        sums = [column_sums(prod[r]) for r, _ in head_rows(heads)]
        for h in range(heads):
            dot_ref[b, :, columns(h)] = sums[h] + sums[heads + h]
    def span(i):
        return pl.ds(pl.multiple_of(origin + i * TILE, 128), TILE)

    def clear(i, carry):
        dk_ref[span(i)] = jnp.zeros((TILE, width), F32)
        dv_ref[span(i)] = jnp.zeros((TILE, width), F32)
        return carry

    lax.fori_loop(0, count, clear, 0)

    def attend_back(b, carry):
        dq_ref[b] = jnp.zeros((width, BLOCK), F32)

        def step(size, start, carry):
            here = pl.ds(pl.multiple_of(start, UNIT), size)
            keys, values = ck_ref[here], cv_ref[here]
            scores = mm(keys, qbig[b], 1, 1)
            dp = mm(values, gbig[b], 1, 1)
            mask = tile_mask(size, start, b)
            shares, scaled = [], []
            for h in range(heads):
                part = jnp.exp(scores[:, columns(h)] - lse_ref[b, :, columns(h)])
                part = jnp.where(mask, part, 0.0)
                shares.append(part.astype(BF16))
                scaled.append((part * (dp[:, columns(h)] - dot_ref[b, :, columns(h)])).astype(BF16))
            shares, scaled = jnp.concatenate(shares, axis=1), jnp.concatenate(scaled, axis=1)
            dv_ref[here] += mm(shares, gbig[b])
            dk_ref[here] += mm(scaled, qbig[b])
            dq_ref[b] += head_diagonal(mm(keys, scaled, 0, 0), heads)
            return carry

        return over_tiles(b, step, carry)

    lax.fori_loop(0, blocks, attend_back, 0)

    @pl.when(jnp.logical_not(beyond))
    def _():
        units(2, "wait")

    dw_ref[...] = jnp.zeros_like(dw_ref)

    def frame_step(i, carry):
        here = span(i)
        dk, dv = dk_ref[here].astype(BF16), dv_ref[here].astype(BF16)
        mgrad_ref[here] = (mm(dk, weight(1)) + mm(dv, weight(2))).astype(BF16)
        frame_rows = mem_ref[here]
        dw_ref[0] += mm(dk, frame_rows, 0, 0)
        dw_ref[1] += mm(dv, frame_rows, 0, 0)
        small_ref[12:13] += column_sums(dv.astype(F32))
        return carry

    lax.fori_loop(0, count, frame_step, 0)
    stores[3].start()
    dq = jnp.concatenate([(dq_ref[b] * 0.125).T for b in range(blocks)], axis=0).astype(BF16)
    small_ref[11:12] = column_sums(dq.astype(F32))
    xhat2, scale2 = normed(after_self)
    n2 = (xhat2 * gain[1:2] + shift[1:2]).astype(BF16)
    dwb_ref[:width] = mm(dq, n2, 0, 0).astype(BF16)
    dwb_ref[width : 2 * width] = dw_ref[0].astype(BF16)
    dwb_ref[2 * width : 3 * width] = dw_ref[1].astype(BF16)
    stores[2].start()
    dn2 = mm(dq, weight(0))
    small_ref[1:2] = column_sums(dn2 * xhat2)
    small_ref[4:5] = column_sums(dn2)
    grad_ref[...] = grad + norm_back(dn2, gain[1:2], xhat2, scale2)
    for store in stores:
        store.wait()


def sum_far(mgrad_in, mgrad_out, own, land, flow_sems, load_sem):
    pieces, piece = land.shape[1:3]
    frames = own.shape[0]
    parts = frames // piece // PIECES
    last = NEAR + pieces
    z, d = lax.axis_index("mp"), lax.axis_index("dp")
    barrier, greetings = greet(z, parts, d, ())
    load = pltpu.make_async_copy(mgrad_in, own, load_sem)
    load.start()

    def rows_of(number):
        return at_rows(number * piece, piece)

    def there(number):
        return (number >= 0) & (number < parts * PIECES)

    def sent(j, up):
        return (z + 1) * PIECES + j if up else z * PIECES - 1 - j

    def comes(j, up):
        return z * PIECES + j if up else (z + 1) * PIECES - 1 - j

    def flow(j, up, number, device):
        kind = 0 if up else 2
        place = land.at[0 if up else 1, j - NEAR]
        sems = flow_sems.at[kind, j - NEAR], flow_sems.at[kind + 1, j - NEAR]
        return rcopy(own.at[rows_of(number)], place, *sems, mp=device)

    def arrive(j):
        for up in (True, False):

            @pl.when(there(comes(j, up)) & (z > 0 if up else z < parts - 1))
            def _():
                number = comes(j, up)
                flow(j, up, number, z - 1 if up else z + 1).wait_recv()
                here = rows_of(number)
                more = land[0 if up else 1, j - NEAR].astype(F32)
                own[here] = (own[here].astype(F32) + more).astype(BF16)

    def each(j, name):
        for up in (True, False):

            @pl.when(there(sent(j, up)) & (z < parts - 1 if up else z > 0))
            def _():
                getattr(flow(j, up, sent(j, up), z + 1 if up else z - 1), name)()

    load.wait()
    pl.semaphore_wait(barrier, greetings)
    for j in reversed(range(NEAR, last)):
        if j + PIECES < last:
            arrive(j + PIECES)
        each(j, "start")
    for j in range(NEAR, min(NEAR + PIECES, last)):
        arrive(j)
    for j in range(NEAR, last):
        each(j, "wait_send")
    store = pltpu.make_async_copy(own, mgrad_out, load_sem)
    store.start()
    store.wait()


def masked(d, mask):
    for bit in (1, 2, 4):
        if mask & bit:
            d = flipped(d, bit)
    return d


CHIPS = (2, 4, 6)


class Reduce:
    def __init__(self, d, z, parts, dp, local, buffers, sems):
        self.d, self.z, self.parts, self.dp, self.local = d, z, parts, dp, local
        self.r1, self.a1, self.r2, self.a3, self.rz, self.a4, self.wide, self.fin = buffers
        self.high, self.low = z // 2, z % 2
        self.sems, self.extra_sems, self.plane_sems = sems
        self.c, self.y, self.x = corner(d)
        self.spread = Chips(d, self.fin, self.plane_sems)
        self.bits = [8 << i for i in range(dp.bit_length() - 4)]

    def to_core(self):
        sems = self.sems
        return rcopy(
            self.local.at[1 - self.c], self.r1, sems.at[0, 0], sems.at[1, 0], dp=flipped(self.d, 1)
        )

    def to_chip(self, i):
        sems, other = self.sems, masked(self.d, CHIPS[i])
        _, y, x = corner(other)
        return rcopy(self.a1.at[y, x], self.r2.at[i], sems.at[0, 1 + i], sems.at[1, 1 + i], dp=other)

    def to_neighbour(self):
        sems = self.sems
        src = self.a3.at[:, 1 - self.low]
        return rcopy(src, self.rz.at[:2], sems.at[0, 4], sems.at[1, 4], mp=flipped(self.z, 1))

    def to_far(self):
        sems = self.sems
        src = self.a4.at[1 - self.high]
        return rcopy(src, self.rz.at[2], sems.at[0, 5], sems.at[1, 5], mp=flipped(self.z, 2))

    def extra(self, i):
        sems = self.extra_sems
        device = flipped(self.d, self.bits[i])
        return rcopy(self.wide.at[2 * i], self.wide.at[2 * i + 1], sems.at[0, i], sems.at[1, i], dp=device)

    def run(self, p):
        if p == 0:
            self.to_core().start()
        elif p == 1:
            self.to_core().wait_recv()
            self.a1[...] = (self.local[self.c].astype(F32) + self.r1[...].astype(F32)).astype(BF16)
            for i in range(3):
                self.to_chip(i).start()
        elif p == 2:
            total = self.a1[self.y, self.x].astype(F32)
            for i in range(3):
                self.to_chip(i).wait_recv()
                total = total + self.r2[i].astype(F32)
            self.a3[...] = total.astype(BF16).reshape(self.a3.shape)
            self.to_neighbour().start()
        elif p == 3:
            self.to_neighbour().wait_recv()
            mine = self.a3[:, self.low].astype(F32) + self.rz[:2].astype(F32)
            self.a4[...] = mine.astype(BF16)
            self.to_far().start()
        elif p == 4:
            self.to_far().wait_recv()
            total = self.a4[self.high].astype(F32) + self.rz[2].astype(F32)
            for i in range(len(self.bits)):
                self.wide[2 * i] = total
                self.extra(i).start()
                self.extra(i).wait_recv()
                total = total + self.wide[2 * i + 1]
            self.fin[self.c, self.y, self.x] = total.astype(BF16)
            self.spread.send(0)
        elif p == 5:
            self.spread.arrived(0)
            self.spread.send(1)
        else:
            self.spread.arrived(1)

    def close(self):
        self.to_core().wait_send()
        for i in range(3):
            self.to_chip(i).wait_send()
        self.to_neighbour().wait_send()
        self.to_far().wait_send()
        for i in range(len(self.bits)):
            self.extra(i).wait_send()
        self.spread.close()


class Spread:
    def __init__(self, d, buffer, sems):
        self.d, self.buffer, self.sems = d, buffer, sems

    def copy(self, m, own):
        neighbour = masked(self.d, m)
        c, y, x = corner(self.d if own else neighbour)
        block = self.buffer.at[c, y, x]
        return rcopy(block, block, self.sems.at[0, m], self.sems.at[1, m], dp=neighbour)

    def send(self):
        for m in range(1, 8):
            self.copy(m, True).start()

    def arrived(self):
        for m in range(1, 8):
            self.copy(m, False).wait_recv()

    def close(self):
        for m in range(1, 8):
            self.copy(m, True).wait_send()


class Chips:
    def __init__(self, d, buffer, sems):
        self.d, self.buffer, self.sems = d, buffer, sems

    def copy(self, m, own):
        neighbour = masked(self.d, m)
        c, y, x = corner(self.d if own else neighbour)
        block = self.buffer.at[c] if m == 1 else self.buffer.at[c, y, x]
        return rcopy(block, block, self.sems.at[0, m], self.sems.at[1, m], dp=neighbour)

    def send(self, p):
        for m in (CHIPS, (1,))[p]:
            self.copy(m, True).start()

    def arrived(self, p):
        for m in (CHIPS, (1,))[p]:
            self.copy(m, False).wait_recv()

    def close(self):
        for m in (1, 2, 4, 6):
            self.copy(m, True).wait_send()


class Total:
    def __init__(self, d, z, bits, buffer, wide, sems, wide_sems):
        self.d, self.z, self.bits, self.wide, self.wide_sems = d, z, bits, wide, wide_sems
        self.buffer = buffer
        self.spread = Spread(d, buffer, sems)

    def extra(self, i):
        sems, count = self.wide_sems, len(self.bits)
        if i < count:
            device = {"dp": flipped(self.d, self.bits[i])}
        else:
            device = {"mp": flipped(self.z, 1 if i == count else 2)}
        return rcopy(self.wide.at[2 * i], self.wide.at[2 * i + 1], sems.at[0, i], sems.at[1, i], **device)

    def run(self, p):
        count = len(self.bits)
        if p == 0:
            self.spread.send()
        elif p == 1:
            self.spread.arrived()
            total = self.buffer[0, 0, 0]
            for c, y, x in [(i // 4, i // 2 % 2, i % 2) for i in range(1, 8)]:
                total = total + self.buffer[c, y, x]
            for i in range(count):
                self.wide[2 * i] = total
                self.extra(i).start()
                self.extra(i).wait_recv()
                total = total + self.wide[2 * i + 1]
            self.wide[2 * count] = total
            self.extra(count).start()
        else:
            self.extra(count).wait_recv()
            self.wide[2 * count + 2] = self.wide[2 * count] + self.wide[2 * count + 1]
            self.extra(count + 1).start()

    def finish(self, out):
        last = len(self.bits) + 1
        self.extra(last).wait_recv()
        out[...] = self.wide[2 * last] + self.wide[2 * last + 1]
        self.spread.close()
        for i in range(last + 1):
            self.extra(i).wait_send()


def give_back(
    window,
    tok, frm, small_in, gain,
    x_in, n1_in, q_in, k_in, v_in, att_in, grad_in, w_in, mgrad_in, dwc_in, dwi_in, dwo_in,
    input_out, mgrad_out, fself, fcross, finner, fouter, small_out,
    x_ref, n1_ref, q_ref, k_ref, v_ref, att_ref, grad_ref, w_ref,
    own, up_land, down_land, local_self, local_cross, local_inner, local_outer,
    dk_ref, dv_ref, dq_ref, halo_out, halo_land, total_buffer, total_wide,
    self_bufs, cross_bufs, inner_bufs, outer_bufs,
    load_sems, flow_sems, reduce_sems, extra_sems, plane_sems, halo_sems, total_sems, wide_sems,
):
    rows, width = q_ref.shape
    heads = width // HEAD
    parts = lax.axis_size("mp")
    shard_rows = mgrad_out.shape[0]
    piece = shard_rows // PIECES
    last = parts * PIECES
    z, d = lax.axis_index("mp"), lax.axis_index("dp")
    dp = lax.axis_size("dp")
    bits = [8 << i for i in range(dp.bit_length() - 4)]
    barrier, greetings = greet(z, parts, d, bits, range(1, 8))
    loads = [
        pltpu.make_async_copy(a, b, load_sems.at[i])
        for i, (a, b) in enumerate(
            (
                (dwi_in, local_inner),
                (dwo_in, local_outer),
                (dwc_in, local_cross),
                (grad_in, grad_ref),
                (w_in, w_ref),
                (q_in, q_ref),
                (k_in, k_ref),
                (v_in, v_ref),
                (n1_in, n1_ref),
                (att_in, att_ref),
                (x_in, x_ref),
                (mgrad_in, own),
            )
        )
    ]
    for load in loads:
        load.start()
    chains = []
    for i, (local, bufs, fin) in enumerate(
        (
            (local_inner, inner_bufs, finner),
            (local_outer, outer_bufs, fouter),
            (local_cross, cross_bufs, fcross),
            (local_self, self_bufs, fself),
        )
    ):
        sems = (reduce_sems.at[i], extra_sems.at[i], plane_sems.at[i])
        chains.append(Reduce(d, z, parts, dp, local, (*bufs, fin), sems))
    inner, outer, cross, own_chain = chains

    def rows_of(number):
        return at_rows(number * piece, piece)

    def crosses(j, up):
        if up:
            return (z < parts - 1) & ((z + 1) * PIECES + j < last)
        return (z > 0) & (z * PIECES - 1 - j >= 0)

    def number(j, up):
        return (z + 1) * PIECES + j if up else z * PIECES - 1 - j

    def flow(j, up, summed):
        land = up_land if up else down_land
        kind = 0 if up else 2
        src = land.at[j + PIECES] if summed else mgrad_in.at[rows_of(number(j, up))]
        device = z + 1 if up else z - 1
        return rcopy(src, land.at[j], flow_sems.at[kind, j], flow_sems.at[kind + 1, j], mp=device)

    def comes(j, up):
        if up:
            return (z > 0) & (z * PIECES + j < last)
        return (z < parts - 1) & ((z + 1) * PIECES - 1 - j >= 0)

    def flow_arrival(j, up):
        land = up_land if up else down_land
        kind = 0 if up else 2
        device = z - 1 if up else z + 1
        return rcopy(
            land.at[j], land.at[j], flow_sems.at[kind, j], flow_sems.at[kind + 1, j], mp=device
        )

    def first_flows(pieces):
        for j in pieces:
            for up in (True, False):

                @pl.when(crosses(j, up))
                def _():
                    flow(j, up, False).start()

    def next_flow(j):
        for up in (True, False):
            land = up_land if up else down_land

            @pl.when(crosses(j, up) & comes(j + PIECES, up))
            def _():
                flow_arrival(j + PIECES, up).wait_recv()
                mine = own[rows_of(number(j, up))]
                land[j + PIECES] = (land[j + PIECES].astype(F32) + mine.astype(F32)).astype(BF16)
                flow(j, up, True).start()

            @pl.when(crosses(j, up) & jnp.logical_not(comes(j + PIECES, up)))
            def _():
                flow(j, up, False).start()

    base = z * rows
    place, first_row, _, _ = token_rows(tok, frm, base, rows)

    def weight(i):
        return w_ref[i * width : (i + 1) * width]

    def halo_copy(other):
        return rcopy(halo_out, halo_land, halo_sems.at[0], halo_sems.at[1], mp=other)

    pl.semaphore_wait(barrier, greetings)
    first_flows((5, 4))
    for load, chain in zip(loads[:3], chains[:3]):
        load.wait()
        chain.run(0)
    c, y, x = corner(d)
    small = total_buffer.at[c, y, x]
    small[...] = small_in[...]
    loads[3].wait()
    loads[4].wait()
    grad = grad_ref[...]
    sent = grad.astype(BF16)
    small[6:7] = column_sums(sent.astype(F32))
    n = local_self.shape[3]

    def keep(i, values):
        for half in range(2):
            s = 2 * i + half
            local_self[s // 4, s // 2 % 2, s % 2] = values[half * n : (half + 1) * n].astype(BF16)

    go = mm(sent, weight(3), 1, 1).astype(BF16)
    dk_ref[...] = jnp.zeros_like(dk_ref)
    dv_ref[...] = jnp.zeros_like(dv_ref)
    count = HALO + BLOCK
    blocks = rows // BLOCK

    def attend_back(b):
        here = slice(b * BLOCK, (b + 1) * BLOCK)
        span = slice(b * BLOCK, b * BLOCK + count)
        queries, grads = head_stack(q_ref[here]), head_stack(go[here])
        mask = window_mask(place, first_row, base, b, count)
        shares = self_probs(queries, k_ref[span], mask, heads)
        dp_ = mm(v_ref[span], grads, 1, 1)
        ds = (shares * (dp_ - jnp.sum(shares * dp_, axis=0, keepdims=True))).astype(BF16)
        dv_ref[span] += mm(shares.astype(BF16), grads)
        dk_ref[span] += mm(ds, queries)
        dq_ref[here] = (head_diagonal(mm(k_ref[span], ds, 0, 0), heads) * 0.125).T.astype(BF16)

    def to_norm(here):
        return mm(dk_ref[here].astype(BF16), weight(1)) + mm(dv_ref[here].astype(BF16), weight(2))

    for chain in chains[:3]:
        chain.run(1)
    for load in loads[5:8]:
        load.wait()
    reaching = HALO // BLOCK
    for b in range(reaching):
        attend_back(b)
    halo_out[...] = to_norm(slice(0, HALO)).astype(BF16)

    @pl.when(z > 0)
    def _():
        halo_copy(z - 1).start()

    first_flows((3, 2))
    for b in range(reaching, blocks):
        attend_back(b)
    dq = dq_ref[...]
    dk, dv = dk_ref[...].astype(BF16), dv_ref[...].astype(BF16)
    for load in loads[8:]:
        load.wait()
    n1 = n1_ref[...]
    keep(0, mm(dq, n1[HALO:], 0, 0))
    keep(1, mm(dk, n1, 0, 0))
    keep(2, mm(dv, n1, 0, 0))
    keep(3, mm(att_ref[...], sent, 0, 0))
    own_chain.run(0)
    small[9:10] = column_sums(dq.astype(F32))
    small[10:11] = column_sums(dv.astype(F32))
    dn = to_norm(slice(HALO, HALO + rows)) + mm(dq, weight(0))
    xhat, scale = normed(x_ref[...].astype(F32))
    own_chain.run(1)

    @pl.when(z < parts - 1)
    def _():
        halo_copy(z + 1).wait_recv()

    @pl.when(z == parts - 1)
    def _():
        halo_land[...] = jnp.zeros_like(halo_land)

    dn = jnp.concatenate([dn[: rows - HALO], dn[rows - HALO :] + halo_land[...].astype(F32)], axis=0)
    small[0:1] = column_sums(dn * xhat)
    small[3:4] = column_sums(dn)
    total = Total(d, z, bits, total_buffer, total_wide, total_sems, wide_sems)
    total.run(0)
    input_out[...] = grad + norm_back(dn, gain[0:1], xhat, scale)
    for chain in chains[:3]:
        chain.run(2)
    next_flow(1)
    own_chain.run(2)
    for chain in chains[:3]:
        chain.run(3)
    total.run(1)
    own_chain.run(3)
    next_flow(0)
    for chain in chains[:3]:
        chain.run(4)
    total.run(2)
    own_chain.run(4)
    for p in range(5, 7):
        for chain in chains:
            chain.run(p)

    @pl.when(z == 0)
    def _():
        up_land[:PIECES] = jnp.zeros((PIECES, piece, width), BF16)

    @pl.when(z == parts - 1)
    def _():
        down_land[:PIECES] = jnp.zeros((PIECES, piece, width), BF16)

    for i in range(PIECES):
        for up in (True, False):
            j = i if up else PIECES - 1 - i

            @pl.when(comes(j, up))
            def _():
                flow_arrival(j, up).wait_recv()

        mine = own[rows_of(z * PIECES + i)].astype(F32)
        sides = up_land[i].astype(F32) + down_land[PIECES - 1 - i].astype(F32)
        mgrad_out[i * piece : (i + 1) * piece] = (mine + sides).astype(BF16)
    total.finish(small_out)
    for chain in chains:
        chain.close()

    @pl.when(z > 0)
    def _():
        halo_copy(z - 1).wait_send()

    for j in range(window):
        for up in (True, False):
            @pl.when(crosses(j, up))
            def _():
                flow(j, up, False).wait_send()


def finals(
    mgrad, input_grad, fself, fcross, finner, fouter, small,
    out_mgrad, out_input, out_gain, out_shift, out_sw, out_sb, out_so, out_soff,
    out_cw, out_cb, out_co, out_coff, out_inner, out_ib, out_outer, out_ooff,
):
    z = lax.axis_index("mp")
    own = out_so.shape[0]
    parts = out_so.shape[1] // own
    out_mgrad[...] = mgrad[...].astype(F32)
    out_input[...] = input_grad[...]
    out_gain[...] = small[0:3]
    out_shift[...] = small[3:6]
    out_soff[...] = small[6:7]
    out_coff[...] = small[7:8]
    out_ooff[...] = small[8:9]

    def chosen(row, size, offset):
        pieces = [small[row : row + 1, offset + o * size : offset + (o + 1) * size] for o in range(parts)]
        result = pieces[0]
        for o in range(1, parts):
            result = jnp.where(z == o, pieces[o], result)
        return result

    for fin, weights, last, biases, first in (
        (fself, out_sw, out_so, out_sb, 9),
        (fcross, out_cw, out_co, out_cb, 11),
    ):
        for i in range(3):
            weights[i] = fin[i // 2, i % 2].reshape(own, -1).astype(F32)
        last[...] = fin[1, 1].reshape(own, -1).astype(F32)
        for i in range(2):
            for half in range(2):
                lanes = slice(half * HALF, (half + 1) * HALF)
                biases[i : i + 1, lanes] = chosen(first + i, HALF, half * parts * HALF)
    out_inner[...] = finner[...].reshape(out_outer.shape).astype(F32).T
    out_outer[...] = fouter[...].reshape(out_outer.shape).astype(F32)
    size = out_ib.shape[1] // SLICES
    for s in range(SLICES):
        out_ib[0:1, s * size : (s + 1) * size] = chosen(16 + s, size, 0)


def call(body, outs, ins, scratch, limit, **params):
    places = {"s": pltpu.SMEM, "v": pltpu.VMEM, "h": pl.ANY}

    def spec(place):
        return pl.BlockSpec(memory_space=places[place])

    def run(*args):
        return pl.pallas_call(
            body,
            out_shape=[jax.ShapeDtypeStruct(shape, kind) for shape, kind, _ in outs],
            in_specs=[spec(place) for place in ins],
            out_specs=[spec(place) for _, _, place in outs],
            scratch_shapes=[pltpu.VMEM(*x) if isinstance(x, tuple) else x for x in scratch],
            compiler_params=pltpu.CompilerParams(vmem_limit_bytes=limit << 20, **params),
        )(*args)

    return run


def shards(
    block_input,
    memory,
    tok_lengths,
    frame_lengths,
    cotangent,
    norm_gain,
    norm_shift,
    self_weights,
    self_biases,
    self_output,
    self_offset,
    cross_weights,
    cross_biases,
    cross_output,
    cross_offset,
    inner_weight,
    inner_bias,
    outer_weight,
    outer_offset,
):
    rows, width = block_input.shape
    parts = lax.axis_size("mp")
    frames = memory.shape[0] * parts
    heads = width // HEAD
    blocks = rows // BLOCK
    own_hidden = inner_weight.shape[1]
    hidden = own_hidden * parts
    own = width // parts
    dma = pltpu.SemaphoreType.DMA
    wide = heads * BLOCK

    n_att, n_ffn = own * 4 // SLICES, own_hidden // SLICES
    n_bits = lax.axis_size("dp").bit_length() - 1
    piece = memory.shape[0] // PIECES
    small_rows = 16 + SLICES
    own_rows = (rows, width)
    halo_rows = (rows + HALO, width)

    def sliced(n):
        return (2, 2, 2, n, width)

    def turned(weights):
        return jnp.swapaxes(weights, 1, 2)

    (
        wself, wcross, inner, outer, inner_row, value_row, segment_rows, bounds, far, memory_rows, ck, cv, spare, n1, q, k, v, att, after, cq
    ) = call(
        gather,
        [
            (sliced(parts * n_att), BF16, "h"),
            (sliced(parts * n_att), BF16, "h"),
            (sliced(parts * n_ffn), BF16, "h"),
            (sliced(parts * n_ffn), BF16, "h"),
            ((SLICES, hidden // SLICES), F32, "v"),
            ((1, width), F32, "v"),
            ((2, rows), jnp.int32, "v"),
            ((2, 128), jnp.int32, "v"),
            ((1, 1), F32, "v"),
            ((frames, width), BF16, "h"),
            ((frames, width), BF16, "h"),
            ((frames, width), BF16, "h"),
            ((parts * frames, width), BF16, "h"),
            (halo_rows, BF16, "h"),
            (own_rows, BF16, "h"),
            (halo_rows, BF16, "h"),
            (halo_rows, BF16, "h"),
            (own_rows, BF16, "h"),
            (own_rows, F32, "h"),
            (own_rows, BF16, "h"),
        ],
        "ssvhvvvvvvvvvvvv",
        [
            (halo_rows, BF16),
            (own_rows, BF16),
            (halo_rows, BF16),
            (halo_rows, BF16),
            (own_rows, BF16),
            (own_rows, F32),
            (own_rows, BF16),
            (sliced(parts * n_att), BF16),
            (sliced(parts * n_att), BF16),
            (sliced(parts * n_ffn), BF16),
            (sliced(parts * n_ffn), BF16),
            ((frames, width), BF16),
            ((frames, width), BF16),
            ((frames, width), BF16),
            ((4 * own, width), BF16),
            ((4 * own, width), BF16),
            ((own_hidden, width), BF16),
            ((HALO, width), BF16),
            ((8, own_hidden), F32),
            ((parts, 8, own_hidden), F32),
            ((n_bits + 1, 8, 128), F32),
            ((n_bits, 8, 128), F32),
            dma((4, 2, 3)),
            dma((4, NEAR)),
            dma((4, 2, 3)),
            dma((2, 3)),
            dma((2,)),
            dma((2, n_bits)),
            dma,
            dma((parts * PIECES, 3)),
            dma((4,)),
            dma((7,)),
        ],
        56,
        collective_id=0,
        has_side_effects=True,
    )(
        tok_lengths, frame_lengths, block_input, memory, turned(self_weights), self_output,
        turned(cross_weights), cross_output, inner_weight, outer_weight, self_biases, cross_biases,
        inner_bias.reshape(1, own_hidden), norm_gain, norm_shift, self_offset.reshape(1, width),
    )
    wcross_rows = wcross.reshape(4 * width, width)
    wself_rows = wself.reshape(4 * width, width)
    inner_rows, outer_rows = inner.reshape(hidden, width), outer.reshape(hidden, width)

    def reduce_buffers(n):
        full = parts * n
        return [
            pltpu.VMEM((2, 2, full, width), BF16),
            pltpu.VMEM((2, 2, full, width), BF16),
            pltpu.VMEM((3, full, width), BF16),
            pltpu.VMEM((parts // 2, 2, n, width), BF16),
            pltpu.VMEM((3, n, width), BF16),
            pltpu.VMEM((2, n, width), BF16),
            pltpu.VMEM((2 * max(n_bits - 3, 1), n, width), F32),
        ]

    window = PIECES * (parts - 1)
    far_shape = (2, window - NEAR, piece, width)
    beyond = far[0, 0] > NEAR * piece

    def fetch_far():
        (far_memory,) = call(
            gather_far,
            [((parts * frames, width), BF16, "h")],
            "h",
            [dma((4, window))],
            8,
            collective_id=2,
            has_side_effects=True,
        )(memory_rows)
        return far_memory

    far_memory = lax.cond(beyond, fetch_far, lambda: spare)
    padded = (frames + SIZES[0], width)
    grad, small, block_output, mgrad, dw_cross, dwi, dwo = call(
        middle,
        [
            (own_rows, F32, "v"),
            ((small_rows, width), F32, "v"),
            (own_rows, F32, "h"),
            ((frames, width), BF16, "h"),
            ((4 * width, width), BF16, "h"),
            ((hidden, width), BF16, "h"),
            ((hidden, width), BF16, "h"),
        ],
        "ssvvvvvvvvhhhhhhhhh",
        [
            (own_rows, F32),
            (own_rows, BF16),
            ((4 * width, width), BF16),
            (own_rows, F32),
            (padded, BF16),
            (padded, BF16),
            (padded, BF16),
            ((hidden, width), BF16),
            ((hidden, width), BF16),
            (padded, BF16),
            ((2, width, width), F32),
            ((4 * width, width), BF16),
            ((hidden, width), BF16),
            ((hidden, width), BF16),
            ((blocks, wide, width), BF16),
            ((blocks, wide, width), BF16),
            ((blocks, 1, wide), F32),
            ((blocks, 1, wide), F32),
            ((blocks, width, BLOCK), F32),
            ((blocks, width, BLOCK), F32),
            (padded, F32),
            (padded, F32),
            ((blocks, 1, BLOCK), jnp.int32),
            ((blocks, 1, BLOCK), jnp.int32),
            dma((5,)),
            dma((5,)),
            dma((3, frames // UNIT)),
            dma((3,)),
        ],
        56,
    )(
        far, bounds, cq, segment_rows, inner_row, value_row, norm_gain,
        norm_shift, cross_offset.reshape(1, width), outer_offset.reshape(1, width),
        after, cotangent, wcross_rows, ck, cv, memory_rows, far_memory, inner_rows, outer_rows,
    )

    def return_far():
        (summed,) = call(
            sum_far,
            [((frames, width), BF16, "h")],
            "h",
            [((frames, width), BF16), (far_shape, BF16), dma((4, window - NEAR)), dma],
            16,
            collective_id=3,
            has_side_effects=True,
        )(mgrad)
        return summed

    mgrad = lax.cond(beyond, return_far, lambda: mgrad)
    partial_results = call(
        functools.partial(give_back, NEAR),
        [
            (own_rows, F32, "v"),
            ((frames // parts, width), BF16, "v"),
            (sliced(n_att), BF16, "v"),
            (sliced(n_att), BF16, "v"),
            (sliced(n_ffn), BF16, "v"),
            (sliced(n_ffn), BF16, "v"),
            ((small_rows, width), F32, "v"),
        ],
        "ssvvhhhhhhhhhhhh",
        [
            (own_rows, BF16),
            (halo_rows, BF16),
            (own_rows, BF16),
            (halo_rows, BF16),
            (halo_rows, BF16),
            (own_rows, BF16),
            (own_rows, F32),
            ((4 * width, width), BF16),
            ((frames, width), BF16),
            ((NEAR, piece, width), BF16),
            ((NEAR, piece, width), BF16),
            (sliced(parts * n_att), BF16),
            (sliced(parts * n_att), BF16),
            (sliced(parts * n_ffn), BF16),
            (sliced(parts * n_ffn), BF16),
            (halo_rows, F32),
            (halo_rows, F32),
            (own_rows, BF16),
            ((HALO, width), BF16),
            ((HALO, width), BF16),
            ((2, 2, 2, small_rows, width), F32),
            ((2 * (n_bits - 1), small_rows, width), F32),
            reduce_buffers(n_att),
            reduce_buffers(n_att),
            reduce_buffers(n_ffn),
            reduce_buffers(n_ffn),
            dma((12,)),
            dma((4, NEAR)),
            dma((4, 2, 6)),
            dma((4, 2, max(n_bits - 3, 1))),
            dma((4, 2, 8)),
            dma((2,)),
            dma((2, 8)),
            dma((2, n_bits - 1)),
        ],
        56,
        collective_id=1,
        has_side_effects=True,
    )(
        tok_lengths, frame_lengths, small, norm_gain, block_input, n1, q, k, v, att, grad, wself_rows,
        mgrad, dw_cross.reshape(sliced(parts * n_att)), dwi.reshape(sliced(parts * n_ffn)),
        dwo.reshape(sliced(parts * n_ffn)),
    )
    input_grad, mgrad_sum, fself, fcross, finner, fouter, small = partial_results
    results = call(
        finals,
        [
            ((frames // parts, width), F32, "v"),
            (own_rows, F32, "v"),
            ((3, width), F32, "v"),
            ((3, width), F32, "v"),
            ((3, own, width), F32, "v"),
            ((2, own), F32, "v"),
            ((own, width), F32, "v"),
            ((1, width), F32, "v"),
            ((3, own, width), F32, "v"),
            ((2, own), F32, "v"),
            ((own, width), F32, "v"),
            ((1, width), F32, "v"),
            ((width, own_hidden), F32, "v"),
            ((1, own_hidden), F32, "v"),
            ((own_hidden, width), F32, "v"),
            ((1, width), F32, "v"),
        ],
        "vvvvvvv",
        [],
        56,
    )(mgrad_sum, input_grad, fself, fcross, finner, fouter, small)
    memory_grad, input_grad, *others = results
    others = [r.reshape(-1) if r.shape[0] == 1 else r for r in others]
    others[2], others[6] = turned(others[2]), turned(others[6])
    return (block_output, input_grad, memory_grad, *others)


def solution(mesh):
    in_specs = (
        P(("dp", "mp"), None),
        P(("dp", "mp"), None),
        P("dp", None),
        P("dp", None),
        P(("dp", "mp"), None),
        P(),
        P(),
        P(None, None, "mp"),
        P(None, "mp"),
        P("mp", None),
        P(),
        P(None, None, "mp"),
        P(None, "mp"),
        P("mp", None),
        P(),
        P(None, "mp"),
        P("mp"),
        P("mp", None),
        P(),
    )
    out_specs = (
        P(("dp", "mp"), None),
        P(("dp", "mp"), None),
        P(("dp", "mp"), None),
        P(),
        P(),
        P(None, None, "mp"),
        P(None, "mp"),
        P("mp", None),
        P(),
        P(None, None, "mp"),
        P(None, "mp"),
        P("mp", None),
        P(),
        P(None, "mp"),
        P("mp"),
        P("mp", None),
        P(),
    )
    return jax.shard_map(shards, mesh=mesh, in_specs=in_specs, out_specs=out_specs, check_vma=False)
```

```python
import functools
import math

import jax
import jax.numpy as jnp
from jax import lax
from jax.experimental import pallas as pl
from jax.experimental.pallas import tpu as pltpu
from jax.sharding import PartitionSpec as P

HEAD = 64
NEGATIVE = -1e30
EPSILON = 1e-05
BLOCK = 128
TILE = 512
UNIT = 128
SIZES = (1024, 512, 256)
HALO = 256
REACH = 208
F32 = jnp.float32
BF16 = jnp.bfloat16
MESH = pl.DeviceIdType.MESH
HALF = HEAD // 2
SLICES = 8
PIECES = 4
NEAR = 6
GELU_A = math.sqrt(2.0 / math.pi)
GELU_B = 0.044715


def mm(a, b, ca=1, cb=0):
    return lax.dot_general(a, b, (((ca,), (cb,)), ((), ())), preferred_element_type=F32)


def normed(values):
    center = values - jnp.mean(values, axis=-1, keepdims=True)
    spread = jnp.mean(center * center, axis=-1, keepdims=True)
    scale = lax.rsqrt(spread + EPSILON)
    return center * scale, scale


def norm_back(grad, gain, xhat, scale):
    gn = grad * gain
    first = jnp.mean(gn, axis=-1, keepdims=True)
    second = jnp.mean(gn * xhat, axis=-1, keepdims=True)
    return (gn - first - xhat * second) * scale


def column_sums(values):
    return jnp.sum(values, axis=0, keepdims=True)


def head_stack(values):
    rows, width = values.shape
    heads = width // HEAD
    lane = lax.broadcasted_iota(jnp.int32, (rows, width), 1) // HALF % heads
    zero = jnp.zeros_like(values)
    return jnp.concatenate([jnp.where(lane == h, values, zero) for h in range(heads)], axis=0)


def head_rows(heads):
    return [
        (slice((i * heads + h) * HALF, (i * heads + h + 1) * HALF), h)
        for i in range(2)
        for h in range(heads)
    ]


def head_diagonal(values, heads):
    rows = values.shape[1] // heads
    return jnp.concatenate(
        [values[r, h * rows : (h + 1) * rows] for r, h in head_rows(heads)], axis=0
    )


def token_rows(tok_ref, frm_ref, base, count):
    place = lax.broadcasted_iota(jnp.int32, (1, count), 1) + base
    zero = jnp.zeros((1, count), jnp.int32)

    def step(u, carry):
        start, first_row, first_frame, end_frame = carry
        tokens, frames = tok_ref[0, u], frm_ref[0, u]
        end = start + tokens
        done = place >= end
        first_row = first_row + jnp.where(done, tokens, 0)
        first_frame = first_frame + jnp.where(done, frames, 0)
        end_frame = end_frame + jnp.where(place >= start, frames, 0)
        return end, first_row, first_frame, end_frame

    _, first_row, first_frame, end_frame = lax.fori_loop(
        0, tok_ref.shape[1], step, (jnp.int32(0), zero, zero, zero)
    )
    return place, first_row, first_frame, end_frame


def excursion(tok_ref, frm_ref, rows, frames, parts):
    lane = lax.broadcasted_iota(jnp.int32, (1, 128), 1)
    zero = jnp.zeros((1, 128), jnp.int32)

    def step(u, carry):
        start, low, high = carry
        tokens, count = tok_ref[0, u], frm_ref[0, u]
        end = start + tokens
        low = low + jnp.where(lane * rows >= end, count, 0)
        high = high + jnp.where((lane + 1) * rows - 1 >= start, count, 0)
        return end, low, high

    _, low, high = lax.fori_loop(0, tok_ref.shape[1], step, (jnp.int32(0), zero, zero))
    beyond = jnp.maximum(high - (lane + 1) * frames, lane * frames - low)
    return jnp.max(jnp.where(lane < parts, beyond, 0), axis=1, keepdims=True).astype(F32)


def block_frames(tok_ref, frm_ref, base):
    lane = lax.broadcasted_iota(jnp.int32, (1, 128), 1) * BLOCK + base
    zero = jnp.zeros((1, 128), jnp.int32)

    def step(u, carry):
        start, low, high = carry
        tokens, frames = tok_ref[0, u], frm_ref[0, u]
        end = start + tokens
        low = low + jnp.where(lane >= end, frames, 0)
        high = high + jnp.where(lane + (BLOCK - 1) >= start, frames, 0)
        return end, low, high

    _, low, high = lax.fori_loop(0, tok_ref.shape[1], step, (jnp.int32(0), zero, zero))
    return low // UNIT * UNIT, high, low


def window_mask(place, first_row, base, block, count):
    keys = lax.broadcasted_iota(jnp.int32, (count, BLOCK), 0) + (base - HALO + block * BLOCK)
    here = slice(block * BLOCK, (block + 1) * BLOCK)
    return (keys >= first_row[:, here]) & (keys <= place[:, here])


def self_probs(queries, key_window, mask, heads):
    scores = mm(key_window, queries, 1, 1)
    parts = []
    for h in range(heads):
        part = jnp.where(mask, scores[:, h * BLOCK : (h + 1) * BLOCK], NEGATIVE)
        raised = jnp.exp(part - jnp.max(part, axis=0, keepdims=True))
        parts.append(raised * (1.0 / jnp.sum(raised, axis=0, keepdims=True)))
    return jnp.concatenate(parts, axis=1)


def rcopy(src, dst, send, recv, **device):
    return pltpu.make_async_remote_copy(
        src_ref=src, dst_ref=dst, send_sem=send, recv_sem=recv, device_id=device, device_id_type=MESH
    )


def at_rows(start, count):
    return pl.ds(pl.multiple_of(start, 16), count)


def flipped(index, bit):
    return index + bit - 2 * bit * (index // bit % 2)


def greet(z, parts, d, bits, masks=()):
    barrier = pltpu.get_barrier_semaphore()
    for mask in masks:
        device = {"dp": masked(d, mask)}
        pl.semaphore_signal(barrier, inc=1, device_id=device, device_id_type=MESH)
    for step in range(1, parts):
        device = {"mp": (z + step) % parts}
        pl.semaphore_signal(barrier, inc=1, device_id=device, device_id_type=MESH)
    for bit in bits:
        device = {"dp": flipped(d, bit)}
        pl.semaphore_signal(barrier, inc=1, device_id=device, device_id_type=MESH)
    return barrier, parts - 1 + len(bits) + len(masks)


class Double:
    def __init__(self, z, own, place, sems):
        self.z, self.own, self.place, self.sems = z, own, place, sems

    def copies(self, step, other):
        z = self.z
        if step == 0:
            far = flipped(z, 2)
            blocks = [(self.place(far) if other else self.own, self.place(far if other else z), 0)]
            device = far
        else:
            device = flipped(z, 1)
            first = device if other else z
            blocks = [(self.place(i), self.place(i), k) for k, i in ((1, first), (2, flipped(first, 2)))]
        sems = self.sems
        return [rcopy(src, dst, sems.at[0, k], sems.at[1, k], mp=device) for src, dst, k in blocks]

    def send(self, step):
        for copy in self.copies(step, False):
            copy.start()

    def arrived(self, step):
        for copy in self.copies(step, True):
            copy.wait_recv()

    def close(self):
        for step in range(2):
            for copy in self.copies(step, False):
                copy.wait_send()


DP_BITS = (2, 4, 1)


def corner(d):
    return d % 2, d // 4 % 2, d // 2 % 2


class Plane:
    def __init__(self, d, buffer, first_y, sems):
        self.d, self.buffer, self.first_y, self.sems = d, buffer, first_y, sems

    def block(self, p, c, y, x):
        if p == 0:
            return self.buffer.at[c, y, x]
        if p == 2:
            return self.buffer.at[c]
        return self.buffer.at[c, :, x] if self.first_y else self.buffer.at[c, y]

    def copy(self, p, other):
        c, y, x = corner(self.d)
        over_y = p == (0 if self.first_y else 1)
        if other:
            if p == 2:
                c = 1 - c
            elif over_y:
                y = 1 - y
            else:
                x = 1 - x
        block = self.block(p, c, y, x)
        device = flipped(self.d, 1 if p == 2 else 4 if over_y else 2)
        return rcopy(block, block, self.sems.at[0, p], self.sems.at[1, p], dp=device)

    def send(self, p):
        self.copy(p, False).start()

    def arrived(self, p):
        self.copy(p, True).wait_recv()

    def close(self):
        for p in range(3):
            self.copy(p, False).wait_send()


class Window:
    def __init__(self, z, parts, source, place, sems):
        self.z, self.parts, self.source, self.place, self.sems = z, parts, source, place, sems

    def number(self, z, j, up):
        return (z + 1) * PIECES - 1 - j if up else z * PIECES + j

    def there(self, number):
        return (number >= 0) & (number < self.parts * PIECES)

    def copy(self, j, up):
        number = self.number(self.z, j, up)
        place, kind = self.place(number, j, up), 0 if up else 2
        return rcopy(
            self.source(number, j, up),
            place,
            self.sems.at[kind, j],
            self.sems.at[kind + 1, j],
            mp=self.z + 1 if up else self.z - 1,
        )

    def sends(self, j, up):
        edge = self.z < self.parts - 1 if up else self.z > 0
        return edge & self.there(self.number(self.z, j, up))

    def send(self, j):
        for up in (True, False):

            @pl.when(self.sends(j, up))
            def _():
                self.copy(j, up).start()

    def comes(self, j, up):
        edge = self.z > 0 if up else self.z < self.parts - 1
        return edge & self.there(self.arrival(j, up))

    def arrival(self, j, up):
        return self.number(self.z - 1 if up else self.z + 1, j, up)

    def arrived(self, j):
        for up in (True, False):

            @pl.when(self.comes(j, up))
            def _():
                number = self.arrival(j, up)
                place, kind = self.place(number, j, up), 0 if up else 2
                rcopy(
                    place,
                    place,
                    self.sems.at[kind, j],
                    self.sems.at[kind + 1, j],
                    mp=self.z - 1 if up else self.z + 1,
                ).wait_recv()

    def each(self, j, use):
        for up in (True, False):

            @pl.when(self.comes(j, up))
            def _():
                use(self.arrival(j, up), j, up)

    def close(self, pieces):
        for j in pieces:
            for up in (True, False):

                @pl.when(self.sends(j, up))
                def _():
                    self.copy(j, up).wait_send()


def gather(
    tok, frm, x_ref, mem, sw, so, cw, co, inner, outer, sb, cb, ib, gain, shift, offset,
    wself_out, wcross_out, inner_out, outer_out, ib_out, vb_out, segment_out, bounds_out, far_out, mem_out, ck_out, cv_out, spare,
    n1_out, q_out, k_out, v_out, att_out, after_out, cq_out,
    n1_ref, q_ref, k_ref, v_ref, att_ref, after_ref, cq_ref,
    gself, gcross, ginner, gouter, gmem, sck, scv, pself, pcross, pinner, halo, pbias, gbias,
    far, far_land, line_sems, mem_sems, plane_sems, bias_sems, halo_sems, far_sems, own_sem, out_sems, weight_sems, row_sems,
):
    rows, width = x_ref.shape
    heads = width // HEAD
    own = sw.shape[1]
    parts = width // own
    shard_rows = mem.shape[0]
    piece = shard_rows // PIECES
    z, d = lax.axis_index("mp"), lax.axis_index("dp")
    dp = lax.axis_size("dp")
    bits = [1 << i for i in range(dp.bit_length() - 1)]
    c, y, x = corner(d)
    s = c * 4 + y * 2 + x
    barrier, greetings = greet(z, parts, d, bits)

    for source, last, packed in ((sw, so, pself), (cw, co, pcross)):
        for i in range(3):
            packed[i * own : (i + 1) * own] = source[i]
        packed[3 * own :] = last[...]
    pbias[...] = jnp.zeros_like(pbias)
    lanes = pbias.shape[1]
    bias_rows = ib.shape[1] // lanes
    for i in range(bias_rows):
        pbias[i : i + 1] = ib[:, i * lanes : (i + 1) * lanes]

    def bias_place(i):
        return slice(bias_rows + i * own // lanes, bias_rows + i * own // lanes + 1), i * own % lanes

    for i in range(4):
        row, lane = bias_place(i)
        pbias[row, lane : lane + own] = (sb, cb)[i // 2][i % 2 : i % 2 + 1]
    pinner[...] = inner[...].T
    groups = []
    for i, (packed, buffer) in enumerate(
        ((pself, gself), (pcross, gcross), (pinner, ginner), (outer, gouter))
    ):
        n = packed.shape[0] // SLICES
        mine = packed.at[at_rows(s * n, n)]

        def place(shard, buffer=buffer, n=n):
            return buffer.at[c, y, x, at_rows(shard * n, n)]

        line = Double(z, mine, place, line_sems.at[i])
        plane = Plane(d, buffer, i % 2 == 1, plane_sems.at[i])
        groups.append((line, plane))
        buffer[c, y, x, at_rows(z * n, n)] = packed[at_rows(s * n, n)]

    def piece_place(number, j, up):
        return gmem.at[at_rows(number * piece, piece)]

    def piece_source(number, j, up):
        if j < PIECES:
            return mem.at[at_rows((number - z * PIECES) * piece, piece)]
        return piece_place(number, j, up)

    memory = Window(z, parts, piece_source, piece_place, mem_sems)

    bias_line = Double(z, pbias, lambda shard: gbias.at[shard], bias_sems)

    def halo_copy(other):
        source, place = x_ref.at[rows - REACH :], halo.at[HALO - REACH :]
        return rcopy(source, place, halo_sems.at[0], halo_sems.at[1], mp=other)

    def far_copy(i):
        device = flipped(d, bits[i])
        return rcopy(far.at[i], far_land.at[i], far_sems.at[0, i], far_sems.at[1, i], dp=device)

    def far_step(i):
        if i > 0:
            far_copy(i - 1).wait_recv()
            far[i] = jnp.maximum(far[i - 1], far_land[i - 1])
        if i < len(bits):
            far_copy(i).start()
        else:
            far_out[...] = far[i, 0:1, 0:1]

    def forward(j):
        memory.arrived(j - PIECES)
        memory.send(j)

    far[0] = jnp.broadcast_to(excursion(tok, frm, rows, shard_rows, parts), far.shape[1:])
    gbias[z] = pbias[...]
    own_rows = gmem.at[at_rows(z * shard_rows, shard_rows)]
    own_copy = pltpu.make_async_copy(mem, own_rows, own_sem)
    own_copy.start()
    pl.semaphore_wait(barrier, greetings)
    for line, _ in groups[:2]:
        line.send(0)
    bias_line.send(0)

    @pl.when(z < parts - 1)
    def _():
        halo_copy(z + 1).start()

    for line, _ in groups[2:]:
        line.send(0)
    for line in (groups[0][0], groups[1][0], bias_line):
        line.arrived(0)
        line.send(1)
    memory.send(0)
    for line, _ in groups[2:]:
        line.arrived(0)
        line.send(1)
    for j in range(1, PIECES):
        memory.send(j)
    far_step(0)
    for line, plane in groups[:2]:
        line.arrived(1)
        plane.send(0)
    for _, plane in groups[:2]:
        plane.arrived(0)
        plane.send(1)
    for line, plane in groups[2:]:
        line.arrived(1)
        plane.send(0)
    far_step(1)
    for _, plane in groups[:2]:
        plane.arrived(1)
        plane.send(2)
    far_step(2)
    groups[0][1].arrived(2)

    bias_line.arrived(1)

    def head_bias(i):
        row, lane = bias_place(i)
        return jnp.concatenate(
            [
                gbias[o, row, lane + half * HALF : lane + (half + 1) * HALF]
                for half in range(2)
                for o in range(parts)
            ],
            axis=1,
        )

    n = ginner.shape[3] // parts
    for i in range(SLICES):
        ib_out[i : i + 1] = jnp.concatenate(
            [
                gbias[o, i * n // lanes : i * n // lanes + 1, i * n % lanes : i * n % lanes + n]
                for o in range(parts)
            ],
            axis=1,
        )

    @pl.when(z > 0)
    def _():
        halo_copy(z - 1).wait_recv()

    halo[: HALO - REACH] = jnp.zeros((HALO - REACH, width), BF16)

    @pl.when(z == 0)
    def _():
        halo[HALO - REACH :] = jnp.zeros((REACH, width), BF16)

    def weight(buffer, i):
        return buffer[i // 2, i % 2].reshape(width, width)

    base = z * rows
    place_row, first_row, first_frame, end_frame = token_rows(tok, frm, base, rows)
    segment_out[0:1], segment_out[1:2] = first_frame, end_frame
    bounds_out[0:1], bounds_out[1:2], bounds_out[2:3] = block_frames(tok, frm, base)
    for src, dst in ((halo, slice(0, HALO)), (x_ref, slice(HALO, HALO + rows))):
        xhat, _ = normed(src[...].astype(F32))
        n1_ref[dst] = (xhat * gain[0:1] + shift[0:1]).astype(BF16)
    n1 = n1_ref[...]
    query = mm(n1[HALO:], weight(gself, 0), 1, 1) + head_bias(0)
    q_ref[...] = query.astype(BF16) * jnp.asarray(0.125, BF16)
    k_ref[...] = mm(n1, weight(gself, 1), 1, 1).astype(BF16)
    v_ref[...] = (mm(n1, weight(gself, 2), 1, 1) + head_bias(1)).astype(BF16)
    count = HALO + BLOCK
    for b in range(rows // BLOCK):
        queries = head_stack(q_ref[b * BLOCK : (b + 1) * BLOCK])
        window = slice(b * BLOCK, b * BLOCK + count)
        mask = window_mask(place_row, first_row, base, b, count)
        probs = self_probs(queries, k_ref[window], mask, heads).astype(BF16)
        out = head_diagonal(mm(v_ref[window], probs, 0, 0), heads)
        att_ref[b * BLOCK : (b + 1) * BLOCK] = out.T.astype(BF16)
        if b == 0:
            for _, plane in groups[2:]:
                plane.arrived(0)
                plane.send(1)
    forward(PIECES)
    after = x_ref[...].astype(F32) + mm(att_ref[...], weight(gself, 3)) + offset[...]
    after_ref[...] = after
    xhat, _ = normed(after)
    groups[1][1].arrived(2)
    n2 = (xhat * gain[1:2] + shift[1:2]).astype(BF16)
    query = mm(n2, weight(gcross, 0), 1, 1) + head_bias(2)
    cq_ref[...] = query.astype(BF16) * jnp.asarray(0.125, BF16)
    value_bias = head_bias(3)
    row_stores = [
        pltpu.make_async_copy(a, b, row_sems.at[i])
        for i, (a, b) in enumerate(
            (
                (n1_ref, n1_out),
                (q_ref, q_out),
                (k_ref, k_out),
                (v_ref, v_out),
                (att_ref, att_out),
                (after_ref, after_out),
                (cq_ref, cq_out),
            )
        )
    ]
    for store in row_stores:
        store.start()
    forward(PIECES + 1)

    def project(start, size):
        here = at_rows(start, size)
        block = gmem[here]
        sck[here] = mm(block, weight(gcross, 1), 1, 1).astype(BF16)
        scv[here] = (mm(block, weight(gcross, 2), 1, 1) + value_bias).astype(BF16)

    def copies_out(number):
        here = at_rows(number * piece, piece)
        return [
            pltpu.make_async_copy(a.at[here], b.at[here], out_sems.at[number, i])
            for i, (a, b) in enumerate(((gmem, mem_out), (sck, ck_out), (scv, cv_out)))
        ]

    def project_piece(number, j=0, up=True):
        project(number * piece, piece)
        for copy in copies_out(number):
            copy.start()

    own_copy.wait()
    lax.fori_loop(0, PIECES, lambda i, _: (project_piece(z * PIECES + i), 0)[1], 0)
    for _, plane in groups[2:]:
        plane.arrived(1)
        plane.send(2)
    for j in range(PIECES):
        if j >= 2:
            memory.arrived(j)
        memory.each(j, project_piece)
    for i in range(3, len(bits) + 1):
        far_step(i)
    for _, plane in groups[2:]:
        plane.arrived(2)
    outs = [
        pltpu.make_async_copy(a, b, weight_sems.at[i])
        for i, (a, b) in enumerate(
            ((gself, wself_out), (gcross, wcross_out), (ginner, inner_out), (gouter, outer_out))
        )
    ]
    for copy in outs:
        copy.start()
    vb_out[...] = value_bias
    for j in range(PIECES, NEAR):
        memory.arrived(j)
        memory.each(j, project_piece)
    for copy in outs + row_stores:
        copy.wait()

    def finish(number, *_):
        for copy in copies_out(number):
            copy.wait()

    for i in range(PIECES):
        finish(z * PIECES + i)
    for j in range(NEAR):
        memory.each(j, finish)
    for line, plane in groups:
        line.close()
        plane.close()
    memory.close(range(NEAR))
    for i in range(len(bits)):
        far_copy(i).wait_send()
    bias_line.close()

    @pl.when(z < parts - 1)
    def _():
        halo_copy(z + 1).wait_send()


def gather_far(mem, far_mem, sems):
    z, d = lax.axis_index("mp"), lax.axis_index("dp")
    parts = lax.axis_size("mp")
    last = PIECES * (parts - 1)
    piece = mem.shape[0] // parts // PIECES
    barrier, greetings = greet(z, parts, d, ())

    def place(number, j, up):
        return far_mem.at[at_rows(number * piece, piece)]

    def source(number, j, up):
        return (mem if j - PIECES < NEAR else far_mem).at[at_rows(number * piece, piece)]

    memory = Window(z, parts, source, place, sems)
    pl.semaphore_wait(barrier, greetings)
    for j in range(NEAR, last):
        if j - PIECES >= NEAR:
            memory.arrived(j - PIECES)
        memory.send(j)
    for j in range(max(NEAR, last - PIECES), last):
        memory.arrived(j)
    memory.close(range(NEAR, last))


def middle(
    far, bounds, cq_ref, segment_ref, ib_ref, vb_ref, gain, shift, cross_offset, outer_offset,
    after_in, cot_in, w_in, ck_in, cv_in, mem_in, far_in, wi_in, wo_in,
    grad_ref, small_ref, block_out, mgrad_out, dw_out, dwi_out, dwo_out,
    after_ref, cot_ref, w_ref, out_ref,
    ck_ref, cv_ref, mem_ref, wi_ref, wo_ref, mgrad_ref, dw_ref, dwb_ref, dwi_ref, dwo_ref,
    qbig, gbig, lse_ref, dot_ref, att_ref, dq_ref, dk_ref, dv_ref, first_ref, end_ref,
    in_sems, out_sems, unit_sems, far_sems,
):
    rows, width = cq_ref.shape
    heads = width // HEAD
    blocks = rows // BLOCK
    z = lax.axis_index("mp")
    parts = lax.axis_size("mp")
    last = parts * PIECES
    frames = mem_in.shape[0]
    piece = frames // last
    beyond = far[0, 0] > NEAR * piece

    def weight(i):
        return w_ref[i * width : (i + 1) * width]

    def rows_of(number):
        return at_rows(jnp.clip(number, 0, last - 1) * piece, piece)

    def spans(i, unit):
        here = pl.ds(pl.multiple_of(origin + unit * UNIT, UNIT), UNIT)
        source, full = arrays[i]
        return pltpu.make_async_copy(source.at[here], full.at[here], unit_sems.at[i, unit])

    def units(i, name):
        def one(unit, carry):
            getattr(spans(i, unit), name)()
            return carry

        lax.fori_loop(0, unit_count, one, 0)

    arrays = ((ck_in, ck_ref), (cv_in, cv_ref), (mem_in, mem_ref))
    for b in range(blocks):
        first_ref[b] = segment_ref[0:1, b * BLOCK : (b + 1) * BLOCK]
        end_ref[b] = segment_ref[1:2, b * BLOCK : (b + 1) * BLOCK]
        qbig[b] = head_stack(cq_ref[b * BLOCK : (b + 1) * BLOCK])
    origin = bounds[0, 0]
    unit_count = (bounds[1, blocks - 1] - origin + UNIT - 1) // UNIT
    count = (unit_count * UNIT + TILE - 1) // TILE
    loads = [
        pltpu.make_async_copy(a, b, in_sems.at[i])
        for i, (a, b) in enumerate(
            ((wi_in, wi_ref), (wo_in, wo_ref), (after_in, after_ref), (cot_in, cot_ref), (w_in, w_ref))
        )
    ]

    @pl.when(jnp.logical_not(beyond))
    def _():
        units(0, "start")
        units(1, "start")

    for load in loads:
        load.start()

    @pl.when(jnp.logical_not(beyond))
    def _():
        units(2, "start")

    @pl.when(beyond)
    def _():
        loads[4].wait()

        def fetch(i, carry):
            number = i
            here = rows_of(number)
            distance = jnp.maximum(z * PIECES - 1 - number, number - (z + 1) * PIECES)

            @pl.when(distance < NEAR)
            def _():
                copies = [
                    pltpu.make_async_copy(a.at[here], b.at[here], far_sems.at[k])
                    for k, (a, b) in enumerate(arrays)
                ]
                for copy in copies:
                    copy.start()
                for copy in copies:
                    copy.wait()

            @pl.when(distance >= NEAR)
            def _():
                copy = pltpu.make_async_copy(far_in.at[here], mem_ref.at[here], far_sems.at[0])
                copy.start()
                copy.wait()
                block = mem_ref[here]
                ck_ref[here] = mm(block, weight(1), 1, 1).astype(BF16)
                cv_ref[here] = (mm(block, weight(2), 1, 1) + vb_ref[...]).astype(BF16)

            return carry

        lax.fori_loop(0, last, fetch, 0)

    tail = pl.ds(pl.multiple_of(origin + unit_count * UNIT, UNIT), SIZES[0])
    for _, full in arrays:
        full[tail] = jnp.zeros((SIZES[0], width), BF16)
    small_ref[...] = jnp.zeros_like(small_ref)
    mgrad_ref[...] = jnp.zeros_like(mgrad_ref)

    def over_tiles(b, step, carry):
        large, medium, small = SIZES
        start = bounds[0, b]
        length = bounds[1, b] - start
        number = (length + medium - 1) // large
        left = length - number * large
        after = start + number * large
        carry = lax.fori_loop(0, number, lambda i, c: step(large, start + i * large, c), carry)
        one = (left > small).astype(jnp.int32)
        carry = lax.fori_loop(0, one, lambda i, c: step(medium, after, c), carry)
        one = ((left > 0) & (left <= small)).astype(jnp.int32)
        return lax.fori_loop(0, one, lambda i, c: step(small, after, c), carry)

    def tile_mask(size, start, b):
        frame = lax.broadcasted_iota(jnp.int32, (size, BLOCK), 0) + start
        return (frame >= first_ref[b]) & (frame < end_ref[b])

    def columns(h):
        return slice(h * BLOCK, (h + 1) * BLOCK)

    @pl.when(jnp.logical_not(beyond))
    def _():
        units(0, "wait")
        units(1, "wait")

    def clear_outside(full):
        for unit in (0, unit_count - 1):
            first = pl.multiple_of(origin + unit * UNIT, UNIT)
            frame = lax.broadcasted_iota(jnp.int32, (UNIT, width), 0) + first
            inside = (frame >= bounds[2, 0]) & (frame < bounds[1, blocks - 1])
            block = full[pl.ds(first, UNIT)].astype(F32)
            full[pl.ds(first, UNIT)] = jnp.where(inside, block, 0.0).astype(BF16)

    clear_outside(ck_ref)
    clear_outside(cv_ref)

    def attend(b, carry):
        att_ref[b] = jnp.zeros((width, BLOCK), F32)

        def step(size, start, carry):
            here = pl.ds(pl.multiple_of(start, UNIT), size)
            scores = mm(ck_ref[here], qbig[b], 1, 1)
            mask = tile_mask(size, start, b)
            values = cv_ref[here].T
            news = []
            for h in range(heads):
                largest, total = carry[h]
                part = jnp.where(mask, scores[:, columns(h)], NEGATIVE)
                now = jnp.maximum(largest, jnp.max(part, axis=0, keepdims=True))
                fade = jnp.exp(largest - now)
                raised = jnp.exp(part - now)
                news.append((now, total * fade + jnp.sum(raised, axis=0, keepdims=True)))
                pieces = [r for r, o in head_rows(heads) if o == h]
                own = jnp.concatenate([values[r] for r in pieces], axis=0)
                out = mm(own, raised.astype(BF16))
                for i, r in enumerate(pieces):
                    att_ref[b, r] = att_ref[b, r] * fade + out[i * HALF : (i + 1) * HALF]
            return tuple(news)

        start = (jnp.full((1, BLOCK), NEGATIVE, F32), jnp.zeros((1, BLOCK), F32))
        done = over_tiles(b, step, (start,) * heads)
        for h, (largest, total) in enumerate(done):
            lse_ref[b, :, columns(h)] = largest + jnp.log(total)
            share = 1.0 / total
            for r, o in head_rows(heads):
                if o == h:
                    att_ref[b, r] = att_ref[b, r] * share
        return carry

    lax.fori_loop(0, blocks, attend, 0)
    att = jnp.concatenate([att_ref[b].T for b in range(blocks)], axis=0).astype(BF16)
    loads[2].wait()
    loads[3].wait()

    @pl.when(jnp.logical_not(beyond))
    def _():
        loads[4].wait()

    after_self = after_ref[...]
    after_cross = after_self + mm(att, weight(3)) + cross_offset[...]
    xhat3, scale3 = normed(after_cross)
    n3 = (xhat3 * gain[2:3] + shift[2:3]).astype(BF16)
    sent = cot_ref[...]
    small_ref[8:9] = column_sums(sent.astype(F32))
    hidden = wi_ref.shape[0]
    group = 1
    tile = hidden // SLICES * group
    loads[0].wait()
    loads[1].wait()
    out_ref[...] = after_cross + outer_offset[...]
    grad_ref[...] = jnp.zeros((rows, width), F32)

    def feed(f, carry):
        here = pl.ds(pl.multiple_of(f * tile, tile), tile)
        bias = jnp.concatenate([ib_ref[pl.ds(f * group + i, 1)] for i in range(group)], axis=1)
        before = mm(n3, wi_ref[here], 1, 1) + bias
        square = before * before
        inner = jnp.tanh(before * (GELU_A + (GELU_A * GELU_B) * square))
        half = 0.5 + 0.5 * inner
        active = (before * half).astype(BF16)
        slope = half + (0.5 * before) * (1.0 - inner * inner) * (
            GELU_A + (3.0 * GELU_A * GELU_B) * square
        )
        out_ref[...] += mm(active, wo_ref[here])
        back = (slope * mm(sent, wo_ref[here], 1, 1)).astype(BF16)
        grad_ref[...] += mm(back, wi_ref[here])
        dwo_ref[here] = mm(active, sent, 0, 0).astype(BF16)
        dwi_ref[here] = mm(back, n3, 0, 0).astype(BF16)
        sums = column_sums(back.astype(F32))
        for i in range(group):
            small_ref[pl.ds(16 + f * group + i, 1)] = sums[:, i * tile // group : (i + 1) * tile // group]
        return carry

    for f in range(SLICES // group):
        feed(f, 0)
    stores = [
        pltpu.make_async_copy(a, b, out_sems.at[i])
        for i, (a, b) in enumerate(
            (
                (dwi_ref, dwi_out),
                (dwo_ref, dwo_out),
                (dwb_ref, dw_out),
                (mgrad_ref.at[:frames], mgrad_out),
                (out_ref, block_out),
            )
        )
    ]
    stores[0].start()
    stores[1].start()
    stores[4].start()
    dn3 = grad_ref[...]
    small_ref[2:3] = column_sums(dn3 * xhat3)
    small_ref[5:6] = column_sums(dn3)
    grad = sent.astype(F32) + norm_back(dn3, gain[2:3], xhat3, scale3)
    sent2 = grad.astype(BF16)
    small_ref[7:8] = column_sums(sent2.astype(F32))
    dwb_ref[3 * width :] = mm(att, sent2, 0, 0).astype(BF16)
    go = mm(sent2, weight(3), 1, 1).astype(BF16)
    got = mm(weight(3), sent2, 1, 1).astype(BF16).astype(F32)
    for b in range(blocks):
        gbig[b] = head_stack(go[b * BLOCK : (b + 1) * BLOCK])
        prod = got[:, b * BLOCK : (b + 1) * BLOCK] * att_ref[b]
        sums = [column_sums(prod[r]) for r, _ in head_rows(heads)]
        for h in range(heads):
            dot_ref[b, :, columns(h)] = sums[h] + sums[heads + h]
    def span(i):
        return pl.ds(pl.multiple_of(origin + i * TILE, 128), TILE)

    def clear(i, carry):
        dk_ref[span(i)] = jnp.zeros((TILE, width), F32)
        dv_ref[span(i)] = jnp.zeros((TILE, width), F32)
        return carry

    lax.fori_loop(0, count, clear, 0)

    def attend_back(b, carry):
        dq_ref[b] = jnp.zeros((width, BLOCK), F32)

        def step(size, start, carry):
            here = pl.ds(pl.multiple_of(start, UNIT), size)
            keys, values = ck_ref[here], cv_ref[here]
            scores = mm(keys, qbig[b], 1, 1)
            dp = mm(values, gbig[b], 1, 1)
            mask = tile_mask(size, start, b)
            shares, scaled = [], []
            for h in range(heads):
                part = jnp.exp(scores[:, columns(h)] - lse_ref[b, :, columns(h)])
                part = jnp.where(mask, part, 0.0)
                shares.append(part.astype(BF16))
                scaled.append((part * (dp[:, columns(h)] - dot_ref[b, :, columns(h)])).astype(BF16))
            shares, scaled = jnp.concatenate(shares, axis=1), jnp.concatenate(scaled, axis=1)
            dv_ref[here] += mm(shares, gbig[b])
            dk_ref[here] += mm(scaled, qbig[b])
            dq_ref[b] += head_diagonal(mm(keys, scaled, 0, 0), heads)
            return carry

        return over_tiles(b, step, carry)

    lax.fori_loop(0, blocks, attend_back, 0)

    @pl.when(jnp.logical_not(beyond))
    def _():
        units(2, "wait")

    clear_outside(mem_ref)
    dw_ref[...] = jnp.zeros_like(dw_ref)

    def frame_step(i, carry):
        here = span(i)
        dk, dv = dk_ref[here].astype(BF16), dv_ref[here].astype(BF16)
        mgrad_ref[here] = (mm(dk, weight(1)) + mm(dv, weight(2))).astype(BF16)
        frame_rows = mem_ref[here]
        dw_ref[0] += mm(dk, frame_rows, 0, 0)
        dw_ref[1] += mm(dv, frame_rows, 0, 0)
        small_ref[12:13] += column_sums(dv.astype(F32))
        return carry

    lax.fori_loop(0, count, frame_step, 0)
    stores[3].start()
    dq = jnp.concatenate([(dq_ref[b] * 0.125).T for b in range(blocks)], axis=0).astype(BF16)
    small_ref[11:12] = column_sums(dq.astype(F32))
    xhat2, scale2 = normed(after_self)
    n2 = (xhat2 * gain[1:2] + shift[1:2]).astype(BF16)
    dwb_ref[:width] = mm(dq, n2, 0, 0).astype(BF16)
    dwb_ref[width : 2 * width] = dw_ref[0].astype(BF16)
    dwb_ref[2 * width : 3 * width] = dw_ref[1].astype(BF16)
    stores[2].start()
    dn2 = mm(dq, weight(0))
    small_ref[1:2] = column_sums(dn2 * xhat2)
    small_ref[4:5] = column_sums(dn2)
    grad_ref[...] = grad + norm_back(dn2, gain[1:2], xhat2, scale2)
    for store in stores:
        store.wait()


def sum_far(mgrad_in, mgrad_out, own, land, flow_sems, load_sem):
    pieces, piece = land.shape[1:3]
    frames = own.shape[0]
    parts = frames // piece // PIECES
    last = NEAR + pieces
    z, d = lax.axis_index("mp"), lax.axis_index("dp")
    barrier, greetings = greet(z, parts, d, ())
    load = pltpu.make_async_copy(mgrad_in, own, load_sem)
    load.start()

    def rows_of(number):
        return at_rows(number * piece, piece)

    def there(number):
        return (number >= 0) & (number < parts * PIECES)

    def sent(j, up):
        return (z + 1) * PIECES + j if up else z * PIECES - 1 - j

    def comes(j, up):
        return z * PIECES + j if up else (z + 1) * PIECES - 1 - j

    def flow(j, up, number, device):
        kind = 0 if up else 2
        place = land.at[0 if up else 1, j - NEAR]
        sems = flow_sems.at[kind, j - NEAR], flow_sems.at[kind + 1, j - NEAR]
        return rcopy(own.at[rows_of(number)], place, *sems, mp=device)

    def arrive(j):
        for up in (True, False):

            @pl.when(there(comes(j, up)) & (z > 0 if up else z < parts - 1))
            def _():
                number = comes(j, up)
                flow(j, up, number, z - 1 if up else z + 1).wait_recv()
                here = rows_of(number)
                more = land[0 if up else 1, j - NEAR].astype(F32)
                own[here] = (own[here].astype(F32) + more).astype(BF16)

    def each(j, name):
        for up in (True, False):

            @pl.when(there(sent(j, up)) & (z < parts - 1 if up else z > 0))
            def _():
                getattr(flow(j, up, sent(j, up), z + 1 if up else z - 1), name)()

    load.wait()
    pl.semaphore_wait(barrier, greetings)
    for j in reversed(range(NEAR, last)):
        if j + PIECES < last:
            arrive(j + PIECES)
        each(j, "start")
    for j in range(NEAR, min(NEAR + PIECES, last)):
        arrive(j)
    for j in range(NEAR, last):
        each(j, "wait_send")
    store = pltpu.make_async_copy(own, mgrad_out, load_sem)
    store.start()
    store.wait()


def masked(d, mask):
    for bit in (1, 2, 4):
        if mask & bit:
            d = flipped(d, bit)
    return d


CHIPS = (2, 4, 6)


class Reduce:
    def __init__(self, d, z, parts, dp, local, buffers, sems):
        self.d, self.z, self.parts, self.dp, self.local = d, z, parts, dp, local
        self.r1, self.a1, self.r2, self.a3, self.rz, self.a4, self.wide, self.fin = buffers
        self.high, self.low = z // 2, z % 2
        self.sems, self.extra_sems, self.plane_sems = sems
        self.c, self.y, self.x = corner(d)
        self.spread = Chips(d, self.fin, self.plane_sems)
        self.bits = [8 << i for i in range(dp.bit_length() - 4)]

    def to_core(self):
        sems = self.sems
        return rcopy(
            self.local.at[1 - self.c], self.r1, sems.at[0, 0], sems.at[1, 0], dp=flipped(self.d, 1)
        )

    def to_chip(self, i):
        sems, other = self.sems, masked(self.d, CHIPS[i])
        _, y, x = corner(other)
        return rcopy(self.a1.at[y, x], self.r2.at[i], sems.at[0, 1 + i], sems.at[1, 1 + i], dp=other)

    def to_neighbour(self):
        sems = self.sems
        src = self.a3.at[:, 1 - self.low]
        return rcopy(src, self.rz.at[:2], sems.at[0, 4], sems.at[1, 4], mp=flipped(self.z, 1))

    def to_far(self):
        sems = self.sems
        src = self.a4.at[1 - self.high]
        return rcopy(src, self.rz.at[2], sems.at[0, 5], sems.at[1, 5], mp=flipped(self.z, 2))

    def extra(self, i):
        sems = self.extra_sems
        device = flipped(self.d, self.bits[i])
        return rcopy(self.wide.at[2 * i], self.wide.at[2 * i + 1], sems.at[0, i], sems.at[1, i], dp=device)

    def run(self, p):
        if p == 0:
            self.to_core().start()
        elif p == 1:
            self.to_core().wait_recv()
            self.a1[...] = (self.local[self.c].astype(F32) + self.r1[...].astype(F32)).astype(BF16)
            for i in range(3):
                self.to_chip(i).start()
        elif p == 2:
            total = self.a1[self.y, self.x].astype(F32)
            for i in range(3):
                self.to_chip(i).wait_recv()
                total = total + self.r2[i].astype(F32)
            self.a3[...] = total.astype(BF16).reshape(self.a3.shape)
            self.to_neighbour().start()
        elif p == 3:
            self.to_neighbour().wait_recv()
            mine = self.a3[:, self.low].astype(F32) + self.rz[:2].astype(F32)
            self.a4[...] = mine.astype(BF16)
            self.to_far().start()
        elif p == 4:
            self.to_far().wait_recv()
            total = self.a4[self.high].astype(F32) + self.rz[2].astype(F32)
            for i in range(len(self.bits)):
                self.wide[2 * i] = total
                self.extra(i).start()
                self.extra(i).wait_recv()
                total = total + self.wide[2 * i + 1]
            self.fin[self.c, self.y, self.x] = total.astype(BF16)
            self.spread.send(0)
        elif p == 5:
            self.spread.arrived(0)
            self.spread.send(1)
        else:
            self.spread.arrived(1)

    def close(self):
        self.to_core().wait_send()
        for i in range(3):
            self.to_chip(i).wait_send()
        self.to_neighbour().wait_send()
        self.to_far().wait_send()
        for i in range(len(self.bits)):
            self.extra(i).wait_send()
        self.spread.close()


class Spread:
    def __init__(self, d, buffer, sems):
        self.d, self.buffer, self.sems = d, buffer, sems

    def copy(self, m, own):
        neighbour = masked(self.d, m)
        c, y, x = corner(self.d if own else neighbour)
        block = self.buffer.at[c, y, x]
        return rcopy(block, block, self.sems.at[0, m], self.sems.at[1, m], dp=neighbour)

    def send(self):
        for m in range(1, 8):
            self.copy(m, True).start()

    def arrived(self):
        for m in range(1, 8):
            self.copy(m, False).wait_recv()

    def close(self):
        for m in range(1, 8):
            self.copy(m, True).wait_send()


class Chips:
    def __init__(self, d, buffer, sems):
        self.d, self.buffer, self.sems = d, buffer, sems

    def copy(self, m, own):
        neighbour = masked(self.d, m)
        c, y, x = corner(self.d if own else neighbour)
        block = self.buffer.at[c] if m == 1 else self.buffer.at[c, y, x]
        return rcopy(block, block, self.sems.at[0, m], self.sems.at[1, m], dp=neighbour)

    def send(self, p):
        for m in (CHIPS, (1,))[p]:
            self.copy(m, True).start()

    def arrived(self, p):
        for m in (CHIPS, (1,))[p]:
            self.copy(m, False).wait_recv()

    def close(self):
        for m in (1, 2, 4, 6):
            self.copy(m, True).wait_send()


class Total:
    def __init__(self, d, z, bits, buffer, wide, sems, wide_sems):
        self.d, self.z, self.bits, self.wide, self.wide_sems = d, z, bits, wide, wide_sems
        self.buffer = buffer
        self.spread = Spread(d, buffer, sems)

    def extra(self, i):
        sems, count = self.wide_sems, len(self.bits)
        if i < count:
            device = {"dp": flipped(self.d, self.bits[i])}
        else:
            device = {"mp": flipped(self.z, 1 if i == count else 2)}
        return rcopy(self.wide.at[2 * i], self.wide.at[2 * i + 1], sems.at[0, i], sems.at[1, i], **device)

    def run(self, p):
        count = len(self.bits)
        if p == 0:
            self.spread.send()
        elif p == 1:
            self.spread.arrived()
            total = self.buffer[0, 0, 0]
            for c, y, x in [(i // 4, i // 2 % 2, i % 2) for i in range(1, 8)]:
                total = total + self.buffer[c, y, x]
            for i in range(count):
                self.wide[2 * i] = total
                self.extra(i).start()
                self.extra(i).wait_recv()
                total = total + self.wide[2 * i + 1]
            self.wide[2 * count] = total
            self.extra(count).start()
        else:
            self.extra(count).wait_recv()
            self.wide[2 * count + 2] = self.wide[2 * count] + self.wide[2 * count + 1]
            self.extra(count + 1).start()

    def finish(self, out):
        last = len(self.bits) + 1
        self.extra(last).wait_recv()
        out[...] = self.wide[2 * last] + self.wide[2 * last + 1]
        self.spread.close()
        for i in range(last + 1):
            self.extra(i).wait_send()


def give_back(
    window,
    tok, frm, small_in, gain,
    x_in, n1_in, q_in, k_in, v_in, att_in, grad_in, w_in, mgrad_in, dwc_in, dwi_in, dwo_in,
    input_out, mgrad_out, fself, fcross, finner, fouter, small_out,
    x_ref, n1_ref, q_ref, k_ref, v_ref, att_ref, grad_ref, w_ref,
    own, up_land, down_land, local_self, local_cross, local_inner, local_outer,
    dk_ref, dv_ref, dq_ref, halo_out, halo_land, total_buffer, total_wide,
    self_bufs, cross_bufs, inner_bufs, outer_bufs,
    load_sems, flow_sems, reduce_sems, extra_sems, plane_sems, halo_sems, total_sems, wide_sems,
):
    rows, width = q_ref.shape
    heads = width // HEAD
    parts = lax.axis_size("mp")
    shard_rows = mgrad_out.shape[0]
    piece = shard_rows // PIECES
    last = parts * PIECES
    z, d = lax.axis_index("mp"), lax.axis_index("dp")
    dp = lax.axis_size("dp")
    bits = [8 << i for i in range(dp.bit_length() - 4)]
    barrier, greetings = greet(z, parts, d, bits, range(1, 8))
    loads = [
        pltpu.make_async_copy(a, b, load_sems.at[i])
        for i, (a, b) in enumerate(
            (
                (dwi_in, local_inner),
                (dwo_in, local_outer),
                (dwc_in, local_cross),
                (grad_in, grad_ref),
                (w_in, w_ref),
                (q_in, q_ref),
                (k_in, k_ref),
                (v_in, v_ref),
                (n1_in, n1_ref),
                (att_in, att_ref),
                (x_in, x_ref),
                (mgrad_in, own),
            )
        )
    ]
    for load in loads:
        load.start()
    chains = []
    for i, (local, bufs, fin) in enumerate(
        (
            (local_inner, inner_bufs, finner),
            (local_outer, outer_bufs, fouter),
            (local_cross, cross_bufs, fcross),
            (local_self, self_bufs, fself),
        )
    ):
        sems = (reduce_sems.at[i], extra_sems.at[i], plane_sems.at[i])
        chains.append(Reduce(d, z, parts, dp, local, (*bufs, fin), sems))
    inner, outer, cross, own_chain = chains

    def rows_of(number):
        return at_rows(number * piece, piece)

    def crosses(j, up):
        if up:
            return (z < parts - 1) & ((z + 1) * PIECES + j < last)
        return (z > 0) & (z * PIECES - 1 - j >= 0)

    def number(j, up):
        return (z + 1) * PIECES + j if up else z * PIECES - 1 - j

    def flow(j, up, summed):
        land = up_land if up else down_land
        kind = 0 if up else 2
        src = land.at[j + PIECES] if summed else mgrad_in.at[rows_of(number(j, up))]
        device = z + 1 if up else z - 1
        return rcopy(src, land.at[j], flow_sems.at[kind, j], flow_sems.at[kind + 1, j], mp=device)

    def comes(j, up):
        if up:
            return (z > 0) & (z * PIECES + j < last)
        return (z < parts - 1) & ((z + 1) * PIECES - 1 - j >= 0)

    def flow_arrival(j, up):
        land = up_land if up else down_land
        kind = 0 if up else 2
        device = z - 1 if up else z + 1
        return rcopy(
            land.at[j], land.at[j], flow_sems.at[kind, j], flow_sems.at[kind + 1, j], mp=device
        )

    def first_flows(pieces):
        for j in pieces:
            for up in (True, False):

                @pl.when(crosses(j, up))
                def _():
                    flow(j, up, False).start()

    def next_flow(j):
        for up in (True, False):
            land = up_land if up else down_land

            @pl.when(crosses(j, up) & comes(j + PIECES, up))
            def _():
                flow_arrival(j + PIECES, up).wait_recv()
                mine = own[rows_of(number(j, up))]
                land[j + PIECES] = (land[j + PIECES].astype(F32) + mine.astype(F32)).astype(BF16)
                flow(j, up, True).start()

            @pl.when(crosses(j, up) & jnp.logical_not(comes(j + PIECES, up)))
            def _():
                flow(j, up, False).start()

    base = z * rows
    place, first_row, _, _ = token_rows(tok, frm, base, rows)

    def weight(i):
        return w_ref[i * width : (i + 1) * width]

    def halo_copy(other):
        return rcopy(halo_out, halo_land, halo_sems.at[0], halo_sems.at[1], mp=other)

    pl.semaphore_wait(barrier, greetings)
    first_flows((5, 4))
    for load, chain in zip(loads[:3], chains[:3]):
        load.wait()
        chain.run(0)
    c, y, x = corner(d)
    small = total_buffer.at[c, y, x]
    small[...] = small_in[...]
    loads[3].wait()
    loads[4].wait()
    grad = grad_ref[...]
    sent = grad.astype(BF16)
    small[6:7] = column_sums(sent.astype(F32))
    n = local_self.shape[3]

    def keep(i, values):
        for half in range(2):
            s = 2 * i + half
            local_self[s // 4, s // 2 % 2, s % 2] = values[half * n : (half + 1) * n].astype(BF16)

    go = mm(sent, weight(3), 1, 1).astype(BF16)
    dk_ref[...] = jnp.zeros_like(dk_ref)
    dv_ref[...] = jnp.zeros_like(dv_ref)
    count = HALO + BLOCK
    blocks = rows // BLOCK

    def attend_back(b):
        here = slice(b * BLOCK, (b + 1) * BLOCK)
        span = slice(b * BLOCK, b * BLOCK + count)
        queries, grads = head_stack(q_ref[here]), head_stack(go[here])
        mask = window_mask(place, first_row, base, b, count)
        shares = self_probs(queries, k_ref[span], mask, heads)
        dp_ = mm(v_ref[span], grads, 1, 1)
        ds = (shares * (dp_ - jnp.sum(shares * dp_, axis=0, keepdims=True))).astype(BF16)
        dv_ref[span] += mm(shares.astype(BF16), grads)
        dk_ref[span] += mm(ds, queries)
        dq_ref[here] = (head_diagonal(mm(k_ref[span], ds, 0, 0), heads) * 0.125).T.astype(BF16)

    def to_norm(here):
        return mm(dk_ref[here].astype(BF16), weight(1)) + mm(dv_ref[here].astype(BF16), weight(2))

    for chain in chains[:3]:
        chain.run(1)
    for load in loads[5:8]:
        load.wait()
    reaching = HALO // BLOCK
    for b in range(reaching):
        attend_back(b)
    halo_out[...] = to_norm(slice(HALO - REACH, HALO)).astype(BF16)

    @pl.when(z > 0)
    def _():
        halo_copy(z - 1).start()

    first_flows((3, 2))
    for b in range(reaching, blocks):
        attend_back(b)
    dq = dq_ref[...]
    dk, dv = dk_ref[...].astype(BF16), dv_ref[...].astype(BF16)
    for load in loads[8:]:
        load.wait()
    n1 = n1_ref[...]
    keep(0, mm(dq, n1[HALO:], 0, 0))
    keep(1, mm(dk, n1, 0, 0))
    keep(2, mm(dv, n1, 0, 0))
    keep(3, mm(att_ref[...], sent, 0, 0))
    own_chain.run(0)
    small[9:10] = column_sums(dq.astype(F32))
    small[10:11] = column_sums(dv.astype(F32))
    dn = to_norm(slice(HALO, HALO + rows)) + mm(dq, weight(0))
    xhat, scale = normed(x_ref[...].astype(F32))
    own_chain.run(1)

    @pl.when(z < parts - 1)
    def _():
        halo_copy(z + 1).wait_recv()

    @pl.when(z == parts - 1)
    def _():
        halo_land[...] = jnp.zeros_like(halo_land)

    dn = jnp.concatenate([dn[: rows - REACH], dn[rows - REACH :] + halo_land[...].astype(F32)], axis=0)
    small[0:1] = column_sums(dn * xhat)
    small[3:4] = column_sums(dn)
    total = Total(d, z, bits, total_buffer, total_wide, total_sems, wide_sems)
    total.run(0)
    input_out[...] = grad + norm_back(dn, gain[0:1], xhat, scale)
    for chain in chains[:3]:
        chain.run(2)
    next_flow(1)
    own_chain.run(2)
    for chain in chains[:3]:
        chain.run(3)
    total.run(1)
    own_chain.run(3)
    next_flow(0)
    for chain in chains[:3]:
        chain.run(4)
    total.run(2)
    own_chain.run(4)
    for p in range(5, 7):
        for chain in chains:
            chain.run(p)

    @pl.when(z == 0)
    def _():
        up_land[:PIECES] = jnp.zeros((PIECES, piece, width), BF16)

    @pl.when(z == parts - 1)
    def _():
        down_land[:PIECES] = jnp.zeros((PIECES, piece, width), BF16)

    for i in range(PIECES):
        for up in (True, False):
            j = i if up else PIECES - 1 - i

            @pl.when(comes(j, up))
            def _():
                flow_arrival(j, up).wait_recv()

        mine = own[rows_of(z * PIECES + i)].astype(F32)
        sides = up_land[i].astype(F32) + down_land[PIECES - 1 - i].astype(F32)
        mgrad_out[i * piece : (i + 1) * piece] = (mine + sides).astype(BF16)
    total.finish(small_out)
    for chain in chains:
        chain.close()

    @pl.when(z > 0)
    def _():
        halo_copy(z - 1).wait_send()

    for j in range(window):
        for up in (True, False):
            @pl.when(crosses(j, up))
            def _():
                flow(j, up, False).wait_send()


def finals(
    mgrad, input_grad, fself, fcross, finner, fouter, small,
    out_mgrad, out_input, out_gain, out_shift, out_sw, out_sb, out_so, out_soff,
    out_cw, out_cb, out_co, out_coff, out_inner, out_ib, out_outer, out_ooff,
):
    z = lax.axis_index("mp")
    own = out_so.shape[0]
    parts = out_so.shape[1] // own
    out_mgrad[...] = mgrad[...].astype(F32)
    out_input[...] = input_grad[...]
    out_gain[...] = small[0:3]
    out_shift[...] = small[3:6]
    out_soff[...] = small[6:7]
    out_coff[...] = small[7:8]
    out_ooff[...] = small[8:9]

    def chosen(row, size, offset):
        pieces = [small[row : row + 1, offset + o * size : offset + (o + 1) * size] for o in range(parts)]
        result = pieces[0]
        for o in range(1, parts):
            result = jnp.where(z == o, pieces[o], result)
        return result

    for fin, weights, last, biases, first in (
        (fself, out_sw, out_so, out_sb, 9),
        (fcross, out_cw, out_co, out_cb, 11),
    ):
        for i in range(3):
            weights[i] = fin[i // 2, i % 2].reshape(own, -1).astype(F32)
        last[...] = fin[1, 1].reshape(own, -1).astype(F32)
        for i in range(2):
            for half in range(2):
                lanes = slice(half * HALF, (half + 1) * HALF)
                biases[i : i + 1, lanes] = chosen(first + i, HALF, half * parts * HALF)
    out_inner[...] = finner[...].reshape(out_outer.shape).astype(F32).T
    out_outer[...] = fouter[...].reshape(out_outer.shape).astype(F32)
    size = out_ib.shape[1] // SLICES
    for s in range(SLICES):
        out_ib[0:1, s * size : (s + 1) * size] = chosen(16 + s, size, 0)


def call(body, outs, ins, scratch, limit, **params):
    places = {"s": pltpu.SMEM, "v": pltpu.VMEM, "h": pl.ANY}

    def spec(place):
        return pl.BlockSpec(memory_space=places[place])

    def run(*args):
        return pl.pallas_call(
            body,
            out_shape=[jax.ShapeDtypeStruct(shape, kind) for shape, kind, _ in outs],
            in_specs=[spec(place) for place in ins],
            out_specs=[spec(place) for _, _, place in outs],
            scratch_shapes=[pltpu.VMEM(*x) if isinstance(x, tuple) else x for x in scratch],
            compiler_params=pltpu.CompilerParams(vmem_limit_bytes=limit << 20, **params),
        )(*args)

    return run


def shards(
    block_input,
    memory,
    tok_lengths,
    frame_lengths,
    cotangent,
    norm_gain,
    norm_shift,
    self_weights,
    self_biases,
    self_output,
    self_offset,
    cross_weights,
    cross_biases,
    cross_output,
    cross_offset,
    inner_weight,
    inner_bias,
    outer_weight,
    outer_offset,
):
    rows, width = block_input.shape
    parts = lax.axis_size("mp")
    frames = memory.shape[0] * parts
    heads = width // HEAD
    blocks = rows // BLOCK
    own_hidden = inner_weight.shape[1]
    hidden = own_hidden * parts
    own = width // parts
    dma = pltpu.SemaphoreType.DMA
    wide = heads * BLOCK

    n_att, n_ffn = own * 4 // SLICES, own_hidden // SLICES
    n_bits = lax.axis_size("dp").bit_length() - 1
    piece = memory.shape[0] // PIECES
    small_rows = 16 + SLICES
    own_rows = (rows, width)
    halo_rows = (rows + HALO, width)

    def sliced(n):
        return (2, 2, 2, n, width)

    def turned(weights):
        return jnp.swapaxes(weights, 1, 2)

    (
        wself, wcross, inner, outer, inner_row, value_row, segment_rows, bounds, far, memory_rows, ck, cv, spare, n1, q, k, v, att, after, cq
    ) = call(
        gather,
        [
            (sliced(parts * n_att), BF16, "h"),
            (sliced(parts * n_att), BF16, "h"),
            (sliced(parts * n_ffn), BF16, "h"),
            (sliced(parts * n_ffn), BF16, "h"),
            ((SLICES, hidden // SLICES), F32, "v"),
            ((1, width), F32, "v"),
            ((2, rows), jnp.int32, "v"),
            ((3, 128), jnp.int32, "v"),
            ((1, 1), F32, "v"),
            ((frames, width), BF16, "h"),
            ((frames, width), BF16, "h"),
            ((frames, width), BF16, "h"),
            ((parts * frames, width), BF16, "h"),
            (halo_rows, BF16, "h"),
            (own_rows, BF16, "h"),
            (halo_rows, BF16, "h"),
            (halo_rows, BF16, "h"),
            (own_rows, BF16, "h"),
            (own_rows, F32, "h"),
            (own_rows, BF16, "h"),
        ],
        "ssvhvvvvvvvvvvvv",
        [
            (halo_rows, BF16),
            (own_rows, BF16),
            (halo_rows, BF16),
            (halo_rows, BF16),
            (own_rows, BF16),
            (own_rows, F32),
            (own_rows, BF16),
            (sliced(parts * n_att), BF16),
            (sliced(parts * n_att), BF16),
            (sliced(parts * n_ffn), BF16),
            (sliced(parts * n_ffn), BF16),
            ((frames, width), BF16),
            ((frames, width), BF16),
            ((frames, width), BF16),
            ((4 * own, width), BF16),
            ((4 * own, width), BF16),
            ((own_hidden, width), BF16),
            ((HALO, width), BF16),
            ((8, 128), F32),
            ((parts, 8, 128), F32),
            ((n_bits + 1, 8, 128), F32),
            ((n_bits, 8, 128), F32),
            dma((4, 2, 3)),
            dma((4, NEAR)),
            dma((4, 2, 3)),
            dma((2, 3)),
            dma((2,)),
            dma((2, n_bits)),
            dma,
            dma((parts * PIECES, 3)),
            dma((4,)),
            dma((7,)),
        ],
        56,
        collective_id=0,
        has_side_effects=True,
    )(
        tok_lengths, frame_lengths, block_input, memory, turned(self_weights), self_output,
        turned(cross_weights), cross_output, inner_weight, outer_weight, self_biases, cross_biases,
        inner_bias.reshape(1, own_hidden), norm_gain, norm_shift, self_offset.reshape(1, width),
    )
    wcross_rows = wcross.reshape(4 * width, width)
    wself_rows = wself.reshape(4 * width, width)
    inner_rows, outer_rows = inner.reshape(hidden, width), outer.reshape(hidden, width)

    def reduce_buffers(n):
        full = parts * n
        return [
            pltpu.VMEM((2, 2, full, width), BF16),
            pltpu.VMEM((2, 2, full, width), BF16),
            pltpu.VMEM((3, full, width), BF16),
            pltpu.VMEM((parts // 2, 2, n, width), BF16),
            pltpu.VMEM((3, n, width), BF16),
            pltpu.VMEM((2, n, width), BF16),
            pltpu.VMEM((2 * max(n_bits - 3, 1), n, width), F32),
        ]

    window = PIECES * (parts - 1)
    far_shape = (2, window - NEAR, piece, width)
    beyond = far[0, 0] > NEAR * piece

    def fetch_far():
        (far_memory,) = call(
            gather_far,
            [((parts * frames, width), BF16, "h")],
            "h",
            [dma((4, window))],
            8,
            collective_id=2,
            has_side_effects=True,
        )(memory_rows)
        return far_memory

    far_memory = lax.cond(beyond, fetch_far, lambda: spare)
    padded = (frames + SIZES[0], width)
    grad, small, block_output, mgrad, dw_cross, dwi, dwo = call(
        middle,
        [
            (own_rows, F32, "v"),
            ((small_rows, width), F32, "v"),
            (own_rows, F32, "h"),
            ((frames, width), BF16, "h"),
            ((4 * width, width), BF16, "h"),
            ((hidden, width), BF16, "h"),
            ((hidden, width), BF16, "h"),
        ],
        "ssvvvvvvvvhhhhhhhhh",
        [
            (own_rows, F32),
            (own_rows, BF16),
            ((4 * width, width), BF16),
            (own_rows, F32),
            (padded, BF16),
            (padded, BF16),
            (padded, BF16),
            ((hidden, width), BF16),
            ((hidden, width), BF16),
            (padded, BF16),
            ((2, width, width), F32),
            ((4 * width, width), BF16),
            ((hidden, width), BF16),
            ((hidden, width), BF16),
            ((blocks, wide, width), BF16),
            ((blocks, wide, width), BF16),
            ((blocks, 1, wide), F32),
            ((blocks, 1, wide), F32),
            ((blocks, width, BLOCK), F32),
            ((blocks, width, BLOCK), F32),
            (padded, F32),
            (padded, F32),
            ((blocks, 1, BLOCK), jnp.int32),
            ((blocks, 1, BLOCK), jnp.int32),
            dma((5,)),
            dma((5,)),
            dma((3, frames // UNIT)),
            dma((3,)),
        ],
        56,
    )(
        far, bounds, cq, segment_rows, inner_row, value_row, norm_gain,
        norm_shift, cross_offset.reshape(1, width), outer_offset.reshape(1, width),
        after, cotangent, wcross_rows, ck, cv, memory_rows, far_memory, inner_rows, outer_rows,
    )

    def return_far():
        (summed,) = call(
            sum_far,
            [((frames, width), BF16, "h")],
            "h",
            [((frames, width), BF16), (far_shape, BF16), dma((4, window - NEAR)), dma],
            16,
            collective_id=3,
            has_side_effects=True,
        )(mgrad)
        return summed

    mgrad = lax.cond(beyond, return_far, lambda: mgrad)
    partial_results = call(
        functools.partial(give_back, NEAR),
        [
            (own_rows, F32, "v"),
            ((frames // parts, width), BF16, "v"),
            (sliced(n_att), BF16, "v"),
            (sliced(n_att), BF16, "v"),
            (sliced(n_ffn), BF16, "v"),
            (sliced(n_ffn), BF16, "v"),
            ((small_rows, width), F32, "v"),
        ],
        "ssvvhhhhhhhhhhhh",
        [
            (own_rows, BF16),
            (halo_rows, BF16),
            (own_rows, BF16),
            (halo_rows, BF16),
            (halo_rows, BF16),
            (own_rows, BF16),
            (own_rows, F32),
            ((4 * width, width), BF16),
            ((frames, width), BF16),
            ((NEAR, piece, width), BF16),
            ((NEAR, piece, width), BF16),
            (sliced(parts * n_att), BF16),
            (sliced(parts * n_att), BF16),
            (sliced(parts * n_ffn), BF16),
            (sliced(parts * n_ffn), BF16),
            (halo_rows, F32),
            (halo_rows, F32),
            (own_rows, BF16),
            ((REACH, width), BF16),
            ((REACH, width), BF16),
            ((2, 2, 2, small_rows, width), F32),
            ((2 * (n_bits - 1), small_rows, width), F32),
            reduce_buffers(n_att),
            reduce_buffers(n_att),
            reduce_buffers(n_ffn),
            reduce_buffers(n_ffn),
            dma((12,)),
            dma((4, NEAR)),
            dma((4, 2, 6)),
            dma((4, 2, max(n_bits - 3, 1))),
            dma((4, 2, 8)),
            dma((2,)),
            dma((2, 8)),
            dma((2, n_bits - 1)),
        ],
        56,
        collective_id=1,
        has_side_effects=True,
    )(
        tok_lengths, frame_lengths, small, norm_gain, block_input, n1, q, k, v, att, grad, wself_rows,
        mgrad, dw_cross.reshape(sliced(parts * n_att)), dwi.reshape(sliced(parts * n_ffn)),
        dwo.reshape(sliced(parts * n_ffn)),
    )
    input_grad, mgrad_sum, fself, fcross, finner, fouter, small = partial_results
    results = call(
        finals,
        [
            ((frames // parts, width), F32, "v"),
            (own_rows, F32, "v"),
            ((3, width), F32, "v"),
            ((3, width), F32, "v"),
            ((3, own, width), F32, "v"),
            ((2, own), F32, "v"),
            ((own, width), F32, "v"),
            ((1, width), F32, "v"),
            ((3, own, width), F32, "v"),
            ((2, own), F32, "v"),
            ((own, width), F32, "v"),
            ((1, width), F32, "v"),
            ((width, own_hidden), F32, "v"),
            ((1, own_hidden), F32, "v"),
            ((own_hidden, width), F32, "v"),
            ((1, width), F32, "v"),
        ],
        "vvvvvvv",
        [],
        56,
    )(mgrad_sum, input_grad, fself, fcross, finner, fouter, small)
    memory_grad, input_grad, *others = results
    others = [r.reshape(-1) if r.shape[0] == 1 else r for r in others]
    others[2], others[6] = turned(others[2]), turned(others[6])
    return (block_output, input_grad, memory_grad, *others)


def solution(mesh):
    in_specs = (
        P(("dp", "mp"), None),
        P(("dp", "mp"), None),
        P("dp", None),
        P("dp", None),
        P(("dp", "mp"), None),
        P(),
        P(),
        P(None, None, "mp"),
        P(None, "mp"),
        P("mp", None),
        P(),
        P(None, None, "mp"),
        P(None, "mp"),
        P("mp", None),
        P(),
        P(None, "mp"),
        P("mp"),
        P("mp", None),
        P(),
    )
    out_specs = (
        P(("dp", "mp"), None),
        P(("dp", "mp"), None),
        P(("dp", "mp"), None),
        P(),
        P(),
        P(None, None, "mp"),
        P(None, "mp"),
        P("mp", None),
        P(),
        P(None, None, "mp"),
        P(None, "mp"),
        P("mp", None),
        P(),
        P(None, "mp"),
        P("mp"),
        P("mp", None),
        P(),
    )
    return jax.shard_map(shards, mesh=mesh, in_specs=in_specs, out_specs=out_specs, check_vma=False)
```
